32 devices in a mesh: parts: 2 (over x), gx: 4 (over y, core), gy: 4 (over z).
Axes of the slice: x: 2, y: 2, z: 4, core: 2. Of those that a mesh axis runs over, the one named last changes fastest.
Arguments:
- forcing_right_side: float32 [32, 32, 1024], P(('parts', 'gx'), 'gy'), parts along dimension 0, may hold values from -18 to 18
- earlier_warmth: float32 [32, 32, 1024], P(('parts', 'gx'), 'gy'), parts along dimension 0, may hold values from 0 to 2
- matter_condition: int32 [32, 32, 1024], P(('parts', 'gx'), 'gy'), parts along dimension 0, may hold values from 0 to 2
- compressed_slot_number: int32 [32, 32, 1024], P(('parts', 'gx'), 'gy'), parts along dimension 0, may hold values from 0 to 127
- normal_draw_factor: float32 [32, 32, 1024], P(('parts', 'gx'), 'gy'), parts along dimension 0, may hold values from -6 to 6
Outputs:
- solution: float32 [32, 32, 1024], P(('parts', 'gx'), 'gy'), parts along dimension 0
- residual: float32 [32, 32, 1024], P(('parts', 'gx'), 'gy'), parts along dimension 0
The draws below stay inside these ranges and needn't reach their ends.
There are 2 independent parts, one for each index of `parts`. The reference program is written for one: setup_inputs(seed, part) draws one part's arguments, and reference() takes and returns one part's arrays. A program takes and returns all parts, laid end to end along the dimension named above; each array names one. Nothing has to cross between parts.
Inputs may be any that keep to these rules, and one draw needn't show every extreme that they name: `matter_condition`: phase labels the cell as powder, solid or liquid. `compressed_slot_number`: each cell's row of the sketch.
All inputs are finite; a program needn't handle non-finite values.
Results may differ from the reference program's by a relative error of at most 0.0003.
Values sent between devices are 32-bit elements; how exact they have to be, the bound alone decides.
No kernel may reach another device: no remote copies, remote signals or barrier semaphores. Data moves between devices by JAX's collectives and lax.ppermute only.
A program may use at most 64 MiB of HBM per device.

```python
import jax
import jax.numpy as jnp
from jax import lax

MESH_SPAN_UPWARD = 1024
BASIS = 2
CYCLES = 1
SKETCH = 128
MESH_SPAN_EAST = 16
MESH_SPAN_NORTH = 32


def set_ends(entries, rng, low, largest):
    place = [jax.random.randint(jax.random.fold_in(rng, axis), (), 0, length) for axis, length in enumerate(entries.shape)]
    widest = entries.shape.index(max(entries.shape))
    next_to = place[:widest] + [(place[widest] + 1) % entries.shape[widest]] + place[widest + 1:]
    return entries.at[tuple(place)].set(low).at[tuple(next_to)].set(largest)


def steps_of(key, dims, shards, low, top_value):
    factor_of, own = 1.0, jax.random.fold_in(key, 6)
    for axis_at, blocks in shards:
        steps = jnp.exp(jax.random.uniform(jax.random.fold_in(own, axis_at), (blocks,), jnp.float32, low / len(shards), top_value / len(shards)))
        factor_of = factor_of * jnp.repeat(steps, dims[axis_at] // blocks).reshape([-1 if axis == axis_at else 1 for axis in range(len(dims))])
    return factor_of


def gaussian(rng, dims, spread, limit, shards=(), kind=jnp.bfloat16):
    factor_of = steps_of(rng, dims, shards, -0.22, 0.18) if shards else 1.0
    entries = jax.random.normal(rng, dims, jnp.float32) * spread * factor_of
    return jnp.minimum(jnp.maximum(entries, -limit), limit).astype(kind)


def setup_inputs(seed: int = 0, part: int = 0) -> dict:
    key_list = jax.random.split(jax.random.key(seed), 6)
    part_splits = jax.random.split(jax.random.fold_in(key_list[5], part), 6)
    forcing_right_side = gaussian(part_splits[0], (MESH_SPAN_EAST, MESH_SPAN_NORTH, MESH_SPAN_UPWARD), 3.0, 18.0, ((0, 4), (1, 4)), jnp.float32)
    earlier_warmth = jnp.clip(2.0 * jax.random.uniform(part_splits[1], (MESH_SPAN_EAST, MESH_SPAN_NORTH, MESH_SPAN_UPWARD), jnp.float32) ** steps_of(part_splits[1], (MESH_SPAN_EAST, MESH_SPAN_NORTH, MESH_SPAN_UPWARD), ((0, 4), (1, 4)), -0.2, 0.2), 0.0, 2.0)
    matter_condition = set_ends(jax.random.randint(part_splits[2], (MESH_SPAN_EAST, MESH_SPAN_NORTH, MESH_SPAN_UPWARD), 0, 3), jax.random.fold_in(part_splits[2], 1), 0, 2).astype(jnp.int32)
    compressed_slot_number = set_ends(jax.random.randint(part_splits[3], (MESH_SPAN_EAST, MESH_SPAN_NORTH, MESH_SPAN_UPWARD), 0, SKETCH), jax.random.fold_in(part_splits[3], 1), 0, SKETCH - 1).astype(jnp.int32)
    normal_draw_factor = gaussian(part_splits[4], (MESH_SPAN_EAST, MESH_SPAN_NORTH, MESH_SPAN_UPWARD), 1.0, 6.0, ((0, 4), (1, 4)), jnp.float32)
    return {"forcing_right_side": forcing_right_side, "earlier_warmth": earlier_warmth, "matter_condition": matter_condition, "compressed_slot_number": compressed_slot_number, "normal_draw_factor": normal_draw_factor}


epsilon = 1e-06
highest = lax.Precision.HIGHEST

def medium_traits(earlier_warmth, matter_condition):
    datum_offset = jnp.where(matter_condition == 0, 0.2, jnp.where(matter_condition == 1, 1.0, 0.6)).astype(jnp.float32)
    spreading_rate = datum_offset * (0.5 + earlier_warmth)
    volumetric_retention = jnp.where(matter_condition == 0, 1.0, jnp.where(matter_condition == 1, 2.0, 1.5)).astype(jnp.float32)
    return (spreading_rate, volumetric_retention)

def harmonic(first, second):
    return 2.0 * first * second / (first + second)

def shifted(field):
    padded = jnp.pad(field, 1)
    return [padded[2:, 1:-1, 1:-1], padded[:-2, 1:-1, 1:-1], padded[1:-1, 2:, 1:-1], padded[1:-1, :-2, 1:-1], padded[1:-1, 1:-1, 2:], padded[1:-1, 1:-1, :-2]]

def operate(field, volumetric_retention, links):
    result = volumetric_retention * field
    for conductance, neighbour in zip(links, shifted(field)):
        result = result + conductance * (field - neighbour)
    return result

def solve_small(hess, scale_norm):
    width_count = hess.shape[1]
    gram_matrix = jnp.dot(hess.T, hess, precision=highest)
    target = scale_norm * hess[0]
    factor = jnp.linalg.cholesky(gram_matrix)
    forward = []
    for row_a in range(width_count):
        partial_sum = target[row_a]
        for prior in range(row_a):
            partial_sum = partial_sum - factor[row_a, prior] * forward[prior]
        forward.append(partial_sum / factor[row_a, row_a])
    backward = [None] * width_count
    for row_a in reversed(range(width_count)):
        partial_sum = forward[row_a]
        for later in range(row_a + 1, width_count):
            partial_sum = partial_sum - factor[later, row_a] * backward[later]
        backward[row_a] = partial_sum / factor[row_a, row_a]
    return backward

def reference(forcing_right_side, earlier_warmth, matter_condition, compressed_slot_number, normal_draw_factor):
    spreading_rate, volumetric_retention = medium_traits(earlier_warmth, matter_condition)
    links = [harmonic(spreading_rate, other) for other in shifted(spreading_rate)]

    def sketch_of(field):
        return jax.ops.segment_sum((normal_draw_factor * field).reshape(-1), compressed_slot_number.reshape(-1), num_segments=SKETCH)
    solution = jnp.zeros_like(forcing_right_side)
    residual = forcing_right_side
    for cycle_number in range(CYCLES):
        if cycle_number > 0:
            residual = forcing_right_side - operate(solution, volumetric_retention, links)
        sketched = sketch_of(residual)
        scale_norm = jnp.sqrt(jnp.sum(sketched * sketched) + epsilon)
        basis_list = [residual / scale_norm]
        sketch_list = [sketched / scale_norm]
        columns = []
        for column in range(BASIS):
            images = operate(basis_list[column], volumetric_retention, links)
            image_sketch = sketch_of(images)
            stacked = jnp.stack(sketch_list, axis=1)
            coeffs = jnp.dot(stacked.T, image_sketch, precision=highest)
            reduced = images
            for prior in range(column + 1):
                reduced = reduced - coeffs[prior] * basis_list[prior]
            remainder = sketch_of(reduced)
            norm_next = jnp.sqrt(jnp.sum(remainder * remainder) + epsilon)
            columns.append(jnp.concatenate([coeffs, norm_next[None], jnp.zeros((BASIS - column - 1,), coeffs.dtype)]))
            if column + 1 < BASIS:
                basis_list.append(reduced / norm_next)
                sketch_list.append(remainder / norm_next)
        hess = jnp.stack(columns, axis=1)
        weights = solve_small(hess, scale_norm)
        for prior in range(BASIS):
            solution = solution + weights[prior] * basis_list[prior]
    residual = forcing_right_side - operate(solution, volumetric_retention, links)
    return (solution, residual)
```

```python
import functools

import jax
import jax.numpy as jnp
from jax import lax
from jax.experimental import pallas as pl
from jax.experimental.pallas import tpu as pltpu
from jax.sharding import PartitionSpec as P

SKETCH = 128
FIELDS = 3
LANES = 128
epsilon = 1e-06
roomy = pltpu.CompilerParams(vmem_limit_bytes=48 * 1024 * 1024)


def traits(warmth, phase):
    powder, solid = phase == 0, phase == 1
    offset = jnp.where(powder, 0.2, jnp.where(solid, 1.0, 0.6))
    return offset * (0.5 + warmth), jnp.where(powder, 1.0, jnp.where(solid, 2.0, 1.5))


def link(first, second):
    total = first + second
    return 2.0 * first * second / jnp.where(total > 0.0, total, 1.0)


def ahead(plane, axis):
    return pltpu.roll(plane, plane.shape[axis] - 1, axis)


def inner_links(cond):
    links = []
    for axis in (0, 1):
        index = lax.broadcasted_iota(jnp.int32, cond.shape, axis)
        links.append(
            jnp.where(index < cond.shape[axis] - 1, link(cond, ahead(cond, axis)), 0.0)
        )
    return links


def inner_flow(field, links):
    total = None
    for axis in (0, 1):
        flow = links[axis] * (field - ahead(field, axis))
        part = flow - pltpu.roll(flow, 1, axis)
        total = part if total is None else total + part
    return total


def first_kernel(b_ref, warmth_ref, phase_ref, cond_ref, inner_ref, down_ref, up_ref):
    planes = b_ref.shape[0]
    images, conds, before = [], [], None
    for i in range(planes):
        cond, cap = traits(warmth_ref[i], phase_ref[i])
        field = b_ref[i]
        image = cap * field + inner_flow(field, inner_links(cond))
        if i:
            flow = link(conds[-1], cond) * (b_ref[i - 1] - field)
            images[-1] = images[-1] + flow
            image = image - flow
        conds.append(cond)
        images.append(image)
    for i in range(planes):
        cond_ref[i] = conds[i]
        inner_ref[i] = images[i]
    for ref, i in ((down_ref, 0), (up_ref, planes - 1)):
        ref[0] = images[i]
        ref[1] = b_ref[i]
        ref[2] = conds[i]


def second_kernel(b_ref, cond_ref, inner_ref, low_ref, high_ref, wide_ref, down_ref, up_ref):
    planes, rows = b_ref.shape[0], b_ref.shape[1]
    low_flow = link(low_ref[2], cond_ref[0]) * (low_ref[1] - b_ref[0])
    high_flow = link(cond_ref[planes - 1], high_ref[2]) * (b_ref[planes - 1] - high_ref[1])
    images = [low_ref[0] + low_flow] + [inner_ref[i] for i in range(planes)]
    images.append(high_ref[0] - high_flow)
    images[1] = images[1] - low_flow
    images[planes] = images[planes] + high_flow
    for i in range(planes + 2):
        wide_ref[i] = images[i]
    for ref, row in ((down_ref, 0), (up_ref, rows - 1)):
        at = slice(row, row + 1)
        for i in range(planes):
            ref[i : i + 1] = images[i + 1][at]
        for base, own, which in ((planes, b_ref, 1), (2 * planes + 2, cond_ref, 2)):
            ref[base : base + 1] = low_ref[which, at]
            for i in range(planes):
                ref[base + 1 + i : base + 2 + i] = own[i, at]
            ref[base + planes + 1 : base + planes + 2] = high_ref[which, at]


def third_kernel(
    b_ref, cond_ref, phase_ref, slot_ref, draw_ref, wide_ref, xlow_ref, xhigh_ref, ylow_ref,
    yhigh_ref, image_ref, twice_ref, sketch_ref, cells_ref,
):
    planes, rows, depth = b_ref.shape
    index = lax.broadcasted_iota(jnp.int32, (rows, depth), 0)
    first, last = index == 0, index == rows - 1

    b_wide = [xlow_ref[1]] + [b_ref[i] for i in range(planes)] + [xhigh_ref[1]]
    c_wide = [xlow_ref[2]] + [cond_ref[i] for i in range(planes)] + [xhigh_ref[2]]
    images, edge_links, edge_values = [], [], []
    for i in range(planes + 2):
        image = wide_ref[i]
        links, values = [], []
        for ref, mask in ((ylow_ref, first), (yhigh_ref, last)):
            base = planes + i
            b_side = jnp.broadcast_to(ref[base : base + 1], (rows, depth))
            base = 2 * planes + 2 + i
            c_side = jnp.broadcast_to(ref[base : base + 1], (rows, depth))
            conductance = jnp.where(mask, link(c_wide[i], c_side), 0.0)
            flow = conductance * (b_wide[i] - b_side)
            image = image + flow
            if 0 < i <= planes:
                beyond = jnp.broadcast_to(ref[i - 1 : i], (rows, depth))
                values.append(beyond - flow)
                links.append(conductance)
        images.append(image)
        edge_links.append(links)
        edge_values.append(values)

    flow_low = link(c_wide[0], c_wide[1]) * (images[0] - images[1])
    for i in range(1, planes + 1):
        unused, cap = traits(0.0, phase_ref[i - 1])
        image = images[i]
        flow = link(c_wide[i], c_wide[i + 1]) * (image - images[i + 1])
        twice = cap * image + inner_flow(image, inner_links(c_wide[i])) + (flow - flow_low)
        flow_low = flow
        for conductance, value in zip(edge_links[i], edge_values[i]):
            twice = twice + conductance * (image - value)
        image_ref[i - 1] = image
        twice_ref[i - 1] = twice
        draw = draw_ref[i - 1]
        for f, field in enumerate((b_wide[i], image, twice)):
            weighted = draw * field
            for t in range(depth // LANES):
                cells_ref[t, pl.ds((i - 1) * rows * 8 + f, rows, stride=8), :] = weighted[
                    :, t * LANES : (t + 1) * LANES
                ]

    slots = lax.broadcasted_iota(jnp.int32, (SKETCH, depth), 0).astype(jnp.float32)
    slots = slots.astype(jnp.bfloat16)
    one = jnp.ones((SKETCH, depth), jnp.bfloat16)
    used = lax.broadcasted_iota(jnp.int32, (8, depth), 0) < FIELDS

    def add_row(r, total):
        at = pl.ds(pl.multiple_of(r * 8, 8), 8)
        cells = [cells_ref[t, at, :] for t in range(depth // LANES)]
        cells = jnp.where(used, jnp.concatenate(cells, axis=1), 0.0)
        coarse = cells.astype(jnp.bfloat16)
        fine = (cells - coarse.astype(jnp.float32)).astype(jnp.bfloat16)
        both = jnp.concatenate([coarse, fine], axis=0)
        ids = slot_ref[pl.ds(r, 1), :].astype(jnp.float32)
        ids = jnp.broadcast_to(ids, (SKETCH, depth)).astype(jnp.bfloat16)
        chosen = jnp.where(ids == slots, one, jnp.zeros_like(one))
        return total + lax.dot_general(
            both, chosen, (((1,), (1,)), ((), ())), preferred_element_type=jnp.float32
        )

    total = lax.fori_loop(
        0, planes * rows, add_row, jnp.zeros((16, SKETCH), jnp.float32), unroll=4
    )
    sketch_ref[...] = total[:8] + total[8:]


def last_kernel(sketch_ref, b_ref, image_ref, twice_ref, solution_ref, residual_ref):
    sketches = jnp.sum(sketch_ref[...], axis=0)

    def inner(first, second):
        return jnp.sum(first * second, axis=1, keepdims=True)

    s0, s1, s2 = (sketches[i : i + 1] for i in range(FIELDS))
    beta = jnp.sqrt(inner(s0, s0) + epsilon)
    q0 = s0 / beta
    p0 = s1 / beta
    h00 = inner(q0, p0)
    t0 = p0 - h00 * q0
    n0 = jnp.sqrt(inner(t0, t0) + epsilon)
    q1 = t0 / n0
    p1 = (s2 / beta - h00 * p0) / n0
    h01 = inner(q0, p1)
    h11 = inner(q1, p1)
    t1 = p1 - h01 * q0 - h11 * q1
    n1 = jnp.sqrt(inner(t1, t1) + epsilon)
    l00 = jnp.sqrt(h00 * h00 + n0 * n0)
    l10 = (h00 * h01 + n0 * h11) / l00
    l11 = jnp.sqrt(h01 * h01 + h11 * h11 + n1 * n1 - l10 * l10)
    z0 = beta * h00 / l00
    z1 = (beta * h01 - l10 * z0) / l11
    y1 = z1 / l11
    y0 = (z0 - l10 * y1) / l00
    c1 = y1 / (beta * n0)
    c0 = y0 / beta - h00 * c1
    for i in range(b_ref.shape[0]):
        b, image = b_ref[i], image_ref[i]
        solution_ref[i] = c0 * b + c1 * image
        residual_ref[i] = b - c0 * image - c1 * twice_ref[i]


def call(kernel, shapes, *operands, scratch=()):
    vmem = pl.BlockSpec(memory_space=pltpu.VMEM)
    return pl.pallas_call(
        kernel,
        out_shape=[jax.ShapeDtypeStruct(shape, jnp.float32) for shape in shapes],
        in_specs=[vmem] * len(operands),
        out_specs=[vmem] * len(shapes),
        scratch_shapes=scratch,
        compiler_params=roomy,
    )(*operands)


def swap(down, up, axis):
    count = lax.axis_size(axis)
    forward = [(i, i + 1) for i in range(count - 1)]
    backward = [(i + 1, i) for i in range(count - 1)]
    return lax.ppermute(up, axis, forward), lax.ppermute(down, axis, backward)


def everyones(sketch):
    count = lax.axis_size("gx") * lax.axis_size("gy")
    copies = jnp.broadcast_to(sketch[None], (count,) + sketch.shape)
    return lax.all_to_all(copies, ("gx", "gy"), 0, 0)


def body(b, warmth, phase, slots, draw):
    planes, rows, depth = b.shape
    block, plane, wide = b.shape, (3, rows, depth), (planes + 2, rows, depth)
    line = (3 * planes + 4, depth)
    cond, inner, down, up = call(first_kernel, [block, block, plane, plane], b, warmth, phase)
    xlow, xhigh = swap(down, up, "gx")
    image_wide, down, up = call(
        second_kernel, [wide, line, line], b, cond, inner, xlow, xhigh
    )
    ylow, yhigh = swap(down, up, "gy")
    image, twice, sketch = call(
        third_kernel,
        [block, block, (8, SKETCH)],
        b, cond, phase, slots.reshape(planes * rows, depth), draw, image_wide, xlow, xhigh,
        ylow, yhigh,
        scratch=[pltpu.VMEM((depth // LANES, planes * rows * 8, LANES), jnp.float32)],
    )
    return tuple(call(last_kernel, [block, block], everyones(sketch), b, image, twice))


def solution(mesh):
    spec = P(("parts", "gx"), "gy", None)
    return jax.shard_map(
        body, mesh=mesh, in_specs=(spec,) * 5, out_specs=(spec,) * 2, check_vma=False
    )
```

```python
import jax
import jax.numpy as jnp
from jax import lax
from jax.experimental import pallas as pl
from jax.experimental.pallas import tpu as pltpu
from jax.sharding import PartitionSpec as P

SKETCH = 128
LOW = 32
HIGH = SKETCH // LOW
FIELDS = 3
LANES = 128
epsilon = 1e-06


def traits(warmth, phase):
    powder, solid = phase == 0, phase == 1
    offset = jnp.where(powder, 0.2, jnp.where(solid, 1.0, 0.6))
    return offset * (0.5 + warmth), jnp.where(powder, 1.0, jnp.where(solid, 2.0, 1.5))


def link(first, second):
    total = first + second
    return 2.0 * first * second / jnp.where(total > 0.0, total, 1.0)


def ahead(plane, axis):
    return pltpu.roll(plane, plane.shape[axis] - 1, axis)


def inner_links(cond):
    links = []
    for axis in (0, 1):
        index = lax.broadcasted_iota(jnp.int32, cond.shape, axis)
        links.append(
            jnp.where(index < cond.shape[axis] - 1, link(cond, ahead(cond, axis)), 0.0)
        )
    return links


def inner_flow(field, links):
    total = None
    for axis in (0, 1):
        flow = links[axis] * (field - ahead(field, axis))
        part = flow - pltpu.roll(flow, 1, axis)
        total = part if total is None else total + part
    return total


def apply_inside(images, c_wide, caps):
    results = []
    flow_low = link(c_wide[0], c_wide[1]) * (images[0] - images[1])
    for i in range(1, len(images) - 1):
        image = images[i]
        flow = link(c_wide[i], c_wide[i + 1]) * (image - images[i + 1])
        results.append(
            caps[i - 1] * image + inner_flow(image, inner_links(c_wide[i])) + (flow - flow_low)
        )
        flow_low = flow
    return results


def sketch_rows(fields, draws, slots, chosen, cells_ref):
    rows, depth = draws[0].shape
    for i, draw in enumerate(draws):
        coarse, fine = [], []
        for field in fields:
            weighted = draw * field[i]
            head = weighted.astype(jnp.bfloat16).astype(jnp.float32)
            coarse.append(head)
            fine.append(weighted - head)
        for f, part in enumerate(coarse + coarse[:1] + fine + fine[:1]):
            for t in range(depth // LANES):
                cells_ref[t, pl.ds(i * rows * 8 + f, rows, stride=8), :] = part[
                    :, t * LANES : (t + 1) * LANES
                ]
    low_index = lax.broadcasted_iota(jnp.int32, (LOW, depth), 0)
    low_index = low_index.astype(jnp.float32).astype(jnp.bfloat16)
    high_index = lax.broadcasted_iota(jnp.int32, (HIGH * 8, depth), 0) // 8
    high_index = high_index.astype(jnp.float32).astype(jnp.bfloat16)
    total = jnp.zeros((HIGH * 8, LOW), jnp.float32)
    for i, slot in enumerate(slots):
        low = (slot & (LOW - 1)).astype(jnp.float32)
        high = (slot >> (LOW.bit_length() - 1)).astype(jnp.float32)
        left, right = [], []
        for j in chosen:
            at = pl.ds((i * rows + j) * 8, 8)
            cells = [cells_ref[t, at, :] for t in range(depth // LANES)]
            cells = jnp.concatenate(cells, axis=1)
            cells = jnp.concatenate([cells] * HIGH, axis=0).astype(jnp.bfloat16)
            row_high = jnp.broadcast_to(high[j : j + 1], cells.shape).astype(jnp.bfloat16)
            row_low = jnp.broadcast_to(low[j : j + 1], (LOW, depth)).astype(jnp.bfloat16)
            left.append(jnp.where(row_high == high_index, cells, jnp.zeros_like(cells)))
            right.append(
                jnp.where(row_low == low_index, jnp.ones_like(row_low), jnp.zeros_like(row_low))
            )
        total = total + lax.dot_general(
            jnp.concatenate(left, axis=1),
            jnp.concatenate(right, axis=1),
            (((1,), (1,)), ((), ())),
            preferred_element_type=jnp.float32,
        )
    parts = jnp.concatenate([total[h * 8 : h * 8 + 8] for h in range(HIGH)], axis=1)
    return parts + pltpu.roll(parts, 4, 0)


def first_kernel(
    b_hbm, warmth_hbm, phase_hbm, b_ref, cond_ref, cap_ref, inner_ref, down_ref, up_ref,
    warmth_ref, phase_ref, arrived,
):
    copies = [
        pltpu.make_async_copy(source, target, arrived.at[k])
        for k, (source, target) in enumerate(
            ((b_hbm, b_ref), (warmth_hbm, warmth_ref), (phase_hbm, phase_ref))
        )
    ]
    for copy in copies:
        copy.start()
    for copy in copies:
        copy.wait()
    planes = b_ref.shape[0]
    images, conds = [], []
    for i in range(planes):
        cond, cap = traits(warmth_ref[i], phase_ref[i])
        cap_ref[i] = cap
        cond_ref[i] = cond
        field = b_ref[i]
        image = cap * field + inner_flow(field, inner_links(cond))
        if i:
            flow = link(conds[-1], cond) * (b_ref[i - 1] - field)
            images[-1] = images[-1] + flow
            image = image - flow
        conds.append(cond)
        images.append(image)
    for i in range(planes):
        inner_ref[i] = images[i]
    for ref, i in ((down_ref, 0), (up_ref, planes - 1)):
        ref[0] = images[i]
        ref[1] = b_ref[i]
        ref[2] = conds[i]


def second_kernel(b_ref, cond_ref, inner_ref, low_ref, high_ref, wide_ref, down_ref, up_ref):
    planes, rows = b_ref.shape[0], b_ref.shape[1]
    low_flow = link(low_ref[2], cond_ref[0]) * (low_ref[1] - b_ref[0])
    high_flow = link(cond_ref[planes - 1], high_ref[2]) * (b_ref[planes - 1] - high_ref[1])
    images = [low_ref[0] + low_flow] + [inner_ref[i] for i in range(planes)]
    images.append(high_ref[0] - high_flow)
    images[1] = images[1] - low_flow
    images[planes] = images[planes] + high_flow
    for i in range(planes + 2):
        wide_ref[i] = images[i]
    for ref, row in ((down_ref, 0), (up_ref, rows - 1)):
        at = slice(row, row + 1)
        for i in range(planes):
            ref[i : i + 1] = images[i + 1][at]
        for base, own, which in ((planes, b_ref, 1), (2 * planes + 2, cond_ref, 2)):
            ref[base : base + 1] = low_ref[which, at]
            for i in range(planes):
                ref[base + 1 + i : base + 2 + i] = own[i, at]
            ref[base + planes + 1 : base + planes + 2] = high_ref[which, at]


def reached(rows):
    others = [j for j in range(rows) if 2 <= j < rows - 2]
    return [j for j in range(rows) if j not in others], others


def widened(ref, low_ref, high_ref, which):
    return [low_ref[which]] + [ref[i] for i in range(ref.shape[0])] + [high_ref[which]]


def inside_kernel(
    b_ref, cond_ref, cap_ref, slot_ref, draw_ref, wide_ref, xlow_ref, xhigh_ref, sketch_ref,
    cells_ref,
):
    planes = range(b_ref.shape[0])
    images = [wide_ref[i] for i in range(wide_ref.shape[0])]
    c_wide = widened(cond_ref, xlow_ref, xhigh_ref, 2)
    twice = apply_inside(images, c_wide, [cap_ref[i] for i in planes])
    sketch_ref[...] = sketch_rows(
        [[b_ref[i] for i in planes], images[1:-1], twice],
        [draw_ref[i] for i in planes],
        [slot_ref[i] for i in planes],
        reached(b_ref.shape[1])[1],
        cells_ref,
    )


def third_kernel(
    b_ref, cond_ref, cap_ref, slot_ref, draw_ref, wide_ref, xlow_ref, xhigh_ref, ylow_ref,
    yhigh_ref, inside_ref, image_ref, twice_ref, sketch_ref, cells_ref,
):
    planes, rows, depth = b_ref.shape
    index = lax.broadcasted_iota(jnp.int32, (rows, depth), 0)
    b_wide = widened(b_ref, xlow_ref, xhigh_ref, 1)
    c_wide = widened(cond_ref, xlow_ref, xhigh_ref, 2)
    images, beside = [], []
    for i in range(planes + 2):
        image = wide_ref[i]
        pairs = []
        for ref, mask in ((ylow_ref, index == 0), (yhigh_ref, index == rows - 1)):
            at = planes + i
            b_side = jnp.broadcast_to(ref[at : at + 1], (rows, depth))
            at = 2 * planes + 2 + i
            c_side = jnp.broadcast_to(ref[at : at + 1], (rows, depth))
            conductance = jnp.where(mask, link(c_wide[i], c_side), 0.0)
            flow = conductance * (b_wide[i] - b_side)
            image = image + flow
            if 0 < i <= planes:
                beyond = jnp.broadcast_to(ref[i - 1 : i], (rows, depth))
                pairs.append((conductance, beyond - flow))
        images.append(image)
        beside.append(pairs)
    twice = apply_inside(images, c_wide, [cap_ref[i] for i in range(planes)])
    for i in range(planes):
        for conductance, value in beside[i + 1]:
            twice[i] = twice[i] + conductance * (images[i + 1] - value)
        image_ref[i] = images[i + 1]
        twice_ref[i] = twice[i]
    sketch_ref[...] = inside_ref[...] + sketch_rows(
        [b_wide[1:-1], images[1:-1], twice],
        [draw_ref[i] for i in range(planes)],
        [slot_ref[i] for i in range(planes)],
        reached(rows)[0],
        cells_ref,
    )


def last_kernel(sketch_ref, b_ref, image_ref, twice_ref, solution_ref, residual_ref):
    sketches = jnp.sum(sketch_ref[...], axis=0)

    def inner(first, second):
        return jnp.sum(first * second, axis=1, keepdims=True)

    s0, s1, s2 = (sketches[i : i + 1] for i in range(FIELDS))
    beta = jnp.sqrt(inner(s0, s0) + epsilon)
    q0 = s0 / beta
    p0 = s1 / beta
    h00 = inner(q0, p0)
    t0 = p0 - h00 * q0
    n0 = jnp.sqrt(inner(t0, t0) + epsilon)
    q1 = t0 / n0
    p1 = (s2 / beta - h00 * p0) / n0
    h01 = inner(q0, p1)
    h11 = inner(q1, p1)
    t1 = p1 - h01 * q0 - h11 * q1
    n1 = jnp.sqrt(inner(t1, t1) + epsilon)
    l00 = jnp.sqrt(h00 * h00 + n0 * n0)
    l10 = (h00 * h01 + n0 * h11) / l00
    l11 = jnp.sqrt(h01 * h01 + h11 * h11 + n1 * n1 - l10 * l10)
    z0 = beta * h00 / l00
    z1 = (beta * h01 - l10 * z0) / l11
    y1 = z1 / l11
    y0 = (z0 - l10 * y1) / l00
    c1 = y1 / (beta * n0)
    c0 = y0 / beta - h00 * c1
    for i in range(b_ref.shape[0]):
        b, image = b_ref[i], image_ref[i]
        solution_ref[i] = c0 * b + c1 * image
        residual_ref[i] = b - c0 * image - c1 * twice_ref[i]


def call(kernel, shapes, *operands, scratch=(), inputs=pltpu.VMEM, flops=0):
    return pl.pallas_call(
        kernel,
        out_shape=[jax.ShapeDtypeStruct(shape, jnp.float32) for shape in shapes],
        in_specs=[pl.BlockSpec(memory_space=inputs)] * len(operands),
        out_specs=[pl.BlockSpec(memory_space=pltpu.VMEM)] * len(shapes),
        scratch_shapes=scratch,
        compiler_params=pltpu.CompilerParams(vmem_limit_bytes=48 * 1024 * 1024),
        cost_estimate=pl.CostEstimate(flops=flops, bytes_accessed=0, transcendentals=0),
    )(*operands)


def swap(down, up, axis):
    count = lax.axis_size(axis)
    forward = [(i, i + 1) for i in range(count - 1)]
    backward = [(i + 1, i) for i in range(count - 1)]
    return lax.ppermute(up, axis, forward), lax.ppermute(down, axis, backward)


def everyones(sketch, axis):
    copies = jnp.broadcast_to(sketch[None], (lax.axis_size(axis),) + sketch.shape)
    return lax.all_to_all(copies, axis, 0, 0)


def body(b, warmth, phase, slots, draw):
    planes, rows, depth = b.shape
    block, plane, wide = b.shape, (3, rows, depth), (planes + 2, rows, depth)
    line, table = (3 * planes + 4, depth), (8, SKETCH)
    cells = pltpu.VMEM((depth // LANES, planes * rows * 8, LANES), jnp.float32)
    work = b.size * SKETCH * 6
    b, cond, cap, inner, down, up = call(
        first_kernel,
        [block, block, block, block, plane, plane],
        *(pltpu.with_memory_space_constraint(x, pltpu.HBM) for x in (b, warmth, phase)),
        scratch=[
            pltpu.VMEM(block, warmth.dtype),
            pltpu.VMEM(block, phase.dtype),
            pltpu.SemaphoreType.DMA((3,)),
        ],
        inputs=pltpu.HBM,
    )
    xlow, xhigh = swap(down, up, "gx")
    image_wide, down, up = call(
        second_kernel, [wide, line, line], b, cond, inner, xlow, xhigh
    )
    ylow, yhigh = swap(down, up, "gy")
    (inside,) = call(
        inside_kernel,
        [table],
        b, cond, cap, slots, draw, image_wide, xlow, xhigh,
        scratch=[cells],
        flops=work,
    )
    image, twice, sketch = call(
        third_kernel,
        [block, block, table],
        b, cond, cap, slots, draw, image_wide, xlow, xhigh, ylow, yhigh, inside,
        scratch=[cells],
        flops=work,
    )
    sketch = jnp.sum(everyones(sketch, "gx"), axis=0)
    return tuple(call(last_kernel, [block, block], everyones(sketch, "gy"), b, image, twice))


def solution(mesh):
    spec = P(("parts", "gx"), "gy", None)
    return jax.shard_map(
        body, mesh=mesh, in_specs=(spec,) * 5, out_specs=(spec,) * 2, check_vma=False
    )
```

```python
import jax
import jax.numpy as jnp
from jax import lax
from jax.experimental import pallas as pl
from jax.experimental.pallas import tpu as pltpu
from jax.sharding import PartitionSpec as P

SKETCH = 128
LOW = 32
HIGH = SKETCH // LOW
FIELDS = 3
LANES = 128
epsilon = 1e-06


def traits(warmth, phase):
    powder, solid = phase == 0, phase == 1
    offset = jnp.where(powder, 0.2, jnp.where(solid, 1.0, 0.6))
    return offset * (0.5 + warmth), jnp.where(powder, 1.0, jnp.where(solid, 2.0, 1.5))


def link(first, second):
    total = first + second
    return 2.0 * first * second / jnp.where(total > 0.0, total, 1.0)


def ahead(plane, axis):
    return pltpu.roll(plane, plane.shape[axis] - 1, axis)


def inner_links(cond):
    links = []
    for axis in (0, 1):
        index = lax.broadcasted_iota(jnp.int32, cond.shape, axis)
        links.append(
            jnp.where(index < cond.shape[axis] - 1, link(cond, ahead(cond, axis)), 0.0)
        )
    return links


def inner_flow(field, links):
    total = None
    for axis in (0, 1):
        flow = links[axis] * (field - ahead(field, axis))
        part = flow - pltpu.roll(flow, 1, axis)
        total = part if total is None else total + part
    return total


def apply_inside(images, c_wide, caps):
    results = []
    flow_low = link(c_wide[0], c_wide[1]) * (images[0] - images[1])
    for i in range(1, len(images) - 1):
        image = images[i]
        flow = link(c_wide[i], c_wide[i + 1]) * (image - images[i + 1])
        results.append(
            caps[i - 1] * image + inner_flow(image, inner_links(c_wide[i])) + (flow - flow_low)
        )
        flow_low = flow
    return results


def sketch_rows(fields, draws, slots, chosen, cells_ref):
    rows, depth = draws[0].shape
    for i, draw in enumerate(draws):
        coarse, fine = [], []
        for field in fields:
            weighted = draw * field[i]
            head = weighted.astype(jnp.bfloat16).astype(jnp.float32)
            coarse.append(head)
            fine.append(weighted - head)
        for f, part in enumerate(coarse + coarse[:1] + fine + fine[:1]):
            for t in range(depth // LANES):
                cells_ref[t, pl.ds(i * rows * 8 + f, rows, stride=8), :] = part[
                    :, t * LANES : (t + 1) * LANES
                ]
    low_index = lax.broadcasted_iota(jnp.int32, (LOW, depth), 0)
    low_index = low_index.astype(jnp.float32).astype(jnp.bfloat16)
    high_index = lax.broadcasted_iota(jnp.int32, (HIGH * 8, depth), 0) // 8
    high_index = high_index.astype(jnp.float32).astype(jnp.bfloat16)
    total = jnp.zeros((HIGH * 8, LOW), jnp.float32)
    for i, slot in enumerate(slots):
        low = (slot & (LOW - 1)).astype(jnp.float32)
        high = (slot >> (LOW.bit_length() - 1)).astype(jnp.float32)
        left, right = [], []
        for j in chosen:
            at = pl.ds((i * rows + j) * 8, 8)
            cells = [cells_ref[t, at, :] for t in range(depth // LANES)]
            cells = jnp.concatenate(cells, axis=1)
            cells = jnp.concatenate([cells] * HIGH, axis=0).astype(jnp.bfloat16)
            row_high = jnp.broadcast_to(high[j : j + 1], cells.shape).astype(jnp.bfloat16)
            row_low = jnp.broadcast_to(low[j : j + 1], (LOW, depth)).astype(jnp.bfloat16)
            left.append(jnp.where(row_high == high_index, cells, jnp.zeros_like(cells)))
            right.append(
                jnp.where(row_low == low_index, jnp.ones_like(row_low), jnp.zeros_like(row_low))
            )
        total = total + lax.dot_general(
            jnp.concatenate(left, axis=1),
            jnp.concatenate(right, axis=1),
            (((1,), (1,)), ((), ())),
            preferred_element_type=jnp.float32,
        )
    parts = jnp.concatenate([total[h * 8 : h * 8 + 8] for h in range(HIGH)], axis=1)
    return parts + pltpu.roll(parts, 4, 0)


def first_kernel(
    b_hbm, warmth_hbm, phase_hbm, b_ref, cond_ref, cap_ref, inner_ref, down_ref, up_ref,
    warmth_ref, phase_ref, arrived,
):
    copies = [
        pltpu.make_async_copy(source, target, arrived.at[k])
        for k, (source, target) in enumerate(
            ((b_hbm, b_ref), (warmth_hbm, warmth_ref), (phase_hbm, phase_ref))
        )
    ]
    for copy in copies:
        copy.start()
    for copy in copies:
        copy.wait()
    planes = b_ref.shape[0]
    images, conds = [], []
    for i in range(planes):
        cond, cap = traits(warmth_ref[i], phase_ref[i])
        cap_ref[i] = cap
        cond_ref[i] = cond
        field = b_ref[i]
        image = cap * field + inner_flow(field, inner_links(cond))
        if i:
            flow = link(conds[-1], cond) * (b_ref[i - 1] - field)
            images[-1] = images[-1] + flow
            image = image - flow
        conds.append(cond)
        images.append(image)
    for i in range(planes):
        inner_ref[i] = images[i]
    for ref, i in ((down_ref, 0), (up_ref, planes - 1)):
        ref[0] = images[i]
        ref[1] = b_ref[i]
        ref[2] = conds[i]


def second_kernel(b_ref, cond_ref, inner_ref, low_ref, high_ref, wide_ref, down_ref, up_ref):
    planes, rows = b_ref.shape[0], b_ref.shape[1]
    low_flow = link(low_ref[2], cond_ref[0]) * (low_ref[1] - b_ref[0])
    high_flow = link(cond_ref[planes - 1], high_ref[2]) * (b_ref[planes - 1] - high_ref[1])
    images = [low_ref[0] + low_flow] + [inner_ref[i] for i in range(planes)]
    images.append(high_ref[0] - high_flow)
    images[1] = images[1] - low_flow
    images[planes] = images[planes] + high_flow
    for i in range(planes + 2):
        wide_ref[i] = images[i]
    for ref, row in ((down_ref, 0), (up_ref, rows - 1)):
        at = slice(row, row + 1)
        for i in range(planes):
            ref[i : i + 1] = images[i + 1][at]
        for base, own, which in ((planes, b_ref, 1), (2 * planes + 2, cond_ref, 2)):
            ref[base : base + 1] = low_ref[which, at]
            for i in range(planes):
                ref[base + 1 + i : base + 2 + i] = own[i, at]
            ref[base + planes + 1 : base + planes + 2] = high_ref[which, at]


def reached(rows):
    others = [j for j in range(rows) if 2 <= j < rows - 2]
    return [j for j in range(rows) if j not in others], others


def widened(ref, low_ref, high_ref, which):
    return [low_ref[which]] + [ref[i] for i in range(ref.shape[0])] + [high_ref[which]]


def inside_kernel(
    b_ref, cond_ref, cap_ref, slot_ref, draw_ref, wide_ref, xlow_ref, xhigh_ref, sketch_ref,
    cells_ref,
):
    planes = range(b_ref.shape[0])
    images = [wide_ref[i] for i in range(wide_ref.shape[0])]
    c_wide = widened(cond_ref, xlow_ref, xhigh_ref, 2)
    twice = apply_inside(images, c_wide, [cap_ref[i] for i in planes])
    sketch_ref[...] = sketch_rows(
        [[b_ref[i] for i in planes], images[1:-1], twice],
        [draw_ref[i] for i in planes],
        [slot_ref[i] for i in planes],
        reached(b_ref.shape[1])[1],
        cells_ref,
    )


def third_kernel(
    b_ref, cond_ref, cap_ref, slot_ref, draw_ref, wide_ref, xlow_ref, xhigh_ref, ylow_ref,
    yhigh_ref, inside_ref, image_ref, twice_ref, sketch_ref, cells_ref,
):
    planes, rows, depth = b_ref.shape
    index = lax.broadcasted_iota(jnp.int32, (rows, depth), 0)
    b_wide = widened(b_ref, xlow_ref, xhigh_ref, 1)
    c_wide = widened(cond_ref, xlow_ref, xhigh_ref, 2)
    images, beside = [], []
    for i in range(planes + 2):
        image = wide_ref[i]
        pairs = []
        for ref, mask in ((ylow_ref, index == 0), (yhigh_ref, index == rows - 1)):
            at = planes + i
            b_side = jnp.broadcast_to(ref[at : at + 1], (rows, depth))
            at = 2 * planes + 2 + i
            c_side = jnp.broadcast_to(ref[at : at + 1], (rows, depth))
            conductance = jnp.where(mask, link(c_wide[i], c_side), 0.0)
            flow = conductance * (b_wide[i] - b_side)
            image = image + flow
            if 0 < i <= planes:
                beyond = jnp.broadcast_to(ref[i - 1 : i], (rows, depth))
                pairs.append((conductance, beyond - flow))
        images.append(image)
        beside.append(pairs)
    twice = apply_inside(images, c_wide, [cap_ref[i] for i in range(planes)])
    for i in range(planes):
        for conductance, value in beside[i + 1]:
            twice[i] = twice[i] + conductance * (images[i + 1] - value)
        image_ref[i] = images[i + 1]
        twice_ref[i] = twice[i]
    sketch_ref[...] = inside_ref[...] + sketch_rows(
        [b_wide[1:-1], images[1:-1], twice],
        [draw_ref[i] for i in range(planes)],
        [slot_ref[i] for i in range(planes)],
        reached(rows)[0],
        cells_ref,
    )


def last_kernel(sketch_ref, b_ref, image_ref, twice_ref, solution_ref, residual_ref):
    sketches = jnp.sum(sketch_ref[...], axis=0)

    def inner(first, second):
        return jnp.sum(first * second, axis=1, keepdims=True)

    s0, s1, s2 = (sketches[i : i + 1] for i in range(FIELDS))
    beta = jnp.sqrt(inner(s0, s0) + epsilon)
    q0 = s0 / beta
    p0 = s1 / beta
    h00 = inner(q0, p0)
    t0 = p0 - h00 * q0
    n0 = jnp.sqrt(inner(t0, t0) + epsilon)
    q1 = t0 / n0
    p1 = (s2 / beta - h00 * p0) / n0
    h01 = inner(q0, p1)
    h11 = inner(q1, p1)
    t1 = p1 - h01 * q0 - h11 * q1
    n1 = jnp.sqrt(inner(t1, t1) + epsilon)
    l00 = jnp.sqrt(h00 * h00 + n0 * n0)
    l10 = (h00 * h01 + n0 * h11) / l00
    l11 = jnp.sqrt(h01 * h01 + h11 * h11 + n1 * n1 - l10 * l10)
    z0 = beta * h00 / l00
    z1 = (beta * h01 - l10 * z0) / l11
    y1 = z1 / l11
    y0 = (z0 - l10 * y1) / l00
    c1 = y1 / (beta * n0)
    c0 = y0 / beta - h00 * c1
    for i in range(b_ref.shape[0]):
        b, image = b_ref[i], image_ref[i]
        solution_ref[i] = c0 * b + c1 * image
        residual_ref[i] = b - c0 * image - c1 * twice_ref[i]


def call(kernel, shapes, *operands, scratch=(), inputs=pltpu.VMEM, flops=0):
    return pl.pallas_call(
        kernel,
        out_shape=[jax.ShapeDtypeStruct(shape, jnp.float32) for shape in shapes],
        in_specs=[pl.BlockSpec(memory_space=inputs)] * len(operands),
        out_specs=[pl.BlockSpec(memory_space=pltpu.VMEM)] * len(shapes),
        scratch_shapes=scratch,
        compiler_params=pltpu.CompilerParams(vmem_limit_bytes=48 * 1024 * 1024),
        cost_estimate=pl.CostEstimate(flops=flops, bytes_accessed=0, transcendentals=0),
    )(*operands)


def swap(down, up, axis):
    count = lax.axis_size(axis)
    forward = [(i, i + 1) for i in range(count - 1)]
    backward = [(i + 1, i) for i in range(count - 1)]
    return lax.ppermute(up, axis, forward), lax.ppermute(down, axis, backward)


def everyones(sketch):
    return lax.all_gather(sketch, ("gx", "gy"))


def body(b, warmth, phase, slots, draw):
    planes, rows, depth = b.shape
    block, plane, wide = b.shape, (3, rows, depth), (planes + 2, rows, depth)
    line, table = (3 * planes + 4, depth), (8, SKETCH)
    cells = pltpu.VMEM((depth // LANES, planes * rows * 8, LANES), jnp.float32)
    work = b.size * SKETCH * 6
    b, cond, cap, inner, down, up = call(
        first_kernel,
        [block, block, block, block, plane, plane],
        *(pltpu.with_memory_space_constraint(x, pltpu.HBM) for x in (b, warmth, phase)),
        scratch=[
            pltpu.VMEM(block, warmth.dtype),
            pltpu.VMEM(block, phase.dtype),
            pltpu.SemaphoreType.DMA((3,)),
        ],
        inputs=pltpu.HBM,
    )
    xlow, xhigh = swap(down, up, "gx")
    image_wide, down, up = call(
        second_kernel, [wide, line, line], b, cond, inner, xlow, xhigh
    )
    ylow, yhigh = swap(down, up, "gy")
    (inside,) = call(
        inside_kernel,
        [table],
        b, cond, cap, slots, draw, image_wide, xlow, xhigh,
        scratch=[cells],
        flops=work,
    )
    image, twice, sketch = call(
        third_kernel,
        [block, block, table],
        b, cond, cap, slots, draw, image_wide, xlow, xhigh, ylow, yhigh, inside,
        scratch=[cells],
        flops=work,
    )
    return tuple(call(last_kernel, [block, block], everyones(sketch), b, image, twice))


def solution(mesh):
    spec = P(("parts", "gx"), "gy", None)
    return jax.shard_map(
        body, mesh=mesh, in_specs=(spec,) * 5, out_specs=(spec,) * 2, check_vma=False
    )
```

```python
import jax
import jax.numpy as jnp
from jax import lax
from jax.experimental import pallas as pl
from jax.experimental.pallas import tpu as pltpu
from jax.sharding import PartitionSpec as P

SKETCH = 128
LOW = 32
HIGH = SKETCH // LOW
FIELDS = 3
LANES = 128
epsilon = 1e-06


def traits(warmth, phase):
    powder, solid = phase == 0, phase == 1
    offset = jnp.where(powder, 0.2, jnp.where(solid, 1.0, 0.6))
    return offset * (0.5 + warmth), jnp.where(powder, 1.0, jnp.where(solid, 2.0, 1.5))


def link(first, second):
    total = first + second
    return 2.0 * first * second / jnp.where(total > 0.0, total, 1.0)


def ahead(plane, axis):
    return pltpu.roll(plane, plane.shape[axis] - 1, axis)


def inner_links(cond):
    links = []
    for axis in (0, 1):
        index = lax.broadcasted_iota(jnp.int32, cond.shape, axis)
        links.append(
            jnp.where(index < cond.shape[axis] - 1, link(cond, ahead(cond, axis)), 0.0)
        )
    return links


def inner_flow(field, links):
    total = None
    for axis in (0, 1):
        flow = links[axis] * (field - ahead(field, axis))
        part = flow - pltpu.roll(flow, 1, axis)
        total = part if total is None else total + part
    return total


def apply_inside(images, c_wide, caps):
    results = []
    flow_low = link(c_wide[0], c_wide[1]) * (images[0] - images[1])
    for i in range(1, len(images) - 1):
        image = images[i]
        flow = link(c_wide[i], c_wide[i + 1]) * (image - images[i + 1])
        results.append(
            caps[i - 1] * image + inner_flow(image, inner_links(c_wide[i])) + (flow - flow_low)
        )
        flow_low = flow
    return results


def sketch_rows(fields, draws, slots, chosen, cells_ref):
    rows, depth = draws[0].shape
    for i, draw in enumerate(draws):
        coarse, fine = [], []
        for field in fields:
            weighted = draw * field[i]
            head = weighted.astype(jnp.bfloat16).astype(jnp.float32)
            coarse.append(head)
            fine.append(weighted - head)
        for f, part in enumerate(coarse + coarse[:1] + fine + fine[:1]):
            for t in range(depth // LANES):
                cells_ref[t, pl.ds(i * rows * 8 + f, rows, stride=8), :] = part[
                    :, t * LANES : (t + 1) * LANES
                ]
    low_index = lax.broadcasted_iota(jnp.int32, (LOW, depth), 0)
    low_index = low_index.astype(jnp.float32).astype(jnp.bfloat16)
    high_index = lax.broadcasted_iota(jnp.int32, (HIGH * 8, depth), 0) // 8
    high_index = high_index.astype(jnp.float32).astype(jnp.bfloat16)
    total = jnp.zeros((HIGH * 8, LOW), jnp.float32)
    for i, slot in enumerate(slots):
        low = (slot & (LOW - 1)).astype(jnp.float32)
        high = (slot >> (LOW.bit_length() - 1)).astype(jnp.float32)
        left, right = [], []
        for j in chosen:
            at = pl.ds((i * rows + j) * 8, 8)
            cells = [cells_ref[t, at, :] for t in range(depth // LANES)]
            cells = jnp.concatenate(cells, axis=1)
            cells = jnp.concatenate([cells] * HIGH, axis=0).astype(jnp.bfloat16)
            row_high = jnp.broadcast_to(high[j : j + 1], cells.shape).astype(jnp.bfloat16)
            row_low = jnp.broadcast_to(low[j : j + 1], (LOW, depth)).astype(jnp.bfloat16)
            left.append(jnp.where(row_high == high_index, cells, jnp.zeros_like(cells)))
            right.append(
                jnp.where(row_low == low_index, jnp.ones_like(row_low), jnp.zeros_like(row_low))
            )
        total = total + lax.dot_general(
            jnp.concatenate(left, axis=1),
            jnp.concatenate(right, axis=1),
            (((1,), (1,)), ((), ())),
            preferred_element_type=jnp.float32,
        )
    parts = jnp.concatenate([total[h * 8 : h * 8 + 8] for h in range(HIGH)], axis=1)
    return parts + pltpu.roll(parts, 4, 0)


def first_kernel(
    b_hbm, warmth_hbm, phase_hbm, b_ref, cond_ref, cap_ref, inner_ref, down_ref, up_ref,
    warmth_ref, phase_ref, arrived,
):
    copies = [
        pltpu.make_async_copy(source, target, arrived.at[k])
        for k, (source, target) in enumerate(
            ((b_hbm, b_ref), (warmth_hbm, warmth_ref), (phase_hbm, phase_ref))
        )
    ]
    for copy in copies:
        copy.start()
    for copy in copies:
        copy.wait()
    planes = b_ref.shape[0]
    images, conds = [], []
    for i in range(planes):
        cond, cap = traits(warmth_ref[i], phase_ref[i])
        cap_ref[i] = cap
        cond_ref[i] = cond
        field = b_ref[i]
        image = cap * field + inner_flow(field, inner_links(cond))
        if i:
            flow = link(conds[-1], cond) * (b_ref[i - 1] - field)
            images[-1] = images[-1] + flow
            image = image - flow
        conds.append(cond)
        images.append(image)
    for i in range(planes):
        inner_ref[i] = images[i]
    for ref, i in ((down_ref, 0), (up_ref, planes - 1)):
        ref[0] = images[i]
        ref[1] = b_ref[i]
        ref[2] = conds[i]


def has_beside(axis):
    at = lax.axis_index(axis)
    return at > 0, at < lax.axis_size(axis) - 1


def conds_beside(low, high, axis):
    below, above = has_beside(axis)
    return jnp.where(below, low, 0.0), jnp.where(above, high, 0.0)


def second_kernel(b_ref, cond_ref, inner_ref, low_ref, high_ref, wide_ref, down_ref, up_ref):
    planes, rows = b_ref.shape[0], b_ref.shape[1]
    c_low, c_high = conds_beside(low_ref[2], high_ref[2], "gx")
    low_flow = link(c_low, cond_ref[0]) * (low_ref[1] - b_ref[0])
    high_flow = link(cond_ref[planes - 1], c_high) * (b_ref[planes - 1] - high_ref[1])
    images = [low_ref[0] + low_flow] + [inner_ref[i] for i in range(planes)]
    images.append(high_ref[0] - high_flow)
    images[1] = images[1] - low_flow
    images[planes] = images[planes] + high_flow
    for i in range(planes + 2):
        wide_ref[i] = images[i]
    for ref, row in ((down_ref, 0), (up_ref, rows - 1)):
        at = slice(row, row + 1)
        for i in range(planes):
            ref[i : i + 1] = images[i + 1][at]
        for base, low, own, high in (
            (planes, low_ref[1], b_ref, high_ref[1]),
            (2 * planes + 2, c_low, cond_ref, c_high),
        ):
            ref[base : base + 1] = low[at]
            for i in range(planes):
                ref[base + 1 + i : base + 2 + i] = own[i, at]
            ref[base + planes + 1 : base + planes + 2] = high[at]


def reached(rows):
    others = [j for j in range(rows) if 2 <= j < rows - 2]
    return [j for j in range(rows) if j not in others], others


def widened_conds(cond_ref, low_ref, high_ref):
    low, high = conds_beside(low_ref[2], high_ref[2], "gx")
    return [low] + [cond_ref[i] for i in range(cond_ref.shape[0])] + [high]


def inside_kernel(
    b_ref, cond_ref, cap_ref, slot_ref, draw_ref, wide_ref, xlow_ref, xhigh_ref, sketch_ref,
    cells_ref,
):
    planes = range(b_ref.shape[0])
    images = [wide_ref[i] for i in range(wide_ref.shape[0])]
    c_wide = widened_conds(cond_ref, xlow_ref, xhigh_ref)
    twice = apply_inside(images, c_wide, [cap_ref[i] for i in planes])
    sketch_ref[...] = sketch_rows(
        [[b_ref[i] for i in planes], images[1:-1], twice],
        [draw_ref[i] for i in planes],
        [slot_ref[i] for i in planes],
        reached(b_ref.shape[1])[1],
        cells_ref,
    )


def third_kernel(
    b_ref, cond_ref, cap_ref, slot_ref, draw_ref, wide_ref, xlow_ref, xhigh_ref, ylow_ref,
    yhigh_ref, inside_ref, image_ref, twice_ref, sketch_ref, cells_ref,
):
    planes, rows, depth = b_ref.shape
    index = lax.broadcasted_iota(jnp.int32, (rows, depth), 0)
    b_wide = [xlow_ref[1]] + [b_ref[i] for i in range(planes)] + [xhigh_ref[1]]
    c_wide = widened_conds(cond_ref, xlow_ref, xhigh_ref)
    below, above = has_beside("gy")
    at_low = (index == 0) & below
    at_high = (index == rows - 1) & above
    images, beside = [], []
    for i in range(planes + 2):
        image = wide_ref[i]
        pairs = []
        for ref, mask in ((ylow_ref, at_low), (yhigh_ref, at_high)):
            at = planes + i
            b_side = jnp.broadcast_to(ref[at : at + 1], (rows, depth))
            at = 2 * planes + 2 + i
            c_side = jnp.broadcast_to(ref[at : at + 1], (rows, depth))
            conductance = jnp.where(mask, link(c_wide[i], c_side), 0.0)
            flow = conductance * (b_wide[i] - b_side)
            image = image + flow
            if 0 < i <= planes:
                beyond = jnp.broadcast_to(ref[i - 1 : i], (rows, depth))
                pairs.append((conductance, beyond - flow))
        images.append(image)
        beside.append(pairs)
    twice = apply_inside(images, c_wide, [cap_ref[i] for i in range(planes)])
    for i in range(planes):
        for conductance, value in beside[i + 1]:
            twice[i] = twice[i] + conductance * (images[i + 1] - value)
        image_ref[i] = images[i + 1]
        twice_ref[i] = twice[i]
    sketch_ref[...] = inside_ref[...] + sketch_rows(
        [b_wide[1:-1], images[1:-1], twice],
        [draw_ref[i] for i in range(planes)],
        [slot_ref[i] for i in range(planes)],
        reached(rows)[0],
        cells_ref,
    )


def last_kernel(sketch_ref, b_ref, image_ref, twice_ref, solution_ref, residual_ref):
    sketches = jnp.sum(sketch_ref[...], axis=0)

    def inner(first, second):
        return jnp.sum(first * second, axis=1, keepdims=True)

    s0, s1, s2 = (sketches[i : i + 1] for i in range(FIELDS))
    beta = jnp.sqrt(inner(s0, s0) + epsilon)
    q0 = s0 / beta
    p0 = s1 / beta
    h00 = inner(q0, p0)
    t0 = p0 - h00 * q0
    n0 = jnp.sqrt(inner(t0, t0) + epsilon)
    q1 = t0 / n0
    p1 = (s2 / beta - h00 * p0) / n0
    h01 = inner(q0, p1)
    h11 = inner(q1, p1)
    t1 = p1 - h01 * q0 - h11 * q1
    n1 = jnp.sqrt(inner(t1, t1) + epsilon)
    l00 = jnp.sqrt(h00 * h00 + n0 * n0)
    l10 = (h00 * h01 + n0 * h11) / l00
    l11 = jnp.sqrt(h01 * h01 + h11 * h11 + n1 * n1 - l10 * l10)
    z0 = beta * h00 / l00
    z1 = (beta * h01 - l10 * z0) / l11
    y1 = z1 / l11
    y0 = (z0 - l10 * y1) / l00
    c1 = y1 / (beta * n0)
    c0 = y0 / beta - h00 * c1
    for i in range(b_ref.shape[0]):
        b, image = b_ref[i], image_ref[i]
        solution_ref[i] = c0 * b + c1 * image
        residual_ref[i] = b - c0 * image - c1 * twice_ref[i]


def call(kernel, shapes, *operands, scratch=(), inputs=pltpu.VMEM, flops=0):
    return pl.pallas_call(
        kernel,
        out_shape=[jax.ShapeDtypeStruct(shape, jnp.float32) for shape in shapes],
        in_specs=[pl.BlockSpec(memory_space=inputs)] * len(operands),
        out_specs=[pl.BlockSpec(memory_space=pltpu.VMEM)] * len(shapes),
        scratch_shapes=scratch,
        compiler_params=pltpu.CompilerParams(vmem_limit_bytes=48 * 1024 * 1024),
        cost_estimate=pl.CostEstimate(flops=flops, bytes_accessed=0, transcendentals=0),
    )(*operands)


def swap(down, up, axis):
    count = lax.axis_size(axis)
    forward = [(i, (i + 1) % count) for i in range(count)]
    backward = [((i + 1) % count, i) for i in range(count)]
    return lax.ppermute(up, axis, forward), lax.ppermute(down, axis, backward)


def everyones(sketch):
    count = lax.axis_size("gx") * lax.axis_size("gy")
    copies = jnp.broadcast_to(sketch[None], (count,) + sketch.shape)
    return lax.all_to_all(copies, ("gx", "gy"), 0, 0)


def body(b, warmth, phase, slots, draw):
    planes, rows, depth = b.shape
    block, plane, wide = b.shape, (3, rows, depth), (planes + 2, rows, depth)
    line, table = (3 * planes + 4, depth), (8, SKETCH)
    cells = pltpu.VMEM((depth // LANES, planes * rows * 8, LANES), jnp.float32)
    work = b.size * SKETCH * 6
    b, cond, cap, inner, down, up = call(
        first_kernel,
        [block, block, block, block, plane, plane],
        *(pltpu.with_memory_space_constraint(x, pltpu.HBM) for x in (b, warmth, phase)),
        scratch=[
            pltpu.VMEM(block, warmth.dtype),
            pltpu.VMEM(block, phase.dtype),
            pltpu.SemaphoreType.DMA((3,)),
        ],
        inputs=pltpu.HBM,
    )
    xlow, xhigh = swap(down, up, "gx")
    image_wide, down, up = call(
        second_kernel, [wide, line, line], b, cond, inner, xlow, xhigh
    )
    ylow, yhigh = swap(down, up, "gy")
    (inside,) = call(
        inside_kernel,
        [table],
        b, cond, cap, slots, draw, image_wide, xlow, xhigh,
        scratch=[cells],
        flops=work,
    )
    image, twice, sketch = call(
        third_kernel,
        [block, block, table],
        b, cond, cap, slots, draw, image_wide, xlow, xhigh, ylow, yhigh, inside,
        scratch=[cells],
        flops=work,
    )
    return tuple(call(last_kernel, [block, block], everyones(sketch), b, image, twice))


def solution(mesh):
    spec = P(("parts", "gx"), "gy", None)
    return jax.shard_map(
        body, mesh=mesh, in_specs=(spec,) * 5, out_specs=(spec,) * 2, check_vma=False
    )
```

```python
import jax
import jax.numpy as jnp
from jax import lax
from jax.experimental import pallas as pl
from jax.experimental.pallas import tpu as pltpu
from jax.sharding import PartitionSpec as P

SKETCH = 128
LOW = 32
HIGH = SKETCH // LOW
FIELDS = 3
LANES = 128
epsilon = 1e-06


def traits(warmth, phase):
    powder, solid = phase == 0, phase == 1
    offset = jnp.where(powder, 0.2, jnp.where(solid, 1.0, 0.6))
    return offset * (0.5 + warmth), jnp.where(powder, 1.0, jnp.where(solid, 2.0, 1.5))


def link(first, second):
    total = first + second
    return 2.0 * first * second / jnp.where(total > 0.0, total, 1.0)


def ahead(plane, axis):
    return pltpu.roll(plane, plane.shape[axis] - 1, axis)


def inner_links(cond):
    links = []
    for axis in (0, 1):
        index = lax.broadcasted_iota(jnp.int32, cond.shape, axis)
        links.append(
            jnp.where(index < cond.shape[axis] - 1, link(cond, ahead(cond, axis)), 0.0)
        )
    return links


def inner_flow(field, links):
    total = None
    for axis in (0, 1):
        flow = links[axis] * (field - ahead(field, axis))
        part = flow - pltpu.roll(flow, 1, axis)
        total = part if total is None else total + part
    return total


def apply_inside(images, c_wide, caps):
    results = []
    flow_low = link(c_wide[0], c_wide[1]) * (images[0] - images[1])
    for i in range(1, len(images) - 1):
        image = images[i]
        flow = link(c_wide[i], c_wide[i + 1]) * (image - images[i + 1])
        results.append(
            caps[i - 1] * image + inner_flow(image, inner_links(c_wide[i])) + (flow - flow_low)
        )
        flow_low = flow
    return results


def sketch_rows(fields, draws, slots, chosen, cells_ref):
    rows, depth = draws[0].shape
    for i, draw in enumerate(draws):
        coarse, fine = [], []
        for field in fields:
            weighted = draw * field[i]
            head = weighted.astype(jnp.bfloat16).astype(jnp.float32)
            coarse.append(head)
            fine.append(weighted - head)
        for f, part in enumerate(coarse + coarse[:1] + fine + fine[:1]):
            for t in range(depth // LANES):
                cells_ref[t, pl.ds(i * rows * 8 + f, rows, stride=8), :] = part[
                    :, t * LANES : (t + 1) * LANES
                ]
    low_index = lax.broadcasted_iota(jnp.int32, (LOW, depth), 0)
    low_index = low_index.astype(jnp.float32).astype(jnp.bfloat16)
    high_index = lax.broadcasted_iota(jnp.int32, (HIGH * 8, depth), 0) // 8
    high_index = high_index.astype(jnp.float32).astype(jnp.bfloat16)
    total = jnp.zeros((HIGH * 8, LOW), jnp.float32)
    for i, slot in enumerate(slots):
        low = (slot & (LOW - 1)).astype(jnp.float32)
        high = (slot >> (LOW.bit_length() - 1)).astype(jnp.float32)
        left, right = [], []
        for j in chosen:
            at = pl.ds((i * rows + j) * 8, 8)
            cells = [cells_ref[t, at, :] for t in range(depth // LANES)]
            cells = jnp.concatenate(cells, axis=1)
            cells = jnp.concatenate([cells] * HIGH, axis=0).astype(jnp.bfloat16)
            row_high = jnp.broadcast_to(high[j : j + 1], cells.shape).astype(jnp.bfloat16)
            row_low = jnp.broadcast_to(low[j : j + 1], (LOW, depth)).astype(jnp.bfloat16)
            left.append(jnp.where(row_high == high_index, cells, jnp.zeros_like(cells)))
            right.append(
                jnp.where(row_low == low_index, jnp.ones_like(row_low), jnp.zeros_like(row_low))
            )
        total = total + lax.dot_general(
            jnp.concatenate(left, axis=1),
            jnp.concatenate(right, axis=1),
            (((1,), (1,)), ((), ())),
            preferred_element_type=jnp.float32,
        )
    parts = jnp.concatenate([total[h * 8 : h * 8 + 8] for h in range(HIGH)], axis=1)
    return parts + pltpu.roll(parts, 4, 0)


def first_kernel(
    b_hbm, warmth_hbm, phase_hbm, b_ref, cond_ref, cap_ref, inner_ref, down_ref, up_ref,
    left_ref, right_ref, *rest,
):
    *corner_refs, warmth_ref, phase_ref, arrived = rest
    copies = [
        pltpu.make_async_copy(source, target, arrived.at[k])
        for k, (source, target) in enumerate(
            ((b_hbm, b_ref), (warmth_hbm, warmth_ref), (phase_hbm, phase_ref))
        )
    ]
    for copy in copies:
        copy.start()
    for copy in copies:
        copy.wait()
    planes, rows = b_ref.shape[:2]
    images, conds = [], []
    for i in range(planes):
        cond, cap = traits(warmth_ref[i], phase_ref[i])
        cap_ref[i] = cap
        cond_ref[i] = cond
        field = b_ref[i]
        image = cap * field + inner_flow(field, inner_links(cond))
        if i:
            flow = link(conds[-1], cond) * (b_ref[i - 1] - field)
            images[-1] = images[-1] + flow
            image = image - flow
        conds.append(cond)
        images.append(image)
    for i in range(planes):
        inner_ref[i] = images[i]
    for ref, i in ((down_ref, 0), (up_ref, planes - 1)):
        for k, value in enumerate((images[i], b_ref[i], conds[i])):
            ref[k] = value
    for ref, j in ((left_ref, 0), (right_ref, rows - 1)):
        for i in range(planes):
            for k, value in enumerate((images[i], b_ref[i], conds[i])):
                at = k * planes + i
                ref[at : at + 1] = value[j : j + 1]
    for ref, i, j in zip(corner_refs, (0, 0, planes - 1, planes - 1), (0, rows - 1) * 2):
        ref[0:1] = b_ref[i, j : j + 1]
        ref[1:2] = conds[i][j : j + 1]


def has_beside(axis):
    at = lax.axis_index(axis)
    return at > 0, at < lax.axis_size(axis) - 1


def widened_conds(cond_ref, low_ref, high_ref):
    below, above = has_beside("gx")
    conds = [cond_ref[i] for i in range(cond_ref.shape[0])]
    return [jnp.where(below, low_ref[2], 0.0)] + conds + [jnp.where(above, high_ref[2], 0.0)]


def reached(rows):
    others = [j for j in range(rows) if 2 <= j < rows - 2]
    return [j for j in range(rows) if j not in others], others


def inside_kernel(
    b_ref, cond_ref, cap_ref, inner_ref, slot_ref, draw_ref, xlow_ref, xhigh_ref, wide_ref,
    sketch_ref, cells_ref,
):
    planes = range(b_ref.shape[0])
    c_wide = widened_conds(cond_ref, xlow_ref, xhigh_ref)
    low_flow = link(c_wide[0], c_wide[1]) * (xlow_ref[1] - b_ref[0])
    high_flow = link(c_wide[-2], c_wide[-1]) * (b_ref[planes[-1]] - xhigh_ref[1])
    images = [xlow_ref[0] + low_flow] + [inner_ref[i] for i in planes]
    images.append(xhigh_ref[0] - high_flow)
    images[1] = images[1] - low_flow
    images[-2] = images[-2] + high_flow
    for i, image in enumerate(images):
        wide_ref[i] = image
    twice = apply_inside(images, c_wide, [cap_ref[i] for i in planes])
    sketch_ref[...] = sketch_rows(
        [[b_ref[i] for i in planes], images[1:-1], twice],
        [draw_ref[i] for i in planes],
        [slot_ref[i] for i in planes],
        reached(b_ref.shape[1])[1],
        cells_ref,
    )


def third_kernel(
    b_ref, cond_ref, cap_ref, slot_ref, draw_ref, wide_ref, xlow_ref, xhigh_ref, ylow_ref,
    yhigh_ref, low_low_ref, low_high_ref, high_low_ref, high_high_ref, inside_ref, image_ref,
    twice_ref, sketch_ref, cells_ref,
):
    planes, rows, depth = b_ref.shape
    index = lax.broadcasted_iota(jnp.int32, (rows, depth), 0)
    b_wide = [xlow_ref[1]] + [b_ref[i] for i in range(planes)] + [xhigh_ref[1]]
    c_wide = widened_conds(cond_ref, xlow_ref, xhigh_ref)
    images = [wide_ref[i] for i in range(planes + 2)]
    beside = []
    for here, j, ref, low_ref, high_ref in zip(
        has_beside("gy"),
        (0, rows - 1),
        (ylow_ref, yhigh_ref),
        (low_low_ref, low_high_ref),
        (high_low_ref, high_high_ref),
    ):
        b_line = [low_ref[0:1]] + [ref[planes + i : planes + i + 1] for i in range(planes)]
        b_line.append(high_ref[0:1])
        c_line = [ref[2 * planes + i : 2 * planes + i + 1] for i in range(planes)]
        below, above = has_beside("gx")
        c_line = [jnp.where(below, low_ref[1:2], 0.0)] + c_line
        c_line.append(jnp.where(above, high_ref[1:2], 0.0))
        c_line = [jnp.where(here, c, 0.0) for c in c_line]
        beyond = [ref[i : i + 1] for i in range(planes)]
        beyond[0] = beyond[0] + link(c_line[0], c_line[1]) * (b_line[1] - b_line[0])
        beyond[-1] = beyond[-1] + link(c_line[-2], c_line[-1]) * (b_line[-2] - b_line[-1])
        for i in range(planes + 2):
            conductance = link(c_wide[i], jnp.broadcast_to(c_line[i], (rows, depth)))
            conductance = jnp.where(index == j, conductance, 0.0)
            flow = conductance * (b_wide[i] - b_line[i])
            images[i] = images[i] + flow
            if 0 < i <= planes:
                beside.append((i, conductance, beyond[i - 1] - flow))
    twice = apply_inside(images, c_wide, [cap_ref[i] for i in range(planes)])
    for i, conductance, value in beside:
        twice[i - 1] = twice[i - 1] + conductance * (images[i] - value)
    for i in range(planes):
        image_ref[i] = images[i + 1]
        twice_ref[i] = twice[i]
    sketch_ref[...] = inside_ref[...] + sketch_rows(
        [b_wide[1:-1], images[1:-1], twice],
        [draw_ref[i] for i in range(planes)],
        [slot_ref[i] for i in range(planes)],
        reached(rows)[0],
        cells_ref,
    )


def last_kernel(sketch_ref, b_ref, image_ref, twice_ref, solution_ref, residual_ref):
    sketches = sketch_ref[...]

    def inner(first, second):
        return jnp.sum(first * second, axis=1, keepdims=True)

    s0, s1, s2 = (sketches[i : i + 1] for i in range(FIELDS))
    beta = jnp.sqrt(inner(s0, s0) + epsilon)
    q0 = s0 / beta
    p0 = s1 / beta
    h00 = inner(q0, p0)
    t0 = p0 - h00 * q0
    n0 = jnp.sqrt(inner(t0, t0) + epsilon)
    q1 = t0 / n0
    p1 = (s2 / beta - h00 * p0) / n0
    h01 = inner(q0, p1)
    h11 = inner(q1, p1)
    t1 = p1 - h01 * q0 - h11 * q1
    n1 = jnp.sqrt(inner(t1, t1) + epsilon)
    l00 = jnp.sqrt(h00 * h00 + n0 * n0)
    l10 = (h00 * h01 + n0 * h11) / l00
    l11 = jnp.sqrt(h01 * h01 + h11 * h11 + n1 * n1 - l10 * l10)
    z0 = beta * h00 / l00
    z1 = (beta * h01 - l10 * z0) / l11
    y1 = z1 / l11
    y0 = (z0 - l10 * y1) / l00
    c1 = y1 / (beta * n0)
    c0 = y0 / beta - h00 * c1
    for i in range(b_ref.shape[0]):
        b, image = b_ref[i], image_ref[i]
        solution_ref[i] = c0 * b + c1 * image
        residual_ref[i] = b - c0 * image - c1 * twice_ref[i]


def call(kernel, shapes, *operands, scratch=(), inputs=pltpu.VMEM, flops=0):
    return pl.pallas_call(
        kernel,
        out_shape=[jax.ShapeDtypeStruct(shape, jnp.float32) for shape in shapes],
        in_specs=[pl.BlockSpec(memory_space=inputs)] * len(operands),
        out_specs=[pl.BlockSpec(memory_space=pltpu.VMEM)] * len(shapes),
        scratch_shapes=scratch,
        compiler_params=pltpu.CompilerParams(vmem_limit_bytes=48 * 1024 * 1024),
        cost_estimate=pl.CostEstimate(flops=flops, bytes_accessed=0, transcendentals=0),
    )(*operands)


def shift(array, steps_x, steps_y):
    nx, ny = lax.axis_size("gx"), lax.axis_size("gy")
    pairs = [
        (x * ny + y, (x + steps_x) % nx * ny + (y + steps_y) % ny)
        for x in range(nx)
        for y in range(ny)
    ]
    return lax.ppermute(array, ("gx", "gy"), pairs)


def sum_over_devices(table):
    for axis, steps in (("gx", (1, 0)), ("gy", (0, 1))):
        others = [
            shift(table, n * steps[0], n * steps[1]) for n in range(1, lax.axis_size(axis))
        ]
        table = sum(others, table)
    return table


def body(b, warmth, phase, slots, draw):
    planes, rows, depth = b.shape
    block, wide, table = b.shape, (planes + 2, rows, depth), (8, SKETCH)
    face, line, corner = (3, rows, depth), (3 * planes, depth), (2, depth)
    cells = pltpu.VMEM((depth // LANES, planes * rows * 8, LANES), jnp.float32)
    work = b.size * SKETCH * 6
    b, cond, cap, inner, down, up, left, right, *corners = call(
        first_kernel,
        [block] * 4 + [face] * 2 + [line] * 2 + [corner] * 4,
        *(pltpu.with_memory_space_constraint(x, pltpu.HBM) for x in (b, warmth, phase)),
        scratch=[
            pltpu.VMEM(block, warmth.dtype),
            pltpu.VMEM(block, phase.dtype),
            pltpu.SemaphoreType.DMA((3,)),
        ],
        inputs=pltpu.HBM,
    )
    xlow, xhigh = shift(up, 1, 0), shift(down, -1, 0)
    ylow, yhigh = shift(right, 0, 1), shift(left, 0, -1)
    high_high, high_low = shift(corners[0], -1, -1), shift(corners[1], -1, 1)
    low_high, low_low = shift(corners[2], 1, -1), shift(corners[3], 1, 1)
    image_wide, inside = call(
        inside_kernel,
        [wide, table],
        b, cond, cap, inner, slots, draw, xlow, xhigh,
        scratch=[cells],
        flops=work,
    )
    image, twice, sketch = call(
        third_kernel,
        [block, block, table],
        b, cond, cap, slots, draw, image_wide, xlow, xhigh, ylow, yhigh, low_low, low_high,
        high_low, high_high, inside,
        scratch=[cells],
        flops=work,
    )
    return tuple(call(last_kernel, [block, block], sum_over_devices(sketch), b, image, twice))


def solution(mesh):
    spec = P(("parts", "gx"), "gy", None)
    return jax.shard_map(
        body, mesh=mesh, in_specs=(spec,) * 5, out_specs=(spec,) * 2, check_vma=False
    )
```

```python
import jax
import jax.numpy as jnp
from jax import lax
from jax.experimental import pallas as pl
from jax.experimental.pallas import tpu as pltpu
from jax.sharding import PartitionSpec as P

SKETCH = 128
LOW = 32
HIGH = SKETCH // LOW
FIELDS = 3
LANES = 128
epsilon = 1e-06


def traits(warmth, phase):
    powder, solid = phase == 0, phase == 1
    offset = jnp.where(powder, 0.2, jnp.where(solid, 1.0, 0.6))
    return offset * (0.5 + warmth), jnp.where(powder, 1.0, jnp.where(solid, 2.0, 1.5))


def link(first, second):
    total = first + second
    return 2.0 * first * second / jnp.where(total > 0.0, total, 1.0)


def ahead(plane, axis):
    return pltpu.roll(plane, plane.shape[axis] - 1, axis)


def inner_links(cond):
    links = []
    for axis in (0, 1):
        index = lax.broadcasted_iota(jnp.int32, cond.shape, axis)
        links.append(
            jnp.where(index < cond.shape[axis] - 1, link(cond, ahead(cond, axis)), 0.0)
        )
    return links


def inner_flow(field, links):
    total = None
    for axis in (0, 1):
        flow = links[axis] * (field - ahead(field, axis))
        part = flow - pltpu.roll(flow, 1, axis)
        total = part if total is None else total + part
    return total


def apply_inside(images, c_wide, caps):
    results = []
    flow_low = link(c_wide[0], c_wide[1]) * (images[0] - images[1])
    for i in range(1, len(images) - 1):
        image = images[i]
        flow = link(c_wide[i], c_wide[i + 1]) * (image - images[i + 1])
        results.append(
            caps[i - 1] * image + inner_flow(image, inner_links(c_wide[i])) + (flow - flow_low)
        )
        flow_low = flow
    return results


def sketch_rows(fields, draws, slots, chosen, cells_ref):
    rows, depth = draws[0].shape
    for i, draw in enumerate(draws):
        coarse, fine = [], []
        for field in fields:
            weighted = draw * field[i]
            head = weighted.astype(jnp.bfloat16).astype(jnp.float32)
            coarse.append(head)
            fine.append(weighted - head)
        for f, part in enumerate(coarse + coarse[:1] + fine + fine[:1]):
            for t in range(depth // LANES):
                cells_ref[t, pl.ds(i * rows * 8 + f, rows, stride=8), :] = part[
                    :, t * LANES : (t + 1) * LANES
                ]
    low_index = lax.broadcasted_iota(jnp.int32, (LOW, depth), 0)
    low_index = low_index.astype(jnp.float32).astype(jnp.bfloat16)
    high_index = lax.broadcasted_iota(jnp.int32, (HIGH * 8, depth), 0) // 8
    high_index = high_index.astype(jnp.float32).astype(jnp.bfloat16)
    total = jnp.zeros((HIGH * 8, LOW), jnp.float32)
    for i, slot in enumerate(slots):
        low = (slot & (LOW - 1)).astype(jnp.float32)
        high = (slot >> (LOW.bit_length() - 1)).astype(jnp.float32)
        left, right = [], []
        for j in chosen:
            at = pl.ds((i * rows + j) * 8, 8)
            cells = [cells_ref[t, at, :] for t in range(depth // LANES)]
            cells = jnp.concatenate(cells, axis=1)
            cells = jnp.concatenate([cells] * HIGH, axis=0).astype(jnp.bfloat16)
            row_high = jnp.broadcast_to(high[j : j + 1], cells.shape).astype(jnp.bfloat16)
            row_low = jnp.broadcast_to(low[j : j + 1], (LOW, depth)).astype(jnp.bfloat16)
            left.append(jnp.where(row_high == high_index, cells, jnp.zeros_like(cells)))
            right.append(
                jnp.where(row_low == low_index, jnp.ones_like(row_low), jnp.zeros_like(row_low))
            )
        total = total + lax.dot_general(
            jnp.concatenate(left, axis=1),
            jnp.concatenate(right, axis=1),
            (((1,), (1,)), ((), ())),
            preferred_element_type=jnp.float32,
        )
    parts = jnp.concatenate([total[h * 8 : h * 8 + 8] for h in range(HIGH)], axis=1)
    return parts + pltpu.roll(parts, 4, 0)


def first_kernel(
    b_hbm, warmth_hbm, phase_hbm, b_ref, cond_ref, cap_ref, inner_ref, first_ref, second_ref,
    warmth_ref, phase_ref, arrived,
):
    copies = [
        pltpu.make_async_copy(source, target, arrived.at[k])
        for k, (source, target) in enumerate(
            ((b_hbm, b_ref), (warmth_hbm, warmth_ref), (phase_hbm, phase_ref))
        )
    ]
    for copy in copies:
        copy.start()
    for copy in copies:
        copy.wait()
    planes = b_ref.shape[0]
    images, conds = [], []
    for i in range(planes):
        cond, cap = traits(warmth_ref[i], phase_ref[i])
        cap_ref[i] = cap
        cond_ref[i] = cond
        field = b_ref[i]
        image = cap * field + inner_flow(field, inner_links(cond))
        if i:
            flow = link(conds[-1], cond) * (b_ref[i - 1] - field)
            images[-1] = images[-1] + flow
            image = image - flow
        conds.append(cond)
        images.append(image)
    for i in range(planes):
        inner_ref[i] = images[i]
    for k, low, high in (
        (0, images[0], images[-1]),
        (1, b_ref[0], b_ref[planes - 1]),
        (2, conds[0], conds[-1]),
    ):
        first_ref[k], second_ref[k] = by_turn(low, high, "gx")


def by_turn(low, high, axis):
    odd = lax.axis_index(axis) % 2 == 1
    return jnp.where(odd, low, high), jnp.where(odd, high, low)


def has_beside(axis):
    at = lax.axis_index(axis)
    return at > 0, at < lax.axis_size(axis) - 1


def second_kernel(
    b_ref, cond_ref, inner_ref, got_first_ref, got_second_ref, wide_ref, beside_ref, first_ref,
    second_ref,
):
    planes, rows = b_ref.shape[0], b_ref.shape[1]
    (image_low, image_high), (b_low, b_high), (c_low, c_high) = (
        by_turn(got_first_ref[k], got_second_ref[k], "gx") for k in range(3)
    )
    below, above = has_beside("gx")
    c_low, c_high = jnp.where(below, c_low, 0.0), jnp.where(above, c_high, 0.0)
    low_flow = link(c_low, cond_ref[0]) * (b_low - b_ref[0])
    high_flow = link(cond_ref[planes - 1], c_high) * (b_ref[planes - 1] - b_high)
    images = [image_low + low_flow] + [inner_ref[i] for i in range(planes)]
    images.append(image_high - high_flow)
    images[1] = images[1] - low_flow
    images[planes] = images[planes] + high_flow
    for i in range(planes + 2):
        wide_ref[i] = images[i]
    for k, plane in enumerate((b_low, b_high, c_low, c_high)):
        beside_ref[k] = plane
    lines = images[1:-1] + [b_low] + [b_ref[i] for i in range(planes)] + [b_high, c_low]
    lines += [cond_ref[i] for i in range(planes)] + [c_high]
    for k, plane in enumerate(lines):
        low, high = by_turn(plane[:1], plane[rows - 1 :], "gy")
        first_ref[k : k + 1] = low
        second_ref[k : k + 1] = high


def reached(rows):
    others = [j for j in range(rows) if 2 <= j < rows - 2]
    return [j for j in range(rows) if j not in others], others


def widened(ref, beside_ref, which):
    inner = [ref[i] for i in range(ref.shape[0])]
    return [beside_ref[which]] + inner + [beside_ref[which + 1]]


def inside_kernel(
    b_ref, cond_ref, cap_ref, slot_ref, draw_ref, wide_ref, beside_ref, sketch_ref,
    cells_ref,
):
    planes = range(b_ref.shape[0])
    images = [wide_ref[i] for i in range(wide_ref.shape[0])]
    c_wide = widened(cond_ref, beside_ref, 2)
    twice = apply_inside(images, c_wide, [cap_ref[i] for i in planes])
    sketch_ref[...] = sketch_rows(
        [[b_ref[i] for i in planes], images[1:-1], twice],
        [draw_ref[i] for i in planes],
        [slot_ref[i] for i in planes],
        reached(b_ref.shape[1])[1],
        cells_ref,
    )


def third_kernel(
    b_ref, cond_ref, cap_ref, slot_ref, draw_ref, wide_ref, beside_ref, got_first_ref,
    got_second_ref, inside_ref, image_ref, twice_ref, sketch_ref, cells_ref,
):
    planes, rows, depth = b_ref.shape
    index = lax.broadcasted_iota(jnp.int32, (rows, depth), 0)
    b_wide = widened(b_ref, beside_ref, 0)
    c_wide = widened(cond_ref, beside_ref, 2)
    below, above = has_beside("gy")
    at_low = (index == 0) & below
    at_high = (index == rows - 1) & above
    lines = by_turn(got_first_ref[...], got_second_ref[...], "gy")
    images, beside = [], []
    for i in range(planes + 2):
        image = wide_ref[i]
        pairs = []
        for line, mask in zip(lines, (at_low, at_high)):
            at = planes + i
            b_side = jnp.broadcast_to(line[at : at + 1], (rows, depth))
            at = 2 * planes + 2 + i
            c_side = jnp.broadcast_to(line[at : at + 1], (rows, depth))
            conductance = jnp.where(mask, link(c_wide[i], c_side), 0.0)
            flow = conductance * (b_wide[i] - b_side)
            image = image + flow
            if 0 < i <= planes:
                beyond = jnp.broadcast_to(line[i - 1 : i], (rows, depth))
                pairs.append((conductance, beyond - flow))
        images.append(image)
        beside.append(pairs)
    twice = apply_inside(images, c_wide, [cap_ref[i] for i in range(planes)])
    for i in range(planes):
        for conductance, value in beside[i + 1]:
            twice[i] = twice[i] + conductance * (images[i + 1] - value)
        image_ref[i] = images[i + 1]
        twice_ref[i] = twice[i]
    sketch = inside_ref[...] + sketch_rows(
        [b_wide[1:-1], images[1:-1], twice],
        [draw_ref[i] for i in range(planes)],
        [slot_ref[i] for i in range(planes)],
        reached(rows)[0],
        cells_ref,
    )
    sketch_ref[...] = sketch[: FIELDS + 1]


def last_kernel(sketch_ref, b_ref, image_ref, twice_ref, solution_ref, residual_ref):
    sketches = jnp.sum(sketch_ref[...], axis=0)

    def inner(first, second):
        return jnp.sum(first * second, axis=1, keepdims=True)

    s0, s1, s2 = (sketches[i : i + 1] for i in range(FIELDS))
    beta = jnp.sqrt(inner(s0, s0) + epsilon)
    q0 = s0 / beta
    p0 = s1 / beta
    h00 = inner(q0, p0)
    t0 = p0 - h00 * q0
    n0 = jnp.sqrt(inner(t0, t0) + epsilon)
    q1 = t0 / n0
    p1 = (s2 / beta - h00 * p0) / n0
    h01 = inner(q0, p1)
    h11 = inner(q1, p1)
    t1 = p1 - h01 * q0 - h11 * q1
    n1 = jnp.sqrt(inner(t1, t1) + epsilon)
    l00 = jnp.sqrt(h00 * h00 + n0 * n0)
    l10 = (h00 * h01 + n0 * h11) / l00
    l11 = jnp.sqrt(h01 * h01 + h11 * h11 + n1 * n1 - l10 * l10)
    z0 = beta * h00 / l00
    z1 = (beta * h01 - l10 * z0) / l11
    y1 = z1 / l11
    y0 = (z0 - l10 * y1) / l00
    c1 = y1 / (beta * n0)
    c0 = y0 / beta - h00 * c1
    for i in range(b_ref.shape[0]):
        b, image = b_ref[i], image_ref[i]
        solution_ref[i] = c0 * b + c1 * image
        residual_ref[i] = b - c0 * image - c1 * twice_ref[i]


def call(kernel, shapes, *operands, scratch=(), inputs=pltpu.VMEM, flops=0):
    return pl.pallas_call(
        kernel,
        out_shape=[jax.ShapeDtypeStruct(shape, jnp.float32) for shape in shapes],
        in_specs=[pl.BlockSpec(memory_space=inputs)] * len(operands),
        out_specs=[pl.BlockSpec(memory_space=pltpu.VMEM)] * len(shapes),
        scratch_shapes=scratch,
        compiler_params=pltpu.CompilerParams(vmem_limit_bytes=48 * 1024 * 1024),
        cost_estimate=pl.CostEstimate(flops=flops, bytes_accessed=0, transcendentals=0),
    )(*operands)


def swap(first, second, axis):
    count = lax.axis_size(axis)
    turns = []
    for array, start in ((first, 0), (second, 1)):
        pairs = [(i, (i + 1) % count) for i in range(start, count, 2)]
        turns.append(lax.ppermute(array, axis, pairs + [(j, i) for i, j in pairs]))
    return turns


def everyones(sketch):
    count = lax.axis_size("gx") * lax.axis_size("gy")
    copies = jnp.broadcast_to(sketch[None], (count,) + sketch.shape)
    return lax.all_to_all(copies, ("gx", "gy"), 0, 0)


def body(b, warmth, phase, slots, draw):
    planes, rows, depth = b.shape
    block, plane, wide = b.shape, (3, rows, depth), (planes + 2, rows, depth)
    line, table = (3 * planes + 4, depth), (8, SKETCH)
    cells = pltpu.VMEM((depth // LANES, planes * rows * 8, LANES), jnp.float32)
    work = b.size * SKETCH * 6
    b, cond, cap, inner, first, second = call(
        first_kernel,
        [block, block, block, block, plane, plane],
        *(pltpu.with_memory_space_constraint(x, pltpu.HBM) for x in (b, warmth, phase)),
        scratch=[
            pltpu.VMEM(block, warmth.dtype),
            pltpu.VMEM(block, phase.dtype),
            pltpu.SemaphoreType.DMA((3,)),
        ],
        inputs=pltpu.HBM,
    )
    image_wide, beside, first, second = call(
        second_kernel,
        [wide, (4, rows, depth), line, line],
        b, cond, inner, *swap(first, second, "gx"),
    )
    got = swap(first, second, "gy")
    (inside,) = call(
        inside_kernel,
        [table],
        b, cond, cap, slots, draw, image_wide, beside,
        scratch=[cells],
        flops=work,
    )
    image, twice, sketch = call(
        third_kernel,
        [block, block, (FIELDS + 1, SKETCH)],
        b, cond, cap, slots, draw, image_wide, beside, *got, inside,
        scratch=[cells],
        flops=work,
    )
    return tuple(call(last_kernel, [block, block], everyones(sketch), b, image, twice))


def solution(mesh):
    spec = P(("parts", "gx"), "gy", None)
    return jax.shard_map(
        body, mesh=mesh, in_specs=(spec,) * 5, out_specs=(spec,) * 2, check_vma=False
    )
```

```python
import jax
import jax.numpy as jnp
from jax import lax
from jax.experimental import pallas as pl
from jax.experimental.pallas import tpu as pltpu
from jax.sharding import PartitionSpec as P

SKETCH = 128
LOW = 32
HIGH = SKETCH // LOW
FIELDS = 3
LANES = 128
epsilon = 1e-06


def traits(warmth, phase):
    powder, solid = phase == 0, phase == 1
    offset = jnp.where(powder, 0.2, jnp.where(solid, 1.0, 0.6))
    return offset * (0.5 + warmth), jnp.where(powder, 1.0, jnp.where(solid, 2.0, 1.5))


def link(first, second):
    total = first + second
    return 2.0 * first * second / jnp.where(total > 0.0, total, 1.0)


def ahead(plane, axis):
    return pltpu.roll(plane, plane.shape[axis] - 1, axis)


def inner_links(cond):
    links = []
    for axis in (0, 1):
        index = lax.broadcasted_iota(jnp.int32, cond.shape, axis)
        links.append(
            jnp.where(index < cond.shape[axis] - 1, link(cond, ahead(cond, axis)), 0.0)
        )
    return links


def inner_flow(field, links):
    total = None
    for axis in (0, 1):
        flow = links[axis] * (field - ahead(field, axis))
        part = flow - pltpu.roll(flow, 1, axis)
        total = part if total is None else total + part
    return total


def apply_inside(images, c_wide, caps):
    results = []
    flow_low = link(c_wide[0], c_wide[1]) * (images[0] - images[1])
    for i in range(1, len(images) - 1):
        image = images[i]
        flow = link(c_wide[i], c_wide[i + 1]) * (image - images[i + 1])
        results.append(
            caps[i - 1] * image + inner_flow(image, inner_links(c_wide[i])) + (flow - flow_low)
        )
        flow_low = flow
    return results


def sketch_rows(fields, draws, slots, chosen, cells_ref):
    rows, depth = draws[0].shape
    for i, draw in enumerate(draws):
        coarse, fine = [], []
        for field in fields:
            weighted = draw * field[i]
            head = weighted.astype(jnp.bfloat16).astype(jnp.float32)
            coarse.append(head)
            fine.append(weighted - head)
        for f, part in enumerate(coarse + coarse[:1] + fine + fine[:1]):
            for t in range(depth // LANES):
                cells_ref[t, pl.ds(i * rows * 8 + f, rows, stride=8), :] = part[
                    :, t * LANES : (t + 1) * LANES
                ]
    low_index = lax.broadcasted_iota(jnp.int32, (LOW, depth), 0)
    low_index = low_index.astype(jnp.float32).astype(jnp.bfloat16)
    high_index = lax.broadcasted_iota(jnp.int32, (HIGH * 8, depth), 0) // 8
    high_index = high_index.astype(jnp.float32).astype(jnp.bfloat16)
    total = jnp.zeros((HIGH * 8, LOW), jnp.float32)
    for i, slot in enumerate(slots):
        low = (slot & (LOW - 1)).astype(jnp.float32)
        high = (slot >> (LOW.bit_length() - 1)).astype(jnp.float32)
        left, right = [], []
        for j in chosen:
            at = pl.ds((i * rows + j) * 8, 8)
            cells = [cells_ref[t, at, :] for t in range(depth // LANES)]
            cells = jnp.concatenate(cells, axis=1)
            cells = jnp.concatenate([cells] * HIGH, axis=0).astype(jnp.bfloat16)
            row_high = jnp.broadcast_to(high[j : j + 1], cells.shape).astype(jnp.bfloat16)
            row_low = jnp.broadcast_to(low[j : j + 1], (LOW, depth)).astype(jnp.bfloat16)
            left.append(jnp.where(row_high == high_index, cells, jnp.zeros_like(cells)))
            right.append(
                jnp.where(row_low == low_index, jnp.ones_like(row_low), jnp.zeros_like(row_low))
            )
        total = total + lax.dot_general(
            jnp.concatenate(left, axis=1),
            jnp.concatenate(right, axis=1),
            (((1,), (1,)), ((), ())),
            preferred_element_type=jnp.float32,
        )
    parts = jnp.concatenate([total[h * 8 : h * 8 + 8] for h in range(HIGH)], axis=1)
    return parts + pltpu.roll(parts, 4, 0)


def first_kernel(
    b_hbm, warmth_hbm, phase_hbm, b_ref, cond_ref, cap_ref, inner_ref, first_ref, second_ref,
    warmth_ref, phase_ref, arrived,
):
    copies = [
        pltpu.make_async_copy(source, target, arrived.at[k])
        for k, (source, target) in enumerate(
            ((b_hbm, b_ref), (warmth_hbm, warmth_ref), (phase_hbm, phase_ref))
        )
    ]
    for copy in copies:
        copy.start()
    for copy in copies:
        copy.wait()
    planes = b_ref.shape[0]
    images, conds = [], []
    for i in range(planes):
        cond, cap = traits(warmth_ref[i], phase_ref[i])
        cap_ref[i] = cap
        cond_ref[i] = cond
        field = b_ref[i]
        image = cap * field + inner_flow(field, inner_links(cond))
        if i:
            flow = link(conds[-1], cond) * (b_ref[i - 1] - field)
            images[-1] = images[-1] + flow
            image = image - flow
        conds.append(cond)
        images.append(image)
    for i in range(planes):
        inner_ref[i] = images[i]
    for k, low, high in (
        (0, images[0], images[-1]),
        (1, b_ref[0], b_ref[planes - 1]),
        (2, conds[0], conds[-1]),
    ):
        first_ref[k], second_ref[k] = by_turn(low, high, "gx")


def by_turn(low, high, axis):
    odd = lax.axis_index(axis) % 2 == 1
    return jnp.where(odd, low, high), jnp.where(odd, high, low)


def has_beside(axis):
    at = lax.axis_index(axis)
    return at > 0, at < lax.axis_size(axis) - 1


def second_kernel(
    b_ref, cond_ref, inner_ref, got_first_ref, got_second_ref, wide_ref, beside_ref, first_ref,
    second_ref,
):
    planes, rows = b_ref.shape[0], b_ref.shape[1]
    (image_low, image_high), (b_low, b_high), (c_low, c_high) = (
        by_turn(got_first_ref[k], got_second_ref[k], "gx") for k in range(3)
    )
    below, above = has_beside("gx")
    c_low, c_high = jnp.where(below, c_low, 0.0), jnp.where(above, c_high, 0.0)
    low_flow = link(c_low, cond_ref[0]) * (b_low - b_ref[0])
    high_flow = link(cond_ref[planes - 1], c_high) * (b_ref[planes - 1] - b_high)
    images = [image_low + low_flow] + [inner_ref[i] for i in range(planes)]
    images.append(image_high - high_flow)
    images[1] = images[1] - low_flow
    images[planes] = images[planes] + high_flow
    for i in range(planes + 2):
        wide_ref[i] = images[i]
    for k, plane in enumerate((b_low, b_high, c_low, c_high)):
        beside_ref[k] = plane
    lines = images[1:-1] + [b_low] + [b_ref[i] for i in range(planes)] + [b_high, c_low]
    lines += [cond_ref[i] for i in range(planes)] + [c_high]
    for k, plane in enumerate(lines):
        low, high = by_turn(plane[:1], plane[rows - 1 :], "gy")
        first_ref[k : k + 1] = low
        second_ref[k : k + 1] = high


def reached(rows):
    others = [j for j in range(rows) if 2 <= j < rows - 2]
    return [j for j in range(rows) if j not in others], others


def widened(ref, beside_ref, which):
    inner = [ref[i] for i in range(ref.shape[0])]
    return [beside_ref[which]] + inner + [beside_ref[which + 1]]


def inside_kernel(
    b_ref, cond_ref, cap_ref, slot_ref, draw_ref, wide_ref, beside_ref, sketch_ref,
    cells_ref,
):
    planes = range(b_ref.shape[0])
    images = [wide_ref[i] for i in range(wide_ref.shape[0])]
    c_wide = widened(cond_ref, beside_ref, 2)
    twice = apply_inside(images, c_wide, [cap_ref[i] for i in planes])
    sketch_ref[...] = sketch_rows(
        [[b_ref[i] for i in planes], images[1:-1], twice],
        [draw_ref[i] for i in planes],
        [slot_ref[i] for i in planes],
        reached(b_ref.shape[1])[1],
        cells_ref,
    )


def third_kernel(
    b_ref, cond_ref, cap_ref, slot_ref, draw_ref, wide_ref, beside_ref, got_first_ref,
    got_second_ref, inside_ref, image_ref, twice_ref, sketch_ref, cells_ref,
):
    planes, rows, depth = b_ref.shape
    index = lax.broadcasted_iota(jnp.int32, (rows, depth), 0)
    b_wide = widened(b_ref, beside_ref, 0)
    c_wide = widened(cond_ref, beside_ref, 2)
    below, above = has_beside("gy")
    at_low = (index == 0) & below
    at_high = (index == rows - 1) & above
    lines = by_turn(got_first_ref[...], got_second_ref[...], "gy")
    images, beside = [], []
    for i in range(planes + 2):
        image = wide_ref[i]
        pairs = []
        for line, mask in zip(lines, (at_low, at_high)):
            at = planes + i
            b_side = jnp.broadcast_to(line[at : at + 1], (rows, depth))
            at = 2 * planes + 2 + i
            c_side = jnp.broadcast_to(line[at : at + 1], (rows, depth))
            conductance = jnp.where(mask, link(c_wide[i], c_side), 0.0)
            flow = conductance * (b_wide[i] - b_side)
            image = image + flow
            if 0 < i <= planes:
                beyond = jnp.broadcast_to(line[i - 1 : i], (rows, depth))
                pairs.append((conductance, beyond - flow))
        images.append(image)
        beside.append(pairs)
    twice = apply_inside(images, c_wide, [cap_ref[i] for i in range(planes)])
    for i in range(planes):
        for conductance, value in beside[i + 1]:
            twice[i] = twice[i] + conductance * (images[i + 1] - value)
        image_ref[i] = images[i + 1]
        twice_ref[i] = twice[i]
    sketch = inside_ref[...] + sketch_rows(
        [b_wide[1:-1], images[1:-1], twice],
        [draw_ref[i] for i in range(planes)],
        [slot_ref[i] for i in range(planes)],
        reached(rows)[0],
        cells_ref,
    )
    sketch_ref[...] = sketch[: FIELDS + 1]


def last_kernel(sketch_ref, b_ref, image_ref, twice_ref, solution_ref, residual_ref):
    sketches = sketch_ref[...]

    def inner(first, second):
        return jnp.sum(first * second, axis=1, keepdims=True)

    s0, s1, s2 = (sketches[i : i + 1] for i in range(FIELDS))
    beta = jnp.sqrt(inner(s0, s0) + epsilon)
    q0 = s0 / beta
    p0 = s1 / beta
    h00 = inner(q0, p0)
    t0 = p0 - h00 * q0
    n0 = jnp.sqrt(inner(t0, t0) + epsilon)
    q1 = t0 / n0
    p1 = (s2 / beta - h00 * p0) / n0
    h01 = inner(q0, p1)
    h11 = inner(q1, p1)
    t1 = p1 - h01 * q0 - h11 * q1
    n1 = jnp.sqrt(inner(t1, t1) + epsilon)
    l00 = jnp.sqrt(h00 * h00 + n0 * n0)
    l10 = (h00 * h01 + n0 * h11) / l00
    l11 = jnp.sqrt(h01 * h01 + h11 * h11 + n1 * n1 - l10 * l10)
    z0 = beta * h00 / l00
    z1 = (beta * h01 - l10 * z0) / l11
    y1 = z1 / l11
    y0 = (z0 - l10 * y1) / l00
    c1 = y1 / (beta * n0)
    c0 = y0 / beta - h00 * c1
    for i in range(b_ref.shape[0]):
        b, image = b_ref[i], image_ref[i]
        solution_ref[i] = c0 * b + c1 * image
        residual_ref[i] = b - c0 * image - c1 * twice_ref[i]


def call(kernel, shapes, *operands, scratch=(), inputs=pltpu.VMEM, flops=0):
    return pl.pallas_call(
        kernel,
        out_shape=[jax.ShapeDtypeStruct(shape, jnp.float32) for shape in shapes],
        in_specs=[pl.BlockSpec(memory_space=inputs)] * len(operands),
        out_specs=[pl.BlockSpec(memory_space=pltpu.VMEM)] * len(shapes),
        scratch_shapes=scratch,
        compiler_params=pltpu.CompilerParams(vmem_limit_bytes=48 * 1024 * 1024),
        cost_estimate=pl.CostEstimate(flops=flops, bytes_accessed=0, transcendentals=0),
    )(*operands)


def swap(first, second, axis):
    count = lax.axis_size(axis)
    turns = []
    for array, start in ((first, 0), (second, 1)):
        pairs = [(i, i + 1) for i in range(start, count - 1, 2)]
        pairs += [(j, i) for i, j in pairs]
        pairs += [(i, i) for i in ((0, count - 1) if start else ())]
        turns.append(lax.ppermute(array, axis, pairs))
    return turns


def sum_over_devices(table):
    for axis in ("gx", "gy"):
        step = 1
        while step < lax.axis_size(axis):
            pairs = [(i, i ^ step) for i in range(lax.axis_size(axis))]
            table = table + lax.ppermute(table, axis, pairs)
            step *= 2
    return table


def body(b, warmth, phase, slots, draw):
    planes, rows, depth = b.shape
    block, plane, wide = b.shape, (3, rows, depth), (planes + 2, rows, depth)
    line, table = (3 * planes + 4, depth), (8, SKETCH)
    cells = pltpu.VMEM((depth // LANES, planes * rows * 8, LANES), jnp.float32)
    work = b.size * SKETCH * 6
    b, cond, cap, inner, first, second = call(
        first_kernel,
        [block, block, block, block, plane, plane],
        *(pltpu.with_memory_space_constraint(x, pltpu.HBM) for x in (b, warmth, phase)),
        scratch=[
            pltpu.VMEM(block, warmth.dtype),
            pltpu.VMEM(block, phase.dtype),
            pltpu.SemaphoreType.DMA((3,)),
        ],
        inputs=pltpu.HBM,
    )
    image_wide, beside, first, second = call(
        second_kernel,
        [wide, (4, rows, depth), line, line],
        b, cond, inner, *swap(first, second, "gx"),
    )
    got = swap(first, second, "gy")
    (inside,) = call(
        inside_kernel,
        [table],
        b, cond, cap, slots, draw, image_wide, beside,
        scratch=[cells],
        flops=work,
    )
    image, twice, sketch = call(
        third_kernel,
        [block, block, (FIELDS + 1, SKETCH)],
        b, cond, cap, slots, draw, image_wide, beside, *got, inside,
        scratch=[cells],
        flops=work,
    )
    return tuple(call(last_kernel, [block, block], sum_over_devices(sketch), b, image, twice))


def solution(mesh):
    spec = P(("parts", "gx"), "gy", None)
    return jax.shard_map(
        body, mesh=mesh, in_specs=(spec,) * 5, out_specs=(spec,) * 2, check_vma=False
    )
```

```python
import jax
import jax.numpy as jnp
from jax import lax
from jax.experimental import pallas as pl
from jax.experimental.pallas import tpu as pltpu
from jax.sharding import PartitionSpec as P

SKETCH = 128
LOW = 32
HIGH = SKETCH // LOW
FIELDS = 3
LANES = 128
epsilon = 1e-06


def traits(warmth, phase):
    powder, solid = phase == 0, phase == 1
    offset = jnp.where(powder, 0.2, jnp.where(solid, 1.0, 0.6))
    return offset * (0.5 + warmth), jnp.where(powder, 1.0, jnp.where(solid, 2.0, 1.5))


def link(first, second):
    total = first + second
    return 2.0 * first * second / jnp.where(total > 0.0, total, 1.0)


def ahead(plane, axis):
    return pltpu.roll(plane, plane.shape[axis] - 1, axis)


def inner_links(cond):
    links = []
    for axis in (0, 1):
        index = lax.broadcasted_iota(jnp.int32, cond.shape, axis)
        links.append(
            jnp.where(index < cond.shape[axis] - 1, link(cond, ahead(cond, axis)), 0.0)
        )
    return links


def inner_flow(field, links):
    total = None
    for axis in (0, 1):
        flow = links[axis] * (field - ahead(field, axis))
        part = flow - pltpu.roll(flow, 1, axis)
        total = part if total is None else total + part
    return total


def apply_inside(images, c_wide, caps):
    results = []
    flow_low = link(c_wide[0], c_wide[1]) * (images[0] - images[1])
    for i in range(1, len(images) - 1):
        image = images[i]
        flow = link(c_wide[i], c_wide[i + 1]) * (image - images[i + 1])
        results.append(
            caps[i - 1] * image + inner_flow(image, inner_links(c_wide[i])) + (flow - flow_low)
        )
        flow_low = flow
    return results


def sketch_rows(fields, draws, slots, chosen, cells_ref):
    rows, depth = draws[0].shape
    for i, draw in enumerate(draws):
        coarse, fine = [], []
        for field in fields:
            weighted = draw * field[i]
            head = weighted.astype(jnp.bfloat16).astype(jnp.float32)
            coarse.append(head)
            fine.append(weighted - head)
        for f, part in enumerate(coarse + coarse[:1] + fine + fine[:1]):
            for t in range(depth // LANES):
                cells_ref[t, pl.ds(i * rows * 8 + f, rows, stride=8), :] = part[
                    :, t * LANES : (t + 1) * LANES
                ]
    low_index = lax.broadcasted_iota(jnp.int32, (LOW, depth), 0)
    low_index = low_index.astype(jnp.float32).astype(jnp.bfloat16)
    high_index = lax.broadcasted_iota(jnp.int32, (HIGH * 8, depth), 0) // 8
    high_index = high_index.astype(jnp.float32).astype(jnp.bfloat16)
    total = jnp.zeros((HIGH * 8, LOW), jnp.float32)
    for i, slot in enumerate(slots):
        low = (slot & (LOW - 1)).astype(jnp.float32)
        high = (slot >> (LOW.bit_length() - 1)).astype(jnp.float32)
        left, right = [], []
        for j in chosen:
            at = pl.ds((i * rows + j) * 8, 8)
            cells = [cells_ref[t, at, :] for t in range(depth // LANES)]
            cells = jnp.concatenate(cells, axis=1)
            cells = jnp.concatenate([cells] * HIGH, axis=0).astype(jnp.bfloat16)
            row_high = jnp.broadcast_to(high[j : j + 1], cells.shape).astype(jnp.bfloat16)
            row_low = jnp.broadcast_to(low[j : j + 1], (LOW, depth)).astype(jnp.bfloat16)
            left.append(jnp.where(row_high == high_index, cells, jnp.zeros_like(cells)))
            right.append(
                jnp.where(row_low == low_index, jnp.ones_like(row_low), jnp.zeros_like(row_low))
            )
        total = total + lax.dot_general(
            jnp.concatenate(left, axis=1),
            jnp.concatenate(right, axis=1),
            (((1,), (1,)), ((), ())),
            preferred_element_type=jnp.float32,
        )
    parts = jnp.concatenate([total[h * 8 : h * 8 + 8] for h in range(HIGH)], axis=1)
    return parts + pltpu.roll(parts, 4, 0)


def first_kernel(
    b_hbm, warmth_hbm, phase_hbm, b_ref, cond_ref, cap_ref, inner_ref, first_ref, second_ref,
    warmth_ref, phase_ref, arrived,
):
    copies = [
        pltpu.make_async_copy(source, target, arrived.at[k])
        for k, (source, target) in enumerate(
            ((b_hbm, b_ref), (warmth_hbm, warmth_ref), (phase_hbm, phase_ref))
        )
    ]
    for copy in copies:
        copy.start()
    for copy in copies:
        copy.wait()
    planes = b_ref.shape[0]
    images, conds = [], []
    for i in range(planes):
        cond, cap = traits(warmth_ref[i], phase_ref[i])
        cap_ref[i] = cap
        cond_ref[i] = cond
        field = b_ref[i]
        image = cap * field + inner_flow(field, inner_links(cond))
        if i:
            flow = link(conds[-1], cond) * (b_ref[i - 1] - field)
            images[-1] = images[-1] + flow
            image = image - flow
        conds.append(cond)
        images.append(image)
    for i in range(planes):
        inner_ref[i] = images[i]
    for k, low, high in (
        (0, images[0], images[-1]),
        (1, b_ref[0], b_ref[planes - 1]),
        (2, conds[0], conds[-1]),
    ):
        first_ref[k], second_ref[k] = to_send(low, high, "gx")


ACROSS = {"gx": "gy", "gy": "gx"}


def to_send(low, high, axis):
    odd = lax.axis_index(ACROSS[axis]) % 2 == 1
    return jnp.where(odd, low, high), jnp.where(odd, high, low)


def from_beside(first, second, axis):
    odd = lax.axis_index(ACROSS[axis]) % 2 == 1
    return jnp.where(odd, second, first), jnp.where(odd, first, second)


def has_beside(axis):
    at = lax.axis_index(axis)
    return at > 0, at < lax.axis_size(axis) - 1


def second_kernel(
    b_ref, cond_ref, inner_ref, got_first_ref, got_second_ref, wide_ref, beside_ref, first_ref,
    second_ref,
):
    planes, rows = b_ref.shape[0], b_ref.shape[1]
    (image_low, image_high), (b_low, b_high), (c_low, c_high) = (
        from_beside(got_first_ref[k], got_second_ref[k], "gx") for k in range(3)
    )
    below, above = has_beside("gx")
    c_low, c_high = jnp.where(below, c_low, 0.0), jnp.where(above, c_high, 0.0)
    low_flow = link(c_low, cond_ref[0]) * (b_low - b_ref[0])
    high_flow = link(cond_ref[planes - 1], c_high) * (b_ref[planes - 1] - b_high)
    images = [image_low + low_flow] + [inner_ref[i] for i in range(planes)]
    images.append(image_high - high_flow)
    images[1] = images[1] - low_flow
    images[planes] = images[planes] + high_flow
    for i in range(planes + 2):
        wide_ref[i] = images[i]
    for k, plane in enumerate((b_low, b_high, c_low, c_high)):
        beside_ref[k] = plane
    lines = images[1:-1] + [b_low] + [b_ref[i] for i in range(planes)] + [b_high, c_low]
    lines += [cond_ref[i] for i in range(planes)] + [c_high]
    for k, plane in enumerate(lines):
        low, high = to_send(plane[:1], plane[rows - 1 :], "gy")
        first_ref[k : k + 1] = low
        second_ref[k : k + 1] = high


def reached(rows):
    others = [j for j in range(rows) if 2 <= j < rows - 2]
    return [j for j in range(rows) if j not in others], others


def widened(ref, beside_ref, which):
    inner = [ref[i] for i in range(ref.shape[0])]
    return [beside_ref[which]] + inner + [beside_ref[which + 1]]


def inside_kernel(
    b_ref, cond_ref, cap_ref, slot_ref, draw_ref, wide_ref, beside_ref, sketch_ref,
    cells_ref,
):
    planes = range(b_ref.shape[0])
    images = [wide_ref[i] for i in range(wide_ref.shape[0])]
    c_wide = widened(cond_ref, beside_ref, 2)
    twice = apply_inside(images, c_wide, [cap_ref[i] for i in planes])
    sketch_ref[...] = sketch_rows(
        [[b_ref[i] for i in planes], images[1:-1], twice],
        [draw_ref[i] for i in planes],
        [slot_ref[i] for i in planes],
        reached(b_ref.shape[1])[1],
        cells_ref,
    )


def third_kernel(
    b_ref, cond_ref, cap_ref, slot_ref, draw_ref, wide_ref, beside_ref, got_first_ref,
    got_second_ref, inside_ref, image_ref, twice_ref, sketch_ref, cells_ref,
):
    planes, rows, depth = b_ref.shape
    index = lax.broadcasted_iota(jnp.int32, (rows, depth), 0)
    b_wide = widened(b_ref, beside_ref, 0)
    c_wide = widened(cond_ref, beside_ref, 2)
    below, above = has_beside("gy")
    at_low = (index == 0) & below
    at_high = (index == rows - 1) & above
    lines = from_beside(got_first_ref[...], got_second_ref[...], "gy")
    images, beside = [], []
    for i in range(planes + 2):
        image = wide_ref[i]
        pairs = []
        for line, mask in zip(lines, (at_low, at_high)):
            at = planes + i
            b_side = jnp.broadcast_to(line[at : at + 1], (rows, depth))
            at = 2 * planes + 2 + i
            c_side = jnp.broadcast_to(line[at : at + 1], (rows, depth))
            conductance = jnp.where(mask, link(c_wide[i], c_side), 0.0)
            flow = conductance * (b_wide[i] - b_side)
            image = image + flow
            if 0 < i <= planes:
                beyond = jnp.broadcast_to(line[i - 1 : i], (rows, depth))
                pairs.append((conductance, beyond - flow))
        images.append(image)
        beside.append(pairs)
    twice = apply_inside(images, c_wide, [cap_ref[i] for i in range(planes)])
    for i in range(planes):
        for conductance, value in beside[i + 1]:
            twice[i] = twice[i] + conductance * (images[i + 1] - value)
        image_ref[i] = images[i + 1]
        twice_ref[i] = twice[i]
    sketch = inside_ref[...] + sketch_rows(
        [b_wide[1:-1], images[1:-1], twice],
        [draw_ref[i] for i in range(planes)],
        [slot_ref[i] for i in range(planes)],
        reached(rows)[0],
        cells_ref,
    )
    sketch_ref[...] = sketch[: FIELDS + 1]


def last_kernel(sketch_ref, b_ref, image_ref, twice_ref, solution_ref, residual_ref):
    sketches = jnp.sum(sketch_ref[...], axis=0)

    def inner(first, second):
        return jnp.sum(first * second, axis=1, keepdims=True)

    s0, s1, s2 = (sketches[i : i + 1] for i in range(FIELDS))
    beta = jnp.sqrt(inner(s0, s0) + epsilon)
    q0 = s0 / beta
    p0 = s1 / beta
    h00 = inner(q0, p0)
    t0 = p0 - h00 * q0
    n0 = jnp.sqrt(inner(t0, t0) + epsilon)
    q1 = t0 / n0
    p1 = (s2 / beta - h00 * p0) / n0
    h01 = inner(q0, p1)
    h11 = inner(q1, p1)
    t1 = p1 - h01 * q0 - h11 * q1
    n1 = jnp.sqrt(inner(t1, t1) + epsilon)
    l00 = jnp.sqrt(h00 * h00 + n0 * n0)
    l10 = (h00 * h01 + n0 * h11) / l00
    l11 = jnp.sqrt(h01 * h01 + h11 * h11 + n1 * n1 - l10 * l10)
    z0 = beta * h00 / l00
    z1 = (beta * h01 - l10 * z0) / l11
    y1 = z1 / l11
    y0 = (z0 - l10 * y1) / l00
    c1 = y1 / (beta * n0)
    c0 = y0 / beta - h00 * c1
    for i in range(b_ref.shape[0]):
        b, image = b_ref[i], image_ref[i]
        solution_ref[i] = c0 * b + c1 * image
        residual_ref[i] = b - c0 * image - c1 * twice_ref[i]


def call(kernel, shapes, *operands, scratch=(), inputs=pltpu.VMEM, flops=0):
    return pl.pallas_call(
        kernel,
        out_shape=[jax.ShapeDtypeStruct(shape, jnp.float32) for shape in shapes],
        in_specs=[pl.BlockSpec(memory_space=inputs)] * len(operands),
        out_specs=[pl.BlockSpec(memory_space=pltpu.VMEM)] * len(shapes),
        scratch_shapes=scratch,
        compiler_params=pltpu.CompilerParams(vmem_limit_bytes=48 * 1024 * 1024),
        cost_estimate=pl.CostEstimate(flops=flops, bytes_accessed=0, transcendentals=0),
    )(*operands)


def swap(first, second, axis):
    count, across = lax.axis_size(axis), lax.axis_size(ACROSS[axis])

    def number(place, line):
        at = (place, line) if axis == "gx" else (line, place)
        return at[0] * lax.axis_size("gy") + at[1]

    pairs = []
    for line in range(0, across, 2):
        cycle = [number(i, line) for i in range(count)]
        cycle += [number(i, line + 1) for i in reversed(range(count))]
        pairs += list(zip(cycle, cycle[1:] + cycle[:1]))
    back = [(j, i) for i, j in pairs]
    return lax.ppermute(first, ("gx", "gy"), pairs), lax.ppermute(second, ("gx", "gy"), back)


def everyones(sketch):
    nx, ny = lax.axis_size("gx"), lax.axis_size("gy")
    pairs = [(i, i ^ 1) for i in range(nx)]
    sketch = sketch + lax.ppermute(sketch, "gx", pairs)
    groups = [[x * ny + y for x in range(turn, nx, 2) for y in range(ny)] for turn in range(2)]
    copies = jnp.broadcast_to(sketch[None], (nx // 2 * ny,) + sketch.shape)
    return lax.all_to_all(copies, ("gx", "gy"), 0, 0, axis_index_groups=groups)


def body(b, warmth, phase, slots, draw):
    planes, rows, depth = b.shape
    block, plane, wide = b.shape, (3, rows, depth), (planes + 2, rows, depth)
    line, table = (3 * planes + 4, depth), (8, SKETCH)
    cells = pltpu.VMEM((depth // LANES, planes * rows * 8, LANES), jnp.float32)
    work = b.size * SKETCH * 6
    b, cond, cap, inner, first, second = call(
        first_kernel,
        [block, block, block, block, plane, plane],
        *(pltpu.with_memory_space_constraint(x, pltpu.HBM) for x in (b, warmth, phase)),
        scratch=[
            pltpu.VMEM(block, warmth.dtype),
            pltpu.VMEM(block, phase.dtype),
            pltpu.SemaphoreType.DMA((3,)),
        ],
        inputs=pltpu.HBM,
    )
    image_wide, beside, first, second = call(
        second_kernel,
        [wide, (4, rows, depth), line, line],
        b, cond, inner, *swap(first, second, "gx"),
    )
    got = swap(first, second, "gy")
    (inside,) = call(
        inside_kernel,
        [table],
        b, cond, cap, slots, draw, image_wide, beside,
        scratch=[cells],
        flops=work,
    )
    image, twice, sketch = call(
        third_kernel,
        [block, block, (FIELDS + 1, SKETCH)],
        b, cond, cap, slots, draw, image_wide, beside, *got, inside,
        scratch=[cells],
        flops=work,
    )
    return tuple(call(last_kernel, [block, block], everyones(sketch), b, image, twice))


def solution(mesh):
    spec = P(("parts", "gx"), "gy", None)
    return jax.shard_map(
        body, mesh=mesh, in_specs=(spec,) * 5, out_specs=(spec,) * 2, check_vma=False
    )
```

```python
import jax
import jax.numpy as jnp
from jax import lax
from jax.experimental import pallas as pl
from jax.experimental.pallas import tpu as pltpu
from jax.sharding import PartitionSpec as P

SKETCH = 128
LOW = 32
HIGH = SKETCH // LOW
FIELDS = 3
LANES = 128
epsilon = 1e-06


def traits(warmth, phase):
    powder, solid = phase == 0, phase == 1
    offset = jnp.where(powder, 0.2, jnp.where(solid, 1.0, 0.6))
    return offset * (0.5 + warmth), jnp.where(powder, 1.0, jnp.where(solid, 2.0, 1.5))


def link(first, second):
    total = first + second
    return 2.0 * first * second / jnp.where(total > 0.0, total, 1.0)


def ahead(plane, axis):
    return pltpu.roll(plane, plane.shape[axis] - 1, axis)


def inner_links(cond):
    links = []
    for axis in (0, 1):
        index = lax.broadcasted_iota(jnp.int32, cond.shape, axis)
        links.append(
            jnp.where(index < cond.shape[axis] - 1, link(cond, ahead(cond, axis)), 0.0)
        )
    return links


def inner_flow(field, links):
    total = None
    for axis in (0, 1):
        flow = links[axis] * (field - ahead(field, axis))
        part = flow - pltpu.roll(flow, 1, axis)
        total = part if total is None else total + part
    return total


def apply_inside(images, c_wide, caps):
    results = []
    flow_low = link(c_wide[0], c_wide[1]) * (images[0] - images[1])
    for i in range(1, len(images) - 1):
        image = images[i]
        flow = link(c_wide[i], c_wide[i + 1]) * (image - images[i + 1])
        results.append(
            caps[i - 1] * image + inner_flow(image, inner_links(c_wide[i])) + (flow - flow_low)
        )
        flow_low = flow
    return results


def sketch_rows(fields, draws, slots, chosen, cells_ref):
    rows, depth = draws[0].shape
    for i, draw in enumerate(draws):
        coarse, fine = [], []
        for field in fields:
            weighted = draw * field[i]
            head = weighted.astype(jnp.bfloat16).astype(jnp.float32)
            coarse.append(head)
            fine.append(weighted - head)
        for f, part in enumerate(coarse + coarse[:1] + fine + fine[:1]):
            for t in range(depth // LANES):
                cells_ref[t, pl.ds(i * rows * 8 + f, rows, stride=8), :] = part[
                    :, t * LANES : (t + 1) * LANES
                ]
    low_index = lax.broadcasted_iota(jnp.int32, (LOW, depth), 0)
    low_index = low_index.astype(jnp.float32).astype(jnp.bfloat16)
    high_index = lax.broadcasted_iota(jnp.int32, (HIGH * 8, depth), 0) // 8
    high_index = high_index.astype(jnp.float32).astype(jnp.bfloat16)
    total = jnp.zeros((HIGH * 8, LOW), jnp.float32)
    for i, slot in enumerate(slots):
        low = (slot & (LOW - 1)).astype(jnp.float32)
        high = (slot >> (LOW.bit_length() - 1)).astype(jnp.float32)
        left, right = [], []
        for j in chosen:
            at = pl.ds((i * rows + j) * 8, 8)
            cells = [cells_ref[t, at, :] for t in range(depth // LANES)]
            cells = jnp.concatenate(cells, axis=1)
            cells = jnp.concatenate([cells] * HIGH, axis=0).astype(jnp.bfloat16)
            row_high = jnp.broadcast_to(high[j : j + 1], cells.shape).astype(jnp.bfloat16)
            row_low = jnp.broadcast_to(low[j : j + 1], (LOW, depth)).astype(jnp.bfloat16)
            left.append(jnp.where(row_high == high_index, cells, jnp.zeros_like(cells)))
            right.append(
                jnp.where(row_low == low_index, jnp.ones_like(row_low), jnp.zeros_like(row_low))
            )
        total = total + lax.dot_general(
            jnp.concatenate(left, axis=1),
            jnp.concatenate(right, axis=1),
            (((1,), (1,)), ((), ())),
            preferred_element_type=jnp.float32,
        )
    parts = jnp.concatenate([total[h * 8 : h * 8 + 8] for h in range(HIGH)], axis=1)
    return parts + pltpu.roll(parts, 4, 0)


def first_kernel(
    b_hbm, warmth_hbm, phase_hbm, b_ref, cond_ref, cap_ref, inner_ref, x_first_ref,
    x_second_ref, y_first_ref, y_second_ref, warmth_ref, phase_ref, arrived,
):
    copies = [
        pltpu.make_async_copy(source, target, arrived.at[k])
        for k, (source, target) in enumerate(
            ((b_hbm, b_ref), (warmth_hbm, warmth_ref), (phase_hbm, phase_ref))
        )
    ]
    for copy in copies:
        copy.start()
    for copy in copies:
        copy.wait()
    planes, rows = b_ref.shape[:2]
    images, conds = [], []
    for i in range(planes):
        cond, cap = traits(warmth_ref[i], phase_ref[i])
        cap_ref[i] = cap
        cond_ref[i] = cond
        field = b_ref[i]
        image = cap * field + inner_flow(field, inner_links(cond))
        if i:
            flow = link(conds[-1], cond) * (b_ref[i - 1] - field)
            images[-1] = images[-1] + flow
            image = image - flow
        conds.append(cond)
        images.append(image)
    for i in range(planes):
        inner_ref[i] = images[i]
    for k, field in enumerate((images, [b_ref[i] for i in range(planes)], conds)):
        x_first_ref[k], x_second_ref[k] = to_send(field[0], field[-1], "gx")
        for i, plane in enumerate(field):
            at = slice(k * planes + i, k * planes + i + 1)
            y_first_ref[at], y_second_ref[at] = to_send(plane[:1], plane[rows - 1 :], "gy")


ACROSS = {"gx": "gy", "gy": "gx"}


def to_send(low, high, axis):
    odd = lax.axis_index(ACROSS[axis]) % 2 == 1
    return jnp.where(odd, low, high), jnp.where(odd, high, low)


def from_beside(first, second, axis):
    odd = lax.axis_index(ACROSS[axis]) % 2 == 1
    return jnp.where(odd, second, first), jnp.where(odd, first, second)


def has_beside(axis):
    at = lax.axis_index(axis)
    return at > 0, at < lax.axis_size(axis) - 1


def second_kernel(
    b_ref, cond_ref, inner_ref, got_first_ref, got_second_ref, wide_ref, beside_ref, first_ref,
    second_ref,
):
    planes, rows = b_ref.shape[0], b_ref.shape[1]
    (image_low, image_high), (b_low, b_high), (c_low, c_high) = (
        from_beside(got_first_ref[k], got_second_ref[k], "gx") for k in range(3)
    )
    below, above = has_beside("gx")
    c_low, c_high = jnp.where(below, c_low, 0.0), jnp.where(above, c_high, 0.0)
    low_flow = link(c_low, cond_ref[0]) * (b_low - b_ref[0])
    high_flow = link(cond_ref[planes - 1], c_high) * (b_ref[planes - 1] - b_high)
    images = [image_low + low_flow] + [inner_ref[i] for i in range(planes)]
    images.append(image_high - high_flow)
    images[1] = images[1] - low_flow
    images[planes] = images[planes] + high_flow
    for i in range(planes + 2):
        wide_ref[i] = images[i]
    for k, plane in enumerate((b_low, b_high, c_low, c_high)):
        beside_ref[k] = plane
        at = slice(k, k + 1)
        first_ref[at], second_ref[at] = to_send(plane[:1], plane[rows - 1 :], "gy")


def reached(rows):
    others = [j for j in range(rows) if 2 <= j < rows - 2]
    return [j for j in range(rows) if j not in others], others


def widened(ref, beside_ref, which):
    inner = [ref[i] for i in range(ref.shape[0])]
    return [beside_ref[which]] + inner + [beside_ref[which + 1]]


def inside_kernel(
    b_ref, cond_ref, cap_ref, slot_ref, draw_ref, wide_ref, beside_ref, sketch_ref,
    cells_ref,
):
    planes = range(b_ref.shape[0])
    images = [wide_ref[i] for i in range(wide_ref.shape[0])]
    c_wide = widened(cond_ref, beside_ref, 2)
    twice = apply_inside(images, c_wide, [cap_ref[i] for i in planes])
    sketch_ref[...] = sketch_rows(
        [[b_ref[i] for i in planes], images[1:-1], twice],
        [draw_ref[i] for i in planes],
        [slot_ref[i] for i in planes],
        reached(b_ref.shape[1])[1],
        cells_ref,
    )


def third_kernel(
    b_ref, cond_ref, cap_ref, slot_ref, draw_ref, wide_ref, beside_ref, got_first_ref,
    got_second_ref, corner_first_ref, corner_second_ref, inside_ref, image_ref, twice_ref, sketch_ref, cells_ref,
):
    planes, rows, depth = b_ref.shape
    index = lax.broadcasted_iota(jnp.int32, (rows, depth), 0)
    b_wide = widened(b_ref, beside_ref, 0)
    c_wide = widened(cond_ref, beside_ref, 2)
    lines = from_beside(got_first_ref[...], got_second_ref[...], "gy")
    corners = from_beside(corner_first_ref[...], corner_second_ref[...], "gy")
    images = [wide_ref[i] for i in range(planes + 2)]
    beside = []
    for j, here, line, corner in zip((0, rows - 1), has_beside("gy"), lines, corners):
        parts = [[line[k * planes + i :][:1] for i in range(planes)] for k in range(3)]
        beyond, b_line, c_line = parts
        b_line = [corner[0:1]] + b_line + [corner[1:2]]
        c_line = [corner[2:3]] + c_line + [corner[3:4]]
        c_line = [jnp.where(here, c, 0.0) for c in c_line]
        beyond[0] = beyond[0] + link(c_line[0], c_line[1]) * (b_line[1] - b_line[0])
        beyond[-1] = beyond[-1] + link(c_line[-2], c_line[-1]) * (b_line[-2] - b_line[-1])
        for i in range(planes + 2):
            conductance = link(c_wide[i], jnp.broadcast_to(c_line[i], (rows, depth)))
            conductance = jnp.where(index == j, conductance, 0.0)
            flow = conductance * (b_wide[i] - b_line[i])
            images[i] = images[i] + flow
            if 0 < i <= planes:
                beside.append((i, conductance, beyond[i - 1] - flow))
    twice = apply_inside(images, c_wide, [cap_ref[i] for i in range(planes)])
    for i, conductance, value in beside:
        twice[i - 1] = twice[i - 1] + conductance * (images[i] - value)
    for i in range(planes):
        image_ref[i] = images[i + 1]
        twice_ref[i] = twice[i]
    sketch = inside_ref[...] + sketch_rows(
        [b_wide[1:-1], images[1:-1], twice],
        [draw_ref[i] for i in range(planes)],
        [slot_ref[i] for i in range(planes)],
        reached(rows)[0],
        cells_ref,
    )
    sketch_ref[...] = sketch[: FIELDS + 1]


def last_kernel(sketch_ref, b_ref, image_ref, twice_ref, solution_ref, residual_ref):
    sketches = jnp.sum(sketch_ref[...], axis=0)

    def inner(first, second):
        return jnp.sum(first * second, axis=1, keepdims=True)

    s0, s1, s2 = (sketches[i : i + 1] for i in range(FIELDS))
    beta = jnp.sqrt(inner(s0, s0) + epsilon)
    q0 = s0 / beta
    p0 = s1 / beta
    h00 = inner(q0, p0)
    t0 = p0 - h00 * q0
    n0 = jnp.sqrt(inner(t0, t0) + epsilon)
    q1 = t0 / n0
    p1 = (s2 / beta - h00 * p0) / n0
    h01 = inner(q0, p1)
    h11 = inner(q1, p1)
    t1 = p1 - h01 * q0 - h11 * q1
    n1 = jnp.sqrt(inner(t1, t1) + epsilon)
    l00 = jnp.sqrt(h00 * h00 + n0 * n0)
    l10 = (h00 * h01 + n0 * h11) / l00
    l11 = jnp.sqrt(h01 * h01 + h11 * h11 + n1 * n1 - l10 * l10)
    z0 = beta * h00 / l00
    z1 = (beta * h01 - l10 * z0) / l11
    y1 = z1 / l11
    y0 = (z0 - l10 * y1) / l00
    c1 = y1 / (beta * n0)
    c0 = y0 / beta - h00 * c1
    for i in range(b_ref.shape[0]):
        b, image = b_ref[i], image_ref[i]
        solution_ref[i] = c0 * b + c1 * image
        residual_ref[i] = b - c0 * image - c1 * twice_ref[i]


def call(kernel, shapes, *operands, scratch=(), inputs=pltpu.VMEM, flops=0):
    return pl.pallas_call(
        kernel,
        out_shape=[jax.ShapeDtypeStruct(shape, jnp.float32) for shape in shapes],
        in_specs=[pl.BlockSpec(memory_space=inputs)] * len(operands),
        out_specs=[pl.BlockSpec(memory_space=pltpu.VMEM)] * len(shapes),
        scratch_shapes=scratch,
        compiler_params=pltpu.CompilerParams(vmem_limit_bytes=48 * 1024 * 1024),
        cost_estimate=pl.CostEstimate(flops=flops, bytes_accessed=0, transcendentals=0),
    )(*operands)


def swap(first, second, axis):
    count, across = lax.axis_size(axis), lax.axis_size(ACROSS[axis])

    def number(place, line):
        at = (place, line) if axis == "gx" else (line, place)
        return at[0] * lax.axis_size("gy") + at[1]

    pairs = []
    for line in range(0, across, 2):
        cycle = [number(i, line) for i in range(count)]
        cycle += [number(i, line + 1) for i in reversed(range(count))]
        pairs += list(zip(cycle, cycle[1:] + cycle[:1]))
    back = [(j, i) for i, j in pairs]
    return lax.ppermute(first, ("gx", "gy"), pairs), lax.ppermute(second, ("gx", "gy"), back)


def everyones(sketch):
    count = lax.axis_size("gx") * lax.axis_size("gy")
    copies = jnp.broadcast_to(sketch[None], (count,) + sketch.shape)
    return lax.all_to_all(copies, ("gx", "gy"), 0, 0)


def body(b, warmth, phase, slots, draw):
    planes, rows, depth = b.shape
    block, plane, wide = b.shape, (3, rows, depth), (planes + 2, rows, depth)
    line, corner, table = (3 * planes, depth), (4, depth), (8, SKETCH)
    cells = pltpu.VMEM((depth // LANES, planes * rows * 8, LANES), jnp.float32)
    work = b.size * SKETCH * 6
    b, cond, cap, inner, x_first, x_second, y_first, y_second = call(
        first_kernel,
        [block, block, block, block, plane, plane, line, line],
        *(pltpu.with_memory_space_constraint(x, pltpu.HBM) for x in (b, warmth, phase)),
        scratch=[
            pltpu.VMEM(block, warmth.dtype),
            pltpu.VMEM(block, phase.dtype),
            pltpu.SemaphoreType.DMA((3,)),
        ],
        inputs=pltpu.HBM,
    )
    got_x = swap(x_first, x_second, "gx")
    got_y = swap(y_first, y_second, "gy")
    image_wide, beside, first, second = call(
        second_kernel, [wide, (4, rows, depth), corner, corner], b, cond, inner, *got_x
    )
    got_corners = swap(first, second, "gy")
    (inside,) = call(
        inside_kernel,
        [table],
        b, cond, cap, slots, draw, image_wide, beside,
        scratch=[cells],
        flops=work,
    )
    image, twice, sketch = call(
        third_kernel,
        [block, block, (FIELDS + 1, SKETCH)],
        b, cond, cap, slots, draw, image_wide, beside, *got_y, *got_corners, inside,
        scratch=[cells],
        flops=work,
    )
    return tuple(call(last_kernel, [block, block], everyones(sketch), b, image, twice))


def solution(mesh):
    spec = P(("parts", "gx"), "gy", None)
    return jax.shard_map(
        body, mesh=mesh, in_specs=(spec,) * 5, out_specs=(spec,) * 2, check_vma=False
    )
```

```python
import jax
import jax.numpy as jnp
from jax import lax
from jax.experimental import pallas as pl
from jax.experimental.pallas import tpu as pltpu
from jax.sharding import PartitionSpec as P

SKETCH = 128
LOW = 32
HIGH = SKETCH // LOW
FIELDS = 3
LANES = 128
epsilon = 1e-06


def traits(warmth, phase):
    powder, solid = phase == 0, phase == 1
    offset = jnp.where(powder, 0.2, jnp.where(solid, 1.0, 0.6))
    return offset * (0.5 + warmth), jnp.where(powder, 1.0, jnp.where(solid, 2.0, 1.5))


def link(first, second):
    total = first + second
    return 2.0 * first * second / jnp.where(total > 0.0, total, 1.0)


def ahead(plane, axis):
    return pltpu.roll(plane, plane.shape[axis] - 1, axis)


def inner_links(cond):
    links = []
    for axis in (0, 1):
        index = lax.broadcasted_iota(jnp.int32, cond.shape, axis)
        links.append(
            jnp.where(index < cond.shape[axis] - 1, link(cond, ahead(cond, axis)), 0.0)
        )
    return links


def inner_flow(field, links):
    total = None
    for axis in (0, 1):
        flow = links[axis] * (field - ahead(field, axis))
        part = flow - pltpu.roll(flow, 1, axis)
        total = part if total is None else total + part
    return total


def apply_inside(images, c_wide, caps):
    results = []
    flow_low = link(c_wide[0], c_wide[1]) * (images[0] - images[1])
    for i in range(1, len(images) - 1):
        image = images[i]
        flow = link(c_wide[i], c_wide[i + 1]) * (image - images[i + 1])
        results.append(
            caps[i - 1] * image + inner_flow(image, inner_links(c_wide[i])) + (flow - flow_low)
        )
        flow_low = flow
    return results


def sketch_rows(fields, draws, slots, chosen, cells_ref):
    rows, depth = draws[0].shape
    for i, draw in enumerate(draws):
        coarse, fine = [], []
        for field in fields:
            weighted = draw * field[i]
            head = weighted.astype(jnp.bfloat16).astype(jnp.float32)
            coarse.append(head)
            fine.append(weighted - head)
        for f, part in enumerate(coarse + coarse[:1] + fine + fine[:1]):
            for t in range(depth // LANES):
                cells_ref[t, pl.ds(i * rows * 8 + f, rows, stride=8), :] = part[
                    :, t * LANES : (t + 1) * LANES
                ]
    low_index = lax.broadcasted_iota(jnp.int32, (LOW, depth), 0)
    low_index = low_index.astype(jnp.float32).astype(jnp.bfloat16)
    high_index = lax.broadcasted_iota(jnp.int32, (HIGH * 8, depth), 0) // 8
    high_index = high_index.astype(jnp.float32).astype(jnp.bfloat16)
    total = jnp.zeros((HIGH * 8, LOW), jnp.float32)
    for i, slot in enumerate(slots):
        low = (slot & (LOW - 1)).astype(jnp.float32)
        high = (slot >> (LOW.bit_length() - 1)).astype(jnp.float32)
        left, right = [], []
        for j in chosen:
            at = pl.ds((i * rows + j) * 8, 8)
            cells = [cells_ref[t, at, :] for t in range(depth // LANES)]
            cells = jnp.concatenate(cells, axis=1)
            cells = jnp.concatenate([cells] * HIGH, axis=0).astype(jnp.bfloat16)
            row_high = jnp.broadcast_to(high[j : j + 1], cells.shape).astype(jnp.bfloat16)
            row_low = jnp.broadcast_to(low[j : j + 1], (LOW, depth)).astype(jnp.bfloat16)
            left.append(jnp.where(row_high == high_index, cells, jnp.zeros_like(cells)))
            right.append(
                jnp.where(row_low == low_index, jnp.ones_like(row_low), jnp.zeros_like(row_low))
            )
        total = total + lax.dot_general(
            jnp.concatenate(left, axis=1),
            jnp.concatenate(right, axis=1),
            (((1,), (1,)), ((), ())),
            preferred_element_type=jnp.float32,
        )
    parts = jnp.concatenate([total[h * 8 : h * 8 + 8] for h in range(HIGH)], axis=1)
    return parts + pltpu.roll(parts, 4, 0)


def first_kernel(
    b_hbm, warmth_hbm, phase_hbm, b_ref, cond_ref, cap_ref, inner_ref, x_first_ref,
    x_second_ref, y_first_ref, y_second_ref, warmth_ref, phase_ref, arrived,
):
    copies = [
        pltpu.make_async_copy(source, target, arrived.at[k])
        for k, (source, target) in enumerate(
            ((b_hbm, b_ref), (warmth_hbm, warmth_ref), (phase_hbm, phase_ref))
        )
    ]
    for copy in copies:
        copy.start()
    for copy in copies:
        copy.wait()
    planes, rows = b_ref.shape[:2]
    images, conds = [], []
    for i in range(planes):
        cond, cap = traits(warmth_ref[i], phase_ref[i])
        cap_ref[i] = cap
        cond_ref[i] = cond
        field = b_ref[i]
        image = cap * field + inner_flow(field, inner_links(cond))
        if i:
            flow = link(conds[-1], cond) * (b_ref[i - 1] - field)
            images[-1] = images[-1] + flow
            image = image - flow
        conds.append(cond)
        images.append(image)
    for i in range(planes):
        inner_ref[i] = images[i]
    for k, field in enumerate((images, [b_ref[i] for i in range(planes)], conds)):
        x_first_ref[k], x_second_ref[k] = by_turn(field[0], field[-1], "gx")
        for i, plane in enumerate(field):
            at = slice(k * planes + i, k * planes + i + 1)
            y_first_ref[at], y_second_ref[at] = by_turn(plane[:1], plane[rows - 1 :], "gy")


def by_turn(one, other, axis):
    odd = lax.axis_index(axis) % 2 == 1
    return jnp.where(odd, one, other), jnp.where(odd, other, one)


def has_beside(axis):
    at = lax.axis_index(axis)
    return at > 0, at < lax.axis_size(axis) - 1


def second_kernel(
    b_ref, cond_ref, inner_ref, got_first_ref, got_second_ref, wide_ref, beside_ref, first_ref,
    second_ref,
):
    planes, rows = b_ref.shape[0], b_ref.shape[1]
    (image_low, image_high), (b_low, b_high), (c_low, c_high) = (
        by_turn(got_first_ref[k], got_second_ref[k], "gx") for k in range(3)
    )
    below, above = has_beside("gx")
    c_low, c_high = jnp.where(below, c_low, 0.0), jnp.where(above, c_high, 0.0)
    low_flow = link(c_low, cond_ref[0]) * (b_low - b_ref[0])
    high_flow = link(cond_ref[planes - 1], c_high) * (b_ref[planes - 1] - b_high)
    images = [image_low + low_flow] + [inner_ref[i] for i in range(planes)]
    images.append(image_high - high_flow)
    images[1] = images[1] - low_flow
    images[planes] = images[planes] + high_flow
    for i in range(planes + 2):
        wide_ref[i] = images[i]
    for k, plane in enumerate((b_low, b_high, c_low, c_high)):
        beside_ref[k] = plane
        at = slice(k, k + 1)
        first_ref[at], second_ref[at] = by_turn(plane[:1], plane[rows - 1 :], "gy")


def reached(rows):
    others = [j for j in range(rows) if 2 <= j < rows - 2]
    return [j for j in range(rows) if j not in others], others


def widened(ref, beside_ref, which):
    inner = [ref[i] for i in range(ref.shape[0])]
    return [beside_ref[which]] + inner + [beside_ref[which + 1]]


def inside_kernel(
    b_ref, cond_ref, cap_ref, slot_ref, draw_ref, wide_ref, beside_ref, sketch_ref,
    cells_ref,
):
    planes = range(b_ref.shape[0])
    images = [wide_ref[i] for i in range(wide_ref.shape[0])]
    c_wide = widened(cond_ref, beside_ref, 2)
    twice = apply_inside(images, c_wide, [cap_ref[i] for i in planes])
    sketch_ref[...] = sketch_rows(
        [[b_ref[i] for i in planes], images[1:-1], twice],
        [draw_ref[i] for i in planes],
        [slot_ref[i] for i in planes],
        reached(b_ref.shape[1])[1],
        cells_ref,
    )


def third_kernel(
    b_ref, cond_ref, cap_ref, slot_ref, draw_ref, wide_ref, beside_ref, got_first_ref,
    got_second_ref, corner_first_ref, corner_second_ref, inside_ref, image_ref, twice_ref, sketch_ref, cells_ref,
):
    planes, rows, depth = b_ref.shape
    index = lax.broadcasted_iota(jnp.int32, (rows, depth), 0)
    b_wide = widened(b_ref, beside_ref, 0)
    c_wide = widened(cond_ref, beside_ref, 2)
    lines = by_turn(got_first_ref[...], got_second_ref[...], "gy")
    corners = by_turn(corner_first_ref[...], corner_second_ref[...], "gy")
    images = [wide_ref[i] for i in range(planes + 2)]
    beside = []
    for j, here, line, corner in zip((0, rows - 1), has_beside("gy"), lines, corners):
        parts = [[line[k * planes + i :][:1] for i in range(planes)] for k in range(3)]
        beyond, b_line, c_line = parts
        b_line = [corner[0:1]] + b_line + [corner[1:2]]
        c_line = [corner[2:3]] + c_line + [corner[3:4]]
        c_line = [jnp.where(here, c, 0.0) for c in c_line]
        beyond[0] = beyond[0] + link(c_line[0], c_line[1]) * (b_line[1] - b_line[0])
        beyond[-1] = beyond[-1] + link(c_line[-2], c_line[-1]) * (b_line[-2] - b_line[-1])
        for i in range(planes + 2):
            conductance = link(c_wide[i], jnp.broadcast_to(c_line[i], (rows, depth)))
            conductance = jnp.where(index == j, conductance, 0.0)
            flow = conductance * (b_wide[i] - b_line[i])
            images[i] = images[i] + flow
            if 0 < i <= planes:
                beside.append((i, conductance, beyond[i - 1] - flow))
    twice = apply_inside(images, c_wide, [cap_ref[i] for i in range(planes)])
    for i, conductance, value in beside:
        twice[i - 1] = twice[i - 1] + conductance * (images[i] - value)
    for i in range(planes):
        image_ref[i] = images[i + 1]
        twice_ref[i] = twice[i]
    sketch = inside_ref[...] + sketch_rows(
        [b_wide[1:-1], images[1:-1], twice],
        [draw_ref[i] for i in range(planes)],
        [slot_ref[i] for i in range(planes)],
        reached(rows)[0],
        cells_ref,
    )
    sketch_ref[...] = sketch[: FIELDS + 1]


def last_kernel(sketch_ref, b_ref, image_ref, twice_ref, solution_ref, residual_ref):
    sketches = jnp.sum(sketch_ref[...], axis=0)

    def inner(first, second):
        return jnp.sum(first * second, axis=1, keepdims=True)

    s0, s1, s2 = (sketches[i : i + 1] for i in range(FIELDS))
    beta = jnp.sqrt(inner(s0, s0) + epsilon)
    q0 = s0 / beta
    p0 = s1 / beta
    h00 = inner(q0, p0)
    t0 = p0 - h00 * q0
    n0 = jnp.sqrt(inner(t0, t0) + epsilon)
    q1 = t0 / n0
    p1 = (s2 / beta - h00 * p0) / n0
    h01 = inner(q0, p1)
    h11 = inner(q1, p1)
    t1 = p1 - h01 * q0 - h11 * q1
    n1 = jnp.sqrt(inner(t1, t1) + epsilon)
    l00 = jnp.sqrt(h00 * h00 + n0 * n0)
    l10 = (h00 * h01 + n0 * h11) / l00
    l11 = jnp.sqrt(h01 * h01 + h11 * h11 + n1 * n1 - l10 * l10)
    z0 = beta * h00 / l00
    z1 = (beta * h01 - l10 * z0) / l11
    y1 = z1 / l11
    y0 = (z0 - l10 * y1) / l00
    c1 = y1 / (beta * n0)
    c0 = y0 / beta - h00 * c1
    for i in range(b_ref.shape[0]):
        b, image = b_ref[i], image_ref[i]
        solution_ref[i] = c0 * b + c1 * image
        residual_ref[i] = b - c0 * image - c1 * twice_ref[i]


def call(kernel, shapes, *operands, scratch=(), inputs=pltpu.VMEM, flops=0):
    return pl.pallas_call(
        kernel,
        out_shape=[jax.ShapeDtypeStruct(shape, jnp.float32) for shape in shapes],
        in_specs=[pl.BlockSpec(memory_space=inputs)] * len(operands),
        out_specs=[pl.BlockSpec(memory_space=pltpu.VMEM)] * len(shapes),
        scratch_shapes=scratch,
        compiler_params=pltpu.CompilerParams(vmem_limit_bytes=48 * 1024 * 1024),
        cost_estimate=pl.CostEstimate(flops=flops, bytes_accessed=0, transcendentals=0),
    )(*operands)


def swap(first, second, axis):
    across = "gy" if axis == "gx" else "gx"
    count, lines = lax.axis_size(axis), lax.axis_size(across)

    def number(place, line):
        at = (place, line) if axis == "gx" else (line, place)
        return at[0] * lax.axis_size("gy") + at[1]

    turns = ([], [])
    for line in range(lines):
        for i in range(count):
            turns[0].append((number(i, line), number(i ^ 1, line)))
            beyond = i + 1 if i % 2 else i - 1
            if 0 <= beyond < count:
                turns[1].append((number(i, line), number(beyond, line)))
            else:
                turns[1].append((number(i, line), number(i, line ^ 1)))
    return [lax.ppermute(x, ("gx", "gy"), turn) for x, turn in zip((first, second), turns)]


def everyones(sketch):
    count = lax.axis_size("gx") * lax.axis_size("gy")
    copies = jnp.broadcast_to(sketch[None], (count,) + sketch.shape)
    return lax.all_to_all(copies, ("gx", "gy"), 0, 0)


def body(b, warmth, phase, slots, draw):
    planes, rows, depth = b.shape
    block, plane, wide = b.shape, (3, rows, depth), (planes + 2, rows, depth)
    line, corner, table = (3 * planes, depth), (4, depth), (8, SKETCH)
    cells = pltpu.VMEM((depth // LANES, planes * rows * 8, LANES), jnp.float32)
    work = b.size * SKETCH * 6
    b, cond, cap, inner, x_first, x_second, y_first, y_second = call(
        first_kernel,
        [block, block, block, block, plane, plane, line, line],
        *(pltpu.with_memory_space_constraint(x, pltpu.HBM) for x in (b, warmth, phase)),
        scratch=[
            pltpu.VMEM(block, warmth.dtype),
            pltpu.VMEM(block, phase.dtype),
            pltpu.SemaphoreType.DMA((3,)),
        ],
        inputs=pltpu.HBM,
    )
    got_x = swap(x_first, x_second, "gx")
    got_y = swap(y_first, y_second, "gy")
    image_wide, beside, first, second = call(
        second_kernel, [wide, (4, rows, depth), corner, corner], b, cond, inner, *got_x
    )
    got_corners = swap(first, second, "gy")
    (inside,) = call(
        inside_kernel,
        [table],
        b, cond, cap, slots, draw, image_wide, beside,
        scratch=[cells],
        flops=work,
    )
    image, twice, sketch = call(
        third_kernel,
        [block, block, (FIELDS + 1, SKETCH)],
        b, cond, cap, slots, draw, image_wide, beside, *got_y, *got_corners, inside,
        scratch=[cells],
        flops=work,
    )
    return tuple(call(last_kernel, [block, block], everyones(sketch), b, image, twice))


def solution(mesh):
    spec = P(("parts", "gx"), "gy", None)
    return jax.shard_map(
        body, mesh=mesh, in_specs=(spec,) * 5, out_specs=(spec,) * 2, check_vma=False
    )
```

```python
import jax
import jax.numpy as jnp
from jax import lax
from jax.experimental import pallas as pl
from jax.experimental.pallas import tpu as pltpu
from jax.sharding import PartitionSpec as P

SKETCH = 128
LOW = 32
HIGH = SKETCH // LOW
FIELDS = 3
LANES = 128
epsilon = 1e-06


def traits(warmth, phase):
    powder, solid = phase == 0, phase == 1
    offset = jnp.where(powder, 0.2, jnp.where(solid, 1.0, 0.6))
    return offset * (0.5 + warmth), jnp.where(powder, 1.0, jnp.where(solid, 2.0, 1.5))


def link(first, second):
    total = first + second
    return 2.0 * first * second / jnp.where(total > 0.0, total, 1.0)


def ahead(plane, axis):
    return pltpu.roll(plane, plane.shape[axis] - 1, axis)


def inner_links(cond):
    links = []
    for axis in (0, 1):
        index = lax.broadcasted_iota(jnp.int32, cond.shape, axis)
        links.append(
            jnp.where(index < cond.shape[axis] - 1, link(cond, ahead(cond, axis)), 0.0)
        )
    return links


def inner_flow(field, links):
    total = None
    for axis in (0, 1):
        flow = links[axis] * (field - ahead(field, axis))
        part = flow - pltpu.roll(flow, 1, axis)
        total = part if total is None else total + part
    return total


def apply_inside(images, c_wide, caps):
    results = []
    flow_low = link(c_wide[0], c_wide[1]) * (images[0] - images[1])
    for i in range(1, len(images) - 1):
        image = images[i]
        flow = link(c_wide[i], c_wide[i + 1]) * (image - images[i + 1])
        results.append(
            caps[i - 1] * image + inner_flow(image, inner_links(c_wide[i])) + (flow - flow_low)
        )
        flow_low = flow
    return results


def sketch_rows(fields, draws, slots, chosen, cells_ref):
    rows, depth = draws[0].shape
    for i, draw in enumerate(draws):
        coarse, fine = [], []
        for field in fields:
            weighted = draw * field[i]
            head = weighted.astype(jnp.bfloat16).astype(jnp.float32)
            coarse.append(head)
            fine.append(weighted - head)
        for f, part in enumerate(coarse + coarse[:1] + fine + fine[:1]):
            for t in range(depth // LANES):
                cells_ref[t, pl.ds(i * rows * 8 + f, rows, stride=8), :] = part[
                    :, t * LANES : (t + 1) * LANES
                ]
    low_index = lax.broadcasted_iota(jnp.int32, (LOW, depth), 0)
    low_index = low_index.astype(jnp.float32).astype(jnp.bfloat16)
    high_index = lax.broadcasted_iota(jnp.int32, (HIGH * 8, depth), 0) // 8
    high_index = high_index.astype(jnp.float32).astype(jnp.bfloat16)
    total = jnp.zeros((HIGH * 8, LOW), jnp.float32)
    for i, slot in enumerate(slots):
        low = (slot & (LOW - 1)).astype(jnp.float32)
        high = (slot >> (LOW.bit_length() - 1)).astype(jnp.float32)
        left, right = [], []
        for j in chosen:
            at = pl.ds((i * rows + j) * 8, 8)
            cells = [cells_ref[t, at, :] for t in range(depth // LANES)]
            cells = jnp.concatenate(cells, axis=1)
            cells = jnp.concatenate([cells] * HIGH, axis=0).astype(jnp.bfloat16)
            row_high = jnp.broadcast_to(high[j : j + 1], cells.shape).astype(jnp.bfloat16)
            row_low = jnp.broadcast_to(low[j : j + 1], (LOW, depth)).astype(jnp.bfloat16)
            left.append(jnp.where(row_high == high_index, cells, jnp.zeros_like(cells)))
            right.append(
                jnp.where(row_low == low_index, jnp.ones_like(row_low), jnp.zeros_like(row_low))
            )
        total = total + lax.dot_general(
            jnp.concatenate(left, axis=1),
            jnp.concatenate(right, axis=1),
            (((1,), (1,)), ((), ())),
            preferred_element_type=jnp.float32,
        )
    parts = jnp.concatenate([total[h * 8 : h * 8 + 8] for h in range(HIGH)], axis=1)
    return parts + pltpu.roll(parts, 4, 0)


def first_kernel(
    b_hbm, warmth_hbm, phase_hbm, b_ref, cond_ref, cap_ref, inner_ref, x_first_ref,
    x_second_ref, y_first_ref, y_second_ref, warmth_ref, phase_ref, arrived,
):
    planes, rows = b_ref.shape[:2]
    pairs = ((b_hbm, b_ref), (warmth_hbm, warmth_ref), (phase_hbm, phase_ref))
    copies = [
        [
            pltpu.make_async_copy(source.at[i], target.at[i], arrived.at[i, k])
            for k, (source, target) in enumerate(pairs)
        ]
        for i in range(planes)
    ]
    for copy in sum(copies, []):
        copy.start()
    images, conds = [], []
    for i in range(planes):
        for copy in copies[i]:
            copy.wait()
        cond, cap = traits(warmth_ref[i], phase_ref[i])
        cap_ref[i] = cap
        cond_ref[i] = cond
        field = b_ref[i]
        image = cap * field + inner_flow(field, inner_links(cond))
        if i:
            flow = link(conds[-1], cond) * (b_ref[i - 1] - field)
            images[-1] = images[-1] + flow
            image = image - flow
        conds.append(cond)
        images.append(image)
    for i in range(planes):
        inner_ref[i] = images[i]
    for k, field in enumerate((images, [b_ref[i] for i in range(planes)], conds)):
        x_first_ref[k], x_second_ref[k] = by_turn(field[0], field[-1], "gx")
        for i, plane in enumerate(field):
            at = slice(k * planes + i, k * planes + i + 1)
            y_first_ref[at], y_second_ref[at] = by_turn(plane[:1], plane[rows - 1 :], "gy")


def by_turn(one, other, axis):
    odd = lax.axis_index(axis) % 2 == 1
    return jnp.where(odd, one, other), jnp.where(odd, other, one)


def has_beside(axis):
    at = lax.axis_index(axis)
    return at > 0, at < lax.axis_size(axis) - 1


def corner_kernel(got_first_ref, got_second_ref, first_ref, second_ref):
    planes = got_first_ref.shape[0] // 3
    sides = zip(by_turn(got_first_ref[...], got_second_ref[...], "gy"), has_beside("gy"))
    for side, (line, here) in enumerate(sides):
        for k, field in ((0, line[planes : 2 * planes]), (2, line[2 * planes :])):
            if k:
                field = jnp.where(here, field, 0.0)
            at = slice(k + side, k + side + 1)
            first_ref[at], second_ref[at] = by_turn(field[:1], field[planes - 1 :], "gx")


def reached(rows):
    others = [j for j in range(rows) if 2 <= j < rows - 2]
    return [j for j in range(rows) if j not in others], others


def widened(ref, beside_ref, which):
    inner = [ref[i] for i in range(ref.shape[0])]
    return [beside_ref[which]] + inner + [beside_ref[which + 1]]


def inside_kernel(
    b_ref, cond_ref, cap_ref, inner_ref, slot_ref, draw_ref, got_first_ref, got_second_ref,
    wide_ref, beside_ref, sketch_ref, cells_ref,
):
    planes = range(b_ref.shape[0])
    (image_low, image_high), (b_low, b_high), (c_low, c_high) = (
        by_turn(got_first_ref[k], got_second_ref[k], "gx") for k in range(3)
    )
    below, above = has_beside("gx")
    c_low, c_high = jnp.where(below, c_low, 0.0), jnp.where(above, c_high, 0.0)
    for k, plane in enumerate((b_low, b_high, c_low, c_high)):
        beside_ref[k] = plane
    c_wide = [c_low] + [cond_ref[i] for i in planes] + [c_high]
    low_flow = link(c_low, c_wide[1]) * (b_low - b_ref[0])
    high_flow = link(c_wide[-2], c_high) * (b_ref[planes[-1]] - b_high)
    images = [image_low + low_flow] + [inner_ref[i] for i in planes] + [image_high - high_flow]
    images[1] = images[1] - low_flow
    images[-2] = images[-2] + high_flow
    for i, image in enumerate(images):
        wide_ref[i] = image
    twice = apply_inside(images, c_wide, [cap_ref[i] for i in planes])
    sketch_ref[...] = sketch_rows(
        [[b_ref[i] for i in planes], images[1:-1], twice],
        [draw_ref[i] for i in planes],
        [slot_ref[i] for i in planes],
        reached(b_ref.shape[1])[1],
        cells_ref,
    )


def third_kernel(
    b_ref, cond_ref, cap_ref, slot_ref, draw_ref, wide_ref, beside_ref, got_first_ref,
    got_second_ref, corner_first_ref, corner_second_ref, inside_ref, image_ref, twice_ref, sketch_ref, cells_ref,
):
    planes, rows, depth = b_ref.shape
    index = lax.broadcasted_iota(jnp.int32, (rows, depth), 0)
    b_wide = widened(b_ref, beside_ref, 0)
    c_wide = widened(cond_ref, beside_ref, 2)
    lines = by_turn(got_first_ref[...], got_second_ref[...], "gy")
    corners = by_turn(corner_first_ref[...], corner_second_ref[...], "gx")
    corners = [[corner[k : k + 1] for k in range(4)] for corner in corners]
    for corner, here in zip(corners, has_beside("gx")):
        corner[2:] = [jnp.where(here, c, 0.0) for c in corner[2:]]
    images = [wide_ref[i] for i in range(planes + 2)]
    beside = []
    for side, (j, here, line) in enumerate(zip((0, rows - 1), has_beside("gy"), lines)):
        parts = [[line[k * planes + i :][:1] for i in range(planes)] for k in range(3)]
        beyond, b_line, c_line = parts
        b_line = [corners[0][side]] + b_line + [corners[1][side]]
        c_line = [corners[0][2 + side]] + c_line + [corners[1][2 + side]]
        c_line = [jnp.where(here, c, 0.0) for c in c_line]
        beyond[0] = beyond[0] + link(c_line[0], c_line[1]) * (b_line[1] - b_line[0])
        beyond[-1] = beyond[-1] + link(c_line[-2], c_line[-1]) * (b_line[-2] - b_line[-1])
        for i in range(planes + 2):
            conductance = link(c_wide[i], jnp.broadcast_to(c_line[i], (rows, depth)))
            conductance = jnp.where(index == j, conductance, 0.0)
            flow = conductance * (b_wide[i] - b_line[i])
            images[i] = images[i] + flow
            if 0 < i <= planes:
                beside.append((i, conductance, beyond[i - 1] - flow))
    twice = apply_inside(images, c_wide, [cap_ref[i] for i in range(planes)])
    for i, conductance, value in beside:
        twice[i - 1] = twice[i - 1] + conductance * (images[i] - value)
    for i in range(planes):
        image_ref[i] = images[i + 1]
        twice_ref[i] = twice[i]
    sketch = inside_ref[...] + sketch_rows(
        [b_wide[1:-1], images[1:-1], twice],
        [draw_ref[i] for i in range(planes)],
        [slot_ref[i] for i in range(planes)],
        reached(rows)[0],
        cells_ref,
    )
    sketch_ref[...] = sketch[: FIELDS + 1]


def last_kernel(
    sketch_ref, b_ref, image_ref, twice_ref, solution_hbm, residual_hbm, solution_ref,
    residual_ref, sent,
):
    sketches = jnp.sum(sketch_ref[...], axis=0)

    def inner(first, second):
        return jnp.sum(first * second, axis=1, keepdims=True)

    s0, s1, s2 = (sketches[i : i + 1] for i in range(FIELDS))
    beta = jnp.sqrt(inner(s0, s0) + epsilon)
    q0 = s0 / beta
    p0 = s1 / beta
    h00 = inner(q0, p0)
    t0 = p0 - h00 * q0
    n0 = jnp.sqrt(inner(t0, t0) + epsilon)
    q1 = t0 / n0
    p1 = (s2 / beta - h00 * p0) / n0
    h01 = inner(q0, p1)
    h11 = inner(q1, p1)
    t1 = p1 - h01 * q0 - h11 * q1
    n1 = jnp.sqrt(inner(t1, t1) + epsilon)
    l00 = jnp.sqrt(h00 * h00 + n0 * n0)
    l10 = (h00 * h01 + n0 * h11) / l00
    l11 = jnp.sqrt(h01 * h01 + h11 * h11 + n1 * n1 - l10 * l10)
    z0 = beta * h00 / l00
    z1 = (beta * h01 - l10 * z0) / l11
    y1 = z1 / l11
    y0 = (z0 - l10 * y1) / l00
    c1 = y1 / (beta * n0)
    c0 = y0 / beta - h00 * c1
    copies = []
    for i in range(b_ref.shape[0]):
        b, image = b_ref[i], image_ref[i]
        solution_ref[i] = c0 * b + c1 * image
        residual_ref[i] = b - c0 * image - c1 * twice_ref[i]
        for k, (source, target) in enumerate(
            ((solution_ref, solution_hbm), (residual_ref, residual_hbm))
        ):
            copies.append(pltpu.make_async_copy(source.at[i], target.at[i], sent.at[i, k]))
            copies[-1].start()
    for copy in copies:
        copy.wait()


def call(
    kernel, shapes, *operands, scratch=(), inputs=pltpu.VMEM, outputs=pltpu.VMEM, flops=0
):
    return pl.pallas_call(
        kernel,
        out_shape=[jax.ShapeDtypeStruct(shape, jnp.float32) for shape in shapes],
        in_specs=[pl.BlockSpec(memory_space=inputs)] * len(operands),
        out_specs=[pl.BlockSpec(memory_space=outputs)] * len(shapes),
        scratch_shapes=scratch,
        compiler_params=pltpu.CompilerParams(vmem_limit_bytes=48 * 1024 * 1024),
        cost_estimate=pl.CostEstimate(flops=flops, bytes_accessed=0, transcendentals=0),
    )(*operands)


def swap(first, second, axis):
    across = "gy" if axis == "gx" else "gx"
    count, lines = lax.axis_size(axis), lax.axis_size(across)

    def number(place, line):
        at = (place, line) if axis == "gx" else (line, place)
        return at[0] * lax.axis_size("gy") + at[1]

    turns = ([], [])
    for line in range(lines):
        for i in range(count):
            turns[0].append((number(i, line), number(i ^ 1, line)))
            beyond = i + 1 if i % 2 else i - 1
            if 0 <= beyond < count:
                turns[1].append((number(i, line), number(beyond, line)))
            else:
                turns[1].append((number(i, line), number(i, line ^ 1)))
    return [lax.ppermute(x, ("gx", "gy"), turn) for x, turn in zip((first, second), turns)]


def everyones(sketch):
    count = lax.axis_size("gx") * lax.axis_size("gy")
    copies = jnp.broadcast_to(sketch[None], (count,) + sketch.shape)
    return lax.all_to_all(copies, ("gx", "gy"), 0, 0)


def body(b, warmth, phase, slots, draw):
    planes, rows, depth = b.shape
    block, plane, wide = b.shape, (3, rows, depth), (planes + 2, rows, depth)
    line, corner, table = (3 * planes, depth), (4, depth), (8, SKETCH)
    cells = pltpu.VMEM((depth // LANES, planes * rows * 8, LANES), jnp.float32)
    work = b.size * SKETCH * 6
    b, cond, cap, inner, x_first, x_second, y_first, y_second = call(
        first_kernel,
        [block, block, block, block, plane, plane, line, line],
        *(pltpu.with_memory_space_constraint(x, pltpu.HBM) for x in (b, warmth, phase)),
        scratch=[
            pltpu.VMEM(block, warmth.dtype),
            pltpu.VMEM(block, phase.dtype),
            pltpu.SemaphoreType.DMA((planes, 3)),
        ],
        inputs=pltpu.HBM,
    )
    got_y = swap(y_first, y_second, "gy")
    got_x = swap(x_first, x_second, "gx")
    got_corners = swap(*call(corner_kernel, [corner, corner], *got_y), "gx")
    image_wide, beside, inside = call(
        inside_kernel,
        [wide, (4, rows, depth), table],
        b, cond, cap, inner, slots, draw, *got_x,
        scratch=[cells],
        flops=work,
    )
    image, twice, sketch = call(
        third_kernel,
        [block, block, (FIELDS + 1, SKETCH)],
        b, cond, cap, slots, draw, image_wide, beside, *got_y, *got_corners, inside,
        scratch=[cells],
        flops=work,
    )
    outputs = call(
        last_kernel,
        [block, block],
        everyones(sketch), b, image, twice,
        scratch=[
            pltpu.VMEM(block, jnp.float32),
            pltpu.VMEM(block, jnp.float32),
            pltpu.SemaphoreType.DMA((planes, 2)),
        ],
        outputs=pltpu.HBM,
    )
    return tuple(outputs)


def solution(mesh):
    spec = P(("parts", "gx"), "gy", None)
    return jax.shard_map(
        body, mesh=mesh, in_specs=(spec,) * 5, out_specs=(spec,) * 2, check_vma=False
    )
```

```python
import jax
import jax.numpy as jnp
from jax import lax
from jax.experimental import pallas as pl
from jax.experimental.pallas import tpu as pltpu
from jax.sharding import PartitionSpec as P

SKETCH = 128
LOW = 32
HIGH = SKETCH // LOW
FIELDS = 3
LANES = 128
epsilon = 1e-06


def traits(warmth, phase):
    powder, solid = phase == 0, phase == 1
    offset = jnp.where(powder, 0.2, jnp.where(solid, 1.0, 0.6))
    return offset * (0.5 + warmth), jnp.where(powder, 1.0, jnp.where(solid, 2.0, 1.5))


def link(first, second):
    total = first + second
    return 2.0 * first * second / jnp.where(total > 0.0, total, 1.0)


def ahead(plane, axis):
    return pltpu.roll(plane, plane.shape[axis] - 1, axis)


def inner_links(cond):
    links = []
    for axis in (0, 1):
        index = lax.broadcasted_iota(jnp.int32, cond.shape, axis)
        links.append(
            jnp.where(index < cond.shape[axis] - 1, link(cond, ahead(cond, axis)), 0.0)
        )
    return links


def inner_flow(field, links):
    total = None
    for axis in (0, 1):
        flow = links[axis] * (field - ahead(field, axis))
        part = flow - pltpu.roll(flow, 1, axis)
        total = part if total is None else total + part
    return total


def apply_inside(images, c_wide, caps):
    results = []
    flow_low = link(c_wide[0], c_wide[1]) * (images[0] - images[1])
    for i in range(1, len(images) - 1):
        image = images[i]
        flow = link(c_wide[i], c_wide[i + 1]) * (image - images[i + 1])
        results.append(
            caps[i - 1] * image + inner_flow(image, inner_links(c_wide[i])) + (flow - flow_low)
        )
        flow_low = flow
    return results


def sketch_rows(planes, cells_ref):
    depth = cells_ref.shape[0] * LANES
    low_index = lax.broadcasted_iota(jnp.int32, (LOW, depth), 0)
    low_index = low_index.astype(jnp.float32).astype(jnp.bfloat16)
    high_index = lax.broadcasted_iota(jnp.int32, (HIGH * 8, depth), 0) // 8
    high_index = high_index.astype(jnp.float32).astype(jnp.bfloat16)
    total = jnp.zeros((HIGH * 8, LOW), jnp.float32)
    start = 0
    for fields, draw, slot, chosen in planes:
        rows = draw.shape[0]
        coarse, fine = [], []
        for field in fields:
            weighted = draw * field
            head = weighted.astype(jnp.bfloat16).astype(jnp.float32)
            coarse.append(head)
            fine.append(weighted - head)
        for f, part in enumerate(coarse + coarse[:1] + fine + fine[:1]):
            for t in range(depth // LANES):
                cells_ref[t, pl.ds(start + f, rows, stride=8), :] = part[
                    :, t * LANES : (t + 1) * LANES
                ]
        high = jnp.floor(slot * (1.0 / LOW))
        low = slot - LOW * high
        left, right = [], []
        for j in chosen:
            at = pl.ds(start + j * 8, 8)
            cells = [cells_ref[t, at, :] for t in range(depth // LANES)]
            cells = jnp.concatenate(cells, axis=1)
            cells = jnp.concatenate([cells] * HIGH, axis=0).astype(jnp.bfloat16)
            row_high = jnp.broadcast_to(high[j : j + 1], cells.shape).astype(jnp.bfloat16)
            row_low = jnp.broadcast_to(low[j : j + 1], (LOW, depth)).astype(jnp.bfloat16)
            left.append(jnp.where(row_high == high_index, cells, jnp.zeros_like(cells)))
            right.append(
                jnp.where(row_low == low_index, jnp.ones_like(row_low), jnp.zeros_like(row_low))
            )
        total = total + lax.dot_general(
            jnp.concatenate(left, axis=1),
            jnp.concatenate(right, axis=1),
            (((1,), (1,)), ((), ())),
            preferred_element_type=jnp.float32,
        )
        start += rows * 8
    parts = jnp.concatenate([total[h * 8 : h * 8 + 8] for h in range(HIGH)], axis=1)
    return parts + pltpu.roll(parts, 4, 0)


def first_kernel(
    b_hbm, warmth_hbm, phase_hbm, draw_hbm, slot_hbm, b_ref, cond_ref, cap_ref, inner_ref,
    draw_ref, slot_ref, x_first_ref, x_second_ref, y_first_ref, y_second_ref, warmth_ref,
    phase_ref, number_ref, arrived,
):
    copies = [
        pltpu.make_async_copy(source, target, arrived.at[k])
        for k, (source, target) in enumerate(
            (
                (b_hbm, b_ref),
                (warmth_hbm, warmth_ref),
                (phase_hbm, phase_ref),
                (draw_hbm, draw_ref),
                (slot_hbm, number_ref),
            )
        )
    ]
    for copy in copies:
        copy.start()
    for copy in copies[:3]:
        copy.wait()
    planes, rows = b_ref.shape[:2]
    images, conds = [], []
    for i in range(planes):
        cond, cap = traits(warmth_ref[i], phase_ref[i])
        cap_ref[i] = cap
        cond_ref[i] = cond
        field = b_ref[i]
        image = cap * field + inner_flow(field, inner_links(cond))
        if i:
            flow = link(conds[-1], cond) * (b_ref[i - 1] - field)
            images[-1] = images[-1] + flow
            image = image - flow
        conds.append(cond)
        images.append(image)
    for i in range(planes):
        inner_ref[i] = images[i]
    for k, field in enumerate((images, [b_ref[i] for i in range(planes)], conds)):
        at = slice(k * rows, (k + 1) * rows)
        x_first_ref[at], x_second_ref[at] = by_turn(field[0], field[-1], "gx")
        for i, plane in enumerate(field):
            at = slice(k * planes + i, k * planes + i + 1)
            y_first_ref[at], y_second_ref[at] = by_turn(plane[:1], plane[rows - 1 :], "gy")
    for copy in copies[3:]:
        copy.wait()
    for i in range(planes):
        slot_ref[i] = number_ref[i].astype(jnp.float32)
    for k, ref in enumerate((draw_ref, slot_ref)):
        ends = [ref[0], ref[planes - 1]]
        for e, j in enumerate((0, rows - 1)):
            at = slice(3 * rows + 2 * k + e, 3 * rows + 2 * k + e + 1)
            lines = [plane[j : j + 1] for plane in ends]
            x_first_ref[at], x_second_ref[at] = by_turn(*lines, "gx")
        for e, plane in enumerate(ends):
            at = slice(3 * planes + 2 * k + e, 3 * planes + 2 * k + e + 1)
            lines = [plane[:1], plane[rows - 1 :]]
            y_first_ref[at], y_second_ref[at] = by_turn(*lines, "gy")


def by_turn(one, other, axis):
    odd = lax.axis_index(axis) % 2 == 1
    return jnp.where(odd, one, other), jnp.where(odd, other, one)


def has_beside(axis):
    at = lax.axis_index(axis)
    return at > 0, at < lax.axis_size(axis) - 1


def reached(rows):
    others = [j for j in range(rows) if 2 <= j < rows - 2]
    return [j for j in range(rows) if j not in others], others


def widened(ref, beside_ref, which):
    inner = [ref[i] for i in range(ref.shape[0])]
    return [beside_ref[which]] + inner + [beside_ref[which + 1]]


def inside_kernel(
    b_ref, cond_ref, cap_ref, inner_ref, draw_ref, slot_ref, got_first_ref, got_second_ref,
    wide_ref, beside_ref, sketch_ref, cells_ref,
):
    planes, rows = b_ref.shape[:2]
    (image_low, image_high), (b_low, b_high), (c_low, c_high) = (
        by_turn(*(ref[k * rows : (k + 1) * rows] for ref in (got_first_ref, got_second_ref)), "gx")
        for k in range(3)
    )
    below, above = has_beside("gx")
    c_low, c_high = jnp.where(below, c_low, 0.0), jnp.where(above, c_high, 0.0)
    for k, plane in enumerate((b_low, b_high, c_low, c_high)):
        beside_ref[k] = plane
    c_wide = [c_low] + [cond_ref[i] for i in range(planes)] + [c_high]
    low_flow = link(c_low, c_wide[1]) * (b_low - b_ref[0])
    high_flow = link(c_wide[-2], c_high) * (b_ref[planes - 1] - b_high)
    images = [image_low + low_flow] + [inner_ref[i] for i in range(planes)]
    images.append(image_high - high_flow)
    images[1] = images[1] - low_flow
    images[-2] = images[-2] + high_flow
    for i, image in enumerate(images):
        wide_ref[i] = image
    twice = apply_inside(images, c_wide, [cap_ref[i] for i in range(planes)])
    chosen = reached(rows)[1]
    sketch_ref[...] = sketch_rows(
        [
            ((b_ref[i], images[i + 1], twice[i]), draw_ref[i], slot_ref[i], chosen)
            for i in range(planes)
        ],
        cells_ref,
    )


def third_kernel(
    b_ref, cond_ref, cap_ref, draw_ref, slot_ref, wide_ref, beside_ref, x_first_ref,
    x_second_ref, y_first_ref, y_second_ref, inside_ref, image_ref, twice_ref, sketch_ref,
    corner_first_ref, corner_second_ref, ends_ref, cells_ref, extra_ref,
):
    planes, rows, depth = b_ref.shape
    index = lax.broadcasted_iota(jnp.int32, (rows, depth), 0)
    b_wide = widened(b_ref, beside_ref, 0)
    c_wide = widened(cond_ref, beside_ref, 2)
    images = [wide_ref[i] for i in range(planes + 2)]
    x_ends = []
    for inner, outer in ((1, 0), (planes, planes + 1)):
        conductance = link(c_wide[inner], c_wide[outer])
        x_ends.append((inner, outer, conductance, conductance * (b_wide[inner] - b_wide[outer])))
    x_tails = by_turn(x_first_ref[3 * rows :], x_second_ref[3 * rows :], "gx")
    y_lines = by_turn(y_first_ref[...], y_second_ref[...], "gy")
    beside = []
    for side, (j, here, line) in enumerate(zip((0, rows - 1), has_beside("gy"), y_lines)):
        row = slice(j, j + 1)
        parts = [[line[k * planes + i :][:1] for i in range(planes)] for k in range(3)]
        beyond, b_line, c_line = parts
        c_line = [jnp.where(here, c, 0.0) for c in c_line]
        flows = []
        for i in range(planes):
            conductance = link(c_wide[i + 1], jnp.broadcast_to(c_line[i], (rows, depth)))
            conductance = jnp.where(index == j, conductance, 0.0)
            flow = conductance * (b_wide[i + 1] - b_line[i])
            images[i + 1] = images[i + 1] + flow
            beside.append((i, conductance, beyond[i] - flow))
            flows.append((conductance, flow))
        for end, (inner, outer, x_link, x_flow) in enumerate(x_ends):
            y_link, y_flow = flows[inner - 1]
            at = 4 * side + 2 * end
            tail = x_tails[end]
            values = (-x_link * y_flow)[row], tail[side : side + 1], tail[2 + side : 3 + side]
            for k, value in enumerate(values):
                extra_ref[k, at : at + 1] = value
            tail = line[3 * planes :]
            values = (-y_link * x_flow)[row], tail[end : end + 1], tail[2 + end : 3 + end]
            for k, value in enumerate(values):
                extra_ref[k, at + 1 : at + 2] = value
            at = 6 * (2 * side + end)
            values = x_link, b_wide[outer], c_wide[outer], y_link
            for k, value in enumerate(values):
                ends_ref[at + k : at + k + 1] = value[row]
            ends_ref[at + 4 : at + 5] = b_line[inner - 1]
            ends_ref[at + 5 : at + 6] = c_line[inner - 1]
    twice = apply_inside(images, c_wide, [cap_ref[i] for i in range(planes)])
    for i, conductance, value in beside:
        twice[i] = twice[i] + conductance * (images[i + 1] - value)
    for i in range(planes):
        image_ref[i] = images[i + 1]
        twice_ref[i] = twice[i]
    chosen = reached(rows)[0]
    cells = [
        ((b_wide[i + 1], images[i + 1], twice[i]), draw_ref[i], slot_ref[i], chosen)
        for i in range(planes)
    ]
    extra, nothing = [extra_ref[k] for k in range(3)], jnp.zeros((8, depth), jnp.float32)
    cells.append(((nothing, nothing, extra[0]), extra[1], extra[2], range(8)))
    sketch = inside_ref[...] + sketch_rows(cells, cells_ref)
    sketch_ref[...] = sketch[: FIELDS + 1]
    for k, plane in enumerate((b_wide[0], b_wide[-1], c_wide[0], c_wide[-1])):
        at = slice(k, k + 1)
        corner_first_ref[at], corner_second_ref[at] = by_turn(
            plane[:1], plane[rows - 1 :], "gy"
        )


def last_kernel(
    sketch_ref, b_ref, image_ref, twice_ref, ends_ref, corner_first_ref, corner_second_ref,
    solution_ref, residual_ref,
):
    sketches = jnp.sum(sketch_ref[...], axis=0)

    def inner(first, second):
        return jnp.sum(first * second, axis=1, keepdims=True)

    s0, s1, s2 = (sketches[i : i + 1] for i in range(FIELDS))
    beta = jnp.sqrt(inner(s0, s0) + epsilon)
    q0 = s0 / beta
    p0 = s1 / beta
    h00 = inner(q0, p0)
    t0 = p0 - h00 * q0
    n0 = jnp.sqrt(inner(t0, t0) + epsilon)
    q1 = t0 / n0
    p1 = (s2 / beta - h00 * p0) / n0
    h01 = inner(q0, p1)
    h11 = inner(q1, p1)
    t1 = p1 - h01 * q0 - h11 * q1
    n1 = jnp.sqrt(inner(t1, t1) + epsilon)
    l00 = jnp.sqrt(h00 * h00 + n0 * n0)
    l10 = (h00 * h01 + n0 * h11) / l00
    l11 = jnp.sqrt(h01 * h01 + h11 * h11 + n1 * n1 - l10 * l10)
    z0 = beta * h00 / l00
    z1 = (beta * h01 - l10 * z0) / l11
    y1 = z1 / l11
    y0 = (z0 - l10 * y1) / l00
    c1 = y1 / (beta * n0)
    c0 = y0 / beta - h00 * c1
    planes, rows, depth = b_ref.shape
    for i in range(planes):
        b, image = b_ref[i], image_ref[i]
        solution_ref[i] = c0 * b + c1 * image
        residual_ref[i] = b - c0 * image - c1 * twice_ref[i]
    corners = by_turn(corner_first_ref[...], corner_second_ref[...], "gy")
    for side, (j, here, corner) in enumerate(zip((0, rows - 1), has_beside("gy"), corners)):
        for end, i in enumerate((0, planes - 1)):
            b, cond = corner[end : end + 1], corner[2 + end : 3 + end]
            cond = jnp.where(here, cond, 0.0)
            at = 6 * (2 * side + end)
            x_link, x_b, x_cond, y_link, y_b, y_cond = (
                ends_ref[at + k : at + k + 1] for k in range(6)
            )
            lacked = x_link * link(x_cond, cond) * (x_b - b)
            lacked = lacked + y_link * link(y_cond, cond) * (y_b - b)
            residual_ref[i, j : j + 1] = residual_ref[i, j : j + 1] + c1 * lacked


def call(kernel, shapes, *operands, scratch=(), inputs=pltpu.VMEM, flops=0):
    return pl.pallas_call(
        kernel,
        out_shape=[jax.ShapeDtypeStruct(shape, jnp.float32) for shape in shapes],
        in_specs=[pl.BlockSpec(memory_space=inputs)] * len(operands),
        out_specs=[pl.BlockSpec(memory_space=pltpu.VMEM)] * len(shapes),
        scratch_shapes=scratch,
        compiler_params=pltpu.CompilerParams(vmem_limit_bytes=48 * 1024 * 1024),
        cost_estimate=pl.CostEstimate(flops=flops, bytes_accessed=0, transcendentals=0),
    )(*operands)


def swap(first, second, axis):
    across = "gy" if axis == "gx" else "gx"
    count, lines = lax.axis_size(axis), lax.axis_size(across)

    def number(place, line):
        at = (place, line) if axis == "gx" else (line, place)
        return at[0] * lax.axis_size("gy") + at[1]

    turns = ([], [])
    for line in range(lines):
        for i in range(count):
            turns[0].append((number(i, line), number(i ^ 1, line)))
            beyond = i + 1 if i % 2 else i - 1
            if 0 <= beyond < count:
                turns[1].append((number(i, line), number(beyond, line)))
            else:
                turns[1].append((number(i, line), number(i, line ^ 1)))
    return [lax.ppermute(x, ("gx", "gy"), turn) for x, turn in zip((first, second), turns)]


def everyones(sketch):
    count = lax.axis_size("gx") * lax.axis_size("gy")
    copies = jnp.broadcast_to(sketch[None], (count,) + sketch.shape)
    return lax.all_to_all(copies, ("gx", "gy"), 0, 0)


def body(b, warmth, phase, slots, draw):
    planes, rows, depth = b.shape
    block, wide, table = b.shape, (planes + 2, rows, depth), (8, SKETCH)
    face, line, corner = (3 * rows + 4, depth), (3 * planes + 4, depth), (4, depth)
    cells = pltpu.VMEM((depth // LANES, (planes * rows + 8) * 8, LANES), jnp.float32)
    work = b.size * SKETCH * 6
    b, cond, cap, inner, draw, slots, x_first, x_second, y_first, y_second = call(
        first_kernel,
        [block] * 6 + [face, face, line, line],
        *(
            pltpu.with_memory_space_constraint(x, pltpu.HBM)
            for x in (b, warmth, phase, draw, slots)
        ),
        scratch=[
            pltpu.VMEM(block, warmth.dtype),
            pltpu.VMEM(block, phase.dtype),
            pltpu.VMEM(block, slots.dtype),
            pltpu.SemaphoreType.DMA((5,)),
        ],
        inputs=pltpu.HBM,
    )
    got_x = swap(x_first, x_second, "gx")
    got_y = swap(y_first, y_second, "gy")
    image_wide, beside, inside = call(
        inside_kernel,
        [wide, (4, rows, depth), table],
        b, cond, cap, inner, draw, slots, *got_x,
        scratch=[cells],
        flops=work,
    )
    image, twice, sketch, first, second, ends = call(
        third_kernel,
        [block, block, (FIELDS + 1, SKETCH), corner, corner, (24, depth)],
        b, cond, cap, draw, slots, image_wide, beside, *got_x, *got_y, inside,
        scratch=[cells, pltpu.VMEM((3, 8, depth), jnp.float32)],
        flops=work,
    )
    got_corners = swap(first, second, "gy")
    sketches = everyones(sketch)
    return tuple(
        call(last_kernel, [block, block], sketches, b, image, twice, ends, *got_corners)
    )


def solution(mesh):
    spec = P(("parts", "gx"), "gy", None)
    return jax.shard_map(
        body, mesh=mesh, in_specs=(spec,) * 5, out_specs=(spec,) * 2, check_vma=False
    )
```

```python
import jax
import jax.numpy as jnp
from jax import lax
from jax.experimental import pallas as pl
from jax.experimental.pallas import tpu as pltpu
from jax.sharding import PartitionSpec as P

SKETCH = 128
LOW = 32
HIGH = SKETCH // LOW
FIELDS = 3
LANES = 128
epsilon = 1e-06


def traits(warmth, phase):
    powder, solid = phase == 0, phase == 1
    offset = jnp.where(powder, 0.2, jnp.where(solid, 1.0, 0.6))
    return offset * (0.5 + warmth), jnp.where(powder, 1.0, jnp.where(solid, 2.0, 1.5))


def link(first, second):
    total = first + second
    return 2.0 * first * second / jnp.where(total > 0.0, total, 1.0)


def ahead(plane, axis):
    return pltpu.roll(plane, plane.shape[axis] - 1, axis)


def inner_links(cond):
    links = []
    for axis in (0, 1):
        index = lax.broadcasted_iota(jnp.int32, cond.shape, axis)
        links.append(
            jnp.where(index < cond.shape[axis] - 1, link(cond, ahead(cond, axis)), 0.0)
        )
    return links


def inner_flow(field, links):
    total = None
    for axis in (0, 1):
        flow = links[axis] * (field - ahead(field, axis))
        part = flow - pltpu.roll(flow, 1, axis)
        total = part if total is None else total + part
    return total


def apply_inside(images, c_wide, caps):
    results = []
    flow_low = link(c_wide[0], c_wide[1]) * (images[0] - images[1])
    for i in range(1, len(images) - 1):
        image = images[i]
        flow = link(c_wide[i], c_wide[i + 1]) * (image - images[i + 1])
        results.append(
            caps[i - 1] * image + inner_flow(image, inner_links(c_wide[i])) + (flow - flow_low)
        )
        flow_low = flow
    return results


def sketch_rows(planes, cells_ref):
    depth = cells_ref.shape[0] * LANES
    low_index = lax.broadcasted_iota(jnp.int32, (LOW, depth), 0)
    low_index = low_index.astype(jnp.float32).astype(jnp.bfloat16)
    high_index = lax.broadcasted_iota(jnp.int32, (HIGH * 8, depth), 0) // 8
    high_index = high_index.astype(jnp.float32).astype(jnp.bfloat16)
    total = jnp.zeros((HIGH * 8, LOW), jnp.float32)
    start = 0
    for fields, draw, slot, chosen in planes:
        rows = draw.shape[0]
        coarse, fine = [], []
        for field in fields:
            weighted = draw * field
            head = weighted.astype(jnp.bfloat16).astype(jnp.float32)
            coarse.append(head)
            fine.append(weighted - head)
        for f, part in enumerate(coarse + coarse[:1] + fine + fine[:1]):
            for t in range(depth // LANES):
                cells_ref[t, pl.ds(start + f, rows, stride=8), :] = part[
                    :, t * LANES : (t + 1) * LANES
                ]
        high = jnp.floor(slot * (1.0 / LOW))
        low = slot - LOW * high
        left, right = [], []
        for j in chosen:
            at = pl.ds(start + j * 8, 8)
            cells = [cells_ref[t, at, :] for t in range(depth // LANES)]
            cells = jnp.concatenate(cells, axis=1)
            cells = jnp.concatenate([cells] * HIGH, axis=0).astype(jnp.bfloat16)
            row_high = jnp.broadcast_to(high[j : j + 1], cells.shape).astype(jnp.bfloat16)
            row_low = jnp.broadcast_to(low[j : j + 1], (LOW, depth)).astype(jnp.bfloat16)
            left.append(jnp.where(row_high == high_index, cells, jnp.zeros_like(cells)))
            right.append(
                jnp.where(row_low == low_index, jnp.ones_like(row_low), jnp.zeros_like(row_low))
            )
        total = total + lax.dot_general(
            jnp.concatenate(left, axis=1),
            jnp.concatenate(right, axis=1),
            (((1,), (1,)), ((), ())),
            preferred_element_type=jnp.float32,
        )
        start += rows * 8
    parts = jnp.concatenate([total[h * 8 : h * 8 + 8] for h in range(HIGH)], axis=1)
    return parts + pltpu.roll(parts, 4, 0)


def first_kernel(
    b_hbm, warmth_hbm, phase_hbm, draw_hbm, slot_hbm, b_ref, cond_ref, cap_ref, inner_ref,
    draw_ref, slot_ref, x_first_ref, x_second_ref, y_first_ref, y_second_ref, warmth_ref,
    phase_ref, number_ref, arrived,
):
    copies = [
        pltpu.make_async_copy(source, target, arrived.at[k])
        for k, (source, target) in enumerate(
            (
                (b_hbm, b_ref),
                (warmth_hbm, warmth_ref),
                (phase_hbm, phase_ref),
                (draw_hbm, draw_ref),
                (slot_hbm, number_ref),
            )
        )
    ]
    for copy in copies:
        copy.start()
    for copy in copies[:3]:
        copy.wait()
    planes, rows = b_ref.shape[:2]
    images, conds = [], []
    for i in range(planes):
        cond, cap = traits(warmth_ref[i], phase_ref[i])
        cap_ref[i] = cap
        cond_ref[i] = cond
        field = b_ref[i]
        image = cap * field + inner_flow(field, inner_links(cond))
        if i:
            flow = link(conds[-1], cond) * (b_ref[i - 1] - field)
            images[-1] = images[-1] + flow
            image = image - flow
        conds.append(cond)
        images.append(image)
    for i in range(planes):
        inner_ref[i] = images[i]
    for k, field in enumerate((images, [b_ref[i] for i in range(planes)], conds)):
        at = slice(k * rows, (k + 1) * rows)
        x_first_ref[at], x_second_ref[at] = by_turn(field[0], field[-1], "gx")
        for i, plane in enumerate(field):
            at = slice(k * planes + i, k * planes + i + 1)
            y_first_ref[at], y_second_ref[at] = by_turn(plane[:1], plane[rows - 1 :], "gy")
    for copy in copies[3:]:
        copy.wait()
    for i in range(planes):
        slot_ref[i] = number_ref[i].astype(jnp.float32)
    for k, ref in enumerate((draw_ref, slot_ref)):
        ends = [ref[0], ref[planes - 1]]
        for e, j in enumerate((0, rows - 1)):
            at = slice(3 * rows + 2 * k + e, 3 * rows + 2 * k + e + 1)
            lines = [plane[j : j + 1] for plane in ends]
            x_first_ref[at], x_second_ref[at] = by_turn(*lines, "gx")
        for e, plane in enumerate(ends):
            at = slice(3 * planes + 2 * k + e, 3 * planes + 2 * k + e + 1)
            lines = [plane[:1], plane[rows - 1 :]]
            y_first_ref[at], y_second_ref[at] = by_turn(*lines, "gy")


def by_turn(one, other, axis):
    odd = lax.axis_index(axis) % 2 == 1
    return jnp.where(odd, one, other), jnp.where(odd, other, one)


def has_beside(axis):
    at = lax.axis_index(axis)
    return at > 0, at < lax.axis_size(axis) - 1


def reached(rows):
    others = [j for j in range(rows) if 2 <= j < rows - 2]
    return [j for j in range(rows) if j not in others], others


def widened(ref, beside_ref, which):
    inner = [ref[i] for i in range(ref.shape[0])]
    return [beside_ref[which]] + inner + [beside_ref[which + 1]]


def inside_kernel(
    b_ref, cond_ref, cap_ref, inner_ref, draw_ref, slot_ref, got_first_ref, got_second_ref,
    wide_ref, beside_ref, sketch_ref, cells_ref,
):
    planes, rows = b_ref.shape[:2]
    (image_low, image_high), (b_low, b_high), (c_low, c_high) = (
        by_turn(*(ref[k * rows : (k + 1) * rows] for ref in (got_first_ref, got_second_ref)), "gx")
        for k in range(3)
    )
    below, above = has_beside("gx")
    c_low, c_high = jnp.where(below, c_low, 0.0), jnp.where(above, c_high, 0.0)
    for k, plane in enumerate((b_low, b_high, c_low, c_high)):
        beside_ref[k] = plane
    c_wide = [c_low] + [cond_ref[i] for i in range(planes)] + [c_high]
    low_flow = link(c_low, c_wide[1]) * (b_low - b_ref[0])
    high_flow = link(c_wide[-2], c_high) * (b_ref[planes - 1] - b_high)
    images = [image_low + low_flow] + [inner_ref[i] for i in range(planes)]
    images.append(image_high - high_flow)
    images[1] = images[1] - low_flow
    images[-2] = images[-2] + high_flow
    for i, image in enumerate(images):
        wide_ref[i] = image
    twice = apply_inside(images, c_wide, [cap_ref[i] for i in range(planes)])
    chosen = reached(rows)[1]
    sketch_ref[...] = sketch_rows(
        [
            ((b_ref[i], images[i + 1], twice[i]), draw_ref[i], slot_ref[i], chosen)
            for i in range(planes)
        ],
        cells_ref,
    )


def third_kernel(
    b_ref, cond_ref, cap_ref, draw_ref, slot_ref, wide_ref, beside_ref, x_first_ref,
    x_second_ref, y_first_ref, y_second_ref, inside_ref, image_ref, twice_ref, sketch_ref,
    corner_first_ref, corner_second_ref, ends_ref, cells_ref, extra_ref,
):
    planes, rows, depth = b_ref.shape
    index = lax.broadcasted_iota(jnp.int32, (rows, depth), 0)
    b_wide = widened(b_ref, beside_ref, 0)
    c_wide = widened(cond_ref, beside_ref, 2)
    images = [wide_ref[i] for i in range(planes + 2)]
    x_ends = []
    for inner, outer in ((1, 0), (planes, planes + 1)):
        conductance = link(c_wide[inner], c_wide[outer])
        x_ends.append((inner, outer, conductance, conductance * (b_wide[inner] - b_wide[outer])))
    x_tails = by_turn(x_first_ref[3 * rows :], x_second_ref[3 * rows :], "gx")
    y_lines = by_turn(y_first_ref[...], y_second_ref[...], "gy")
    beside = []
    for side, (j, here, line) in enumerate(zip((0, rows - 1), has_beside("gy"), y_lines)):
        row = slice(j, j + 1)
        parts = [[line[k * planes + i :][:1] for i in range(planes)] for k in range(3)]
        beyond, b_line, c_line = parts
        c_line = [jnp.where(here, c, 0.0) for c in c_line]
        flows = []
        for i in range(planes):
            conductance = link(c_wide[i + 1], jnp.broadcast_to(c_line[i], (rows, depth)))
            conductance = jnp.where(index == j, conductance, 0.0)
            flow = conductance * (b_wide[i + 1] - b_line[i])
            images[i + 1] = images[i + 1] + flow
            beside.append((i, conductance, beyond[i] - flow))
            flows.append((conductance, flow))
        for end, (inner, outer, x_link, x_flow) in enumerate(x_ends):
            y_link, y_flow = flows[inner - 1]
            at = 4 * side + 2 * end
            tail = x_tails[end]
            values = (-x_link * y_flow)[row], tail[side : side + 1], tail[2 + side : 3 + side]
            for k, value in enumerate(values):
                extra_ref[k, at : at + 1] = value
            tail = line[3 * planes :]
            values = (-y_link * x_flow)[row], tail[end : end + 1], tail[2 + end : 3 + end]
            for k, value in enumerate(values):
                extra_ref[k, at + 1 : at + 2] = value
            at = 6 * (2 * side + end)
            values = x_link, b_wide[outer], c_wide[outer], y_link
            for k, value in enumerate(values):
                ends_ref[at + k : at + k + 1] = value[row]
            ends_ref[at + 4 : at + 5] = b_line[inner - 1]
            ends_ref[at + 5 : at + 6] = c_line[inner - 1]
    twice = apply_inside(images, c_wide, [cap_ref[i] for i in range(planes)])
    for i, conductance, value in beside:
        twice[i] = twice[i] + conductance * (images[i + 1] - value)
    for i in range(planes):
        image_ref[i] = images[i + 1]
        twice_ref[i] = twice[i]
    chosen = reached(rows)[0]
    cells = [
        ((b_wide[i + 1], images[i + 1], twice[i]), draw_ref[i], slot_ref[i], chosen)
        for i in range(planes)
    ]
    extra, nothing = [extra_ref[k] for k in range(3)], jnp.zeros((8, depth), jnp.float32)
    cells.append(((nothing, nothing, extra[0]), extra[1], extra[2], range(8)))
    sketch = inside_ref[...] + sketch_rows(cells, cells_ref)
    for device in range(sketch_ref.shape[0]):
        sketch_ref[device] = sketch[: FIELDS + 1]
    for k, plane in enumerate((b_wide[0], b_wide[-1], c_wide[0], c_wide[-1])):
        at = slice(k, k + 1)
        corner_first_ref[at], corner_second_ref[at] = by_turn(
            plane[:1], plane[rows - 1 :], "gy"
        )


def last_kernel(
    sketch_ref, b_ref, image_ref, twice_ref, ends_ref, corner_first_ref, corner_second_ref,
    solution_ref, residual_ref,
):
    sketches = jnp.sum(sketch_ref[...], axis=0)

    def inner(first, second):
        return jnp.sum(first * second, axis=1, keepdims=True)

    s0, s1, s2 = (sketches[i : i + 1] for i in range(FIELDS))
    beta = jnp.sqrt(inner(s0, s0) + epsilon)
    q0 = s0 / beta
    p0 = s1 / beta
    h00 = inner(q0, p0)
    t0 = p0 - h00 * q0
    n0 = jnp.sqrt(inner(t0, t0) + epsilon)
    q1 = t0 / n0
    p1 = (s2 / beta - h00 * p0) / n0
    h01 = inner(q0, p1)
    h11 = inner(q1, p1)
    t1 = p1 - h01 * q0 - h11 * q1
    n1 = jnp.sqrt(inner(t1, t1) + epsilon)
    l00 = jnp.sqrt(h00 * h00 + n0 * n0)
    l10 = (h00 * h01 + n0 * h11) / l00
    l11 = jnp.sqrt(h01 * h01 + h11 * h11 + n1 * n1 - l10 * l10)
    z0 = beta * h00 / l00
    z1 = (beta * h01 - l10 * z0) / l11
    y1 = z1 / l11
    y0 = (z0 - l10 * y1) / l00
    c1 = y1 / (beta * n0)
    c0 = y0 / beta - h00 * c1
    planes, rows, depth = b_ref.shape
    for i in range(planes):
        b, image = b_ref[i], image_ref[i]
        solution_ref[i] = c0 * b + c1 * image
        residual_ref[i] = b - c0 * image - c1 * twice_ref[i]
    corners = by_turn(corner_first_ref[...], corner_second_ref[...], "gy")
    for side, (j, here, corner) in enumerate(zip((0, rows - 1), has_beside("gy"), corners)):
        for end, i in enumerate((0, planes - 1)):
            b, cond = corner[end : end + 1], corner[2 + end : 3 + end]
            cond = jnp.where(here, cond, 0.0)
            at = 6 * (2 * side + end)
            x_link, x_b, x_cond, y_link, y_b, y_cond = (
                ends_ref[at + k : at + k + 1] for k in range(6)
            )
            lacked = x_link * link(x_cond, cond) * (x_b - b)
            lacked = lacked + y_link * link(y_cond, cond) * (y_b - b)
            residual_ref[i, j : j + 1] = residual_ref[i, j : j + 1] + c1 * lacked


def call(kernel, shapes, *operands, scratch=(), inputs=pltpu.VMEM, flops=0):
    return pl.pallas_call(
        kernel,
        out_shape=[jax.ShapeDtypeStruct(shape, jnp.float32) for shape in shapes],
        in_specs=[pl.BlockSpec(memory_space=inputs)] * len(operands),
        out_specs=[pl.BlockSpec(memory_space=pltpu.VMEM)] * len(shapes),
        scratch_shapes=scratch,
        compiler_params=pltpu.CompilerParams(vmem_limit_bytes=48 * 1024 * 1024),
        cost_estimate=pl.CostEstimate(flops=flops, bytes_accessed=0, transcendentals=0),
    )(*operands)


def swap(first, second, axis):
    parts, nx, ny = (lax.axis_size(name) for name in ("parts", "gx", "gy"))

    def number(part, x, y):
        return (part * nx + x) * ny + y

    turns = ([], [])
    for part in range(parts):
        for x in range(nx):
            for y in range(ny):
                if axis == "gx":
                    near, far = number(part, x ^ 1, y), x + 1 if x % 2 else x - 1
                    aside = number(part, x, y ^ 1) if parts % 2 else number(part ^ 1, x, y)
                    far = number(part, far, y) if 0 <= far < nx else aside
                else:
                    near, far = number(part, x, y ^ 1), y + 1 if y % 2 else y - 1
                    far = number(part, x, far) if 0 <= far < ny else number(part, x ^ 1, y)
                turns[0].append((number(part, x, y), near))
                turns[1].append((number(part, x, y), far))
    axes = ("parts", "gx", "gy")
    return [lax.ppermute(array, axes, turn) for array, turn in zip((first, second), turns)]


def body(b, warmth, phase, slots, draw):
    planes, rows, depth = b.shape
    block, wide, table = b.shape, (planes + 2, rows, depth), (8, SKETCH)
    face, line, corner = (3 * rows + 4, depth), (3 * planes + 4, depth), (4, depth)
    cells = pltpu.VMEM((depth // LANES, (planes * rows + 8) * 8, LANES), jnp.float32)
    work = b.size * SKETCH * 6
    b, cond, cap, inner, draw, slots, x_first, x_second, y_first, y_second = call(
        first_kernel,
        [block] * 6 + [face, face, line, line],
        *(
            pltpu.with_memory_space_constraint(x, pltpu.HBM)
            for x in (b, warmth, phase, draw, slots)
        ),
        scratch=[
            pltpu.VMEM(block, warmth.dtype),
            pltpu.VMEM(block, phase.dtype),
            pltpu.VMEM(block, slots.dtype),
            pltpu.SemaphoreType.DMA((5,)),
        ],
        inputs=pltpu.HBM,
    )
    got_x = swap(x_first, x_second, "gx")
    got_y = swap(y_first, y_second, "gy")
    image_wide, beside, inside = call(
        inside_kernel,
        [wide, (4, rows, depth), table],
        b, cond, cap, inner, draw, slots, *got_x,
        scratch=[cells],
        flops=work,
    )
    devices = lax.axis_size("gx") * lax.axis_size("gy")
    image, twice, copies, first, second, ends = call(
        third_kernel,
        [block, block, (devices, FIELDS + 1, SKETCH), corner, corner, (24, depth)],
        b, cond, cap, draw, slots, image_wide, beside, *got_x, *got_y, inside,
        scratch=[cells, pltpu.VMEM((3, 8, depth), jnp.float32)],
        flops=work,
    )
    got_corners = swap(first, second, "gy")
    sketches = lax.all_to_all(copies, ("gx", "gy"), 0, 0)
    return tuple(
        call(last_kernel, [block, block], sketches, b, image, twice, ends, *got_corners)
    )


def solution(mesh):
    spec = P(("parts", "gx"), "gy", None)
    return jax.shard_map(
        body, mesh=mesh, in_specs=(spec,) * 5, out_specs=(spec,) * 2, check_vma=False
    )
```

```python
import jax
import jax.numpy as jnp
from jax import lax
from jax.experimental import pallas as pl
from jax.experimental.pallas import tpu as pltpu
from jax.sharding import PartitionSpec as P

SKETCH = 128
LOW = 32
HIGH = SKETCH // LOW
FIELDS = 3
LANES = 128
epsilon = 1e-06


def traits(warmth, phase):
    powder, solid = phase == 0, phase == 1
    offset = jnp.where(powder, 0.2, jnp.where(solid, 1.0, 0.6))
    return offset * (0.5 + warmth), jnp.where(powder, 1.0, jnp.where(solid, 2.0, 1.5))


def link(first, second):
    total = first + second
    return 2.0 * first * second / jnp.where(total > 0.0, total, 1.0)


def ahead(plane, axis):
    return pltpu.roll(plane, plane.shape[axis] - 1, axis)


def inner_links(cond):
    links = []
    for axis in (0, 1):
        index = lax.broadcasted_iota(jnp.int32, cond.shape, axis)
        links.append(
            jnp.where(index < cond.shape[axis] - 1, link(cond, ahead(cond, axis)), 0.0)
        )
    return links


def inner_flow(field, links):
    total = None
    for axis in (0, 1):
        flow = links[axis] * (field - ahead(field, axis))
        part = flow - pltpu.roll(flow, 1, axis)
        total = part if total is None else total + part
    return total


def apply_inside(images, c_wide, caps):
    results = []
    flow_low = link(c_wide[0], c_wide[1]) * (images[0] - images[1])
    for i in range(1, len(images) - 1):
        image = images[i]
        flow = link(c_wide[i], c_wide[i + 1]) * (image - images[i + 1])
        results.append(
            caps[i - 1] * image + inner_flow(image, inner_links(c_wide[i])) + (flow - flow_low)
        )
        flow_low = flow
    return results


def sketch_rows(planes, cells_ref):
    depth = cells_ref.shape[0] * LANES
    low_index = lax.broadcasted_iota(jnp.int32, (LOW, depth), 0)
    low_index = low_index.astype(jnp.float32).astype(jnp.bfloat16)
    high_index = lax.broadcasted_iota(jnp.int32, (HIGH * 8, depth), 0) // 8
    high_index = high_index.astype(jnp.float32).astype(jnp.bfloat16)
    total = jnp.zeros((HIGH * 8, LOW), jnp.float32)
    start = 0
    for fields, draw, slot, chosen in planes:
        rows = draw.shape[0]
        coarse, fine = [], []
        for field in fields:
            weighted = draw * field
            head = weighted.astype(jnp.bfloat16).astype(jnp.float32)
            coarse.append(head)
            fine.append(weighted - head)
        for f, part in enumerate(coarse + coarse[:1] + fine + fine[:1]):
            for t in range(depth // LANES):
                cells_ref[t, pl.ds(start + f, rows, stride=8), :] = part[
                    :, t * LANES : (t + 1) * LANES
                ]
        high = jnp.floor(slot * (1.0 / LOW))
        low = slot - LOW * high
        left, right = [], []
        for j in chosen:
            at = pl.ds(start + j * 8, 8)
            cells = [cells_ref[t, at, :] for t in range(depth // LANES)]
            cells = jnp.concatenate(cells, axis=1)
            cells = jnp.concatenate([cells] * HIGH, axis=0).astype(jnp.bfloat16)
            row_high = jnp.broadcast_to(high[j : j + 1], cells.shape).astype(jnp.bfloat16)
            row_low = jnp.broadcast_to(low[j : j + 1], (LOW, depth)).astype(jnp.bfloat16)
            left.append(jnp.where(row_high == high_index, cells, jnp.zeros_like(cells)))
            right.append(
                jnp.where(row_low == low_index, jnp.ones_like(row_low), jnp.zeros_like(row_low))
            )
        total = total + lax.dot_general(
            jnp.concatenate(left, axis=1),
            jnp.concatenate(right, axis=1),
            (((1,), (1,)), ((), ())),
            preferred_element_type=jnp.float32,
        )
        start += rows * 8
    parts = jnp.concatenate([total[h * 8 : h * 8 + 8] for h in range(HIGH)], axis=1)
    return parts + pltpu.roll(parts, 4, 0)


def first_kernel(
    b_hbm, warmth_hbm, phase_hbm, draw_hbm, slot_hbm, b_ref, cond_ref, cap_ref, inner_ref,
    draw_ref, slot_ref, x_first_ref, x_second_ref, y_first_ref, y_second_ref, warmth_ref,
    phase_ref, number_ref, arrived,
):
    copies = [
        pltpu.make_async_copy(source, target, arrived.at[k])
        for k, (source, target) in enumerate(
            (
                (b_hbm, b_ref),
                (warmth_hbm, warmth_ref),
                (phase_hbm, phase_ref),
                (draw_hbm, draw_ref),
                (slot_hbm, number_ref),
            )
        )
    ]
    for copy in copies:
        copy.start()
    for copy in copies[:3]:
        copy.wait()
    planes, rows = b_ref.shape[:2]
    images, conds = [], []
    for i in range(planes):
        cond, cap = traits(warmth_ref[i], phase_ref[i])
        cap_ref[i] = cap
        cond_ref[i] = cond
        field = b_ref[i]
        image = cap * field + inner_flow(field, inner_links(cond))
        if i:
            flow = link(conds[-1], cond) * (b_ref[i - 1] - field)
            images[-1] = images[-1] + flow
            image = image - flow
        conds.append(cond)
        images.append(image)
    for i in range(planes):
        inner_ref[i] = images[i]
    for k, field in enumerate((images, [b_ref[i] for i in range(planes)], conds)):
        at = slice(k * rows, (k + 1) * rows)
        x_first_ref[at], x_second_ref[at] = by_turn(field[0], field[-1], "gx")
        for i, plane in enumerate(field):
            at = slice(k * planes + i, k * planes + i + 1)
            y_first_ref[at], y_second_ref[at] = by_turn(plane[:1], plane[rows - 1 :], "gy")
    for copy in copies[3:]:
        copy.wait()
    for i in range(planes):
        slot_ref[i] = number_ref[i].astype(jnp.float32)
    for k, ref in enumerate((draw_ref, slot_ref)):
        ends = [ref[0], ref[planes - 1]]
        for e, j in enumerate((0, rows - 1)):
            at = slice(3 * rows + 2 * k + e, 3 * rows + 2 * k + e + 1)
            lines = [plane[j : j + 1] for plane in ends]
            x_first_ref[at], x_second_ref[at] = by_turn(*lines, "gx")
        for e, plane in enumerate(ends):
            at = slice(3 * planes + 2 * k + e, 3 * planes + 2 * k + e + 1)
            lines = [plane[:1], plane[rows - 1 :]]
            y_first_ref[at], y_second_ref[at] = by_turn(*lines, "gy")


def by_turn(one, other, axis):
    odd = lax.axis_index(axis) % 2 == 1
    return jnp.where(odd, one, other), jnp.where(odd, other, one)


def has_beside(axis):
    at = lax.axis_index(axis)
    return at > 0, at < lax.axis_size(axis) - 1


def reached(rows):
    others = [j for j in range(rows) if 2 <= j < rows - 2]
    return [j for j in range(rows) if j not in others], others


def widened(ref, beside_ref, which):
    inner = [ref[i] for i in range(ref.shape[0])]
    return [beside_ref[which]] + inner + [beside_ref[which + 1]]


def inside_kernel(
    b_ref, cond_ref, cap_ref, inner_ref, draw_ref, slot_ref, got_first_ref, got_second_ref,
    wide_ref, beside_ref, sketch_ref, cells_ref,
):
    planes, rows = b_ref.shape[:2]
    (image_low, image_high), (b_low, b_high), (c_low, c_high) = (
        by_turn(*(ref[k * rows : (k + 1) * rows] for ref in (got_first_ref, got_second_ref)), "gx")
        for k in range(3)
    )
    below, above = has_beside("gx")
    c_low, c_high = jnp.where(below, c_low, 0.0), jnp.where(above, c_high, 0.0)
    for k, plane in enumerate((b_low, b_high, c_low, c_high)):
        beside_ref[k] = plane
    c_wide = [c_low] + [cond_ref[i] for i in range(planes)] + [c_high]
    low_flow = link(c_low, c_wide[1]) * (b_low - b_ref[0])
    high_flow = link(c_wide[-2], c_high) * (b_ref[planes - 1] - b_high)
    images = [image_low + low_flow] + [inner_ref[i] for i in range(planes)]
    images.append(image_high - high_flow)
    images[1] = images[1] - low_flow
    images[-2] = images[-2] + high_flow
    for i, image in enumerate(images):
        wide_ref[i] = image
    twice = apply_inside(images, c_wide, [cap_ref[i] for i in range(planes)])
    chosen = reached(rows)[1]
    sketch_ref[...] = sketch_rows(
        [
            ((b_ref[i], images[i + 1], twice[i]), draw_ref[i], slot_ref[i], chosen)
            for i in range(planes)
        ],
        cells_ref,
    )


def third_kernel(
    b_ref, cond_ref, cap_ref, draw_ref, slot_ref, wide_ref, beside_ref, x_first_ref,
    x_second_ref, y_first_ref, y_second_ref, inside_ref, image_ref, twice_ref, sketch_ref,
    corner_first_ref, corner_second_ref, ends_ref, cells_ref, extra_ref,
):
    planes, rows, depth = b_ref.shape
    index = lax.broadcasted_iota(jnp.int32, (rows, depth), 0)
    b_wide = widened(b_ref, beside_ref, 0)
    c_wide = widened(cond_ref, beside_ref, 2)
    images = [wide_ref[i] for i in range(planes + 2)]
    x_ends = []
    for inner, outer in ((1, 0), (planes, planes + 1)):
        conductance = link(c_wide[inner], c_wide[outer])
        x_ends.append((inner, outer, conductance, conductance * (b_wide[inner] - b_wide[outer])))
    x_tails = by_turn(x_first_ref[3 * rows :], x_second_ref[3 * rows :], "gx")
    y_lines = by_turn(y_first_ref[...], y_second_ref[...], "gy")
    beside = []
    for side, (j, here, line) in enumerate(zip((0, rows - 1), has_beside("gy"), y_lines)):
        row = slice(j, j + 1)
        parts = [[line[k * planes + i :][:1] for i in range(planes)] for k in range(3)]
        beyond, b_line, c_line = parts
        c_line = [jnp.where(here, c, 0.0) for c in c_line]
        flows = []
        for i in range(planes):
            conductance = link(c_wide[i + 1], jnp.broadcast_to(c_line[i], (rows, depth)))
            conductance = jnp.where(index == j, conductance, 0.0)
            flow = conductance * (b_wide[i + 1] - b_line[i])
            images[i + 1] = images[i + 1] + flow
            beside.append((i, conductance, beyond[i] - flow))
            flows.append((conductance, flow))
        for end, (inner, outer, x_link, x_flow) in enumerate(x_ends):
            y_link, y_flow = flows[inner - 1]
            at = 4 * side + 2 * end
            tail = x_tails[end]
            values = (-x_link * y_flow)[row], tail[side : side + 1], tail[2 + side : 3 + side]
            for k, value in enumerate(values):
                extra_ref[k, at : at + 1] = value
            tail = line[3 * planes :]
            values = (-y_link * x_flow)[row], tail[end : end + 1], tail[2 + end : 3 + end]
            for k, value in enumerate(values):
                extra_ref[k, at + 1 : at + 2] = value
            at = 6 * (2 * side + end)
            values = x_link, b_wide[outer], c_wide[outer], y_link
            for k, value in enumerate(values):
                ends_ref[at + k : at + k + 1] = value[row]
            ends_ref[at + 4 : at + 5] = b_line[inner - 1]
            ends_ref[at + 5 : at + 6] = c_line[inner - 1]
    twice = apply_inside(images, c_wide, [cap_ref[i] for i in range(planes)])
    for i, conductance, value in beside:
        twice[i] = twice[i] + conductance * (images[i + 1] - value)
    for i in range(planes):
        image_ref[i] = images[i + 1]
        twice_ref[i] = twice[i]
    chosen = reached(rows)[0]
    cells = [
        ((b_wide[i + 1], images[i + 1], twice[i]), draw_ref[i], slot_ref[i], chosen)
        for i in range(planes)
    ]
    extra, nothing = [extra_ref[k] for k in range(3)], jnp.zeros((8, depth), jnp.float32)
    cells.append(((nothing, nothing, extra[0]), extra[1], extra[2], range(8)))
    sketch = inside_ref[...] + sketch_rows(cells, cells_ref)
    for device in range(sketch_ref.shape[0]):
        sketch_ref[device] = sketch[: FIELDS + 1]
    for k, plane in enumerate((b_wide[0], b_wide[-1], c_wide[0], c_wide[-1])):
        at = slice(k, k + 1)
        corner_first_ref[at], corner_second_ref[at] = by_turn(
            plane[:1], plane[rows - 1 :], "gy"
        )


def last_kernel(
    sketch_ref, b_ref, image_ref, twice_ref, ends_ref, corner_first_ref, corner_second_ref,
    solution_ref, residual_ref,
):
    sketches = jnp.sum(sketch_ref[...], axis=0)

    def inner(first, second):
        return jnp.sum(first * second, axis=1, keepdims=True)

    s0, s1, s2 = (sketches[i : i + 1] for i in range(FIELDS))
    beta = jnp.sqrt(inner(s0, s0) + epsilon)
    q0 = s0 / beta
    p0 = s1 / beta
    h00 = inner(q0, p0)
    t0 = p0 - h00 * q0
    n0 = jnp.sqrt(inner(t0, t0) + epsilon)
    q1 = t0 / n0
    p1 = (s2 / beta - h00 * p0) / n0
    h01 = inner(q0, p1)
    h11 = inner(q1, p1)
    t1 = p1 - h01 * q0 - h11 * q1
    n1 = jnp.sqrt(inner(t1, t1) + epsilon)
    l00 = jnp.sqrt(h00 * h00 + n0 * n0)
    l10 = (h00 * h01 + n0 * h11) / l00
    l11 = jnp.sqrt(h01 * h01 + h11 * h11 + n1 * n1 - l10 * l10)
    z0 = beta * h00 / l00
    z1 = (beta * h01 - l10 * z0) / l11
    y1 = z1 / l11
    y0 = (z0 - l10 * y1) / l00
    c1 = y1 / (beta * n0)
    c0 = y0 / beta - h00 * c1
    planes, rows, depth = b_ref.shape
    for i in range(planes):
        b, image = b_ref[i], image_ref[i]
        solution_ref[i] = c0 * b + c1 * image
        residual_ref[i] = b - c0 * image - c1 * twice_ref[i]
    corners = by_turn(corner_first_ref[...], corner_second_ref[...], "gy")
    for side, (j, here, corner) in enumerate(zip((0, rows - 1), has_beside("gy"), corners)):
        for end, i in enumerate((0, planes - 1)):
            b, cond = corner[end : end + 1], corner[2 + end : 3 + end]
            cond = jnp.where(here, cond, 0.0)
            at = 6 * (2 * side + end)
            x_link, x_b, x_cond, y_link, y_b, y_cond = (
                ends_ref[at + k : at + k + 1] for k in range(6)
            )
            lacked = x_link * link(x_cond, cond) * (x_b - b)
            lacked = lacked + y_link * link(y_cond, cond) * (y_b - b)
            residual_ref[i, j : j + 1] = residual_ref[i, j : j + 1] + c1 * lacked


def call(
    kernel, shapes, *operands, scratch=(), inputs=pltpu.VMEM, outputs=pltpu.VMEM, flops=0
):
    return pl.pallas_call(
        kernel,
        out_shape=[outputs(shape, jnp.float32) for shape in shapes],
        in_specs=[pl.BlockSpec(memory_space=inputs)] * len(operands),
        out_specs=[pl.BlockSpec(memory_space=pltpu.VMEM)] * len(shapes),
        scratch_shapes=scratch,
        compiler_params=pltpu.CompilerParams(vmem_limit_bytes=48 * 1024 * 1024),
        cost_estimate=pl.CostEstimate(flops=flops, bytes_accessed=0, transcendentals=0),
    )(*operands)


def swap(first, second, axis):
    nx, ny = lax.axis_size("gx"), lax.axis_size("gy")
    turns = ([], [])
    for x in range(nx):
        for y in range(ny):
            if axis == "gx":
                near, far = (x ^ 1, y), ((x + 1 if x % 2 else x - 1) % nx, y)
            else:
                near, far = (x, y ^ 1), (x, y + 1 if y % 2 else y - 1)
                far = far if 0 <= far[1] < ny else (x ^ 1, y)
            for turn, partner in zip(turns, (near, far)):
                turn.append((x * ny + y, partner[0] * ny + partner[1]))
    return [
        lax.ppermute(array, ("gx", "gy"), turn) for array, turn in zip((first, second), turns)
    ]


def body(b, warmth, phase, slots, draw):
    planes, rows, depth = b.shape
    block, wide, table = b.shape, (planes + 2, rows, depth), (8, SKETCH)
    face, line, corner = (3 * rows + 4, depth), (3 * planes + 4, depth), (4, depth)
    cells = pltpu.VMEM((depth // LANES, (planes * rows + 8) * 8, LANES), jnp.float32)
    work = b.size * SKETCH * 6
    b, cond, cap, inner, draw, slots, x_first, x_second, y_first, y_second = call(
        first_kernel,
        [block] * 6 + [face, face, line, line],
        *(
            pltpu.with_memory_space_constraint(x, pltpu.HBM)
            for x in (b, warmth, phase, draw, slots)
        ),
        scratch=[
            pltpu.VMEM(block, warmth.dtype),
            pltpu.VMEM(block, phase.dtype),
            pltpu.VMEM(block, slots.dtype),
            pltpu.SemaphoreType.DMA((5,)),
        ],
        inputs=pltpu.HBM,
    )
    got_x = swap(x_first, x_second, "gx")
    got_y = swap(y_first, y_second, "gy")
    image_wide, beside, inside = call(
        inside_kernel,
        [wide, (4, rows, depth), table],
        b, cond, cap, inner, draw, slots, *got_x,
        scratch=[cells],
        flops=work,
    )
    devices = lax.axis_size("gx") * lax.axis_size("gy")
    image, twice, copies, first, second, ends = call(
        third_kernel,
        [block, block, (devices, FIELDS + 1, SKETCH), corner, corner, (24, depth)],
        b, cond, cap, draw, slots, image_wide, beside, *got_x, *got_y, inside,
        scratch=[cells, pltpu.VMEM((3, 8, depth), jnp.float32)],
        flops=work,
    )
    got_corners = swap(first, second, "gy")
    sketches = lax.all_to_all(copies, ("gx", "gy"), 0, 0)
    return tuple(
        call(
            last_kernel,
            [block, block],
            sketches, b, image, twice, ends, *got_corners,
            outputs=jax.ShapeDtypeStruct,
        )
    )


def solution(mesh):
    spec = P(("parts", "gx"), "gy", None)
    return jax.shard_map(
        body, mesh=mesh, in_specs=(spec,) * 5, out_specs=(spec,) * 2, check_vma=False
    )
```

```python
import jax
import jax.numpy as jnp
from jax import lax
from jax.experimental import pallas as pl
from jax.experimental.pallas import tpu as pltpu
from jax.sharding import PartitionSpec as P

SKETCH = 128
LOW = 32
HIGH = SKETCH // LOW
FIELDS = 3
LANES = 128
epsilon = 1e-06


def traits(warmth, phase):
    powder, solid = phase == 0, phase == 1
    offset = jnp.where(powder, 0.2, jnp.where(solid, 1.0, 0.6))
    return offset * (0.5 + warmth), jnp.where(powder, 1.0, jnp.where(solid, 2.0, 1.5))


def link(first, second):
    total = first + second
    return 2.0 * first * second / jnp.where(total > 0.0, total, 1.0)


def ahead(plane, axis):
    return pltpu.roll(plane, plane.shape[axis] - 1, axis)


def inner_links(cond):
    links = []
    for axis in (0, 1):
        index = lax.broadcasted_iota(jnp.int32, cond.shape, axis)
        links.append(
            jnp.where(index < cond.shape[axis] - 1, link(cond, ahead(cond, axis)), 0.0)
        )
    return links


def inner_flow(field, links):
    total = None
    for axis in (0, 1):
        flow = links[axis] * (field - ahead(field, axis))
        part = flow - pltpu.roll(flow, 1, axis)
        total = part if total is None else total + part
    return total


def apply_inside(images, c_wide, caps):
    results = []
    flow_low = link(c_wide[0], c_wide[1]) * (images[0] - images[1])
    for i in range(1, len(images) - 1):
        image = images[i]
        flow = link(c_wide[i], c_wide[i + 1]) * (image - images[i + 1])
        results.append(
            caps[i - 1] * image + inner_flow(image, inner_links(c_wide[i])) + (flow - flow_low)
        )
        flow_low = flow
    return results


def sketch_rows(planes, cells_ref):
    depth = cells_ref.shape[0] * LANES
    low_index = lax.broadcasted_iota(jnp.int32, (LOW, depth), 0)
    low_index = low_index.astype(jnp.float32).astype(jnp.bfloat16)
    high_index = lax.broadcasted_iota(jnp.int32, (HIGH * 8, depth), 0) // 8
    high_index = high_index.astype(jnp.float32).astype(jnp.bfloat16)
    total = jnp.zeros((HIGH * 8, LOW), jnp.float32)
    start = 0
    for fields, draw, slot, chosen in planes:
        rows = draw.shape[0]
        coarse, fine = [], []
        for field in fields:
            weighted = draw * field
            head = weighted.astype(jnp.bfloat16).astype(jnp.float32)
            coarse.append(head)
            fine.append(weighted - head)
        for f, part in enumerate(coarse + coarse[:1] + fine + fine[:1]):
            for t in range(depth // LANES):
                cells_ref[t, pl.ds(start + f, rows, stride=8), :] = part[
                    :, t * LANES : (t + 1) * LANES
                ]
        high = jnp.floor(slot * (1.0 / LOW))
        low = slot - LOW * high
        left, right = [], []
        for j in chosen:
            at = pl.ds(start + j * 8, 8)
            cells = [cells_ref[t, at, :] for t in range(depth // LANES)]
            cells = jnp.concatenate(cells, axis=1)
            cells = jnp.concatenate([cells] * HIGH, axis=0).astype(jnp.bfloat16)
            row_high = jnp.broadcast_to(high[j : j + 1], cells.shape).astype(jnp.bfloat16)
            row_low = jnp.broadcast_to(low[j : j + 1], (LOW, depth)).astype(jnp.bfloat16)
            left.append(jnp.where(row_high == high_index, cells, jnp.zeros_like(cells)))
            right.append(
                jnp.where(row_low == low_index, jnp.ones_like(row_low), jnp.zeros_like(row_low))
            )
        total = total + lax.dot_general(
            jnp.concatenate(left, axis=1),
            jnp.concatenate(right, axis=1),
            (((1,), (1,)), ((), ())),
            preferred_element_type=jnp.float32,
        )
        start += rows * 8
    parts = jnp.concatenate([total[h * 8 : h * 8 + 8] for h in range(HIGH)], axis=1)
    return parts + pltpu.roll(parts, 4, 0)


def first_kernel(
    b_hbm, warmth_hbm, phase_hbm, draw_hbm, slot_hbm, b_ref, cond_ref, cap_ref, inner_ref,
    draw_ref, slot_ref, x_first_ref, x_second_ref, y_first_ref, y_second_ref, warmth_ref,
    phase_ref, number_ref, arrived,
):
    copies = [
        pltpu.make_async_copy(source, target, arrived.at[k])
        for k, (source, target) in enumerate(
            (
                (b_hbm, b_ref),
                (warmth_hbm, warmth_ref),
                (phase_hbm, phase_ref),
                (draw_hbm, draw_ref),
                (slot_hbm, number_ref),
            )
        )
    ]
    for copy in copies:
        copy.start()
    for copy in copies[:3]:
        copy.wait()
    planes, rows = b_ref.shape[:2]
    images, conds = [], []
    for i in range(planes):
        cond, cap = traits(warmth_ref[i], phase_ref[i])
        cap_ref[i] = cap
        cond_ref[i] = cond
        field = b_ref[i]
        image = cap * field + inner_flow(field, inner_links(cond))
        if i:
            flow = link(conds[-1], cond) * (b_ref[i - 1] - field)
            images[-1] = images[-1] + flow
            image = image - flow
        conds.append(cond)
        images.append(image)
    for i in range(planes):
        inner_ref[i] = images[i]
    for k, field in enumerate((images, [b_ref[i] for i in range(planes)], conds)):
        at = slice(k * rows, (k + 1) * rows)
        x_first_ref[at], x_second_ref[at] = by_turn(field[0], field[-1], "gx")
        for i, plane in enumerate(field):
            at = slice(k * planes + i, k * planes + i + 1)
            y_first_ref[at], y_second_ref[at] = by_turn(plane[:1], plane[rows - 1 :], "gy")
    for copy in copies[3:]:
        copy.wait()
    for i in range(planes):
        slot_ref[i] = number_ref[i].astype(jnp.float32)
    for k, ref in enumerate((draw_ref, slot_ref)):
        ends = [ref[0], ref[planes - 1]]
        for e, j in enumerate((0, rows - 1)):
            at = slice(3 * rows + 2 * k + e, 3 * rows + 2 * k + e + 1)
            lines = [plane[j : j + 1] for plane in ends]
            x_first_ref[at], x_second_ref[at] = by_turn(*lines, "gx")
        for e, plane in enumerate(ends):
            at = slice(3 * planes + 2 * k + e, 3 * planes + 2 * k + e + 1)
            lines = [plane[:1], plane[rows - 1 :]]
            y_first_ref[at], y_second_ref[at] = by_turn(*lines, "gy")


def by_turn(one, other, axis):
    odd = lax.axis_index(axis) % 2 == 1
    return jnp.where(odd, one, other), jnp.where(odd, other, one)


def has_beside(axis):
    at = lax.axis_index(axis)
    return at > 0, at < lax.axis_size(axis) - 1


def reached(rows):
    others = [j for j in range(rows) if 2 <= j < rows - 2]
    return [j for j in range(rows) if j not in others], others


def widened(ref, beside_ref, which):
    inner = [ref[i] for i in range(ref.shape[0])]
    return [beside_ref[which]] + inner + [beside_ref[which + 1]]


def inside_kernel(
    b_ref, cond_ref, cap_ref, inner_ref, draw_ref, slot_ref, got_second_ref, got_first_ref,
    wide_ref, beside_ref, sketch_ref, cells_ref,
):
    planes, rows = b_ref.shape[:2]
    (image_low, image_high), (b_low, b_high), (c_low, c_high) = (
        by_turn(*(ref[k * rows : (k + 1) * rows] for ref in (got_first_ref, got_second_ref)), "gx")
        for k in range(3)
    )
    below, above = has_beside("gx")
    c_low, c_high = jnp.where(below, c_low, 0.0), jnp.where(above, c_high, 0.0)
    for k, plane in enumerate((b_low, b_high, c_low, c_high)):
        beside_ref[k] = plane
    c_wide = [c_low] + [cond_ref[i] for i in range(planes)] + [c_high]
    low_flow = link(c_low, c_wide[1]) * (b_low - b_ref[0])
    high_flow = link(c_wide[-2], c_high) * (b_ref[planes - 1] - b_high)
    images = [image_low + low_flow] + [inner_ref[i] for i in range(planes)]
    images.append(image_high - high_flow)
    images[1] = images[1] - low_flow
    images[-2] = images[-2] + high_flow
    for i, image in enumerate(images):
        wide_ref[i] = image
    twice = apply_inside(images, c_wide, [cap_ref[i] for i in range(planes)])
    chosen = reached(rows)[1]
    sketch_ref[...] = sketch_rows(
        [
            ((b_ref[i], images[i + 1], twice[i]), draw_ref[i], slot_ref[i], chosen)
            for i in range(planes)
        ],
        cells_ref,
    )


def third_kernel(
    b_ref, cond_ref, cap_ref, draw_ref, slot_ref, wide_ref, beside_ref, x_second_ref,
    x_first_ref, y_first_ref, y_second_ref, inside_ref, image_ref, twice_ref, sketch_ref,
    corner_first_ref, corner_second_ref, ends_ref, cells_ref, extra_ref,
):
    planes, rows, depth = b_ref.shape
    index = lax.broadcasted_iota(jnp.int32, (rows, depth), 0)
    b_wide = widened(b_ref, beside_ref, 0)
    c_wide = widened(cond_ref, beside_ref, 2)
    images = [wide_ref[i] for i in range(planes + 2)]
    x_ends = []
    for inner, outer in ((1, 0), (planes, planes + 1)):
        conductance = link(c_wide[inner], c_wide[outer])
        x_ends.append((inner, outer, conductance, conductance * (b_wide[inner] - b_wide[outer])))
    x_tails = by_turn(x_first_ref[3 * rows :], x_second_ref[3 * rows :], "gx")
    y_lines = by_turn(y_first_ref[...], y_second_ref[...], "gy")
    beside = []
    for side, (j, here, line) in enumerate(zip((0, rows - 1), has_beside("gy"), y_lines)):
        row = slice(j, j + 1)
        parts = [[line[k * planes + i :][:1] for i in range(planes)] for k in range(3)]
        beyond, b_line, c_line = parts
        c_line = [jnp.where(here, c, 0.0) for c in c_line]
        flows = []
        for i in range(planes):
            conductance = link(c_wide[i + 1], jnp.broadcast_to(c_line[i], (rows, depth)))
            conductance = jnp.where(index == j, conductance, 0.0)
            flow = conductance * (b_wide[i + 1] - b_line[i])
            images[i + 1] = images[i + 1] + flow
            beside.append((i, conductance, beyond[i] - flow))
            flows.append((conductance, flow))
        for end, (inner, outer, x_link, x_flow) in enumerate(x_ends):
            y_link, y_flow = flows[inner - 1]
            at = 4 * side + 2 * end
            tail = x_tails[end]
            values = (-x_link * y_flow)[row], tail[side : side + 1], tail[2 + side : 3 + side]
            for k, value in enumerate(values):
                extra_ref[k, at : at + 1] = value
            tail = line[3 * planes :]
            values = (-y_link * x_flow)[row], tail[end : end + 1], tail[2 + end : 3 + end]
            for k, value in enumerate(values):
                extra_ref[k, at + 1 : at + 2] = value
            at = 6 * (2 * side + end)
            values = x_link, b_wide[outer], c_wide[outer], y_link
            for k, value in enumerate(values):
                ends_ref[at + k : at + k + 1] = value[row]
            ends_ref[at + 4 : at + 5] = b_line[inner - 1]
            ends_ref[at + 5 : at + 6] = c_line[inner - 1]
    twice = apply_inside(images, c_wide, [cap_ref[i] for i in range(planes)])
    for i, conductance, value in beside:
        twice[i] = twice[i] + conductance * (images[i + 1] - value)
    for i in range(planes):
        image_ref[i] = images[i + 1]
        twice_ref[i] = twice[i]
    chosen = reached(rows)[0]
    cells = [
        ((b_wide[i + 1], images[i + 1], twice[i]), draw_ref[i], slot_ref[i], chosen)
        for i in range(planes)
    ]
    extra, nothing = [extra_ref[k] for k in range(3)], jnp.zeros((8, depth), jnp.float32)
    cells.append(((nothing, nothing, extra[0]), extra[1], extra[2], range(8)))
    sketch = inside_ref[...] + sketch_rows(cells, cells_ref)
    sketch_ref[...] = sketch[: FIELDS + 1]
    for k, plane in enumerate((b_wide[0], b_wide[-1], c_wide[0], c_wide[-1])):
        at = slice(k, k + 1)
        corner_first_ref[at], corner_second_ref[at] = by_turn(
            plane[:1], plane[rows - 1 :], "gy"
        )


def last_kernel(
    sketch_ref, b_ref, image_ref, twice_ref, ends_ref, corner_first_ref, corner_second_ref,
    solution_ref, residual_ref,
):
    sketches = jnp.sum(sketch_ref[...], axis=0)

    def inner(first, second):
        return jnp.sum(first * second, axis=1, keepdims=True)

    s0, s1, s2 = (sketches[i : i + 1] for i in range(FIELDS))
    beta = jnp.sqrt(inner(s0, s0) + epsilon)
    q0 = s0 / beta
    p0 = s1 / beta
    h00 = inner(q0, p0)
    t0 = p0 - h00 * q0
    n0 = jnp.sqrt(inner(t0, t0) + epsilon)
    q1 = t0 / n0
    p1 = (s2 / beta - h00 * p0) / n0
    h01 = inner(q0, p1)
    h11 = inner(q1, p1)
    t1 = p1 - h01 * q0 - h11 * q1
    n1 = jnp.sqrt(inner(t1, t1) + epsilon)
    l00 = jnp.sqrt(h00 * h00 + n0 * n0)
    l10 = (h00 * h01 + n0 * h11) / l00
    l11 = jnp.sqrt(h01 * h01 + h11 * h11 + n1 * n1 - l10 * l10)
    z0 = beta * h00 / l00
    z1 = (beta * h01 - l10 * z0) / l11
    y1 = z1 / l11
    y0 = (z0 - l10 * y1) / l00
    c1 = y1 / (beta * n0)
    c0 = y0 / beta - h00 * c1
    planes, rows, depth = b_ref.shape
    for i in range(planes):
        b, image = b_ref[i], image_ref[i]
        solution_ref[i] = c0 * b + c1 * image
        residual_ref[i] = b - c0 * image - c1 * twice_ref[i]
    corners = by_turn(corner_first_ref[...], corner_second_ref[...], "gy")
    for side, (j, here, corner) in enumerate(zip((0, rows - 1), has_beside("gy"), corners)):
        for end, i in enumerate((0, planes - 1)):
            b, cond = corner[end : end + 1], corner[2 + end : 3 + end]
            cond = jnp.where(here, cond, 0.0)
            at = 6 * (2 * side + end)
            x_link, x_b, x_cond, y_link, y_b, y_cond = (
                ends_ref[at + k : at + k + 1] for k in range(6)
            )
            lacked = x_link * link(x_cond, cond) * (x_b - b)
            lacked = lacked + y_link * link(y_cond, cond) * (y_b - b)
            residual_ref[i, j : j + 1] = residual_ref[i, j : j + 1] + c1 * lacked


def call(kernel, shapes, *operands, scratch=(), inputs=pltpu.VMEM, flops=0):
    return pl.pallas_call(
        kernel,
        out_shape=[jax.ShapeDtypeStruct(shape, jnp.float32) for shape in shapes],
        in_specs=[pl.BlockSpec(memory_space=inputs)] * len(operands),
        out_specs=[pl.BlockSpec(memory_space=pltpu.VMEM)] * len(shapes),
        scratch_shapes=scratch,
        compiler_params=pltpu.CompilerParams(vmem_limit_bytes=48 * 1024 * 1024),
        cost_estimate=pl.CostEstimate(flops=flops, bytes_accessed=0, transcendentals=0),
    )(*operands)


def swap(array, axis, turn):
    nx, ny = lax.axis_size("gx"), lax.axis_size("gy")
    pairs = []
    for x in range(nx):
        for y in range(ny):
            here, count = (x, nx) if axis == "gx" else (y, ny)
            there = here + 1 if here % 2 == turn else here - 1
            if 0 <= there < count:
                partner = (there, y) if axis == "gx" else (x, there)
            else:
                partner = (x, y ^ 1) if axis == "gx" else (x ^ 1, y)
            pairs.append((x * ny + y, partner[0] * ny + partner[1]))
    return lax.ppermute(array, ("gx", "gy"), pairs)


def everyones(sketch):
    count = lax.axis_size("gx") * lax.axis_size("gy")
    copies = jnp.broadcast_to(sketch[None], (count,) + sketch.shape)
    return lax.all_to_all(copies, ("gx", "gy"), 0, 0)


def body(b, warmth, phase, slots, draw):
    planes, rows, depth = b.shape
    block, wide, table = b.shape, (planes + 2, rows, depth), (8, SKETCH)
    face, line, corner = (3 * rows + 4, depth), (3 * planes + 4, depth), (4, depth)
    cells = pltpu.VMEM((depth // LANES, (planes * rows + 8) * 8, LANES), jnp.float32)
    work = b.size * SKETCH * 6
    b, cond, cap, inner, draw, slots, x_first, x_second, y_first, y_second = call(
        first_kernel,
        [block] * 6 + [face, face, line, line],
        *(
            pltpu.with_memory_space_constraint(x, pltpu.HBM)
            for x in (b, warmth, phase, draw, slots)
        ),
        scratch=[
            pltpu.VMEM(block, warmth.dtype),
            pltpu.VMEM(block, phase.dtype),
            pltpu.VMEM(block, slots.dtype),
            pltpu.SemaphoreType.DMA((5,)),
        ],
        inputs=pltpu.HBM,
    )
    x_second = swap(x_second, "gx", 1)
    got_y = [swap(array, "gy", turn) for turn, array in enumerate((y_first, y_second))]
    got_x = x_second, swap(x_first, "gx", 0)
    image_wide, beside, inside = call(
        inside_kernel,
        [wide, (4, rows, depth), table],
        b, cond, cap, inner, draw, slots, *got_x,
        scratch=[cells],
        flops=work,
    )
    image, twice, sketch, first, second, ends = call(
        third_kernel,
        [block, block, (FIELDS + 1, SKETCH), corner, corner, (24, depth)],
        b, cond, cap, draw, slots, image_wide, beside, *got_x, *got_y, inside,
        scratch=[cells, pltpu.VMEM((3, 8, depth), jnp.float32)],
        flops=work,
    )
    got_corners = [swap(array, "gy", turn) for turn, array in enumerate((first, second))]
    sketches = everyones(sketch)
    return tuple(
        call(last_kernel, [block, block], sketches, b, image, twice, ends, *got_corners)
    )


def solution(mesh):
    spec = P(("parts", "gx"), "gy", None)
    return jax.shard_map(
        body, mesh=mesh, in_specs=(spec,) * 5, out_specs=(spec,) * 2, check_vma=False
    )
```

```python
import jax
import jax.numpy as jnp
from jax import lax
from jax.experimental import pallas as pl
from jax.experimental.pallas import tpu as pltpu
from jax.sharding import PartitionSpec as P

SKETCH = 128
LOW = 32
HIGH = SKETCH // LOW
FIELDS = 3
LANES = 128
epsilon = 1e-06


def traits(warmth, phase):
    powder, solid = phase == 0, phase == 1
    offset = jnp.where(powder, 0.2, jnp.where(solid, 1.0, 0.6))
    return offset * (0.5 + warmth), jnp.where(powder, 1.0, jnp.where(solid, 2.0, 1.5))


def link(first, second):
    total = first + second
    return 2.0 * first * second / jnp.where(total > 0.0, total, 1.0)


def ahead(plane, axis):
    return pltpu.roll(plane, plane.shape[axis] - 1, axis)


def inner_links(cond):
    links = []
    for axis in (0, 1):
        index = lax.broadcasted_iota(jnp.int32, cond.shape, axis)
        links.append(
            jnp.where(index < cond.shape[axis] - 1, link(cond, ahead(cond, axis)), 0.0)
        )
    return links


def inner_flow(field, links):
    total = None
    for axis in (0, 1):
        flow = links[axis] * (field - ahead(field, axis))
        part = flow - pltpu.roll(flow, 1, axis)
        total = part if total is None else total + part
    return total


def apply_inside(images, c_wide, caps):
    results = []
    flow_low = link(c_wide[0], c_wide[1]) * (images[0] - images[1])
    for i in range(1, len(images) - 1):
        image = images[i]
        flow = link(c_wide[i], c_wide[i + 1]) * (image - images[i + 1])
        results.append(
            caps[i - 1] * image + inner_flow(image, inner_links(c_wide[i])) + (flow - flow_low)
        )
        flow_low = flow
    return results


def sketch_rows(planes, cells_ref):
    depth = cells_ref.shape[0] * LANES
    low_index = lax.broadcasted_iota(jnp.int32, (LOW, depth), 0)
    low_index = low_index.astype(jnp.float32).astype(jnp.bfloat16)
    high_index = lax.broadcasted_iota(jnp.int32, (HIGH * 8, depth), 0) // 8
    high_index = high_index.astype(jnp.float32).astype(jnp.bfloat16)
    total = jnp.zeros((HIGH * 8, LOW), jnp.float32)
    start = 0
    for fields, draw, slot, chosen in planes:
        rows = draw.shape[0]
        coarse, fine = [], []
        for field in fields:
            weighted = draw * field
            head = weighted.astype(jnp.bfloat16).astype(jnp.float32)
            coarse.append(head)
            fine.append(weighted - head)
        for f, part in enumerate(coarse + coarse[:1] + fine + fine[:1]):
            for t in range(depth // LANES):
                cells_ref[t, pl.ds(start + f, rows, stride=8), :] = part[
                    :, t * LANES : (t + 1) * LANES
                ]
        high = jnp.floor(slot * (1.0 / LOW))
        low = slot - LOW * high
        left, right = [], []
        for j in chosen:
            at = pl.ds(start + j * 8, 8)
            cells = [cells_ref[t, at, :] for t in range(depth // LANES)]
            cells = jnp.concatenate(cells, axis=1)
            cells = jnp.concatenate([cells] * HIGH, axis=0).astype(jnp.bfloat16)
            row_high = jnp.broadcast_to(high[j : j + 1], cells.shape).astype(jnp.bfloat16)
            row_low = jnp.broadcast_to(low[j : j + 1], (LOW, depth)).astype(jnp.bfloat16)
            left.append(jnp.where(row_high == high_index, cells, jnp.zeros_like(cells)))
            right.append(
                jnp.where(row_low == low_index, jnp.ones_like(row_low), jnp.zeros_like(row_low))
            )
        total = total + lax.dot_general(
            jnp.concatenate(left, axis=1),
            jnp.concatenate(right, axis=1),
            (((1,), (1,)), ((), ())),
            preferred_element_type=jnp.float32,
        )
        start += rows * 8
    parts = jnp.concatenate([total[h * 8 : h * 8 + 8] for h in range(HIGH)], axis=1)
    return parts + pltpu.roll(parts, 4, 0)


def first_kernel(
    b_hbm, warmth_hbm, phase_hbm, draw_hbm, slot_hbm, b_ref, cond_ref, cap_ref, inner_ref,
    draw_ref, slot_ref, x_first_ref, x_second_ref, y_first_ref, y_second_ref, warmth_ref,
    phase_ref, number_ref, arrived,
):
    copies = [
        pltpu.make_async_copy(source, target, arrived.at[k])
        for k, (source, target) in enumerate(
            (
                (b_hbm, b_ref),
                (warmth_hbm, warmth_ref),
                (phase_hbm, phase_ref),
                (draw_hbm, draw_ref),
                (slot_hbm, number_ref),
            )
        )
    ]
    for copy in copies:
        copy.start()
    for copy in copies[:3]:
        copy.wait()
    planes, rows = b_ref.shape[:2]
    images, conds = [], []
    for i in range(planes):
        cond, cap = traits(warmth_ref[i], phase_ref[i])
        cap_ref[i] = cap
        cond_ref[i] = cond
        field = b_ref[i]
        image = cap * field + inner_flow(field, inner_links(cond))
        if i:
            flow = link(conds[-1], cond) * (b_ref[i - 1] - field)
            images[-1] = images[-1] + flow
            image = image - flow
        conds.append(cond)
        images.append(image)
    for i in range(planes):
        inner_ref[i] = images[i]
    for k, field in enumerate((images, [b_ref[i] for i in range(planes)], conds)):
        at = slice(k * rows, (k + 1) * rows)
        x_first_ref[at], x_second_ref[at] = by_turn(field[0], field[-1], "gx")
        for i, plane in enumerate(field):
            at = slice(k * planes + i, k * planes + i + 1)
            y_first_ref[at], y_second_ref[at] = by_turn(plane[:1], plane[rows - 1 :], "gy")
    for copy in copies[3:]:
        copy.wait()
    for i in range(planes):
        slot_ref[i] = number_ref[i].astype(jnp.float32)
    for k, ref in enumerate((draw_ref, slot_ref)):
        ends = [ref[0], ref[planes - 1]]
        for e, j in enumerate((0, rows - 1)):
            at = slice(3 * rows + 2 * k + e, 3 * rows + 2 * k + e + 1)
            lines = [plane[j : j + 1] for plane in ends]
            x_first_ref[at], x_second_ref[at] = by_turn(*lines, "gx")
        for e, plane in enumerate(ends):
            at = slice(3 * planes + 2 * k + e, 3 * planes + 2 * k + e + 1)
            lines = [plane[:1], plane[rows - 1 :]]
            y_first_ref[at], y_second_ref[at] = by_turn(*lines, "gy")


def by_turn(one, other, axis):
    odd = lax.axis_index(axis) % 2 == 1
    return jnp.where(odd, one, other), jnp.where(odd, other, one)


def has_beside(axis):
    at = lax.axis_index(axis)
    return at > 0, at < lax.axis_size(axis) - 1


def reached(rows):
    others = [j for j in range(rows) if 2 <= j < rows - 2]
    return [j for j in range(rows) if j not in others], others


def widened(ref, beside_ref, which):
    inner = [ref[i] for i in range(ref.shape[0])]
    return [beside_ref[which]] + inner + [beside_ref[which + 1]]


def inside_kernel(
    b_ref, cond_ref, cap_ref, inner_ref, draw_ref, slot_ref, got_second_ref, got_first_ref,
    wide_ref, beside_ref, sketch_ref, cells_ref,
):
    planes, rows = b_ref.shape[:2]
    (image_low, image_high), (b_low, b_high), (c_low, c_high) = (
        by_turn(*(ref[k * rows : (k + 1) * rows] for ref in (got_first_ref, got_second_ref)), "gx")
        for k in range(3)
    )
    below, above = has_beside("gx")
    c_low, c_high = jnp.where(below, c_low, 0.0), jnp.where(above, c_high, 0.0)
    for k, plane in enumerate((b_low, b_high, c_low, c_high)):
        beside_ref[k] = plane
    c_wide = [c_low] + [cond_ref[i] for i in range(planes)] + [c_high]
    low_flow = link(c_low, c_wide[1]) * (b_low - b_ref[0])
    high_flow = link(c_wide[-2], c_high) * (b_ref[planes - 1] - b_high)
    images = [image_low + low_flow] + [inner_ref[i] for i in range(planes)]
    images.append(image_high - high_flow)
    images[1] = images[1] - low_flow
    images[-2] = images[-2] + high_flow
    for i, image in enumerate(images):
        wide_ref[i] = image
    twice = apply_inside(images, c_wide, [cap_ref[i] for i in range(planes)])
    chosen = reached(rows)[1]
    sketch_ref[...] = sketch_rows(
        [
            ((b_ref[i], images[i + 1], twice[i]), draw_ref[i], slot_ref[i], chosen)
            for i in range(planes)
        ],
        cells_ref,
    )


def third_kernel(
    b_ref, cond_ref, cap_ref, draw_ref, slot_ref, wide_ref, beside_ref, x_second_ref,
    x_first_ref, y_second_ref, y_first_ref, inside_ref, image_ref, twice_ref, sketch_ref,
    corner_first_ref, corner_second_ref, ends_ref, cells_ref, extra_ref,
):
    planes, rows, depth = b_ref.shape
    index = lax.broadcasted_iota(jnp.int32, (rows, depth), 0)
    b_wide = widened(b_ref, beside_ref, 0)
    c_wide = widened(cond_ref, beside_ref, 2)
    images = [wide_ref[i] for i in range(planes + 2)]
    x_ends = []
    for inner, outer in ((1, 0), (planes, planes + 1)):
        conductance = link(c_wide[inner], c_wide[outer])
        x_ends.append((inner, outer, conductance, conductance * (b_wide[inner] - b_wide[outer])))
    x_tails = by_turn(x_first_ref[3 * rows :], x_second_ref[3 * rows :], "gx")
    y_lines = by_turn(y_first_ref[...], y_second_ref[...], "gy")
    beside = []
    for side, (j, here, line) in enumerate(zip((0, rows - 1), has_beside("gy"), y_lines)):
        row = slice(j, j + 1)
        parts = [[line[k * planes + i :][:1] for i in range(planes)] for k in range(3)]
        beyond, b_line, c_line = parts
        c_line = [jnp.where(here, c, 0.0) for c in c_line]
        flows = []
        for i in range(planes):
            conductance = link(c_wide[i + 1], jnp.broadcast_to(c_line[i], (rows, depth)))
            conductance = jnp.where(index == j, conductance, 0.0)
            flow = conductance * (b_wide[i + 1] - b_line[i])
            images[i + 1] = images[i + 1] + flow
            beside.append((i, conductance, beyond[i] - flow))
            flows.append((conductance, flow))
        for end, (inner, outer, x_link, x_flow) in enumerate(x_ends):
            y_link, y_flow = flows[inner - 1]
            at = 4 * side + 2 * end
            tail = x_tails[end]
            values = (-x_link * y_flow)[row], tail[side : side + 1], tail[2 + side : 3 + side]
            for k, value in enumerate(values):
                extra_ref[k, at : at + 1] = value
            tail = line[3 * planes :]
            values = (-y_link * x_flow)[row], tail[end : end + 1], tail[2 + end : 3 + end]
            for k, value in enumerate(values):
                extra_ref[k, at + 1 : at + 2] = value
            at = 6 * (2 * side + end)
            values = x_link, b_wide[outer], c_wide[outer], y_link
            for k, value in enumerate(values):
                ends_ref[at + k : at + k + 1] = value[row]
            ends_ref[at + 4 : at + 5] = b_line[inner - 1]
            ends_ref[at + 5 : at + 6] = c_line[inner - 1]
    twice = apply_inside(images, c_wide, [cap_ref[i] for i in range(planes)])
    for i, conductance, value in beside:
        twice[i] = twice[i] + conductance * (images[i + 1] - value)
    for i in range(planes):
        image_ref[i] = images[i + 1]
        twice_ref[i] = twice[i]
    chosen = reached(rows)[0]
    cells = [
        ((b_wide[i + 1], images[i + 1], twice[i]), draw_ref[i], slot_ref[i], chosen)
        for i in range(planes)
    ]
    extra, nothing = [extra_ref[k] for k in range(3)], jnp.zeros((8, depth), jnp.float32)
    cells.append(((nothing, nothing, extra[0]), extra[1], extra[2], range(8)))
    sketch = inside_ref[...] + sketch_rows(cells, cells_ref)
    sketch_ref[...] = sketch[: FIELDS + 1]
    for k, plane in enumerate((b_wide[0], b_wide[-1], c_wide[0], c_wide[-1])):
        at = slice(k, k + 1)
        corner_first_ref[at], corner_second_ref[at] = by_turn(
            plane[:1], plane[rows - 1 :], "gy"
        )


def last_kernel(
    sketch_ref, b_ref, image_ref, twice_ref, ends_ref, corner_first_ref, corner_second_ref,
    solution_ref, residual_ref,
):
    sketches = jnp.sum(sketch_ref[...], axis=0)

    def inner(first, second):
        return jnp.sum(first * second, axis=1, keepdims=True)

    s0, s1, s2 = (sketches[i : i + 1] for i in range(FIELDS))
    beta = jnp.sqrt(inner(s0, s0) + epsilon)
    q0 = s0 / beta
    p0 = s1 / beta
    h00 = inner(q0, p0)
    t0 = p0 - h00 * q0
    n0 = jnp.sqrt(inner(t0, t0) + epsilon)
    q1 = t0 / n0
    p1 = (s2 / beta - h00 * p0) / n0
    h01 = inner(q0, p1)
    h11 = inner(q1, p1)
    t1 = p1 - h01 * q0 - h11 * q1
    n1 = jnp.sqrt(inner(t1, t1) + epsilon)
    l00 = jnp.sqrt(h00 * h00 + n0 * n0)
    l10 = (h00 * h01 + n0 * h11) / l00
    l11 = jnp.sqrt(h01 * h01 + h11 * h11 + n1 * n1 - l10 * l10)
    z0 = beta * h00 / l00
    z1 = (beta * h01 - l10 * z0) / l11
    y1 = z1 / l11
    y0 = (z0 - l10 * y1) / l00
    c1 = y1 / (beta * n0)
    c0 = y0 / beta - h00 * c1
    planes, rows, depth = b_ref.shape
    for i in range(planes):
        b, image = b_ref[i], image_ref[i]
        solution_ref[i] = c0 * b + c1 * image
        residual_ref[i] = b - c0 * image - c1 * twice_ref[i]
    corners = by_turn(corner_first_ref[...], corner_second_ref[...], "gy")
    for side, (j, here, corner) in enumerate(zip((0, rows - 1), has_beside("gy"), corners)):
        for end, i in enumerate((0, planes - 1)):
            b, cond = corner[end : end + 1], corner[2 + end : 3 + end]
            cond = jnp.where(here, cond, 0.0)
            at = 6 * (2 * side + end)
            x_link, x_b, x_cond, y_link, y_b, y_cond = (
                ends_ref[at + k : at + k + 1] for k in range(6)
            )
            lacked = x_link * link(x_cond, cond) * (x_b - b)
            lacked = lacked + y_link * link(y_cond, cond) * (y_b - b)
            residual_ref[i, j : j + 1] = residual_ref[i, j : j + 1] + c1 * lacked


def call(kernel, shapes, *operands, scratch=(), inputs=pltpu.VMEM, flops=0):
    return pl.pallas_call(
        kernel,
        out_shape=[jax.ShapeDtypeStruct(shape, jnp.float32) for shape in shapes],
        in_specs=[pl.BlockSpec(memory_space=inputs)] * len(operands),
        out_specs=[pl.BlockSpec(memory_space=pltpu.VMEM)] * len(shapes),
        scratch_shapes=scratch,
        compiler_params=pltpu.CompilerParams(vmem_limit_bytes=48 * 1024 * 1024),
        cost_estimate=pl.CostEstimate(flops=flops, bytes_accessed=0, transcendentals=0),
    )(*operands)


def swap(array, axis, turn):
    nx, ny = lax.axis_size("gx"), lax.axis_size("gy")
    pairs = []
    for x in range(nx):
        for y in range(ny):
            here, count = (x, nx) if axis == "gx" else (y, ny)
            there = here + 1 if here % 2 == turn else here - 1
            if 0 <= there < count:
                partner = (there, y) if axis == "gx" else (x, there)
            else:
                partner = (x, y ^ 1) if axis == "gx" else (x ^ 1, y)
            pairs.append((x * ny + y, partner[0] * ny + partner[1]))
    return lax.ppermute(array, ("gx", "gy"), pairs)


def everyones(sketch):
    count = lax.axis_size("gx") * lax.axis_size("gy")
    copies = jnp.broadcast_to(sketch[None], (count,) + sketch.shape)
    return lax.all_to_all(copies, ("gx", "gy"), 0, 0)


def body(b, warmth, phase, slots, draw):
    planes, rows, depth = b.shape
    block, wide, table = b.shape, (planes + 2, rows, depth), (8, SKETCH)
    face, line, corner = (3 * rows + 4, depth), (3 * planes + 4, depth), (4, depth)
    cells = pltpu.VMEM((depth // LANES, (planes * rows + 8) * 8, LANES), jnp.float32)
    work = b.size * SKETCH * 6
    b, cond, cap, inner, draw, slots, x_first, x_second, y_first, y_second = call(
        first_kernel,
        [block] * 6 + [face, face, line, line],
        *(
            pltpu.with_memory_space_constraint(x, pltpu.HBM)
            for x in (b, warmth, phase, draw, slots)
        ),
        scratch=[
            pltpu.VMEM(block, warmth.dtype),
            pltpu.VMEM(block, phase.dtype),
            pltpu.VMEM(block, slots.dtype),
            pltpu.SemaphoreType.DMA((5,)),
        ],
        inputs=pltpu.HBM,
    )
    x_second = swap(x_second, "gx", 1)
    got_y = swap(y_second, "gy", 1), swap(y_first, "gy", 0)
    got_x = x_second, swap(x_first, "gx", 0)
    image_wide, beside, inside = call(
        inside_kernel,
        [wide, (4, rows, depth), table],
        b, cond, cap, inner, draw, slots, *got_x,
        scratch=[cells],
        flops=work,
    )
    image, twice, sketch, first, second, ends = call(
        third_kernel,
        [block, block, (FIELDS + 1, SKETCH), corner, corner, (24, depth)],
        b, cond, cap, draw, slots, image_wide, beside, *got_x, *got_y, inside,
        scratch=[cells, pltpu.VMEM((3, 8, depth), jnp.float32)],
        flops=work,
    )
    got_corners = [swap(array, "gy", turn) for turn, array in enumerate((first, second))]
    sketches = everyones(sketch)
    return tuple(
        call(last_kernel, [block, block], sketches, b, image, twice, ends, *got_corners)
    )


def solution(mesh):
    spec = P(("parts", "gx"), "gy", None)
    return jax.shard_map(
        body, mesh=mesh, in_specs=(spec,) * 5, out_specs=(spec,) * 2, check_vma=False
    )
```

```python
import jax
import jax.numpy as jnp
from jax import lax
from jax.experimental import pallas as pl
from jax.experimental.pallas import tpu as pltpu
from jax.sharding import PartitionSpec as P

SKETCH = 128
LOW = 32
HIGH = SKETCH // LOW
FIELDS = 3
LANES = 128
epsilon = 1e-06


def traits(warmth, phase):
    powder, solid = phase == 0, phase == 1
    offset = jnp.where(powder, 0.2, jnp.where(solid, 1.0, 0.6))
    return offset * (0.5 + warmth), jnp.where(powder, 1.0, jnp.where(solid, 2.0, 1.5))


def link(first, second):
    total = first + second
    return 2.0 * first * second / jnp.where(total > 0.0, total, 1.0)


def ahead(plane, axis):
    return pltpu.roll(plane, plane.shape[axis] - 1, axis)


def inner_links(cond):
    links = []
    for axis in (0, 1):
        index = lax.broadcasted_iota(jnp.int32, cond.shape, axis)
        links.append(
            jnp.where(index < cond.shape[axis] - 1, link(cond, ahead(cond, axis)), 0.0)
        )
    return links


def inner_flow(field, links):
    total = None
    for axis in (0, 1):
        flow = links[axis] * (field - ahead(field, axis))
        part = flow - pltpu.roll(flow, 1, axis)
        total = part if total is None else total + part
    return total


def apply_inside(images, c_wide, caps):
    results = []
    flow_low = link(c_wide[0], c_wide[1]) * (images[0] - images[1])
    for i in range(1, len(images) - 1):
        image = images[i]
        flow = link(c_wide[i], c_wide[i + 1]) * (image - images[i + 1])
        results.append(
            caps[i - 1] * image + inner_flow(image, inner_links(c_wide[i])) + (flow - flow_low)
        )
        flow_low = flow
    return results


def sketch_rows(planes, cells_ref):
    depth = cells_ref.shape[0] * LANES
    low_index = lax.broadcasted_iota(jnp.int32, (LOW, depth), 0)
    low_index = low_index.astype(jnp.float32).astype(jnp.bfloat16)
    high_index = lax.broadcasted_iota(jnp.int32, (HIGH * 8, depth), 0) // 8
    high_index = high_index.astype(jnp.float32).astype(jnp.bfloat16)
    total = jnp.zeros((HIGH * 8, LOW), jnp.float32)
    start = 0
    for fields, draw, slot, chosen in planes:
        rows = draw.shape[0]
        coarse, fine = [], []
        for field in fields:
            weighted = draw * field
            head = weighted.astype(jnp.bfloat16).astype(jnp.float32)
            coarse.append(head)
            fine.append(weighted - head)
        for f, part in enumerate(coarse + coarse[:1] + fine + fine[:1]):
            for t in range(depth // LANES):
                cells_ref[t, pl.ds(start + f, rows, stride=8), :] = part[
                    :, t * LANES : (t + 1) * LANES
                ]
        high = jnp.floor(slot * (1.0 / LOW))
        low = slot - LOW * high
        left, right = [], []
        for j in chosen:
            at = pl.ds(start + j * 8, 8)
            cells = [cells_ref[t, at, :] for t in range(depth // LANES)]
            cells = jnp.concatenate(cells, axis=1)
            cells = jnp.concatenate([cells] * HIGH, axis=0).astype(jnp.bfloat16)
            row_high = jnp.broadcast_to(high[j : j + 1], cells.shape).astype(jnp.bfloat16)
            row_low = jnp.broadcast_to(low[j : j + 1], (LOW, depth)).astype(jnp.bfloat16)
            left.append(jnp.where(row_high == high_index, cells, jnp.zeros_like(cells)))
            right.append(
                jnp.where(row_low == low_index, jnp.ones_like(row_low), jnp.zeros_like(row_low))
            )
        total = total + lax.dot_general(
            jnp.concatenate(left, axis=1),
            jnp.concatenate(right, axis=1),
            (((1,), (1,)), ((), ())),
            preferred_element_type=jnp.float32,
        )
        start += rows * 8
    parts = jnp.concatenate([total[h * 8 : h * 8 + 8] for h in range(HIGH)], axis=1)
    return parts + pltpu.roll(parts, 4, 0)


def first_kernel(
    b_hbm, warmth_hbm, phase_hbm, draw_hbm, slot_hbm, b_ref, cond_ref, cap_ref, inner_ref,
    draw_ref, slot_ref, x_first_ref, x_second_ref, y_first_ref, y_second_ref, warmth_ref,
    phase_ref, number_ref, arrived,
):
    copies = [
        pltpu.make_async_copy(source, target, arrived.at[k])
        for k, (source, target) in enumerate(
            (
                (b_hbm, b_ref),
                (warmth_hbm, warmth_ref),
                (phase_hbm, phase_ref),
                (draw_hbm, draw_ref),
                (slot_hbm, number_ref),
            )
        )
    ]
    for copy in copies:
        copy.start()
    for copy in copies[:3]:
        copy.wait()
    planes, rows = b_ref.shape[:2]
    images, conds = [], []
    for i in range(planes):
        cond, cap = traits(warmth_ref[i], phase_ref[i])
        cap_ref[i] = cap
        cond_ref[i] = cond
        field = b_ref[i]
        image = cap * field + inner_flow(field, inner_links(cond))
        if i:
            flow = link(conds[-1], cond) * (b_ref[i - 1] - field)
            images[-1] = images[-1] + flow
            image = image - flow
        conds.append(cond)
        images.append(image)
    for i in range(planes):
        inner_ref[i] = images[i]
    for k, field in enumerate((images, [b_ref[i] for i in range(planes)], conds)):
        at = slice(k * rows, (k + 1) * rows)
        x_first_ref[at], x_second_ref[at] = by_turn(field[0], field[-1], "gx")
        for i, plane in enumerate(field):
            at = slice(k * planes + i, k * planes + i + 1)
            y_first_ref[at], y_second_ref[at] = by_turn(plane[:1], plane[rows - 1 :], "gy")
    for copy in copies[3:]:
        copy.wait()
    for i in range(planes):
        slot_ref[i] = number_ref[i].astype(jnp.float32)
    for k, ref in enumerate((draw_ref, slot_ref)):
        ends = [ref[0], ref[planes - 1]]
        for e, j in enumerate((0, rows - 1)):
            at = slice(3 * rows + 2 * k + e, 3 * rows + 2 * k + e + 1)
            lines = [plane[j : j + 1] for plane in ends]
            x_first_ref[at], x_second_ref[at] = by_turn(*lines, "gx")
        for e, plane in enumerate(ends):
            at = slice(3 * planes + 2 * k + e, 3 * planes + 2 * k + e + 1)
            lines = [plane[:1], plane[rows - 1 :]]
            y_first_ref[at], y_second_ref[at] = by_turn(*lines, "gy")


def by_turn(one, other, axis):
    odd = lax.axis_index(axis) % 2 == 1
    return jnp.where(odd, one, other), jnp.where(odd, other, one)


def has_beside(axis):
    at = lax.axis_index(axis)
    return at > 0, at < lax.axis_size(axis) - 1


def reached(rows):
    others = [j for j in range(rows) if 2 <= j < rows - 2]
    return [j for j in range(rows) if j not in others], others


def widened(ref, beside_ref, which):
    inner = [ref[i] for i in range(ref.shape[0])]
    return [beside_ref[which]] + inner + [beside_ref[which + 1]]


def inside_kernel(
    b_ref, cond_ref, cap_ref, inner_ref, draw_ref, slot_ref, got_second_ref, got_first_ref,
    wide_ref, beside_ref, sketch_ref, cells_ref,
):
    planes, rows = b_ref.shape[:2]
    (image_low, image_high), (b_low, b_high), (c_low, c_high) = (
        by_turn(*(ref[k * rows : (k + 1) * rows] for ref in (got_first_ref, got_second_ref)), "gx")
        for k in range(3)
    )
    below, above = has_beside("gx")
    c_low, c_high = jnp.where(below, c_low, 0.0), jnp.where(above, c_high, 0.0)
    for k, plane in enumerate((b_low, b_high, c_low, c_high)):
        beside_ref[k] = plane
    c_wide = [c_low] + [cond_ref[i] for i in range(planes)] + [c_high]
    low_flow = link(c_low, c_wide[1]) * (b_low - b_ref[0])
    high_flow = link(c_wide[-2], c_high) * (b_ref[planes - 1] - b_high)
    images = [image_low + low_flow] + [inner_ref[i] for i in range(planes)]
    images.append(image_high - high_flow)
    images[1] = images[1] - low_flow
    images[-2] = images[-2] + high_flow
    for i, image in enumerate(images):
        wide_ref[i] = image
    twice = apply_inside(images, c_wide, [cap_ref[i] for i in range(planes)])
    chosen = reached(rows)[1]
    sketch_ref[...] = sketch_rows(
        [
            ((b_ref[i], images[i + 1], twice[i]), draw_ref[i], slot_ref[i], chosen)
            for i in range(planes)
        ],
        cells_ref,
    )


def third_kernel(
    b_ref, cond_ref, cap_ref, draw_ref, slot_ref, wide_ref, beside_ref, x_second_ref,
    x_first_ref, y_second_ref, y_first_ref, inside_ref, image_ref, twice_ref, sketch_ref,
    corner_first_ref, corner_second_ref, ends_ref, cells_ref, extra_ref,
):
    planes, rows, depth = b_ref.shape
    index = lax.broadcasted_iota(jnp.int32, (rows, depth), 0)
    b_wide = widened(b_ref, beside_ref, 0)
    c_wide = widened(cond_ref, beside_ref, 2)
    images = [wide_ref[i] for i in range(planes + 2)]
    x_ends = []
    for inner, outer in ((1, 0), (planes, planes + 1)):
        conductance = link(c_wide[inner], c_wide[outer])
        x_ends.append((inner, outer, conductance, conductance * (b_wide[inner] - b_wide[outer])))
    x_tails = by_turn(x_first_ref[3 * rows :], x_second_ref[3 * rows :], "gx")
    y_lines = by_turn(y_first_ref[...], y_second_ref[...], "gy")
    beside = []
    for side, (j, here, line) in enumerate(zip((0, rows - 1), has_beside("gy"), y_lines)):
        row = slice(j, j + 1)
        parts = [[line[k * planes + i :][:1] for i in range(planes)] for k in range(3)]
        beyond, b_line, c_line = parts
        c_line = [jnp.where(here, c, 0.0) for c in c_line]
        flows = []
        for i in range(planes):
            conductance = link(c_wide[i + 1], jnp.broadcast_to(c_line[i], (rows, depth)))
            conductance = jnp.where(index == j, conductance, 0.0)
            flow = conductance * (b_wide[i + 1] - b_line[i])
            images[i + 1] = images[i + 1] + flow
            beside.append((i, conductance, beyond[i] - flow))
            flows.append((conductance, flow))
        for end, (inner, outer, x_link, x_flow) in enumerate(x_ends):
            y_link, y_flow = flows[inner - 1]
            at = 4 * side + 2 * end
            tail = x_tails[end]
            values = (-x_link * y_flow)[row], tail[side : side + 1], tail[2 + side : 3 + side]
            for k, value in enumerate(values):
                extra_ref[k, at : at + 1] = value
            tail = line[3 * planes :]
            values = (-y_link * x_flow)[row], tail[end : end + 1], tail[2 + end : 3 + end]
            for k, value in enumerate(values):
                extra_ref[k, at + 1 : at + 2] = value
            at = 6 * (2 * side + end)
            values = x_link, b_wide[outer], c_wide[outer], y_link
            for k, value in enumerate(values):
                ends_ref[at + k : at + k + 1] = value[row]
            ends_ref[at + 4 : at + 5] = b_line[inner - 1]
            ends_ref[at + 5 : at + 6] = c_line[inner - 1]
    twice = apply_inside(images, c_wide, [cap_ref[i] for i in range(planes)])
    for i, conductance, value in beside:
        twice[i] = twice[i] + conductance * (images[i + 1] - value)
    for i in range(planes):
        image_ref[i] = images[i + 1]
        twice_ref[i] = twice[i]
    chosen = reached(rows)[0]
    cells = [
        ((b_wide[i + 1], images[i + 1], twice[i]), draw_ref[i], slot_ref[i], chosen)
        for i in range(planes)
    ]
    extra, nothing = [extra_ref[k] for k in range(3)], jnp.zeros((8, depth), jnp.float32)
    cells.append(((nothing, nothing, extra[0]), extra[1], extra[2], range(8)))
    sketch = inside_ref[...] + sketch_rows(cells, cells_ref)
    sketch_ref[...] = sketch[: FIELDS + 1]
    for k, plane in enumerate((b_wide[0], b_wide[-1], c_wide[0], c_wide[-1])):
        at = slice(k, k + 1)
        corner_first_ref[at], corner_second_ref[at] = by_turn(
            plane[:1], plane[rows - 1 :], "gy"
        )


def last_kernel(
    sketch_ref, b_ref, image_ref, twice_ref, ends_ref, corner_first_ref, corner_second_ref,
    solution_ref, residual_ref,
):
    sketches = sketch_ref[...]

    def inner(first, second):
        return jnp.sum(first * second, axis=1, keepdims=True)

    s0, s1, s2 = (sketches[i : i + 1] for i in range(FIELDS))
    beta = jnp.sqrt(inner(s0, s0) + epsilon)
    q0 = s0 / beta
    p0 = s1 / beta
    h00 = inner(q0, p0)
    t0 = p0 - h00 * q0
    n0 = jnp.sqrt(inner(t0, t0) + epsilon)
    q1 = t0 / n0
    p1 = (s2 / beta - h00 * p0) / n0
    h01 = inner(q0, p1)
    h11 = inner(q1, p1)
    t1 = p1 - h01 * q0 - h11 * q1
    n1 = jnp.sqrt(inner(t1, t1) + epsilon)
    l00 = jnp.sqrt(h00 * h00 + n0 * n0)
    l10 = (h00 * h01 + n0 * h11) / l00
    l11 = jnp.sqrt(h01 * h01 + h11 * h11 + n1 * n1 - l10 * l10)
    z0 = beta * h00 / l00
    z1 = (beta * h01 - l10 * z0) / l11
    y1 = z1 / l11
    y0 = (z0 - l10 * y1) / l00
    c1 = y1 / (beta * n0)
    c0 = y0 / beta - h00 * c1
    planes, rows, depth = b_ref.shape
    for i in range(planes):
        b, image = b_ref[i], image_ref[i]
        solution_ref[i] = c0 * b + c1 * image
        residual_ref[i] = b - c0 * image - c1 * twice_ref[i]
    corners = by_turn(corner_first_ref[...], corner_second_ref[...], "gy")
    for side, (j, here, corner) in enumerate(zip((0, rows - 1), has_beside("gy"), corners)):
        for end, i in enumerate((0, planes - 1)):
            b, cond = corner[end : end + 1], corner[2 + end : 3 + end]
            cond = jnp.where(here, cond, 0.0)
            at = 6 * (2 * side + end)
            x_link, x_b, x_cond, y_link, y_b, y_cond = (
                ends_ref[at + k : at + k + 1] for k in range(6)
            )
            lacked = x_link * link(x_cond, cond) * (x_b - b)
            lacked = lacked + y_link * link(y_cond, cond) * (y_b - b)
            residual_ref[i, j : j + 1] = residual_ref[i, j : j + 1] + c1 * lacked


def call(kernel, shapes, *operands, scratch=(), inputs=pltpu.VMEM, flops=0):
    return pl.pallas_call(
        kernel,
        out_shape=[jax.ShapeDtypeStruct(shape, jnp.float32) for shape in shapes],
        in_specs=[pl.BlockSpec(memory_space=inputs)] * len(operands),
        out_specs=[pl.BlockSpec(memory_space=pltpu.VMEM)] * len(shapes),
        scratch_shapes=scratch,
        compiler_params=pltpu.CompilerParams(vmem_limit_bytes=48 * 1024 * 1024),
        cost_estimate=pl.CostEstimate(flops=flops, bytes_accessed=0, transcendentals=0),
    )(*operands)


def swap(array, axis, turn):
    nx, ny = lax.axis_size("gx"), lax.axis_size("gy")
    pairs = []
    for x in range(nx):
        for y in range(ny):
            here, count = (x, nx) if axis == "gx" else (y, ny)
            there = here + 1 if here % 2 == turn else here - 1
            if 0 <= there < count:
                partner = (there, y) if axis == "gx" else (x, there)
            else:
                partner = (x, y ^ 1) if axis == "gx" else (x ^ 1, y)
            pairs.append((x * ny + y, partner[0] * ny + partner[1]))
    return lax.ppermute(array, ("gx", "gy"), pairs)


def sum_over(table, axis):
    count = lax.axis_size(axis)
    others = [
        lax.ppermute(table, axis, [(i, i ^ step) for i in range(count)])
        for step in range(1, count)
    ]
    return sum(others, table)


def body(b, warmth, phase, slots, draw):
    planes, rows, depth = b.shape
    block, wide, table = b.shape, (planes + 2, rows, depth), (8, SKETCH)
    face, line, corner = (3 * rows + 4, depth), (3 * planes + 4, depth), (4, depth)
    cells = pltpu.VMEM((depth // LANES, (planes * rows + 8) * 8, LANES), jnp.float32)
    work = b.size * SKETCH * 6
    b, cond, cap, inner, draw, slots, x_first, x_second, y_first, y_second = call(
        first_kernel,
        [block] * 6 + [face, face, line, line],
        *(
            pltpu.with_memory_space_constraint(x, pltpu.HBM)
            for x in (b, warmth, phase, draw, slots)
        ),
        scratch=[
            pltpu.VMEM(block, warmth.dtype),
            pltpu.VMEM(block, phase.dtype),
            pltpu.VMEM(block, slots.dtype),
            pltpu.SemaphoreType.DMA((5,)),
        ],
        inputs=pltpu.HBM,
    )
    x_second = swap(x_second, "gx", 1)
    got_y = swap(y_second, "gy", 1), swap(y_first, "gy", 0)
    got_x = x_second, swap(x_first, "gx", 0)
    image_wide, beside, inside = call(
        inside_kernel,
        [wide, (4, rows, depth), table],
        b, cond, cap, inner, draw, slots, *got_x,
        scratch=[cells],
        flops=work,
    )
    image, twice, sketch, first, second, ends = call(
        third_kernel,
        [block, block, (FIELDS + 1, SKETCH), corner, corner, (24, depth)],
        b, cond, cap, draw, slots, image_wide, beside, *got_x, *got_y, inside,
        scratch=[cells, pltpu.VMEM((3, 8, depth), jnp.float32)],
        flops=work,
    )
    got_corners = [swap(array, "gy", turn) for turn, array in enumerate((first, second))]
    sketches = sum_over(sum_over(sketch, "gx"), "gy")
    return tuple(
        call(last_kernel, [block, block], sketches, b, image, twice, ends, *got_corners)
    )


def solution(mesh):
    spec = P(("parts", "gx"), "gy", None)
    return jax.shard_map(
        body, mesh=mesh, in_specs=(spec,) * 5, out_specs=(spec,) * 2, check_vma=False
    )
```

```python
import jax
import jax.numpy as jnp
from jax import lax
from jax.experimental import pallas as pl
from jax.experimental.pallas import tpu as pltpu
from jax.sharding import PartitionSpec as P

SKETCH = 128
LOW = 32
HIGH = SKETCH // LOW
FIELDS = 3
LANES = 128
epsilon = 1e-06


def traits(warmth, phase):
    powder, solid = phase == 0, phase == 1
    offset = jnp.where(powder, 0.2, jnp.where(solid, 1.0, 0.6))
    return offset * (0.5 + warmth), jnp.where(powder, 1.0, jnp.where(solid, 2.0, 1.5))


def link(first, second):
    total = first + second
    return 2.0 * first * second / jnp.where(total > 0.0, total, 1.0)


def ahead(plane, axis):
    return pltpu.roll(plane, plane.shape[axis] - 1, axis)


def inner_links(cond):
    links = []
    for axis in (0, 1):
        index = lax.broadcasted_iota(jnp.int32, cond.shape, axis)
        links.append(
            jnp.where(index < cond.shape[axis] - 1, link(cond, ahead(cond, axis)), 0.0)
        )
    return links


def inner_flow(field, links):
    total = None
    for axis in (0, 1):
        flow = links[axis] * (field - ahead(field, axis))
        part = flow - pltpu.roll(flow, 1, axis)
        total = part if total is None else total + part
    return total


def apply_inside(images, c_wide, caps):
    results = []
    flow_low = link(c_wide[0], c_wide[1]) * (images[0] - images[1])
    for i in range(1, len(images) - 1):
        image = images[i]
        flow = link(c_wide[i], c_wide[i + 1]) * (image - images[i + 1])
        results.append(
            caps[i - 1] * image + inner_flow(image, inner_links(c_wide[i])) + (flow - flow_low)
        )
        flow_low = flow
    return results


def sketch_rows(planes, cells_ref):
    depth = cells_ref.shape[0] * LANES
    low_index = lax.broadcasted_iota(jnp.int32, (LOW, depth), 0)
    low_index = low_index.astype(jnp.float32).astype(jnp.bfloat16)
    high_index = lax.broadcasted_iota(jnp.int32, (HIGH * 8, depth), 0) // 8
    high_index = high_index.astype(jnp.float32).astype(jnp.bfloat16)
    total = jnp.zeros((HIGH * 8, LOW), jnp.float32)
    start = 0
    for fields, draw, slot, chosen in planes:
        rows = draw.shape[0]
        coarse, fine = [], []
        for field in fields:
            weighted = draw * field
            head = weighted.astype(jnp.bfloat16).astype(jnp.float32)
            coarse.append(head)
            fine.append(weighted - head)
        for f, part in enumerate(coarse + coarse[:1] + fine + fine[:1]):
            for t in range(depth // LANES):
                cells_ref[t, pl.ds(start + f, rows, stride=8), :] = part[
                    :, t * LANES : (t + 1) * LANES
                ]
        high = jnp.floor(slot * (1.0 / LOW))
        low = slot - LOW * high
        left, right = [], []
        for j in chosen:
            at = pl.ds(start + j * 8, 8)
            cells = [cells_ref[t, at, :] for t in range(depth // LANES)]
            cells = jnp.concatenate(cells, axis=1)
            cells = jnp.concatenate([cells] * HIGH, axis=0).astype(jnp.bfloat16)
            row_high = jnp.broadcast_to(high[j : j + 1], cells.shape).astype(jnp.bfloat16)
            row_low = jnp.broadcast_to(low[j : j + 1], (LOW, depth)).astype(jnp.bfloat16)
            left.append(jnp.where(row_high == high_index, cells, jnp.zeros_like(cells)))
            right.append(
                jnp.where(row_low == low_index, jnp.ones_like(row_low), jnp.zeros_like(row_low))
            )
        total = total + lax.dot_general(
            jnp.concatenate(left, axis=1),
            jnp.concatenate(right, axis=1),
            (((1,), (1,)), ((), ())),
            preferred_element_type=jnp.float32,
        )
        start += rows * 8
    parts = jnp.concatenate([total[h * 8 : h * 8 + 8] for h in range(HIGH)], axis=1)
    return parts + pltpu.roll(parts, 4, 0)


def first_kernel(
    b_hbm, warmth_hbm, phase_hbm, draw_hbm, slot_hbm, b_ref, cond_ref, cap_ref, inner_ref,
    draw_ref, slot_ref, x_first_ref, x_second_ref, y_first_ref, y_second_ref, warmth_ref,
    phase_ref, number_ref, arrived,
):
    copies = [
        pltpu.make_async_copy(source, target, arrived.at[k])
        for k, (source, target) in enumerate(
            (
                (b_hbm, b_ref),
                (warmth_hbm, warmth_ref),
                (phase_hbm, phase_ref),
                (draw_hbm, draw_ref),
                (slot_hbm, number_ref),
            )
        )
    ]
    for copy in copies:
        copy.start()
    for copy in copies[:3]:
        copy.wait()
    planes, rows = b_ref.shape[:2]
    images, conds = [], []
    for i in range(planes):
        cond, cap = traits(warmth_ref[i], phase_ref[i])
        cap_ref[i] = cap
        cond_ref[i] = cond
        field = b_ref[i]
        image = cap * field + inner_flow(field, inner_links(cond))
        if i:
            flow = link(conds[-1], cond) * (b_ref[i - 1] - field)
            images[-1] = images[-1] + flow
            image = image - flow
        conds.append(cond)
        images.append(image)
    for i in range(planes):
        inner_ref[i] = images[i]
    for k, field in enumerate((images, [b_ref[i] for i in range(planes)], conds)):
        at = slice(k * rows, (k + 1) * rows)
        x_first_ref[at], x_second_ref[at] = by_turn(field[0], field[-1], "gx")
        for i, plane in enumerate(field):
            at = slice(k * planes + i, k * planes + i + 1)
            y_first_ref[at], y_second_ref[at] = by_turn(plane[:1], plane[rows - 1 :], "gy")
    for copy in copies[3:]:
        copy.wait()
    for i in range(planes):
        slot_ref[i] = number_ref[i].astype(jnp.float32)
    for k, ref in enumerate((draw_ref, slot_ref)):
        ends = [ref[0], ref[planes - 1]]
        for e, j in enumerate((0, rows - 1)):
            at = slice(3 * rows + 2 * k + e, 3 * rows + 2 * k + e + 1)
            lines = [plane[j : j + 1] for plane in ends]
            x_first_ref[at], x_second_ref[at] = by_turn(*lines, "gx")
        for e, plane in enumerate(ends):
            at = slice(3 * planes + 2 * k + e, 3 * planes + 2 * k + e + 1)
            lines = [plane[:1], plane[rows - 1 :]]
            y_first_ref[at], y_second_ref[at] = by_turn(*lines, "gy")


def by_turn(one, other, axis):
    odd = lax.axis_index(axis) % 2 == 1
    return jnp.where(odd, one, other), jnp.where(odd, other, one)


def has_beside(axis):
    at = lax.axis_index(axis)
    return at > 0, at < lax.axis_size(axis) - 1


def reached(rows):
    others = [j for j in range(rows) if 2 <= j < rows - 2]
    return [j for j in range(rows) if j not in others], others


def widened(ref, beside_ref, which):
    inner = [ref[i] for i in range(ref.shape[0])]
    return [beside_ref[which]] + inner + [beside_ref[which + 1]]


def inside_kernel(
    b_ref, cond_ref, cap_ref, inner_ref, draw_ref, slot_ref, got_second_ref, got_first_ref,
    wide_ref, beside_ref, sketch_ref, cells_ref,
):
    planes, rows = b_ref.shape[:2]
    (image_low, image_high), (b_low, b_high), (c_low, c_high) = (
        by_turn(*(ref[k * rows : (k + 1) * rows] for ref in (got_first_ref, got_second_ref)), "gx")
        for k in range(3)
    )
    below, above = has_beside("gx")
    c_low, c_high = jnp.where(below, c_low, 0.0), jnp.where(above, c_high, 0.0)
    for k, plane in enumerate((b_low, b_high, c_low, c_high)):
        beside_ref[k] = plane
    c_wide = [c_low] + [cond_ref[i] for i in range(planes)] + [c_high]
    low_flow = link(c_low, c_wide[1]) * (b_low - b_ref[0])
    high_flow = link(c_wide[-2], c_high) * (b_ref[planes - 1] - b_high)
    images = [image_low + low_flow] + [inner_ref[i] for i in range(planes)]
    images.append(image_high - high_flow)
    images[1] = images[1] - low_flow
    images[-2] = images[-2] + high_flow
    for i, image in enumerate(images):
        wide_ref[i] = image
    twice = apply_inside(images, c_wide, [cap_ref[i] for i in range(planes)])
    chosen = reached(rows)[1]
    sketch_ref[...] = sketch_rows(
        [
            ((b_ref[i], images[i + 1], twice[i]), draw_ref[i], slot_ref[i], chosen)
            for i in range(planes)
        ],
        cells_ref,
    )


def third_kernel(
    b_ref, cond_ref, cap_ref, draw_ref, slot_ref, wide_ref, beside_ref, x_second_ref,
    x_first_ref, y_second_ref, y_first_ref, inside_ref, image_ref, twice_ref, sketch_ref,
    first_ref, second_ref, ends_ref, cells_ref, extra_ref,
):
    planes, rows, depth = b_ref.shape
    index = lax.broadcasted_iota(jnp.int32, (rows, depth), 0)
    b_wide = widened(b_ref, beside_ref, 0)
    c_wide = widened(cond_ref, beside_ref, 2)
    images = [wide_ref[i] for i in range(planes + 2)]
    x_ends = []
    for inner, outer in ((1, 0), (planes, planes + 1)):
        conductance = link(c_wide[inner], c_wide[outer])
        x_ends.append((inner, outer, conductance, conductance * (b_wide[inner] - b_wide[outer])))
    x_tails = by_turn(x_first_ref[3 * rows :], x_second_ref[3 * rows :], "gx")
    y_lines = by_turn(y_first_ref[...], y_second_ref[...], "gy")
    beside = []
    for side, (j, here, line) in enumerate(zip((0, rows - 1), has_beside("gy"), y_lines)):
        row = slice(j, j + 1)
        parts = [[line[k * planes + i :][:1] for i in range(planes)] for k in range(3)]
        beyond, b_line, c_line = parts
        c_line = [jnp.where(here, c, 0.0) for c in c_line]
        flows = []
        for i in range(planes):
            conductance = link(c_wide[i + 1], jnp.broadcast_to(c_line[i], (rows, depth)))
            conductance = jnp.where(index == j, conductance, 0.0)
            flow = conductance * (b_wide[i + 1] - b_line[i])
            images[i + 1] = images[i + 1] + flow
            beside.append((i, conductance, beyond[i] - flow))
            flows.append((conductance, flow))
        for end, (inner, outer, x_link, x_flow) in enumerate(x_ends):
            y_link, y_flow = flows[inner - 1]
            at = 4 * side + 2 * end
            tail = x_tails[end]
            values = (-x_link * y_flow)[row], tail[side : side + 1], tail[2 + side : 3 + side]
            for k, value in enumerate(values):
                extra_ref[k, at : at + 1] = value
            tail = line[3 * planes :]
            values = (-y_link * x_flow)[row], tail[end : end + 1], tail[2 + end : 3 + end]
            for k, value in enumerate(values):
                extra_ref[k, at + 1 : at + 2] = value
            at = 6 * (2 * side + end)
            values = x_link, b_wide[outer], c_wide[outer], y_link
            for k, value in enumerate(values):
                ends_ref[at + k : at + k + 1] = value[row]
            ends_ref[at + 4 : at + 5] = b_line[inner - 1]
            ends_ref[at + 5 : at + 6] = c_line[inner - 1]
    twice = apply_inside(images, c_wide, [cap_ref[i] for i in range(planes)])
    for i, conductance, value in beside:
        twice[i] = twice[i] + conductance * (images[i + 1] - value)
    for i in range(planes):
        image_ref[i] = images[i + 1]
        twice_ref[i] = twice[i]
    chosen = reached(rows)[0]
    cells = [
        ((b_wide[i + 1], images[i + 1], twice[i]), draw_ref[i], slot_ref[i], chosen)
        for i in range(planes)
    ]
    extra, nothing = [extra_ref[k] for k in range(3)], jnp.zeros((8, depth), jnp.float32)
    cells.append(((nothing, nothing, extra[0]), extra[1], extra[2], range(8)))
    sketch = inside_ref[...] + sketch_rows(cells, cells_ref)
    for ref in (sketch_ref, first_ref, second_ref):
        ref[:, :SKETCH] = sketch[: FIELDS + 1]
    for k, plane in enumerate((b_wide[0], b_wide[-1], c_wide[0], c_wide[-1])):
        at = slice(k, k + 1), slice(SKETCH, None)
        first_ref[at], second_ref[at] = by_turn(plane[:1], plane[rows - 1 :], "gy")


def last_kernel(
    sketch_ref, b_ref, image_ref, twice_ref, ends_ref, got_first_ref, got_second_ref,
    solution_ref, residual_ref,
):
    sketches = sketch_ref[...]

    def inner(first, second):
        return jnp.sum(first * second, axis=1, keepdims=True)

    s0, s1, s2 = (sketches[i : i + 1] for i in range(FIELDS))
    beta = jnp.sqrt(inner(s0, s0) + epsilon)
    q0 = s0 / beta
    p0 = s1 / beta
    h00 = inner(q0, p0)
    t0 = p0 - h00 * q0
    n0 = jnp.sqrt(inner(t0, t0) + epsilon)
    q1 = t0 / n0
    p1 = (s2 / beta - h00 * p0) / n0
    h01 = inner(q0, p1)
    h11 = inner(q1, p1)
    t1 = p1 - h01 * q0 - h11 * q1
    n1 = jnp.sqrt(inner(t1, t1) + epsilon)
    l00 = jnp.sqrt(h00 * h00 + n0 * n0)
    l10 = (h00 * h01 + n0 * h11) / l00
    l11 = jnp.sqrt(h01 * h01 + h11 * h11 + n1 * n1 - l10 * l10)
    z0 = beta * h00 / l00
    z1 = (beta * h01 - l10 * z0) / l11
    y1 = z1 / l11
    y0 = (z0 - l10 * y1) / l00
    c1 = y1 / (beta * n0)
    c0 = y0 / beta - h00 * c1
    planes, rows, depth = b_ref.shape
    for i in range(planes):
        b, image = b_ref[i], image_ref[i]
        solution_ref[i] = c0 * b + c1 * image
        residual_ref[i] = b - c0 * image - c1 * twice_ref[i]
    corners = by_turn(got_first_ref[:, SKETCH:], got_second_ref[:, SKETCH:], "gy")
    for side, (j, here, corner) in enumerate(zip((0, rows - 1), has_beside("gy"), corners)):
        for end, i in enumerate((0, planes - 1)):
            b, cond = corner[end : end + 1], corner[2 + end : 3 + end]
            cond = jnp.where(here, cond, 0.0)
            at = 6 * (2 * side + end)
            x_link, x_b, x_cond, y_link, y_b, y_cond = (
                ends_ref[at + k : at + k + 1] for k in range(6)
            )
            lacked = x_link * link(x_cond, cond) * (x_b - b)
            lacked = lacked + y_link * link(y_cond, cond) * (y_b - b)
            residual_ref[i, j : j + 1] = residual_ref[i, j : j + 1] + c1 * lacked


def call(kernel, shapes, *operands, scratch=(), inputs=pltpu.VMEM, flops=0):
    return pl.pallas_call(
        kernel,
        out_shape=[jax.ShapeDtypeStruct(shape, jnp.float32) for shape in shapes],
        in_specs=[pl.BlockSpec(memory_space=inputs)] * len(operands),
        out_specs=[pl.BlockSpec(memory_space=pltpu.VMEM)] * len(shapes),
        scratch_shapes=scratch,
        compiler_params=pltpu.CompilerParams(vmem_limit_bytes=48 * 1024 * 1024),
        cost_estimate=pl.CostEstimate(flops=flops, bytes_accessed=0, transcendentals=0),
    )(*operands)


def swap(array, axis, turn):
    nx, ny = lax.axis_size("gx"), lax.axis_size("gy")
    pairs = []
    for x in range(nx):
        for y in range(ny):
            here, count = (x, nx) if axis == "gx" else (y, ny)
            there = here + 1 if here % 2 == turn else here - 1
            if 0 <= there < count:
                partner = (there, y) if axis == "gx" else (x, there)
            else:
                partner = (x, y ^ 1) if axis == "gx" else (x ^ 1, y)
            pairs.append((x * ny + y, partner[0] * ny + partner[1]))
    return lax.ppermute(array, ("gx", "gy"), pairs)


def meet(array, axis, turn):
    count = lax.axis_size(axis)

    def partner(player, turn):
        if player in (turn, count - 1):
            return count - 1 if player == turn else turn
        return (2 * turn - player) % (count - 1)

    players = [count - 1]
    while len(players) < count:
        players.append(partner(players[-1], (len(players) - 1) % 2))
    pairs = [(i, players.index(partner(player, turn))) for i, player in enumerate(players)]
    return lax.ppermute(array, axis, pairs)


def body(b, warmth, phase, slots, draw):
    planes, rows, depth = b.shape
    block, wide, table = b.shape, (planes + 2, rows, depth), (8, SKETCH)
    face, line, corner = (3 * rows + 4, depth), (3 * planes + 4, depth), (4, depth)
    cells = pltpu.VMEM((depth // LANES, (planes * rows + 8) * 8, LANES), jnp.float32)
    work = b.size * SKETCH * 6
    b, cond, cap, inner, draw, slots, x_first, x_second, y_first, y_second = call(
        first_kernel,
        [block] * 6 + [face, face, line, line],
        *(
            pltpu.with_memory_space_constraint(x, pltpu.HBM)
            for x in (b, warmth, phase, draw, slots)
        ),
        scratch=[
            pltpu.VMEM(block, warmth.dtype),
            pltpu.VMEM(block, phase.dtype),
            pltpu.VMEM(block, slots.dtype),
            pltpu.SemaphoreType.DMA((5,)),
        ],
        inputs=pltpu.HBM,
    )
    x_second = swap(x_second, "gx", 1)
    got_y = swap(y_second, "gy", 1), swap(y_first, "gy", 0)
    got_x = x_second, swap(x_first, "gx", 0)
    image_wide, beside, inside = call(
        inside_kernel,
        [wide, (4, rows, depth), table],
        b, cond, cap, inner, draw, slots, *got_x,
        scratch=[cells],
        flops=work,
    )
    message = (FIELDS + 1, SKETCH + depth)
    image, twice, sketch, first, second, ends = call(
        third_kernel,
        [block, block, (FIELDS + 1, SKETCH), message, message, (24, depth)],
        b, cond, cap, draw, slots, image_wide, beside, *got_x, *got_y, inside,
        scratch=[cells, pltpu.VMEM((3, 8, depth), jnp.float32)],
        flops=work,
    )
    first, second = meet(first, "gy", 0), meet(second, "gy", 1)
    others = [meet(sketch, "gy", turn) for turn in range(2, lax.axis_size("gy") - 1)]
    sketch = sum(others, sketch + first[:, :SKETCH] + second[:, :SKETCH])
    others = [meet(sketch, "gx", turn) for turn in range(lax.axis_size("gx") - 1)]
    sketch = sum(others, sketch)
    return tuple(
        call(last_kernel, [block, block], sketch, b, image, twice, ends, first, second)
    )


def solution(mesh):
    spec = P(("parts", "gx"), "gy", None)
    return jax.shard_map(
        body, mesh=mesh, in_specs=(spec,) * 5, out_specs=(spec,) * 2, check_vma=False
    )
```

```python
import jax
import jax.numpy as jnp
from jax import lax
from jax.experimental import pallas as pl
from jax.experimental.pallas import tpu as pltpu
from jax.sharding import PartitionSpec as P

SKETCH = 128
LOW = 32
HIGH = SKETCH // LOW
FIELDS = 3
LANES = 128
epsilon = 1e-06


def traits(warmth, phase):
    powder, solid = phase == 0, phase == 1
    offset = jnp.where(powder, 0.2, jnp.where(solid, 1.0, 0.6))
    return offset * (0.5 + warmth), jnp.where(powder, 1.0, jnp.where(solid, 2.0, 1.5))


def link(first, second):
    total = first + second
    return 2.0 * first * second / jnp.where(total > 0.0, total, 1.0)


def ahead(plane, axis):
    return pltpu.roll(plane, plane.shape[axis] - 1, axis)


def inner_links(cond):
    links = []
    for axis in (0, 1):
        index = lax.broadcasted_iota(jnp.int32, cond.shape, axis)
        links.append(
            jnp.where(index < cond.shape[axis] - 1, link(cond, ahead(cond, axis)), 0.0)
        )
    return links


def inner_flow(field, links):
    total = None
    for axis in (0, 1):
        flow = links[axis] * (field - ahead(field, axis))
        part = flow - pltpu.roll(flow, 1, axis)
        total = part if total is None else total + part
    return total


def apply_inside(images, x_links, links, caps):
    results = []
    flow_low = x_links[0] * (images[0] - images[1])
    for i in range(1, len(images) - 1):
        image = images[i]
        flow = x_links[i] * (image - images[i + 1])
        inside = inner_flow(image, links[i - 1])
        results.append(caps[i - 1] * image + inside + (flow - flow_low))
        flow_low = flow
    return results


def sketch_rows(planes, cells_ref):
    depth = cells_ref.shape[0] * LANES
    low_index = lax.broadcasted_iota(jnp.int32, (LOW, depth), 0)
    low_index = low_index.astype(jnp.float32).astype(jnp.bfloat16)
    high_index = lax.broadcasted_iota(jnp.int32, (HIGH * 8, depth), 0) // 8
    high_index = high_index.astype(jnp.float32).astype(jnp.bfloat16)
    total = jnp.zeros((HIGH * 8, LOW), jnp.float32)
    start = 0
    for fields, draw, slot, chosen in planes:
        rows = draw.shape[0]
        coarse, fine = [], []
        for field in fields:
            weighted = draw * field
            head = weighted.astype(jnp.bfloat16).astype(jnp.float32)
            coarse.append(head)
            fine.append(weighted - head)
        for f, part in enumerate(coarse + coarse[:1] + fine + fine[:1]):
            for t in range(depth // LANES):
                cells_ref[t, pl.ds(start + f, rows, stride=8), :] = part[
                    :, t * LANES : (t + 1) * LANES
                ]
        high = jnp.floor(slot * (1.0 / LOW))
        low = slot - LOW * high
        left, right = [], []
        for j in chosen:
            at = pl.ds(start + j * 8, 8)
            cells = [cells_ref[t, at, :] for t in range(depth // LANES)]
            cells = jnp.concatenate(cells, axis=1)
            cells = jnp.concatenate([cells] * HIGH, axis=0).astype(jnp.bfloat16)
            row_high = jnp.broadcast_to(high[j : j + 1], cells.shape).astype(jnp.bfloat16)
            row_low = jnp.broadcast_to(low[j : j + 1], (LOW, depth)).astype(jnp.bfloat16)
            left.append(jnp.where(row_high == high_index, cells, jnp.zeros_like(cells)))
            right.append(
                jnp.where(row_low == low_index, jnp.ones_like(row_low), jnp.zeros_like(row_low))
            )
        total = total + lax.dot_general(
            jnp.concatenate(left, axis=1),
            jnp.concatenate(right, axis=1),
            (((1,), (1,)), ((), ())),
            preferred_element_type=jnp.float32,
        )
        start += rows * 8
    parts = jnp.concatenate([total[h * 8 : h * 8 + 8] for h in range(HIGH)], axis=1)
    return parts + pltpu.roll(parts, 4, 0)


def first_kernel(
    b_hbm, warmth_hbm, phase_hbm, draw_hbm, slot_hbm, b_ref, cond_ref, cap_ref, y_link_ref,
    z_link_ref, inner_ref, draw_ref, slot_ref, x_first_ref, x_second_ref, y_first_ref,
    y_second_ref, warmth_ref, phase_ref, number_ref, arrived,
):
    copies = [
        pltpu.make_async_copy(source, target, arrived.at[k])
        for k, (source, target) in enumerate(
            (
                (b_hbm, b_ref),
                (warmth_hbm, warmth_ref),
                (phase_hbm, phase_ref),
                (draw_hbm, draw_ref),
                (slot_hbm, number_ref),
            )
        )
    ]
    for copy in copies:
        copy.start()
    for copy in copies[:3]:
        copy.wait()
    planes, rows = b_ref.shape[:2]
    images, conds = [], []
    for i in range(planes):
        cond, cap = traits(warmth_ref[i], phase_ref[i])
        cap_ref[i] = cap
        cond_ref[i] = cond
        y_link_ref[i], z_link_ref[i] = links = inner_links(cond)
        field = b_ref[i]
        image = cap * field + inner_flow(field, links)
        if i:
            flow = link(conds[-1], cond) * (b_ref[i - 1] - field)
            images[-1] = images[-1] + flow
            image = image - flow
        conds.append(cond)
        images.append(image)
    for i in range(planes):
        inner_ref[i] = images[i]
    for k, field in enumerate((images, [b_ref[i] for i in range(planes)], conds)):
        at = slice(k * rows, (k + 1) * rows)
        x_first_ref[at], x_second_ref[at] = by_turn(field[0], field[-1], "gx")
        for i, plane in enumerate(field):
            at = slice(k * planes + i, k * planes + i + 1)
            y_first_ref[at], y_second_ref[at] = by_turn(plane[:1], plane[rows - 1 :], "gy")
    for copy in copies[3:]:
        copy.wait()
    for i in range(planes):
        slot_ref[i] = number_ref[i].astype(jnp.float32)
    for k, ref in enumerate((draw_ref, slot_ref)):
        ends = [ref[0], ref[planes - 1]]
        for e, j in enumerate((0, rows - 1)):
            at = slice(3 * rows + 2 * k + e, 3 * rows + 2 * k + e + 1)
            lines = [plane[j : j + 1] for plane in ends]
            x_first_ref[at], x_second_ref[at] = by_turn(*lines, "gx")
        for e, plane in enumerate(ends):
            at = slice(3 * planes + 2 * k + e, 3 * planes + 2 * k + e + 1)
            lines = [plane[:1], plane[rows - 1 :]]
            y_first_ref[at], y_second_ref[at] = by_turn(*lines, "gy")


def by_turn(one, other, axis):
    odd = lax.axis_index(axis) % 2 == 1
    return jnp.where(odd, one, other), jnp.where(odd, other, one)


def has_beside(axis):
    at = lax.axis_index(axis)
    return at > 0, at < lax.axis_size(axis) - 1


def reached(rows):
    others = [j for j in range(rows) if 2 <= j < rows - 2]
    return [j for j in range(rows) if j not in others], others


def inside_kernel(
    b_ref, cond_ref, cap_ref, y_link_ref, z_link_ref, inner_ref, draw_ref, slot_ref,
    got_second_ref, got_first_ref, wide_ref, x_link_ref, beside_ref, sketch_ref, cells_ref,
):
    planes, rows = b_ref.shape[:2]
    (image_low, image_high), (b_low, b_high), (c_low, c_high) = (
        by_turn(*(ref[k * rows : (k + 1) * rows] for ref in (got_first_ref, got_second_ref)), "gx")
        for k in range(3)
    )
    below, above = has_beside("gx")
    c_low, c_high = jnp.where(below, c_low, 0.0), jnp.where(above, c_high, 0.0)
    for k, plane in enumerate((b_low, b_high, c_low, c_high)):
        beside_ref[k] = plane
    conds = [c_low] + [cond_ref[i] for i in range(planes)] + [c_high]
    x_links = [link(conds[i], conds[i + 1]) for i in range(planes + 1)]
    for i, conductance in enumerate(x_links):
        x_link_ref[i] = conductance
    low_flow = x_links[0] * (b_low - b_ref[0])
    high_flow = x_links[-1] * (b_ref[planes - 1] - b_high)
    images = [image_low + low_flow] + [inner_ref[i] for i in range(planes)]
    images.append(image_high - high_flow)
    images[1] = images[1] - low_flow
    images[-2] = images[-2] + high_flow
    for i, image in enumerate(images):
        wide_ref[i] = image
    links = [(y_link_ref[i], z_link_ref[i]) for i in range(planes)]
    twice = apply_inside(images, x_links, links, [cap_ref[i] for i in range(planes)])
    chosen = reached(rows)[1]
    sketch_ref[...] = sketch_rows(
        [
            ((b_ref[i], images[i + 1], twice[i]), draw_ref[i], slot_ref[i], chosen)
            for i in range(planes)
        ],
        cells_ref,
    )


def third_kernel(
    b_ref, cap_ref, y_link_ref, z_link_ref, draw_ref, slot_ref, own_second_ref, own_first_ref,
    wide_ref, x_link_ref, beside_ref, x_second_ref, x_first_ref, y_second_ref, y_first_ref,
    inside_ref, image_ref, twice_ref, sketch_ref, corner_first_ref, corner_second_ref, ends_ref,
    cells_ref, extra_ref,
):
    planes, rows, depth = b_ref.shape
    index = lax.broadcasted_iota(jnp.int32, (rows, depth), 0)
    images = [wide_ref[i] for i in range(planes + 2)]
    x_links = [x_link_ref[i] for i in range(planes + 1)]
    b_beside, c_beside = (beside_ref[0], beside_ref[1]), (beside_ref[2], beside_ref[3])
    x_ends = []
    for end, i in enumerate((0, planes - 1)):
        conductance = x_links[-end]
        x_ends.append((i, conductance, conductance * (b_ref[i] - b_beside[end])))
    x_tails = by_turn(x_first_ref[3 * rows :], x_second_ref[3 * rows :], "gx")
    own_lines = by_turn(own_first_ref[...], own_second_ref[...], "gy")
    y_lines = by_turn(y_first_ref[...], y_second_ref[...], "gy")
    beside = []
    for side, (j, here, own, line) in enumerate(
        zip((0, rows - 1), has_beside("gy"), own_lines, y_lines)
    ):
        row = slice(j, j + 1)
        beyond, b_line, c_line = (line[k * planes : (k + 1) * planes] for k in range(3))
        c_line = jnp.where(here, c_line, 0.0)
        y_link = link(own[2 * planes : 3 * planes], c_line)
        y_flow = y_link * (own[planes : 2 * planes] - b_line)
        beyond = beyond - y_flow
        for i in range(planes):
            at = slice(i, i + 1)
            images[i + 1] = images[i + 1] + jnp.where(index == j, y_flow[at], 0.0)
            beside.append((i, jnp.where(index == j, y_link[at], 0.0), beyond[at]))
        for end, (i, x_link, x_flow) in enumerate(x_ends):
            line_at, at = slice(i, i + 1), 4 * side + 2 * end
            tail = x_tails[end]
            values = -x_link[row] * y_flow[line_at], tail[side:][:1], tail[2 + side :][:1]
            for k, value in enumerate(values):
                extra_ref[k, at : at + 1] = value
            tail = line[3 * planes :]
            values = -y_link[line_at] * x_flow[row], tail[end:][:1], tail[2 + end :][:1]
            for k, value in enumerate(values):
                extra_ref[k, at + 1 : at + 2] = value
            at = 6 * (2 * side + end)
            values = x_link[row], b_beside[end][row], c_beside[end][row]
            values += y_link[line_at], b_line[line_at], c_line[line_at]
            for k, value in enumerate(values):
                ends_ref[at + k : at + k + 1] = value
    links = [(y_link_ref[i], z_link_ref[i]) for i in range(planes)]
    twice = apply_inside(images, x_links, links, [cap_ref[i] for i in range(planes)])
    for i, conductance, value in beside:
        twice[i] = twice[i] + conductance * (images[i + 1] - value)
    for i in range(planes):
        image_ref[i] = images[i + 1]
        twice_ref[i] = twice[i]
    chosen = reached(rows)[0]
    cells = [
        ((b_ref[i], images[i + 1], twice[i]), draw_ref[i], slot_ref[i], chosen)
        for i in range(planes)
    ]
    extra, nothing = [extra_ref[k] for k in range(3)], jnp.zeros((8, depth), jnp.float32)
    cells.append(((nothing, nothing, extra[0]), extra[1], extra[2], range(8)))
    sketch = inside_ref[...] + sketch_rows(cells, cells_ref)
    sketch_ref[...] = sketch[: FIELDS + 1]
    for k, plane in enumerate(b_beside + c_beside):
        at = slice(k, k + 1)
        corner_first_ref[at], corner_second_ref[at] = by_turn(
            plane[:1], plane[rows - 1 :], "gy"
        )


def last_kernel(
    sketch_ref, b_ref, image_ref, twice_ref, ends_ref, corner_first_ref, corner_second_ref,
    solution_ref, residual_ref,
):
    sketches = jnp.sum(sketch_ref[...], axis=0)

    def inner(first, second):
        return jnp.sum(first * second, axis=1, keepdims=True)

    s0, s1, s2 = (sketches[i : i + 1] for i in range(FIELDS))
    beta_inverse = 1.0 / jnp.sqrt(inner(s0, s0) + epsilon)
    h00 = inner(s0, s1) * beta_inverse * beta_inverse
    q0, p0 = s0 * beta_inverse, s1 * beta_inverse
    t0 = p0 - h00 * q0
    p1 = s2 * beta_inverse - h00 * p0
    n0 = jnp.sqrt(inner(t0, t0) + epsilon)
    n0_inverse = 1.0 / n0
    h01 = inner(q0, p1) * n0_inverse
    h11 = inner(t0, p1) * n0_inverse * n0_inverse
    t1 = p1 * n0_inverse - h01 * q0 - h11 * (t0 * n0_inverse)
    n1_square = inner(t1, t1) + epsilon
    first = h00 * h00 + n0 * n0
    cross = h00 * h01 + n0 * h11
    ratio = cross / first
    second = h01 * h01 + h11 * h11 + n1_square - cross * ratio
    y1 = (h01 - ratio * h00) / second
    y0 = h00 / first - ratio * y1
    c1 = y1 * n0_inverse
    c0 = y0 - h00 * c1
    planes, rows, depth = b_ref.shape
    for i in range(planes):
        b, image = b_ref[i], image_ref[i]
        solution_ref[i] = c0 * b + c1 * image
        residual_ref[i] = b - c0 * image - c1 * twice_ref[i]
    corners = by_turn(corner_first_ref[...], corner_second_ref[...], "gy")
    for side, (j, here, corner) in enumerate(zip((0, rows - 1), has_beside("gy"), corners)):
        for end, i in enumerate((0, planes - 1)):
            b, cond = corner[end : end + 1], corner[2 + end : 3 + end]
            cond = jnp.where(here, cond, 0.0)
            at = 6 * (2 * side + end)
            x_link, x_b, x_cond, y_link, y_b, y_cond = (
                ends_ref[at + k : at + k + 1] for k in range(6)
            )
            lacked = x_link * link(x_cond, cond) * (x_b - b)
            lacked = lacked + y_link * link(y_cond, cond) * (y_b - b)
            residual_ref[i, j : j + 1] = residual_ref[i, j : j + 1] + c1 * lacked


def call(kernel, shapes, *operands, scratch=(), inputs=pltpu.VMEM, flops=0):
    return pl.pallas_call(
        kernel,
        out_shape=[jax.ShapeDtypeStruct(shape, jnp.float32) for shape in shapes],
        in_specs=[pl.BlockSpec(memory_space=inputs)] * len(operands),
        out_specs=[pl.BlockSpec(memory_space=pltpu.VMEM)] * len(shapes),
        scratch_shapes=scratch,
        compiler_params=pltpu.CompilerParams(vmem_limit_bytes=48 * 1024 * 1024),
        cost_estimate=pl.CostEstimate(flops=flops, bytes_accessed=0, transcendentals=0),
    )(*operands)


def swap(array, axis, turn):
    nx, ny = lax.axis_size("gx"), lax.axis_size("gy")
    pairs = []
    for x in range(nx):
        for y in range(ny):
            here, count = (x, nx) if axis == "gx" else (y, ny)
            there = here + 1 if here % 2 == turn else here - 1
            if 0 <= there < count:
                partner = (there, y) if axis == "gx" else (x, there)
            else:
                partner = (x, y ^ 1) if axis == "gx" else (x ^ 1, y)
            pairs.append((x * ny + y, partner[0] * ny + partner[1]))
    return lax.ppermute(array, ("gx", "gy"), pairs)


def everyones(sketch):
    count = lax.axis_size("gx") * lax.axis_size("gy")
    copies = jnp.broadcast_to(sketch[None], (count,) + sketch.shape)
    return lax.all_to_all(copies, ("gx", "gy"), 0, 0)


def body(b, warmth, phase, slots, draw):
    planes, rows, depth = b.shape
    block, wide, table = b.shape, (planes + 2, rows, depth), (8, SKETCH)
    face, line, corner = (3 * rows + 4, depth), (3 * planes + 4, depth), (4, depth)
    cells = pltpu.VMEM((depth // LANES, (planes * rows + 8) * 8, LANES), jnp.float32)
    work = b.size * SKETCH * 6
    b, cond, cap, y_link, z_link, inner, draw, slots, x_first, x_second, y_first, y_second = call(
        first_kernel,
        [block] * 8 + [face, face, line, line],
        *(
            pltpu.with_memory_space_constraint(x, pltpu.HBM)
            for x in (b, warmth, phase, draw, slots)
        ),
        scratch=[
            pltpu.VMEM(block, warmth.dtype),
            pltpu.VMEM(block, phase.dtype),
            pltpu.VMEM(block, slots.dtype),
            pltpu.SemaphoreType.DMA((5,)),
        ],
        inputs=pltpu.HBM,
    )
    got_x = swap(x_second, "gx", 1), swap(x_first, "gx", 0)
    got_y = swap(y_second, "gy", 1), swap(y_first, "gy", 0)
    image_wide, x_link, beside, inside = call(
        inside_kernel,
        [wide, (planes + 1, rows, depth), (4, rows, depth), table],
        b, cond, cap, y_link, z_link, inner, draw, slots, *got_x,
        scratch=[cells],
        flops=work,
    )
    image, twice, sketch, first, second, ends = call(
        third_kernel,
        [block, block, (FIELDS + 1, SKETCH), corner, corner, (24, depth)],
        b, cap, y_link, z_link, draw, slots, y_second, y_first, image_wide, x_link, beside,
        *got_x, *got_y, inside,
        scratch=[cells, pltpu.VMEM((3, 8, depth), jnp.float32)],
        flops=work,
    )
    got_corners = [swap(array, "gy", turn) for turn, array in enumerate((first, second))]
    sketches = everyones(sketch)
    return tuple(
        call(last_kernel, [block, block], sketches, b, image, twice, ends, *got_corners)
    )


def solution(mesh):
    spec = P(("parts", "gx"), "gy", None)
    return jax.shard_map(
        body, mesh=mesh, in_specs=(spec,) * 5, out_specs=(spec,) * 2, check_vma=False
    )
```

```python
import jax
import jax.numpy as jnp
from jax import lax
from jax.experimental import pallas as pl
from jax.experimental.pallas import tpu as pltpu
from jax.sharding import PartitionSpec as P

SKETCH = 128
LOW = 32
HIGH = SKETCH // LOW
FIELDS = 3
GROUP = 4
LANES = 128
epsilon = 1e-06


def traits(warmth, phase):
    powder, solid = phase == 0, phase == 1
    offset = jnp.where(powder, 0.2, jnp.where(solid, 1.0, 0.6))
    return offset * (0.5 + warmth), jnp.where(powder, 1.0, jnp.where(solid, 2.0, 1.5))


def link(first, second):
    total = first + second
    return 2.0 * first * second / jnp.where(total > 0.0, total, 1.0)


def ahead(plane, axis):
    return pltpu.roll(plane, plane.shape[axis] - 1, axis)


def inner_links(cond):
    links = []
    for axis in (0, 1):
        index = lax.broadcasted_iota(jnp.int32, cond.shape, axis)
        links.append(
            jnp.where(index < cond.shape[axis] - 1, link(cond, ahead(cond, axis)), 0.0)
        )
    return links


def inner_flow(field, links):
    total = None
    for axis in (0, 1):
        flow = links[axis] * (field - ahead(field, axis))
        part = flow - pltpu.roll(flow, 1, axis)
        total = part if total is None else total + part
    return total


def apply_inside(images, x_links, links, caps):
    results = []
    flow_low = x_links[0] * (images[0] - images[1])
    for i in range(1, len(images) - 1):
        image = images[i]
        flow = x_links[i] * (image - images[i + 1])
        inside = inner_flow(image, links[i - 1])
        results.append(caps[i - 1] * image + inside + (flow - flow_low))
        flow_low = flow
    return results


def sketch_rows(planes, cells_ref):
    depth = cells_ref.shape[0] * LANES
    low_index = lax.broadcasted_iota(jnp.int32, (LOW, depth), 0)
    low_index = low_index.astype(jnp.float32).astype(jnp.bfloat16)
    high_index = lax.broadcasted_iota(jnp.int32, (HIGH * 8, depth), 0) // 8
    high_index = high_index.astype(jnp.float32).astype(jnp.bfloat16)
    totals = {}
    start = 0
    for fields, draw, slot, chosen in planes:
        rows = draw.shape[0]
        coarse, fine = [], []
        for field in fields:
            weighted = draw * field
            head = weighted.astype(jnp.bfloat16).astype(jnp.float32)
            coarse.append(head)
            fine.append(weighted - head)
        for f, part in enumerate(coarse + coarse[:1] + fine + fine[:1]):
            for t in range(depth // LANES):
                cells_ref[t, pl.ds(start + f, rows, stride=8), :] = part[
                    :, t * LANES : (t + 1) * LANES
                ]
        high = jnp.floor(slot * (1.0 / LOW))
        low = slot - LOW * high
        for first in range(0, len(chosen), GROUP):
            left, right = [], []
            for j in chosen[first : first + GROUP]:
                at = pl.ds(start + j * 8, 8)
                cells = [cells_ref[t, at, :] for t in range(depth // LANES)]
                cells = jnp.concatenate(cells, axis=1)
                cells = jnp.concatenate([cells] * HIGH, axis=0).astype(jnp.bfloat16)
                row_high = jnp.broadcast_to(high[j : j + 1], cells.shape).astype(jnp.bfloat16)
                row_low = jnp.broadcast_to(low[j : j + 1], (LOW, depth)).astype(jnp.bfloat16)
                one = jnp.ones_like(row_low)
                left.append(jnp.where(row_high == high_index, cells, jnp.zeros_like(cells)))
                right.append(jnp.where(row_low == low_index, one, jnp.zeros_like(one)))
            product = lax.dot_general(
                jnp.concatenate(left, axis=0),
                jnp.concatenate(right, axis=0),
                (((1,), (1,)), ((), ())),
                preferred_element_type=jnp.float32,
            )
            totals[len(left)] = totals.get(len(left), 0.0) + product
        start += rows * 8
    total = 0.0
    for count, product in totals.items():
        for k in range(count):
            total = total + product[k * HIGH * 8 :, k * LOW :][: HIGH * 8, :LOW]
    parts = jnp.concatenate([total[h * 8 : h * 8 + 8] for h in range(HIGH)], axis=1)
    return parts + pltpu.roll(parts, 4, 0)


def first_kernel(
    b_hbm, warmth_hbm, phase_hbm, draw_hbm, slot_hbm, b_ref, cond_ref, cap_ref, y_link_ref,
    z_link_ref, inner_ref, draw_ref, slot_ref, x_first_ref, x_second_ref, y_first_ref,
    y_second_ref, warmth_ref, phase_ref, number_ref, arrived,
):
    copies = [
        pltpu.make_async_copy(source, target, arrived.at[k])
        for k, (source, target) in enumerate(
            (
                (b_hbm, b_ref),
                (warmth_hbm, warmth_ref),
                (phase_hbm, phase_ref),
                (draw_hbm, draw_ref),
                (slot_hbm, number_ref),
            )
        )
    ]
    for copy in copies:
        copy.start()
    for copy in copies[:3]:
        copy.wait()
    planes, rows = b_ref.shape[:2]
    images, conds = [], []
    for i in range(planes):
        cond, cap = traits(warmth_ref[i], phase_ref[i])
        cap_ref[i] = cap
        cond_ref[i] = cond
        y_link_ref[i], z_link_ref[i] = links = inner_links(cond)
        field = b_ref[i]
        image = cap * field + inner_flow(field, links)
        if i:
            flow = link(conds[-1], cond) * (b_ref[i - 1] - field)
            images[-1] = images[-1] + flow
            image = image - flow
        conds.append(cond)
        images.append(image)
    for i in range(planes):
        inner_ref[i] = images[i]
    for k, field in enumerate((images, [b_ref[i] for i in range(planes)], conds)):
        at = slice(k * rows, (k + 1) * rows)
        x_first_ref[at], x_second_ref[at] = by_turn(field[0], field[-1], "gx")
        for i, plane in enumerate(field):
            at = slice(k * planes + i, k * planes + i + 1)
            y_first_ref[at], y_second_ref[at] = by_turn(plane[:1], plane[rows - 1 :], "gy")
    for copy in copies[3:]:
        copy.wait()
    for i in range(planes):
        slot_ref[i] = number_ref[i].astype(jnp.float32)
    for k, ref in enumerate((draw_ref, slot_ref)):
        ends = [ref[0], ref[planes - 1]]
        for e, j in enumerate((0, rows - 1)):
            at = slice(3 * rows + 2 * k + e, 3 * rows + 2 * k + e + 1)
            lines = [plane[j : j + 1] for plane in ends]
            x_first_ref[at], x_second_ref[at] = by_turn(*lines, "gx")
        for e, plane in enumerate(ends):
            at = slice(3 * planes + 2 * k + e, 3 * planes + 2 * k + e + 1)
            lines = [plane[:1], plane[rows - 1 :]]
            y_first_ref[at], y_second_ref[at] = by_turn(*lines, "gy")


def by_turn(one, other, axis):
    odd = lax.axis_index(axis) % 2 == 1
    return jnp.where(odd, one, other), jnp.where(odd, other, one)


def has_beside(axis):
    at = lax.axis_index(axis)
    return at > 0, at < lax.axis_size(axis) - 1


def reached(rows):
    others = [j for j in range(rows) if 2 <= j < rows - 2]
    return [j for j in range(rows) if j not in others], others


def inside_kernel(
    b_ref, cond_ref, cap_ref, y_link_ref, z_link_ref, inner_ref, draw_ref, slot_ref,
    got_second_ref, got_first_ref, wide_ref, x_link_ref, beside_ref, sketch_ref, cells_ref,
):
    planes, rows = b_ref.shape[:2]
    (image_low, image_high), (b_low, b_high), (c_low, c_high) = (
        by_turn(*(ref[k * rows : (k + 1) * rows] for ref in (got_first_ref, got_second_ref)), "gx")
        for k in range(3)
    )
    below, above = has_beside("gx")
    c_low, c_high = jnp.where(below, c_low, 0.0), jnp.where(above, c_high, 0.0)
    for k, plane in enumerate((b_low, b_high, c_low, c_high)):
        beside_ref[k] = plane
    conds = [c_low] + [cond_ref[i] for i in range(planes)] + [c_high]
    x_links = [link(conds[i], conds[i + 1]) for i in range(planes + 1)]
    for i, conductance in enumerate(x_links):
        x_link_ref[i] = conductance
    low_flow = x_links[0] * (b_low - b_ref[0])
    high_flow = x_links[-1] * (b_ref[planes - 1] - b_high)
    images = [image_low + low_flow] + [inner_ref[i] for i in range(planes)]
    images.append(image_high - high_flow)
    images[1] = images[1] - low_flow
    images[-2] = images[-2] + high_flow
    for i, image in enumerate(images):
        wide_ref[i] = image
    links = [(y_link_ref[i], z_link_ref[i]) for i in range(planes)]
    twice = apply_inside(images, x_links, links, [cap_ref[i] for i in range(planes)])
    chosen = reached(rows)[1]
    sketch_ref[...] = sketch_rows(
        [
            ((b_ref[i], images[i + 1], twice[i]), draw_ref[i], slot_ref[i], chosen)
            for i in range(planes)
        ],
        cells_ref,
    )


def third_kernel(
    b_ref, cap_ref, y_link_ref, z_link_ref, draw_ref, slot_ref, own_second_ref, own_first_ref,
    wide_ref, x_link_ref, beside_ref, x_second_ref, x_first_ref, y_second_ref, y_first_ref,
    inside_ref, image_ref, twice_ref, sketch_ref, corner_first_ref, corner_second_ref, ends_ref,
    cells_ref, extra_ref,
):
    planes, rows, depth = b_ref.shape
    index = lax.broadcasted_iota(jnp.int32, (rows, depth), 0)
    images = [wide_ref[i] for i in range(planes + 2)]
    x_links = [x_link_ref[i] for i in range(planes + 1)]
    b_beside, c_beside = (beside_ref[0], beside_ref[1]), (beside_ref[2], beside_ref[3])
    x_ends = []
    for end, i in enumerate((0, planes - 1)):
        conductance = x_links[-end]
        x_ends.append((i, conductance, conductance * (b_ref[i] - b_beside[end])))
    x_tails = by_turn(x_first_ref[3 * rows :], x_second_ref[3 * rows :], "gx")
    own_lines = by_turn(own_first_ref[...], own_second_ref[...], "gy")
    y_lines = by_turn(y_first_ref[...], y_second_ref[...], "gy")
    beside = []
    for side, (j, here, own, line) in enumerate(
        zip((0, rows - 1), has_beside("gy"), own_lines, y_lines)
    ):
        row = slice(j, j + 1)
        beyond, b_line, c_line = (line[k * planes : (k + 1) * planes] for k in range(3))
        c_line = jnp.where(here, c_line, 0.0)
        y_link = link(own[2 * planes : 3 * planes], c_line)
        y_flow = y_link * (own[planes : 2 * planes] - b_line)
        beyond = beyond - y_flow
        for i in range(planes):
            at = slice(i, i + 1)
            images[i + 1] = images[i + 1] + jnp.where(index == j, y_flow[at], 0.0)
            beside.append((i, jnp.where(index == j, y_link[at], 0.0), beyond[at]))
        for end, (i, x_link, x_flow) in enumerate(x_ends):
            line_at, at = slice(i, i + 1), 4 * side + 2 * end
            tail = x_tails[end]
            values = -x_link[row] * y_flow[line_at], tail[side:][:1], tail[2 + side :][:1]
            for k, value in enumerate(values):
                extra_ref[k, at : at + 1] = value
            tail = line[3 * planes :]
            values = -y_link[line_at] * x_flow[row], tail[end:][:1], tail[2 + end :][:1]
            for k, value in enumerate(values):
                extra_ref[k, at + 1 : at + 2] = value
            at = 6 * (2 * side + end)
            values = x_link[row], b_beside[end][row], c_beside[end][row]
            values += y_link[line_at], b_line[line_at], c_line[line_at]
            for k, value in enumerate(values):
                ends_ref[at + k : at + k + 1] = value
    links = [(y_link_ref[i], z_link_ref[i]) for i in range(planes)]
    twice = apply_inside(images, x_links, links, [cap_ref[i] for i in range(planes)])
    for i, conductance, value in beside:
        twice[i] = twice[i] + conductance * (images[i + 1] - value)
    for i in range(planes):
        image_ref[i] = images[i + 1]
        twice_ref[i] = twice[i]
    chosen = reached(rows)[0]
    cells = [
        ((b_ref[i], images[i + 1], twice[i]), draw_ref[i], slot_ref[i], chosen)
        for i in range(planes)
    ]
    extra, nothing = [extra_ref[k] for k in range(3)], jnp.zeros((8, depth), jnp.float32)
    cells.append(((nothing, nothing, extra[0]), extra[1], extra[2], range(8)))
    sketch = inside_ref[...] + sketch_rows(cells, cells_ref)
    sketch_ref[...] = sketch[: FIELDS + 1]
    for k, plane in enumerate(b_beside + c_beside):
        at = slice(k, k + 1)
        corner_first_ref[at], corner_second_ref[at] = by_turn(
            plane[:1], plane[rows - 1 :], "gy"
        )


def last_kernel(
    sketch_ref, b_ref, image_ref, twice_ref, ends_ref, corner_first_ref, corner_second_ref,
    solution_ref, residual_ref,
):
    sketches = jnp.sum(sketch_ref[...], axis=0)

    def inner(first, second):
        return jnp.sum(first * second, axis=1, keepdims=True)

    s0, s1, s2 = (sketches[i : i + 1] for i in range(FIELDS))
    beta_inverse = 1.0 / jnp.sqrt(inner(s0, s0) + epsilon)
    h00 = inner(s0, s1) * beta_inverse * beta_inverse
    q0, p0 = s0 * beta_inverse, s1 * beta_inverse
    t0 = p0 - h00 * q0
    p1 = s2 * beta_inverse - h00 * p0
    n0 = jnp.sqrt(inner(t0, t0) + epsilon)
    n0_inverse = 1.0 / n0
    h01 = inner(q0, p1) * n0_inverse
    h11 = inner(t0, p1) * n0_inverse * n0_inverse
    t1 = p1 * n0_inverse - h01 * q0 - h11 * (t0 * n0_inverse)
    n1_square = inner(t1, t1) + epsilon
    first = h00 * h00 + n0 * n0
    cross = h00 * h01 + n0 * h11
    ratio = cross / first
    second = h01 * h01 + h11 * h11 + n1_square - cross * ratio
    y1 = (h01 - ratio * h00) / second
    y0 = h00 / first - ratio * y1
    c1 = y1 * n0_inverse
    c0 = y0 - h00 * c1
    planes, rows, depth = b_ref.shape
    for i in range(planes):
        b, image = b_ref[i], image_ref[i]
        solution_ref[i] = c0 * b + c1 * image
        residual_ref[i] = b - c0 * image - c1 * twice_ref[i]
    corners = by_turn(corner_first_ref[...], corner_second_ref[...], "gy")
    for side, (j, here, corner) in enumerate(zip((0, rows - 1), has_beside("gy"), corners)):
        for end, i in enumerate((0, planes - 1)):
            b, cond = corner[end : end + 1], corner[2 + end : 3 + end]
            cond = jnp.where(here, cond, 0.0)
            at = 6 * (2 * side + end)
            x_link, x_b, x_cond, y_link, y_b, y_cond = (
                ends_ref[at + k : at + k + 1] for k in range(6)
            )
            lacked = x_link * link(x_cond, cond) * (x_b - b)
            lacked = lacked + y_link * link(y_cond, cond) * (y_b - b)
            residual_ref[i, j : j + 1] = residual_ref[i, j : j + 1] + c1 * lacked


def call(kernel, shapes, *operands, scratch=(), inputs=pltpu.VMEM, flops=0):
    return pl.pallas_call(
        kernel,
        out_shape=[jax.ShapeDtypeStruct(shape, jnp.float32) for shape in shapes],
        in_specs=[pl.BlockSpec(memory_space=inputs)] * len(operands),
        out_specs=[pl.BlockSpec(memory_space=pltpu.VMEM)] * len(shapes),
        scratch_shapes=scratch,
        compiler_params=pltpu.CompilerParams(vmem_limit_bytes=48 * 1024 * 1024),
        cost_estimate=pl.CostEstimate(flops=flops, bytes_accessed=0, transcendentals=0),
    )(*operands)


def swap(array, axis, turn):
    nx, ny = lax.axis_size("gx"), lax.axis_size("gy")
    pairs = []
    for x in range(nx):
        for y in range(ny):
            here, count = (x, nx) if axis == "gx" else (y, ny)
            there = here + 1 if here % 2 == turn else here - 1
            if 0 <= there < count:
                partner = (there, y) if axis == "gx" else (x, there)
            else:
                partner = (x, y ^ 1) if axis == "gx" else (x ^ 1, y)
            pairs.append((x * ny + y, partner[0] * ny + partner[1]))
    return lax.ppermute(array, ("gx", "gy"), pairs)


def everyones(sketch):
    count = lax.axis_size("gx") * lax.axis_size("gy")
    copies = jnp.broadcast_to(sketch[None], (count,) + sketch.shape)
    return lax.all_to_all(copies, ("gx", "gy"), 0, 0)


def body(b, warmth, phase, slots, draw):
    planes, rows, depth = b.shape
    block, wide, table = b.shape, (planes + 2, rows, depth), (8, SKETCH)
    face, line, corner = (3 * rows + 4, depth), (3 * planes + 4, depth), (4, depth)
    cells = pltpu.VMEM((depth // LANES, (planes * rows + 8) * 8, LANES), jnp.float32)
    work = b.size * SKETCH * 6
    b, cond, cap, y_link, z_link, inner, draw, slots, x_first, x_second, y_first, y_second = call(
        first_kernel,
        [block] * 8 + [face, face, line, line],
        *(
            pltpu.with_memory_space_constraint(x, pltpu.HBM)
            for x in (b, warmth, phase, draw, slots)
        ),
        scratch=[
            pltpu.VMEM(block, warmth.dtype),
            pltpu.VMEM(block, phase.dtype),
            pltpu.VMEM(block, slots.dtype),
            pltpu.SemaphoreType.DMA((5,)),
        ],
        inputs=pltpu.HBM,
    )
    got_x = swap(x_second, "gx", 1), swap(x_first, "gx", 0)
    got_y = swap(y_second, "gy", 1), swap(y_first, "gy", 0)
    image_wide, x_link, beside, inside = call(
        inside_kernel,
        [wide, (planes + 1, rows, depth), (4, rows, depth), table],
        b, cond, cap, y_link, z_link, inner, draw, slots, *got_x,
        scratch=[cells],
        flops=work,
    )
    image, twice, sketch, first, second, ends = call(
        third_kernel,
        [block, block, (FIELDS + 1, SKETCH), corner, corner, (24, depth)],
        b, cap, y_link, z_link, draw, slots, y_second, y_first, image_wide, x_link, beside,
        *got_x, *got_y, inside,
        scratch=[cells, pltpu.VMEM((3, 8, depth), jnp.float32)],
        flops=work,
    )
    got_corners = [swap(array, "gy", turn) for turn, array in enumerate((first, second))]
    sketches = everyones(sketch)
    return tuple(
        call(last_kernel, [block, block], sketches, b, image, twice, ends, *got_corners)
    )


def solution(mesh):
    spec = P(("parts", "gx"), "gy", None)
    return jax.shard_map(
        body, mesh=mesh, in_specs=(spec,) * 5, out_specs=(spec,) * 2, check_vma=False
    )
```

```python
import jax
import jax.numpy as jnp
from jax import lax
from jax.experimental import pallas as pl
from jax.experimental.pallas import tpu as pltpu
from jax.sharding import PartitionSpec as P

SKETCH = 128
LOW = 32
HIGH = SKETCH // LOW
FIELDS = 3
PAIR = 2
LANES = 128
epsilon = 1e-06


def traits(warmth, phase):
    powder, solid = phase == 0, phase == 1
    offset = jnp.where(powder, 0.2, jnp.where(solid, 1.0, 0.6))
    return offset * (0.5 + warmth), jnp.where(powder, 1.0, jnp.where(solid, 2.0, 1.5))


def link(first, second):
    total = first + second
    return 2.0 * first * second / jnp.where(total > 0.0, total, 1.0)


def ahead(plane, axis):
    return pltpu.roll(plane, plane.shape[axis] - 1, axis)


def inner_links(cond):
    links = []
    for axis in (0, 1):
        index = lax.broadcasted_iota(jnp.int32, cond.shape, axis)
        links.append(
            jnp.where(index < cond.shape[axis] - 1, link(cond, ahead(cond, axis)), 0.0)
        )
    return links


def inner_flow(field, links):
    total = None
    for axis in (0, 1):
        flow = links[axis] * (field - ahead(field, axis))
        part = flow - pltpu.roll(flow, 1, axis)
        total = part if total is None else total + part
    return total


def apply_inside(images, x_links, links, caps):
    results = []
    flow_low = x_links[0] * (images[0] - images[1])
    for i in range(1, len(images) - 1):
        image = images[i]
        flow = x_links[i] * (image - images[i + 1])
        inside = inner_flow(image, links[i - 1])
        results.append(caps[i - 1] * image + inside + (flow - flow_low))
        flow_low = flow
    return results


def parts_of(slot):
    high = jnp.floor(slot * (1.0 / LOW))
    return slot - LOW * high, high


def one_hot(values, j, count, each):
    shape = (count * each, values.shape[1])
    index = lax.broadcasted_iota(jnp.int32, shape, 0) // each
    index = index.astype(jnp.float32).astype(jnp.bfloat16)
    row = jnp.broadcast_to(values[j : j + 1], shape).astype(jnp.bfloat16)
    one = jnp.ones_like(row)
    return jnp.where(row == index, one, jnp.zeros_like(one))


def put_cells(fields, draw, start, cells_ref):
    coarse, fine = [], []
    for field in fields:
        weighted = draw * field
        head = weighted.astype(jnp.bfloat16).astype(jnp.float32)
        coarse.append(head)
        fine.append(weighted - head)
    for f, part in enumerate((coarse + fine) * 2):
        for t in range(cells_ref.shape[0]):
            cells_ref[t, pl.ds(start + f, draw.shape[0], stride=8), :] = part[
                :, t * LANES : (t + 1) * LANES
            ]


def masked_cells(mask, start, j, cells_ref):
    at = pl.ds(start + j * 8, 8)
    cells = jnp.concatenate([cells_ref[t, at, :] for t in range(cells_ref.shape[0])], axis=1)
    return jnp.concatenate([cells, cells], axis=0).astype(jnp.bfloat16) * mask


def product(left, right):
    return lax.dot_general(
        jnp.concatenate(left, axis=1),
        jnp.concatenate(right, axis=1),
        (((1,), (1,)), ((), ())),
        preferred_element_type=jnp.float32,
    )


def as_sketch(total):
    each = 2 * PAIR
    total = jnp.concatenate([total[h * each : (h + 1) * each] for h in range(HIGH)], axis=1)
    return total[:PAIR] + total[PAIR:]


def sketch_rows(planes, low_ref, high_ref, cells_ref):
    total = 0.0
    each = HIGH * 2 * PAIR
    for i, (fields, draw, chosen) in enumerate(planes):
        rows = draw.shape[0]
        start = i * rows * 8
        put_cells(fields, draw, start, cells_ref)
        left, right = [], []
        for j in chosen:
            at = i * rows + j
            mask = high_ref[at * each : (at + 1) * each]
            left.append(masked_cells(mask, start, j, cells_ref))
            right.append(low_ref[at * LOW : (at + 1) * LOW])
        total = total + product(left, right)
    return total


def slot_kernel(b_ref, draw_ref, slot_ref, low_ref, high_ref, sketch_ref, cells_ref):
    planes, rows = b_ref.shape[:2]
    each = HIGH * 2 * PAIR
    total = 0.0
    for i in range(planes):
        start = i * rows * 8
        put_cells((b_ref[i],) * PAIR, draw_ref[i], start, cells_ref)
        low, high = parts_of(slot_ref[i])
        left, right = [], []
        for j in range(rows):
            at = i * rows + j
            mask, hot = one_hot(high, j, HIGH, 2 * PAIR), one_hot(low, j, LOW, 1)
            high_ref[at * each : (at + 1) * each] = mask
            low_ref[at * LOW : (at + 1) * LOW] = hot
            left.append(masked_cells(mask, start, j, cells_ref))
            right.append(hot)
        total = total + product(left, right)
    sketch_ref[...] = as_sketch(total)


def first_kernel(
    b_hbm, warmth_hbm, phase_hbm, draw_hbm, slot_hbm, b_ref, cond_ref, cap_ref, y_link_ref,
    z_link_ref, inner_ref, draw_ref, slot_ref, x_first_ref, x_second_ref, y_first_ref,
    y_second_ref, warmth_ref, phase_ref, number_ref, arrived,
):
    copies = [
        pltpu.make_async_copy(source, target, arrived.at[k])
        for k, (source, target) in enumerate(
            (
                (b_hbm, b_ref),
                (warmth_hbm, warmth_ref),
                (phase_hbm, phase_ref),
                (draw_hbm, draw_ref),
                (slot_hbm, number_ref),
            )
        )
    ]
    for copy in copies:
        copy.start()
    for copy in copies[:3]:
        copy.wait()
    planes, rows = b_ref.shape[:2]
    images, conds = [], []
    for i in range(planes):
        cond, cap = traits(warmth_ref[i], phase_ref[i])
        cap_ref[i] = cap
        cond_ref[i] = cond
        y_link_ref[i], z_link_ref[i] = links = inner_links(cond)
        field = b_ref[i]
        image = cap * field + inner_flow(field, links)
        if i:
            flow = link(conds[-1], cond) * (b_ref[i - 1] - field)
            images[-1] = images[-1] + flow
            image = image - flow
        conds.append(cond)
        images.append(image)
    for i in range(planes):
        inner_ref[i] = images[i]
    for k, field in enumerate((images, [b_ref[i] for i in range(planes)], conds)):
        at = slice(k * rows, (k + 1) * rows)
        x_first_ref[at], x_second_ref[at] = by_turn(field[0], field[-1], "gx")
        for i, plane in enumerate(field):
            at = slice(k * planes + i, k * planes + i + 1)
            y_first_ref[at], y_second_ref[at] = by_turn(plane[:1], plane[rows - 1 :], "gy")
    for copy in copies[3:]:
        copy.wait()
    for i in range(planes):
        slot_ref[i] = number_ref[i].astype(jnp.float32)
    for k, ref in enumerate((draw_ref, slot_ref)):
        ends = [ref[0], ref[planes - 1]]
        for e, j in enumerate((0, rows - 1)):
            at = slice(3 * rows + 2 * k + e, 3 * rows + 2 * k + e + 1)
            lines = [plane[j : j + 1] for plane in ends]
            x_first_ref[at], x_second_ref[at] = by_turn(*lines, "gx")
        for e, plane in enumerate(ends):
            at = slice(3 * planes + 2 * k + e, 3 * planes + 2 * k + e + 1)
            lines = [plane[:1], plane[rows - 1 :]]
            y_first_ref[at], y_second_ref[at] = by_turn(*lines, "gy")


def by_turn(one, other, axis):
    odd = lax.axis_index(axis) % 2 == 1
    return jnp.where(odd, one, other), jnp.where(odd, other, one)


def has_beside(axis):
    at = lax.axis_index(axis)
    return at > 0, at < lax.axis_size(axis) - 1


def reached(rows):
    others = [j for j in range(rows) if 2 <= j < rows - 2]
    return [j for j in range(rows) if j not in others], others


def inside_kernel(
    b_ref, cond_ref, cap_ref, y_link_ref, z_link_ref, inner_ref, draw_ref, low_ref, high_ref,
    got_second_ref, got_first_ref, wide_ref, x_link_ref, beside_ref, sketch_ref, cells_ref,
):
    planes, rows = b_ref.shape[:2]
    (image_low, image_high), (b_low, b_high), (c_low, c_high) = (
        by_turn(*(ref[k * rows : (k + 1) * rows] for ref in (got_first_ref, got_second_ref)), "gx")
        for k in range(3)
    )
    below, above = has_beside("gx")
    c_low, c_high = jnp.where(below, c_low, 0.0), jnp.where(above, c_high, 0.0)
    for k, plane in enumerate((b_low, b_high, c_low, c_high)):
        beside_ref[k] = plane
    conds = [c_low] + [cond_ref[i] for i in range(planes)] + [c_high]
    x_links = [link(conds[i], conds[i + 1]) for i in range(planes + 1)]
    for i, conductance in enumerate(x_links):
        x_link_ref[i] = conductance
    low_flow = x_links[0] * (b_low - b_ref[0])
    high_flow = x_links[-1] * (b_ref[planes - 1] - b_high)
    images = [image_low + low_flow] + [inner_ref[i] for i in range(planes)]
    images.append(image_high - high_flow)
    images[1] = images[1] - low_flow
    images[-2] = images[-2] + high_flow
    for i, image in enumerate(images):
        wide_ref[i] = image
    links = [(y_link_ref[i], z_link_ref[i]) for i in range(planes)]
    twice = apply_inside(images, x_links, links, [cap_ref[i] for i in range(planes)])
    chosen = reached(rows)[1]
    cells = [((images[i + 1], twice[i]), draw_ref[i], chosen) for i in range(planes)]
    sketch_ref[...] = sketch_rows(cells, low_ref, high_ref, cells_ref)


def third_kernel(
    b_ref, cap_ref, y_link_ref, z_link_ref, draw_ref, low_ref, high_ref, own_second_ref,
    own_first_ref, wide_ref, x_link_ref, beside_ref, x_second_ref, x_first_ref, y_second_ref,
    y_first_ref, b_sketch_ref, inside_ref, image_ref, twice_ref, sketch_ref, corner_first_ref,
    corner_second_ref, ends_ref, cells_ref, extra_ref,
):
    planes, rows, depth = b_ref.shape
    index = lax.broadcasted_iota(jnp.int32, (rows, depth), 0)
    images = [wide_ref[i] for i in range(planes + 2)]
    x_links = [x_link_ref[i] for i in range(planes + 1)]
    b_beside, c_beside = (beside_ref[0], beside_ref[1]), (beside_ref[2], beside_ref[3])
    x_ends = []
    for end, i in enumerate((0, planes - 1)):
        conductance = x_links[-end]
        x_ends.append((i, conductance, conductance * (b_ref[i] - b_beside[end])))
    x_tails = by_turn(x_first_ref[3 * rows :], x_second_ref[3 * rows :], "gx")
    own_lines = by_turn(own_first_ref[...], own_second_ref[...], "gy")
    y_lines = by_turn(y_first_ref[...], y_second_ref[...], "gy")
    beside = []
    for side, (j, here, own, line) in enumerate(
        zip((0, rows - 1), has_beside("gy"), own_lines, y_lines)
    ):
        row = slice(j, j + 1)
        beyond, b_line, c_line = (line[k * planes : (k + 1) * planes] for k in range(3))
        c_line = jnp.where(here, c_line, 0.0)
        y_link = link(own[2 * planes : 3 * planes], c_line)
        y_flow = y_link * (own[planes : 2 * planes] - b_line)
        beyond = beyond - y_flow
        for i in range(planes):
            at = slice(i, i + 1)
            images[i + 1] = images[i + 1] + jnp.where(index == j, y_flow[at], 0.0)
            beside.append((i, jnp.where(index == j, y_link[at], 0.0), beyond[at]))
        for end, (i, x_link, x_flow) in enumerate(x_ends):
            line_at, at = slice(i, i + 1), 4 * side + 2 * end
            tail = x_tails[end]
            values = -x_link[row] * y_flow[line_at], tail[side:][:1], tail[2 + side :][:1]
            for k, value in enumerate(values):
                extra_ref[k, at : at + 1] = value
            tail = line[3 * planes :]
            values = -y_link[line_at] * x_flow[row], tail[end:][:1], tail[2 + end :][:1]
            for k, value in enumerate(values):
                extra_ref[k, at + 1 : at + 2] = value
            at = 6 * (2 * side + end)
            values = x_link[row], b_beside[end][row], c_beside[end][row]
            values += y_link[line_at], b_line[line_at], c_line[line_at]
            for k, value in enumerate(values):
                ends_ref[at + k : at + k + 1] = value
    links = [(y_link_ref[i], z_link_ref[i]) for i in range(planes)]
    twice = apply_inside(images, x_links, links, [cap_ref[i] for i in range(planes)])
    for i, conductance, value in beside:
        twice[i] = twice[i] + conductance * (images[i + 1] - value)
    for i in range(planes):
        image_ref[i] = images[i + 1]
        twice_ref[i] = twice[i]
    chosen = reached(rows)[0]
    cells = [((images[i + 1], twice[i]), draw_ref[i], chosen) for i in range(planes)]
    total = inside_ref[...] + sketch_rows(cells, low_ref, high_ref, cells_ref)
    start = planes * rows * 8
    put_cells((jnp.zeros((8, depth), jnp.float32), extra_ref[0]), extra_ref[1], start, cells_ref)
    low, high = parts_of(extra_ref[2])
    left, right = [], []
    for j in range(8):
        mask = one_hot(high, j, HIGH, 2 * PAIR)
        left.append(masked_cells(mask, start, j, cells_ref))
        right.append(one_hot(low, j, LOW, 1))
    sketch_ref[1 : 1 + PAIR] = as_sketch(total + product(left, right))
    sketch_ref[:1] = b_sketch_ref[:1]
    sketch_ref[1 + PAIR :] = b_sketch_ref[:1]
    for k, plane in enumerate(b_beside + c_beside):
        at = slice(k, k + 1)
        corner_first_ref[at], corner_second_ref[at] = by_turn(
            plane[:1], plane[rows - 1 :], "gy"
        )


def last_kernel(
    sketch_ref, b_ref, image_ref, twice_ref, ends_ref, corner_first_ref, corner_second_ref,
    solution_ref, residual_ref,
):
    sketches = jnp.sum(sketch_ref[...], axis=0)

    def inner(first, second):
        return jnp.sum(first * second, axis=1, keepdims=True)

    s0, s1, s2 = (sketches[i : i + 1] for i in range(FIELDS))
    beta_inverse = 1.0 / jnp.sqrt(inner(s0, s0) + epsilon)
    h00 = inner(s0, s1) * beta_inverse * beta_inverse
    q0, p0 = s0 * beta_inverse, s1 * beta_inverse
    t0 = p0 - h00 * q0
    p1 = s2 * beta_inverse - h00 * p0
    n0 = jnp.sqrt(inner(t0, t0) + epsilon)
    n0_inverse = 1.0 / n0
    h01 = inner(q0, p1) * n0_inverse
    h11 = inner(t0, p1) * n0_inverse * n0_inverse
    t1 = p1 * n0_inverse - h01 * q0 - h11 * (t0 * n0_inverse)
    n1_square = inner(t1, t1) + epsilon
    first = h00 * h00 + n0 * n0
    cross = h00 * h01 + n0 * h11
    ratio = cross / first
    second = h01 * h01 + h11 * h11 + n1_square - cross * ratio
    y1 = (h01 - ratio * h00) / second
    y0 = h00 / first - ratio * y1
    c1 = y1 * n0_inverse
    c0 = y0 - h00 * c1
    planes, rows, depth = b_ref.shape
    for i in range(planes):
        b, image = b_ref[i], image_ref[i]
        solution_ref[i] = c0 * b + c1 * image
        residual_ref[i] = b - c0 * image - c1 * twice_ref[i]
    corners = by_turn(corner_first_ref[...], corner_second_ref[...], "gy")
    for side, (j, here, corner) in enumerate(zip((0, rows - 1), has_beside("gy"), corners)):
        for end, i in enumerate((0, planes - 1)):
            b, cond = corner[end : end + 1], corner[2 + end : 3 + end]
            cond = jnp.where(here, cond, 0.0)
            at = 6 * (2 * side + end)
            x_link, x_b, x_cond, y_link, y_b, y_cond = (
                ends_ref[at + k : at + k + 1] for k in range(6)
            )
            lacked = x_link * link(x_cond, cond) * (x_b - b)
            lacked = lacked + y_link * link(y_cond, cond) * (y_b - b)
            residual_ref[i, j : j + 1] = residual_ref[i, j : j + 1] + c1 * lacked


def call(kernel, shapes, *operands, scratch=(), inputs=pltpu.VMEM, flops=0):
    return pl.pallas_call(
        kernel,
        out_shape=[
            shape if hasattr(shape, "dtype") else jax.ShapeDtypeStruct(shape, jnp.float32)
            for shape in shapes
        ],
        in_specs=[pl.BlockSpec(memory_space=inputs)] * len(operands),
        out_specs=[pl.BlockSpec(memory_space=pltpu.VMEM)] * len(shapes),
        scratch_shapes=scratch,
        compiler_params=pltpu.CompilerParams(vmem_limit_bytes=48 * 1024 * 1024),
        cost_estimate=pl.CostEstimate(flops=flops, bytes_accessed=0, transcendentals=0),
    )(*operands)


def swap(array, axis, turn):
    nx, ny = lax.axis_size("gx"), lax.axis_size("gy")
    pairs = []
    for x in range(nx):
        for y in range(ny):
            here, count = (x, nx) if axis == "gx" else (y, ny)
            there = here + 1 if here % 2 == turn else here - 1
            if 0 <= there < count:
                partner = (there, y) if axis == "gx" else (x, there)
            else:
                partner = (x, y ^ 1) if axis == "gx" else (x ^ 1, y)
            pairs.append((x * ny + y, partner[0] * ny + partner[1]))
    return lax.ppermute(array, ("gx", "gy"), pairs)


def everyones(sketch):
    count = lax.axis_size("gx") * lax.axis_size("gy")
    copies = jnp.broadcast_to(sketch[None], (count,) + sketch.shape)
    return lax.all_to_all(copies, ("gx", "gy"), 0, 0)


def body(b, warmth, phase, slots, draw):
    planes, rows, depth = b.shape
    block, wide = b.shape, (planes + 2, rows, depth)
    face, line, corner = (3 * rows + 4, depth), (3 * planes + 4, depth), (4, depth)
    cells = pltpu.VMEM((depth // LANES, (planes * rows + 8) * 8, LANES), jnp.float32)
    total = HIGH * 2 * PAIR, LOW
    hots = [
        jax.ShapeDtypeStruct((planes * rows * count, depth), jnp.bfloat16)
        for count in (LOW, HIGH * 2 * PAIR)
    ]
    work = b.size * SKETCH * 6
    b, cond, cap, y_link, z_link, inner, draw, slots, x_first, x_second, y_first, y_second = call(
        first_kernel,
        [block] * 8 + [face, face, line, line],
        *(
            pltpu.with_memory_space_constraint(x, pltpu.HBM)
            for x in (b, warmth, phase, draw, slots)
        ),
        scratch=[
            pltpu.VMEM(block, warmth.dtype),
            pltpu.VMEM(block, phase.dtype),
            pltpu.VMEM(block, slots.dtype),
            pltpu.SemaphoreType.DMA((5,)),
        ],
        inputs=pltpu.HBM,
    )
    got_x = swap(x_second, "gx", 1), swap(x_first, "gx", 0)
    got_y = swap(y_second, "gy", 1), swap(y_first, "gy", 0)
    *hots, b_sketch = call(
        slot_kernel, [*hots, (PAIR, SKETCH)], b, draw, slots, scratch=[cells], flops=work
    )
    image_wide, x_link, beside, inside = call(
        inside_kernel,
        [wide, (planes + 1, rows, depth), (4, rows, depth), total],
        b, cond, cap, y_link, z_link, inner, draw, *hots, *got_x,
        scratch=[cells],
        flops=work,
    )
    image, twice, sketch, first, second, ends = call(
        third_kernel,
        [block, block, (FIELDS + 1, SKETCH), corner, corner, (24, depth)],
        b, cap, y_link, z_link, draw, *hots, y_second, y_first, image_wide, x_link, beside,
        *got_x, *got_y, b_sketch, inside,
        scratch=[cells, pltpu.VMEM((3, 8, depth), jnp.float32)],
        flops=work,
    )
    got_corners = [swap(array, "gy", turn) for turn, array in enumerate((first, second))]
    sketches = everyones(sketch)
    return tuple(
        call(last_kernel, [block, block], sketches, b, image, twice, ends, *got_corners)
    )


def solution(mesh):
    spec = P(("parts", "gx"), "gy", None)
    return jax.shard_map(
        body, mesh=mesh, in_specs=(spec,) * 5, out_specs=(spec,) * 2, check_vma=False
    )
```

```python
import jax
import jax.numpy as jnp
from jax import lax
from jax.experimental import pallas as pl
from jax.experimental.pallas import tpu as pltpu
from jax.sharding import PartitionSpec as P

SKETCH = 128
LOW = 32
HIGH = SKETCH // LOW
FIELDS = 3
PAIR = 2
LANES = 128
epsilon = 1e-06


def traits(warmth, phase):
    powder, solid = phase == 0, phase == 1
    offset = jnp.where(powder, 0.2, jnp.where(solid, 1.0, 0.6))
    return offset * (0.5 + warmth), jnp.where(powder, 1.0, jnp.where(solid, 2.0, 1.5))


def link(first, second):
    total = first + second
    return 2.0 * first * second / jnp.where(total > 0.0, total, 1.0)


def ahead(plane, axis):
    return pltpu.roll(plane, plane.shape[axis] - 1, axis)


def inner_links(cond):
    links = []
    for axis in (0, 1):
        index = lax.broadcasted_iota(jnp.int32, cond.shape, axis)
        links.append(
            jnp.where(index < cond.shape[axis] - 1, link(cond, ahead(cond, axis)), 0.0)
        )
    return links


def inner_flow(field, links):
    total = None
    for axis in (0, 1):
        flow = links[axis] * (field - ahead(field, axis))
        part = flow - pltpu.roll(flow, 1, axis)
        total = part if total is None else total + part
    return total


def apply_inside(images, x_links, links, caps):
    results = []
    flow_low = x_links[0] * (images[0] - images[1])
    for i in range(1, len(images) - 1):
        image = images[i]
        flow = x_links[i] * (image - images[i + 1])
        inside = inner_flow(image, links[i - 1])
        results.append(caps[i - 1] * image + inside + (flow - flow_low))
        flow_low = flow
    return results


def parts_of(slot):
    high = jnp.floor(slot * (1.0 / LOW))
    return slot - LOW * high, high


def one_hot(values, j, count, each):
    shape = (count * each, values.shape[1])
    index = lax.broadcasted_iota(jnp.int32, shape, 0) // each
    index = index.astype(jnp.float32).astype(jnp.bfloat16)
    row = jnp.broadcast_to(values[j : j + 1], shape).astype(jnp.bfloat16)
    one = jnp.ones_like(row)
    return jnp.where(row == index, one, jnp.zeros_like(one))


def put_cells(fields, draw, start, cells_ref):
    coarse, fine = [], []
    for field in fields:
        weighted = draw * field
        head = weighted.astype(jnp.bfloat16).astype(jnp.float32)
        coarse.append(head)
        fine.append(weighted - head)
    for f, part in enumerate((coarse + fine) * 2):
        for t in range(cells_ref.shape[0]):
            cells_ref[t, pl.ds(start + f, draw.shape[0], stride=8), :] = part[
                :, t * LANES : (t + 1) * LANES
            ]


def masked_cells(mask, start, j, cells_ref):
    at = pl.ds(start + j * 8, 8)
    cells = jnp.concatenate([cells_ref[t, at, :] for t in range(cells_ref.shape[0])], axis=1)
    return jnp.concatenate([cells, cells], axis=0).astype(jnp.bfloat16) * mask


def product(left, right):
    return lax.dot_general(
        jnp.concatenate(left, axis=1),
        jnp.concatenate(right, axis=1),
        (((1,), (1,)), ((), ())),
        preferred_element_type=jnp.float32,
    )


def as_sketch(total):
    each = 2 * PAIR
    total = jnp.concatenate([total[h * each : (h + 1) * each] for h in range(HIGH)], axis=1)
    return total[:PAIR] + total[PAIR:]


def sketch_rows(planes, low_ref, high_ref, cells_ref):
    total = 0.0
    each = HIGH * 2 * PAIR
    for i, (fields, draw, chosen) in enumerate(planes):
        rows = draw.shape[0]
        start = i * rows * 8
        put_cells(fields, draw, start, cells_ref)
        left, right = [], []
        for j in chosen:
            at = i * rows + j
            mask = high_ref[at * each : (at + 1) * each]
            left.append(masked_cells(mask, start, j, cells_ref))
            right.append(low_ref[at * LOW : (at + 1) * LOW])
        total = total + product(left, right)
    return total


def slot_kernel(b_ref, draw_ref, slot_ref, low_ref, high_ref, sketch_ref, cells_ref):
    planes, rows = b_ref.shape[:2]
    each = HIGH * 2 * PAIR
    total = 0.0
    for i in range(planes):
        start = i * rows * 8
        put_cells((b_ref[i],) * PAIR, draw_ref[i], start, cells_ref)
        low, high = parts_of(slot_ref[i])
        left, right = [], []
        for j in range(rows):
            at = i * rows + j
            mask, hot = one_hot(high, j, HIGH, 2 * PAIR), one_hot(low, j, LOW, 1)
            high_ref[at * each : (at + 1) * each] = mask
            low_ref[at * LOW : (at + 1) * LOW] = hot
            left.append(masked_cells(mask, start, j, cells_ref))
            right.append(hot)
        total = total + product(left, right)
    sketch_ref[...] = as_sketch(total)


def first_kernel(
    b_hbm, warmth_hbm, phase_hbm, draw_hbm, slot_hbm, b_ref, cond_ref, cap_ref, y_link_ref,
    z_link_ref, inner_ref, draw_ref, slot_ref, x_first_ref, x_second_ref, y_first_ref,
    y_second_ref, warmth_ref, phase_ref, number_ref, arrived,
):
    copies = [
        pltpu.make_async_copy(source, target, arrived.at[k])
        for k, (source, target) in enumerate(
            (
                (b_hbm, b_ref),
                (warmth_hbm, warmth_ref),
                (phase_hbm, phase_ref),
                (draw_hbm, draw_ref),
                (slot_hbm, number_ref),
            )
        )
    ]
    for copy in copies:
        copy.start()
    for copy in copies[:3]:
        copy.wait()
    planes, rows = b_ref.shape[:2]
    images, conds = [], []
    for i in range(planes):
        cond, cap = traits(warmth_ref[i], phase_ref[i])
        cap_ref[i] = cap
        cond_ref[i] = cond
        y_link_ref[i], z_link_ref[i] = links = inner_links(cond)
        field = b_ref[i]
        image = cap * field + inner_flow(field, links)
        if i:
            flow = link(conds[-1], cond) * (b_ref[i - 1] - field)
            images[-1] = images[-1] + flow
            image = image - flow
        conds.append(cond)
        images.append(image)
    for i in range(planes):
        inner_ref[i] = images[i]
    for k, field in enumerate((images, [b_ref[i] for i in range(planes)], conds)):
        at = slice(k * rows, (k + 1) * rows)
        x_first_ref[at], x_second_ref[at] = by_turn(field[0], field[-1], "gx")
        for i, plane in enumerate(field):
            at = slice(k * planes + i, k * planes + i + 1)
            y_first_ref[at], y_second_ref[at] = by_turn(plane[:1], plane[rows - 1 :], "gy")
    for copy in copies[3:]:
        copy.wait()
    for i in range(planes):
        slot_ref[i] = number_ref[i].astype(jnp.float32)
    for k, ref in enumerate((draw_ref, slot_ref)):
        ends = [ref[0], ref[planes - 1]]
        for e, j in enumerate((0, rows - 1)):
            at = slice(3 * rows + 2 * k + e, 3 * rows + 2 * k + e + 1)
            lines = [plane[j : j + 1] for plane in ends]
            x_first_ref[at], x_second_ref[at] = by_turn(*lines, "gx")
        for e, plane in enumerate(ends):
            at = slice(3 * planes + 2 * k + e, 3 * planes + 2 * k + e + 1)
            lines = [plane[:1], plane[rows - 1 :]]
            y_first_ref[at], y_second_ref[at] = by_turn(*lines, "gy")


def by_turn(one, other, axis):
    odd = lax.axis_index(axis) % 2 == 1
    return jnp.where(odd, one, other), jnp.where(odd, other, one)


def has_beside(axis):
    at = lax.axis_index(axis)
    return at > 0, at < lax.axis_size(axis) - 1


def reached(rows):
    others = [j for j in range(rows) if 2 <= j < rows - 2]
    return [j for j in range(rows) if j not in others], others


def inside_kernel(
    b_ref, cond_ref, cap_ref, y_link_ref, z_link_ref, inner_ref, draw_ref, low_ref, high_ref,
    got_second_ref, got_first_ref, wide_ref, x_link_ref, beside_ref, sketch_ref, cells_ref,
):
    planes, rows = b_ref.shape[:2]
    (image_low, image_high), (b_low, b_high), (c_low, c_high) = (
        by_turn(*(ref[k * rows : (k + 1) * rows] for ref in (got_first_ref, got_second_ref)), "gx")
        for k in range(3)
    )
    below, above = has_beside("gx")
    c_low, c_high = jnp.where(below, c_low, 0.0), jnp.where(above, c_high, 0.0)
    for k, plane in enumerate((b_low, b_high, c_low, c_high)):
        beside_ref[k] = plane
    conds = [c_low] + [cond_ref[i] for i in range(planes)] + [c_high]
    x_links = [link(conds[i], conds[i + 1]) for i in range(planes + 1)]
    for i, conductance in enumerate(x_links):
        x_link_ref[i] = conductance
    low_flow = x_links[0] * (b_low - b_ref[0])
    high_flow = x_links[-1] * (b_ref[planes - 1] - b_high)
    images = [image_low + low_flow] + [inner_ref[i] for i in range(planes)]
    images.append(image_high - high_flow)
    images[1] = images[1] - low_flow
    images[-2] = images[-2] + high_flow
    for i, image in enumerate(images):
        wide_ref[i] = image
    links = [(y_link_ref[i], z_link_ref[i]) for i in range(planes)]
    twice = apply_inside(images, x_links, links, [cap_ref[i] for i in range(planes)])
    chosen = reached(rows)[1]
    cells = [((images[i + 1], twice[i]), draw_ref[i], chosen) for i in range(planes)]
    sketch_ref[...] = sketch_rows(cells, low_ref, high_ref, cells_ref)


def third_kernel(
    b_ref, cap_ref, y_link_ref, z_link_ref, draw_ref, low_ref, high_ref, own_second_ref,
    own_first_ref, wide_ref, x_link_ref, beside_ref, x_second_ref, x_first_ref, y_second_ref,
    y_first_ref, b_sketch_ref, inside_ref, image_ref, twice_ref, sketch_ref, corner_first_ref,
    corner_second_ref, ends_ref, cells_ref, extra_ref,
):
    planes, rows, depth = b_ref.shape
    index = lax.broadcasted_iota(jnp.int32, (rows, depth), 0)
    images = [wide_ref[i] for i in range(planes + 2)]
    x_links = [x_link_ref[i] for i in range(planes + 1)]
    b_beside, c_beside = (beside_ref[0], beside_ref[1]), (beside_ref[2], beside_ref[3])
    x_ends = []
    for end, i in enumerate((0, planes - 1)):
        conductance = x_links[-end]
        x_ends.append((i, conductance, conductance * (b_ref[i] - b_beside[end])))
    x_tails = by_turn(x_first_ref[3 * rows :], x_second_ref[3 * rows :], "gx")
    own_lines = by_turn(own_first_ref[...], own_second_ref[...], "gy")
    y_lines = by_turn(y_first_ref[...], y_second_ref[...], "gy")
    beside = []
    for side, (j, here, own, line) in enumerate(
        zip((0, rows - 1), has_beside("gy"), own_lines, y_lines)
    ):
        row = slice(j, j + 1)
        beyond, b_line, c_line = (line[k * planes : (k + 1) * planes] for k in range(3))
        c_line = jnp.where(here, c_line, 0.0)
        y_link = link(own[2 * planes : 3 * planes], c_line)
        y_flow = y_link * (own[planes : 2 * planes] - b_line)
        beyond = beyond - y_flow
        for i in range(planes):
            at = slice(i, i + 1)
            images[i + 1] = images[i + 1] + jnp.where(index == j, y_flow[at], 0.0)
            beside.append((i, jnp.where(index == j, y_link[at], 0.0), beyond[at]))
        for end, (i, x_link, x_flow) in enumerate(x_ends):
            line_at, at = slice(i, i + 1), 4 * side + 2 * end
            tail = x_tails[end]
            values = -x_link[row] * y_flow[line_at], tail[side:][:1], tail[2 + side :][:1]
            for k, value in enumerate(values):
                extra_ref[k, at : at + 1] = value
            tail = line[3 * planes :]
            values = -y_link[line_at] * x_flow[row], tail[end:][:1], tail[2 + end :][:1]
            for k, value in enumerate(values):
                extra_ref[k, at + 1 : at + 2] = value
            at = 6 * (2 * side + end)
            values = x_link[row], b_beside[end][row], c_beside[end][row]
            values += y_link[line_at], b_line[line_at], c_line[line_at]
            for k, value in enumerate(values):
                ends_ref[at + k : at + k + 1] = value
    links = [(y_link_ref[i], z_link_ref[i]) for i in range(planes)]
    twice = apply_inside(images, x_links, links, [cap_ref[i] for i in range(planes)])
    for i, conductance, value in beside:
        twice[i] = twice[i] + conductance * (images[i + 1] - value)
    for i in range(planes):
        image_ref[i] = images[i + 1]
        twice_ref[i] = twice[i]
    chosen = reached(rows)[0]
    cells = [((images[i + 1], twice[i]), draw_ref[i], chosen) for i in range(planes)]
    total = inside_ref[...] + sketch_rows(cells, low_ref, high_ref, cells_ref)
    start = planes * rows * 8
    put_cells((jnp.zeros((8, depth), jnp.float32), extra_ref[0]), extra_ref[1], start, cells_ref)
    low, high = parts_of(extra_ref[2])
    left, right = [], []
    for j in range(8):
        mask = one_hot(high, j, HIGH, 2 * PAIR)
        left.append(masked_cells(mask, start, j, cells_ref))
        right.append(one_hot(low, j, LOW, 1))
    sketch_ref[1 : 1 + PAIR] = as_sketch(total + product(left, right))
    sketch_ref[:1] = b_sketch_ref[:1]
    sketch_ref[1 + PAIR :] = b_sketch_ref[:1]
    for k, plane in enumerate(b_beside + c_beside):
        at = slice(k, k + 1)
        corner_first_ref[at], corner_second_ref[at] = by_turn(
            plane[:1], plane[rows - 1 :], "gy"
        )


def last_kernel(
    sketch_ref, b_ref, image_ref, twice_ref, ends_ref, corner_first_ref, corner_second_ref,
    solution_ref, residual_ref,
):
    sketches = jnp.sum(sketch_ref[...], axis=0)

    def inner(first, second):
        return jnp.sum(first * second, axis=1, keepdims=True)

    s0, s1, s2 = (sketches[i : i + 1] for i in range(FIELDS))
    beta_inverse = 1.0 / jnp.sqrt(inner(s0, s0) + epsilon)
    h00 = inner(s0, s1) * beta_inverse * beta_inverse
    q0, p0 = s0 * beta_inverse, s1 * beta_inverse
    t0 = p0 - h00 * q0
    p1 = s2 * beta_inverse - h00 * p0
    n0 = jnp.sqrt(inner(t0, t0) + epsilon)
    n0_inverse = 1.0 / n0
    h01 = inner(q0, p1) * n0_inverse
    h11 = inner(t0, p1) * n0_inverse * n0_inverse
    t1 = p1 * n0_inverse - h01 * q0 - h11 * (t0 * n0_inverse)
    n1_square = inner(t1, t1) + epsilon
    first = h00 * h00 + n0 * n0
    cross = h00 * h01 + n0 * h11
    ratio = cross / first
    second = h01 * h01 + h11 * h11 + n1_square - cross * ratio
    y1 = (h01 - ratio * h00) / second
    y0 = h00 / first - ratio * y1
    c1 = y1 * n0_inverse
    c0 = y0 - h00 * c1
    planes, rows, depth = b_ref.shape
    for i in range(planes):
        b, image = b_ref[i], image_ref[i]
        solution_ref[i] = c0 * b + c1 * image
        residual_ref[i] = b - c0 * image - c1 * twice_ref[i]
    corners = by_turn(corner_first_ref[...], corner_second_ref[...], "gy")
    for side, (j, here, corner) in enumerate(zip((0, rows - 1), has_beside("gy"), corners)):
        for end, i in enumerate((0, planes - 1)):
            b, cond = corner[end : end + 1], corner[2 + end : 3 + end]
            cond = jnp.where(here, cond, 0.0)
            at = 6 * (2 * side + end)
            x_link, x_b, x_cond, y_link, y_b, y_cond = (
                ends_ref[at + k : at + k + 1] for k in range(6)
            )
            lacked = x_link * link(x_cond, cond) * (x_b - b)
            lacked = lacked + y_link * link(y_cond, cond) * (y_b - b)
            residual_ref[i, j : j + 1] = residual_ref[i, j : j + 1] + c1 * lacked


def call(kernel, shapes, *operands, scratch=(), inputs=pltpu.VMEM, flops=0):
    return pl.pallas_call(
        kernel,
        out_shape=[
            shape if hasattr(shape, "dtype") else jax.ShapeDtypeStruct(shape, jnp.float32)
            for shape in shapes
        ],
        in_specs=[pl.BlockSpec(memory_space=inputs)] * len(operands),
        out_specs=[pl.BlockSpec(memory_space=pltpu.VMEM)] * len(shapes),
        scratch_shapes=scratch,
        compiler_params=pltpu.CompilerParams(vmem_limit_bytes=48 * 1024 * 1024),
        cost_estimate=pl.CostEstimate(flops=flops, bytes_accessed=0, transcendentals=0),
    )(*operands)


def swap(array, axis, turn):
    parts, nx, ny = (lax.axis_size(name) for name in ("parts", "gx", "gy"))
    pairs = []
    for part in range(parts):
        for x in range(nx):
            for y in range(ny):
                here, count = (x, nx) if axis == "gx" else (y, ny)
                there = here + 1 if here % 2 == turn else here - 1
                if 0 <= there < count:
                    partner = (part, there, y) if axis == "gx" else (part, x, there)
                elif axis == "gy":
                    partner = (part, x ^ 1, y)
                else:
                    partner = (part, x, y ^ 1) if parts % 2 else (part ^ 1, x, y)
                source, target = (
                    (p * nx + i) * ny + j for p, i, j in ((part, x, y), partner)
                )
                pairs.append((source, target))
    return lax.ppermute(array, ("parts", "gx", "gy"), pairs)


def everyones(sketch):
    count = lax.axis_size("gx") * lax.axis_size("gy")
    copies = jnp.broadcast_to(sketch[None], (count,) + sketch.shape)
    return lax.all_to_all(copies, ("gx", "gy"), 0, 0)


def body(b, warmth, phase, slots, draw):
    planes, rows, depth = b.shape
    block, wide = b.shape, (planes + 2, rows, depth)
    face, line, corner = (3 * rows + 4, depth), (3 * planes + 4, depth), (4, depth)
    cells = pltpu.VMEM((depth // LANES, (planes * rows + 8) * 8, LANES), jnp.float32)
    total = HIGH * 2 * PAIR, LOW
    hots = [
        jax.ShapeDtypeStruct((planes * rows * count, depth), jnp.bfloat16)
        for count in (LOW, HIGH * 2 * PAIR)
    ]
    work = b.size * SKETCH * 6
    b, cond, cap, y_link, z_link, inner, draw, slots, x_first, x_second, y_first, y_second = call(
        first_kernel,
        [block] * 8 + [face, face, line, line],
        *(
            pltpu.with_memory_space_constraint(x, pltpu.HBM)
            for x in (b, warmth, phase, draw, slots)
        ),
        scratch=[
            pltpu.VMEM(block, warmth.dtype),
            pltpu.VMEM(block, phase.dtype),
            pltpu.VMEM(block, slots.dtype),
            pltpu.SemaphoreType.DMA((5,)),
        ],
        inputs=pltpu.HBM,
    )
    got_x = swap(x_second, "gx", 1), swap(x_first, "gx", 0)
    got_y = swap(y_second, "gy", 1), swap(y_first, "gy", 0)
    *hots, b_sketch = call(
        slot_kernel, [*hots, (PAIR, SKETCH)], b, draw, slots, scratch=[cells], flops=work
    )
    image_wide, x_link, beside, inside = call(
        inside_kernel,
        [wide, (planes + 1, rows, depth), (4, rows, depth), total],
        b, cond, cap, y_link, z_link, inner, draw, *hots, *got_x,
        scratch=[cells],
        flops=work,
    )
    image, twice, sketch, first, second, ends = call(
        third_kernel,
        [block, block, (FIELDS + 1, SKETCH), corner, corner, (24, depth)],
        b, cap, y_link, z_link, draw, *hots, y_second, y_first, image_wide, x_link, beside,
        *got_x, *got_y, b_sketch, inside,
        scratch=[cells, pltpu.VMEM((3, 8, depth), jnp.float32)],
        flops=work,
    )
    got_corners = [swap(array, "gy", turn) for turn, array in enumerate((first, second))]
    sketches = everyones(sketch)
    return tuple(
        call(last_kernel, [block, block], sketches, b, image, twice, ends, *got_corners)
    )


def solution(mesh):
    spec = P(("parts", "gx"), "gy", None)
    return jax.shard_map(
        body, mesh=mesh, in_specs=(spec,) * 5, out_specs=(spec,) * 2, check_vma=False
    )
```

```python
import jax
import jax.numpy as jnp
from jax import lax
from jax.experimental import pallas as pl
from jax.experimental.pallas import tpu as pltpu
from jax.sharding import PartitionSpec as P

SKETCH = 128
LOW = 32
HIGH = SKETCH // LOW
FIELDS = 3
PAIR = 2
LANES = 128
epsilon = 1e-06


def traits(warmth, phase):
    powder, solid = phase == 0, phase == 1
    offset = jnp.where(powder, 0.2, jnp.where(solid, 1.0, 0.6))
    return offset * (0.5 + warmth), jnp.where(powder, 1.0, jnp.where(solid, 2.0, 1.5))


def link(first, second):
    total = first + second
    return 2.0 * first * second / jnp.where(total > 0.0, total, 1.0)


def ahead(plane, axis):
    return pltpu.roll(plane, plane.shape[axis] - 1, axis)


def inner_links(cond):
    links = []
    for axis in (0, 1):
        index = lax.broadcasted_iota(jnp.int32, cond.shape, axis)
        links.append(
            jnp.where(index < cond.shape[axis] - 1, link(cond, ahead(cond, axis)), 0.0)
        )
    return links


def inner_flow(field, links):
    total = None
    for axis in (0, 1):
        flow = links[axis] * (field - ahead(field, axis))
        part = flow - pltpu.roll(flow, 1, axis)
        total = part if total is None else total + part
    return total


def apply_inside(images, x_links, links, caps):
    results = []
    flow_low = x_links[0] * (images[0] - images[1])
    for i in range(1, len(images) - 1):
        image = images[i]
        flow = x_links[i] * (image - images[i + 1])
        inside = inner_flow(image, links[i - 1])
        results.append(caps[i - 1] * image + inside + (flow - flow_low))
        flow_low = flow
    return results


def parts_of(slot):
    high = jnp.floor(slot * (1.0 / LOW))
    return slot - LOW * high, high


def one_hot(values, j, count, each):
    shape = (count * each, values.shape[1])
    index = lax.broadcasted_iota(jnp.int32, shape, 0) // each
    index = index.astype(jnp.float32).astype(jnp.bfloat16)
    row = jnp.broadcast_to(values[j : j + 1], shape).astype(jnp.bfloat16)
    one = jnp.ones_like(row)
    return jnp.where(row == index, one, jnp.zeros_like(one))


def put_cells(fields, draw, start, cells_ref):
    coarse, fine = [], []
    for field in fields:
        weighted = draw * field
        head = weighted.astype(jnp.bfloat16).astype(jnp.float32)
        coarse.append(head)
        fine.append(weighted - head)
    for f, part in enumerate((coarse + fine) * 2):
        for t in range(cells_ref.shape[0]):
            cells_ref[t, pl.ds(start + f, draw.shape[0], stride=8), :] = part[
                :, t * LANES : (t + 1) * LANES
            ]


def masked_cells(mask, start, j, cells_ref):
    at = pl.ds(start + j * 8, 8)
    cells = jnp.concatenate([cells_ref[t, at, :] for t in range(cells_ref.shape[0])], axis=1)
    return jnp.concatenate([cells, cells], axis=0).astype(jnp.bfloat16) * mask


def product(left, right):
    return lax.dot_general(
        jnp.concatenate(left, axis=1),
        jnp.concatenate(right, axis=1),
        (((1,), (1,)), ((), ())),
        preferred_element_type=jnp.float32,
    )


def as_sketch(total):
    each = 2 * PAIR
    total = jnp.concatenate([total[h * each : (h + 1) * each] for h in range(HIGH)], axis=1)
    return total[:PAIR] + total[PAIR:]


def sketch_rows(planes, low_ref, high_ref, cells_ref):
    total = 0.0
    each = HIGH * 2 * PAIR
    for i, (fields, draw, chosen) in enumerate(planes):
        rows = draw.shape[0]
        start = i * rows * 8
        put_cells(fields, draw, start, cells_ref)
        left, right = [], []
        for j in chosen:
            at = i * rows + j
            mask = high_ref[at * each : (at + 1) * each]
            left.append(masked_cells(mask, start, j, cells_ref))
            right.append(low_ref[at * LOW : (at + 1) * LOW])
        total = total + product(left, right)
    return total


def slot_kernel(b_ref, draw_ref, slot_ref, low_ref, high_ref, sketch_ref, cells_ref):
    planes, rows = b_ref.shape[:2]
    each = HIGH * 2 * PAIR
    total = 0.0
    for i in range(planes):
        start = i * rows * 8
        put_cells((b_ref[i],) * PAIR, draw_ref[i], start, cells_ref)
        low, high = parts_of(slot_ref[i])
        left, right = [], []
        for j in range(rows):
            at = i * rows + j
            mask, hot = one_hot(high, j, HIGH, 2 * PAIR), one_hot(low, j, LOW, 1)
            high_ref[at * each : (at + 1) * each] = mask
            low_ref[at * LOW : (at + 1) * LOW] = hot
            left.append(masked_cells(mask, start, j, cells_ref))
            right.append(hot)
        total = total + product(left, right)
    sketch_ref[...] = as_sketch(total)


def first_kernel(
    b_hbm, warmth_hbm, phase_hbm, draw_hbm, slot_hbm, b_ref, cond_ref, cap_ref, y_link_ref,
    z_link_ref, inner_ref, draw_ref, slot_ref, x_first_ref, x_second_ref, y_first_ref,
    y_second_ref, warmth_ref, phase_ref, number_ref, arrived,
):
    copies = [
        pltpu.make_async_copy(source, target, arrived.at[k])
        for k, (source, target) in enumerate(
            (
                (b_hbm, b_ref),
                (warmth_hbm, warmth_ref),
                (phase_hbm, phase_ref),
                (draw_hbm, draw_ref),
                (slot_hbm, number_ref),
            )
        )
    ]
    for copy in copies:
        copy.start()
    for copy in copies[:3]:
        copy.wait()
    planes, rows = b_ref.shape[:2]
    images, conds = [], []
    for i in range(planes):
        cond, cap = traits(warmth_ref[i], phase_ref[i])
        cap_ref[i] = cap
        cond_ref[i] = cond
        y_link_ref[i], z_link_ref[i] = links = inner_links(cond)
        field = b_ref[i]
        image = cap * field + inner_flow(field, links)
        if i:
            flow = link(conds[-1], cond) * (b_ref[i - 1] - field)
            images[-1] = images[-1] + flow
            image = image - flow
        conds.append(cond)
        images.append(image)
    for i in range(planes):
        inner_ref[i] = images[i]
    for k, field in enumerate((images, [b_ref[i] for i in range(planes)], conds)):
        at = slice(k * rows, (k + 1) * rows)
        x_first_ref[at], x_second_ref[at] = by_turn(field[0], field[-1], "gx")
        for i, plane in enumerate(field):
            at = slice(k * planes + i, k * planes + i + 1)
            y_first_ref[at], y_second_ref[at] = by_turn(plane[:1], plane[rows - 1 :], "gy")
    for copy in copies[3:]:
        copy.wait()
    for i in range(planes):
        slot_ref[i] = number_ref[i].astype(jnp.float32)
    for k, ref in enumerate((draw_ref, slot_ref)):
        ends = [ref[0], ref[planes - 1]]
        for e, j in enumerate((0, rows - 1)):
            at = slice(3 * rows + 2 * k + e, 3 * rows + 2 * k + e + 1)
            lines = [plane[j : j + 1] for plane in ends]
            x_first_ref[at], x_second_ref[at] = by_turn(*lines, "gx")
        for e, plane in enumerate(ends):
            at = slice(3 * planes + 2 * k + e, 3 * planes + 2 * k + e + 1)
            lines = [plane[:1], plane[rows - 1 :]]
            y_first_ref[at], y_second_ref[at] = by_turn(*lines, "gy")


def by_turn(one, other, axis):
    odd = lax.axis_index(axis) % 2 == 1
    return jnp.where(odd, one, other), jnp.where(odd, other, one)


def has_beside(axis):
    at = lax.axis_index(axis)
    return at > 0, at < lax.axis_size(axis) - 1


def reached(rows):
    others = [j for j in range(rows) if 2 <= j < rows - 2]
    return [j for j in range(rows) if j not in others], others


def inside_kernel(
    b_ref, cond_ref, cap_ref, y_link_ref, z_link_ref, inner_ref, draw_ref, low_ref, high_ref,
    got_second_ref, got_first_ref, wide_ref, x_link_ref, beside_ref, sketch_ref, cells_ref,
):
    planes, rows = b_ref.shape[:2]
    (image_low, image_high), (b_low, b_high), (c_low, c_high) = (
        by_turn(*(ref[k * rows : (k + 1) * rows] for ref in (got_first_ref, got_second_ref)), "gx")
        for k in range(3)
    )
    below, above = has_beside("gx")
    c_low, c_high = jnp.where(below, c_low, 0.0), jnp.where(above, c_high, 0.0)
    for k, plane in enumerate((b_low, b_high, c_low, c_high)):
        beside_ref[k] = plane
    conds = [c_low] + [cond_ref[i] for i in range(planes)] + [c_high]
    x_links = [link(conds[i], conds[i + 1]) for i in range(planes + 1)]
    for i, conductance in enumerate(x_links):
        x_link_ref[i] = conductance
    low_flow = x_links[0] * (b_low - b_ref[0])
    high_flow = x_links[-1] * (b_ref[planes - 1] - b_high)
    images = [image_low + low_flow] + [inner_ref[i] for i in range(planes)]
    images.append(image_high - high_flow)
    images[1] = images[1] - low_flow
    images[-2] = images[-2] + high_flow
    for i, image in enumerate(images):
        wide_ref[i] = image
    links = [(y_link_ref[i], z_link_ref[i]) for i in range(planes)]
    twice = apply_inside(images, x_links, links, [cap_ref[i] for i in range(planes)])
    chosen = reached(rows)[1]
    cells = [((images[i + 1], twice[i]), draw_ref[i], chosen) for i in range(planes)]
    sketch_ref[...] = sketch_rows(cells, low_ref, high_ref, cells_ref)


def third_kernel(
    b_ref, cap_ref, y_link_ref, z_link_ref, draw_ref, low_ref, high_ref, own_second_ref,
    own_first_ref, wide_ref, x_link_ref, beside_ref, x_second_ref, x_first_ref, y_second_ref,
    y_first_ref, b_sketch_ref, inside_ref, image_ref, twice_ref, sketch_ref, corner_first_ref,
    corner_second_ref, ends_ref, cells_ref, extra_ref,
):
    planes, rows, depth = b_ref.shape
    index = lax.broadcasted_iota(jnp.int32, (rows, depth), 0)
    images = [wide_ref[i] for i in range(planes + 2)]
    x_links = [x_link_ref[i] for i in range(planes + 1)]
    b_beside, c_beside = (beside_ref[0], beside_ref[1]), (beside_ref[2], beside_ref[3])
    x_ends = []
    for end, i in enumerate((0, planes - 1)):
        conductance = x_links[-end]
        x_ends.append((i, conductance, conductance * (b_ref[i] - b_beside[end])))
    x_tails = by_turn(x_first_ref[3 * rows :], x_second_ref[3 * rows :], "gx")
    own_lines = by_turn(own_first_ref[...], own_second_ref[...], "gy")
    y_lines = by_turn(y_first_ref[...], y_second_ref[...], "gy")
    beside = []
    for side, (j, here, own, line) in enumerate(
        zip((0, rows - 1), has_beside("gy"), own_lines, y_lines)
    ):
        row = slice(j, j + 1)
        beyond, b_line, c_line = (line[k * planes : (k + 1) * planes] for k in range(3))
        c_line = jnp.where(here, c_line, 0.0)
        y_link = link(own[2 * planes : 3 * planes], c_line)
        y_flow = y_link * (own[planes : 2 * planes] - b_line)
        beyond = beyond - y_flow
        for i in range(planes):
            at = slice(i, i + 1)
            images[i + 1] = images[i + 1] + jnp.where(index == j, y_flow[at], 0.0)
            beside.append((i, jnp.where(index == j, y_link[at], 0.0), beyond[at]))
        for end, (i, x_link, x_flow) in enumerate(x_ends):
            line_at, at = slice(i, i + 1), 4 * side + 2 * end
            tail = x_tails[end]
            values = -x_link[row] * y_flow[line_at], tail[side:][:1], tail[2 + side :][:1]
            for k, value in enumerate(values):
                extra_ref[k, at : at + 1] = value
            tail = line[3 * planes :]
            values = -y_link[line_at] * x_flow[row], tail[end:][:1], tail[2 + end :][:1]
            for k, value in enumerate(values):
                extra_ref[k, at + 1 : at + 2] = value
            at = 6 * (2 * side + end)
            values = x_link[row], b_beside[end][row], c_beside[end][row]
            values += y_link[line_at], b_line[line_at], c_line[line_at]
            for k, value in enumerate(values):
                ends_ref[at + k : at + k + 1] = value
    links = [(y_link_ref[i], z_link_ref[i]) for i in range(planes)]
    twice = apply_inside(images, x_links, links, [cap_ref[i] for i in range(planes)])
    for i, conductance, value in beside:
        twice[i] = twice[i] + conductance * (images[i + 1] - value)
    for i in range(planes):
        image_ref[i] = images[i + 1]
        twice_ref[i] = twice[i]
    chosen = reached(rows)[0]
    cells = [((images[i + 1], twice[i]), draw_ref[i], chosen) for i in range(planes)]
    total = inside_ref[...] + sketch_rows(cells, low_ref, high_ref, cells_ref)
    start = planes * rows * 8
    put_cells((jnp.zeros((8, depth), jnp.float32), extra_ref[0]), extra_ref[1], start, cells_ref)
    low, high = parts_of(extra_ref[2])
    left, right = [], []
    for j in range(8):
        mask = one_hot(high, j, HIGH, 2 * PAIR)
        left.append(masked_cells(mask, start, j, cells_ref))
        right.append(one_hot(low, j, LOW, 1))
    sketch_ref[1 : 1 + PAIR] = as_sketch(total + product(left, right))
    sketch_ref[:1] = b_sketch_ref[:1]
    sketch_ref[1 + PAIR :] = b_sketch_ref[:1]
    for k, plane in enumerate(b_beside + c_beside):
        at = slice(k, k + 1)
        corner_first_ref[at], corner_second_ref[at] = by_turn(
            plane[:1], plane[rows - 1 :], "gy"
        )


def last_kernel(
    sketch_ref, b_ref, image_ref, twice_ref, ends_ref, corner_first_ref, corner_second_ref,
    solution_ref, residual_ref,
):
    sketches = jnp.sum(sketch_ref[...], axis=0)

    def inner(first, second):
        return jnp.sum(first * second, axis=1, keepdims=True)

    s0, s1, s2 = (sketches[i : i + 1] for i in range(FIELDS))
    beta_inverse = 1.0 / jnp.sqrt(inner(s0, s0) + epsilon)
    h00 = inner(s0, s1) * beta_inverse * beta_inverse
    q0, p0 = s0 * beta_inverse, s1 * beta_inverse
    t0 = p0 - h00 * q0
    p1 = s2 * beta_inverse - h00 * p0
    n0 = jnp.sqrt(inner(t0, t0) + epsilon)
    n0_inverse = 1.0 / n0
    h01 = inner(q0, p1) * n0_inverse
    h11 = inner(t0, p1) * n0_inverse * n0_inverse
    t1 = p1 * n0_inverse - h01 * q0 - h11 * (t0 * n0_inverse)
    n1_square = inner(t1, t1) + epsilon
    first = h00 * h00 + n0 * n0
    cross = h00 * h01 + n0 * h11
    ratio = cross / first
    second = h01 * h01 + h11 * h11 + n1_square - cross * ratio
    y1 = (h01 - ratio * h00) / second
    y0 = h00 / first - ratio * y1
    c1 = y1 * n0_inverse
    c0 = y0 - h00 * c1
    planes, rows, depth = b_ref.shape
    for i in range(planes):
        b, image = b_ref[i], image_ref[i]
        solution_ref[i] = c0 * b + c1 * image
        residual_ref[i] = b - c0 * image - c1 * twice_ref[i]
    corners = by_turn(corner_first_ref[...], corner_second_ref[...], "gy")
    for side, (j, here, corner) in enumerate(zip((0, rows - 1), has_beside("gy"), corners)):
        for end, i in enumerate((0, planes - 1)):
            b, cond = corner[end : end + 1], corner[2 + end : 3 + end]
            cond = jnp.where(here, cond, 0.0)
            at = 6 * (2 * side + end)
            x_link, x_b, x_cond, y_link, y_b, y_cond = (
                ends_ref[at + k : at + k + 1] for k in range(6)
            )
            lacked = x_link * link(x_cond, cond) * (x_b - b)
            lacked = lacked + y_link * link(y_cond, cond) * (y_b - b)
            residual_ref[i, j : j + 1] = residual_ref[i, j : j + 1] + c1 * lacked


def call(kernel, shapes, *operands, scratch=(), inputs=pltpu.VMEM, flops=0):
    return pl.pallas_call(
        kernel,
        out_shape=[
            shape if hasattr(shape, "dtype") else jax.ShapeDtypeStruct(shape, jnp.float32)
            for shape in shapes
        ],
        in_specs=[pl.BlockSpec(memory_space=inputs)] * len(operands),
        out_specs=[pl.BlockSpec(memory_space=pltpu.VMEM)] * len(shapes),
        scratch_shapes=scratch,
        compiler_params=pltpu.CompilerParams(vmem_limit_bytes=48 * 1024 * 1024),
        cost_estimate=pl.CostEstimate(flops=flops, bytes_accessed=0, transcendentals=0),
    )(*operands)


def swap(array, axis, turn):
    nx, ny = lax.axis_size("gx"), lax.axis_size("gy")
    pairs = []
    for x in range(nx):
        for y in range(ny):
            here, count = (x, nx) if axis == "gx" else (y, ny)
            there = here + 1 if here % 2 == turn else here - 1
            if 0 <= there < count:
                partner = (there, y) if axis == "gx" else (x, there)
            else:
                partner = (x, y ^ 1) if axis == "gx" else (x ^ 1, y)
            pairs.append((x * ny + y, partner[0] * ny + partner[1]))
    return lax.ppermute(array, ("gx", "gy"), pairs)


def everyones(sketch):
    nx, ny = lax.axis_size("gx"), lax.axis_size("gy")
    middle = nx // 2 - 1, ny // 2
    places = [(x, y) for x in range(nx) for y in range(ny)]
    places.sort(key=lambda at: (abs(at[1] - middle[1]), abs(at[0] - middle[0]), at))
    group = [x * ny + y for x, y in places]
    copies = jnp.broadcast_to(sketch[None], (nx * ny,) + sketch.shape)
    return lax.all_to_all(copies, ("gx", "gy"), 0, 0, axis_index_groups=[group])


def body(b, warmth, phase, slots, draw):
    planes, rows, depth = b.shape
    block, wide = b.shape, (planes + 2, rows, depth)
    face, line, corner = (3 * rows + 4, depth), (3 * planes + 4, depth), (4, depth)
    cells = pltpu.VMEM((depth // LANES, (planes * rows + 8) * 8, LANES), jnp.float32)
    total = HIGH * 2 * PAIR, LOW
    hots = [
        jax.ShapeDtypeStruct((planes * rows * count, depth), jnp.bfloat16)
        for count in (LOW, HIGH * 2 * PAIR)
    ]
    work = b.size * SKETCH * 6
    b, cond, cap, y_link, z_link, inner, draw, slots, x_first, x_second, y_first, y_second = call(
        first_kernel,
        [block] * 8 + [face, face, line, line],
        *(
            pltpu.with_memory_space_constraint(x, pltpu.HBM)
            for x in (b, warmth, phase, draw, slots)
        ),
        scratch=[
            pltpu.VMEM(block, warmth.dtype),
            pltpu.VMEM(block, phase.dtype),
            pltpu.VMEM(block, slots.dtype),
            pltpu.SemaphoreType.DMA((5,)),
        ],
        inputs=pltpu.HBM,
    )
    got_x = swap(x_second, "gx", 1), swap(x_first, "gx", 0)
    got_y = swap(y_second, "gy", 1), swap(y_first, "gy", 0)
    *hots, b_sketch = call(
        slot_kernel, [*hots, (PAIR, SKETCH)], b, draw, slots, scratch=[cells], flops=work
    )
    image_wide, x_link, beside, inside = call(
        inside_kernel,
        [wide, (planes + 1, rows, depth), (4, rows, depth), total],
        b, cond, cap, y_link, z_link, inner, draw, *hots, *got_x,
        scratch=[cells],
        flops=work,
    )
    image, twice, sketch, first, second, ends = call(
        third_kernel,
        [block, block, (FIELDS + 1, SKETCH), corner, corner, (24, depth)],
        b, cap, y_link, z_link, draw, *hots, y_second, y_first, image_wide, x_link, beside,
        *got_x, *got_y, b_sketch, inside,
        scratch=[cells, pltpu.VMEM((3, 8, depth), jnp.float32)],
        flops=work,
    )
    got_corners = [swap(array, "gy", turn) for turn, array in enumerate((first, second))]
    sketches = everyones(sketch)
    return tuple(
        call(last_kernel, [block, block], sketches, b, image, twice, ends, *got_corners)
    )


def solution(mesh):
    spec = P(("parts", "gx"), "gy", None)
    return jax.shard_map(
        body, mesh=mesh, in_specs=(spec,) * 5, out_specs=(spec,) * 2, check_vma=False
    )
```

```python
import jax
import jax.numpy as jnp
from jax import lax
from jax.experimental import pallas as pl
from jax.experimental.pallas import tpu as pltpu
from jax.sharding import PartitionSpec as P

SKETCH = 128
LOW = 32
HIGH = SKETCH // LOW
FIELDS = 3
PAIR = 2
LANES = 128
epsilon = 1e-06


def traits(warmth, phase):
    powder, solid = phase == 0, phase == 1
    offset = jnp.where(powder, 0.2, jnp.where(solid, 1.0, 0.6))
    return offset * (0.5 + warmth), jnp.where(powder, 1.0, jnp.where(solid, 2.0, 1.5))


def link(first, second):
    total = first + second
    return 2.0 * first * second / jnp.where(total > 0.0, total, 1.0)


def ahead(plane, axis):
    return pltpu.roll(plane, plane.shape[axis] - 1, axis)


def inner_links(cond):
    links = []
    for axis in (0, 1):
        index = lax.broadcasted_iota(jnp.int32, cond.shape, axis)
        links.append(
            jnp.where(index < cond.shape[axis] - 1, link(cond, ahead(cond, axis)), 0.0)
        )
    return links


def inner_flow(field, links):
    total = None
    for axis in (0, 1):
        flow = links[axis] * (field - ahead(field, axis))
        part = flow - pltpu.roll(flow, 1, axis)
        total = part if total is None else total + part
    return total


def apply_inside(images, x_links, links, caps):
    results = []
    flow_low = x_links[0] * (images[0] - images[1])
    for i in range(1, len(images) - 1):
        image = images[i]
        flow = x_links[i] * (image - images[i + 1])
        inside = inner_flow(image, links[i - 1])
        results.append(caps[i - 1] * image + inside + (flow - flow_low))
        flow_low = flow
    return results


def parts_of(slot):
    high = jnp.floor(slot * (1.0 / LOW))
    return slot - LOW * high, high


def one_hot(values, j, count, each):
    shape = (count * each, values.shape[1])
    index = lax.broadcasted_iota(jnp.int32, shape, 0) // each
    index = index.astype(jnp.float32).astype(jnp.bfloat16)
    row = jnp.broadcast_to(values[j : j + 1], shape).astype(jnp.bfloat16)
    one = jnp.ones_like(row)
    return jnp.where(row == index, one, jnp.zeros_like(one))


def put_cells(fields, draw, start, cells_ref):
    coarse, fine = [], []
    for field in fields:
        weighted = draw * field
        head = weighted.astype(jnp.bfloat16).astype(jnp.float32)
        coarse.append(head)
        fine.append(weighted - head)
    for f, part in enumerate((coarse + fine) * 2):
        for t in range(cells_ref.shape[0]):
            cells_ref[t, pl.ds(start + f, draw.shape[0], stride=8), :] = part[
                :, t * LANES : (t + 1) * LANES
            ]


def masked_cells(mask, start, j, cells_ref):
    at = pl.ds(start + j * 8, 8)
    cells = jnp.concatenate([cells_ref[t, at, :] for t in range(cells_ref.shape[0])], axis=1)
    return jnp.concatenate([cells, cells], axis=0).astype(jnp.bfloat16) * mask


def product(left, right):
    return lax.dot_general(
        jnp.concatenate(left, axis=1),
        jnp.concatenate(right, axis=1),
        (((1,), (1,)), ((), ())),
        preferred_element_type=jnp.float32,
    )


def as_sketch(total):
    each = 2 * PAIR
    total = jnp.concatenate([total[h * each : (h + 1) * each] for h in range(HIGH)], axis=1)
    return total[:PAIR] + total[PAIR:]


def sketch_rows(planes, low_ref, high_ref, cells_ref):
    total = 0.0
    each = HIGH * 2 * PAIR
    for i, (fields, draw, chosen) in enumerate(planes):
        rows = draw.shape[0]
        start = i * rows * 8
        put_cells(fields, draw, start, cells_ref)
        left, right = [], []
        for j in chosen:
            at = i * rows + j
            mask = high_ref[at * each : (at + 1) * each]
            left.append(masked_cells(mask, start, j, cells_ref))
            right.append(low_ref[at * LOW : (at + 1) * LOW])
        total = total + product(left, right)
    return total


def slot_kernel(b_ref, draw_ref, slot_ref, low_ref, high_ref, sketch_ref, cells_ref):
    planes, rows = b_ref.shape[:2]
    each = HIGH * 2 * PAIR
    total = 0.0
    for i in range(planes):
        start = i * rows * 8
        put_cells((b_ref[i],) * PAIR, draw_ref[i], start, cells_ref)
        low, high = parts_of(slot_ref[i])
        left, right = [], []
        for j in range(rows):
            at = i * rows + j
            mask, hot = one_hot(high, j, HIGH, 2 * PAIR), one_hot(low, j, LOW, 1)
            high_ref[at * each : (at + 1) * each] = mask
            low_ref[at * LOW : (at + 1) * LOW] = hot
            left.append(masked_cells(mask, start, j, cells_ref))
            right.append(hot)
        total = total + product(left, right)
    sketch_ref[...] = as_sketch(total)


def first_kernel(
    b_hbm, warmth_hbm, phase_hbm, draw_hbm, slot_hbm, b_ref, cond_ref, cap_ref, y_link_ref,
    z_link_ref, inner_ref, draw_ref, slot_ref, x_first_ref, x_second_ref, y_first_ref,
    y_second_ref, warmth_ref, phase_ref, number_ref, arrived,
):
    copies = [
        pltpu.make_async_copy(source, target, arrived.at[k])
        for k, (source, target) in enumerate(
            (
                (b_hbm, b_ref),
                (warmth_hbm, warmth_ref),
                (phase_hbm, phase_ref),
                (draw_hbm, draw_ref),
                (slot_hbm, number_ref),
            )
        )
    ]
    for copy in copies:
        copy.start()
    for copy in copies[:3]:
        copy.wait()
    planes, rows = b_ref.shape[:2]
    images, conds = [], []
    for i in range(planes):
        cond, cap = traits(warmth_ref[i], phase_ref[i])
        cap_ref[i] = cap
        cond_ref[i] = cond
        y_link_ref[i], z_link_ref[i] = links = inner_links(cond)
        field = b_ref[i]
        image = cap * field + inner_flow(field, links)
        if i:
            flow = link(conds[-1], cond) * (b_ref[i - 1] - field)
            images[-1] = images[-1] + flow
            image = image - flow
        conds.append(cond)
        images.append(image)
    for i in range(planes):
        inner_ref[i] = images[i]
    for k, field in enumerate((images, [b_ref[i] for i in range(planes)], conds)):
        at = slice(k * rows, (k + 1) * rows)
        x_first_ref[at], x_second_ref[at] = by_turn(field[0], field[-1], "gx")
        for i, plane in enumerate(field):
            at = slice(k * planes + i, k * planes + i + 1)
            y_first_ref[at], y_second_ref[at] = by_turn(plane[:1], plane[rows - 1 :], "gy")
    for copy in copies[3:]:
        copy.wait()
    for i in range(planes):
        slot_ref[i] = number_ref[i].astype(jnp.float32)
    for k, ref in enumerate((draw_ref, slot_ref)):
        ends = [ref[0], ref[planes - 1]]
        for e, j in enumerate((0, rows - 1)):
            at = slice(3 * rows + 2 * k + e, 3 * rows + 2 * k + e + 1)
            lines = [plane[j : j + 1] for plane in ends]
            x_first_ref[at], x_second_ref[at] = by_turn(*lines, "gx")
        for e, plane in enumerate(ends):
            at = slice(3 * planes + 2 * k + e, 3 * planes + 2 * k + e + 1)
            lines = [plane[:1], plane[rows - 1 :]]
            y_first_ref[at], y_second_ref[at] = by_turn(*lines, "gy")


def by_turn(one, other, axis):
    odd = lax.axis_index(axis) % 2 == 1
    return jnp.where(odd, one, other), jnp.where(odd, other, one)


def has_beside(axis):
    at = lax.axis_index(axis)
    return at > 0, at < lax.axis_size(axis) - 1


def reached(rows):
    others = [j for j in range(rows) if 2 <= j < rows - 2]
    return [j for j in range(rows) if j not in others], others


def inside_kernel(
    b_ref, cond_ref, cap_ref, y_link_ref, z_link_ref, inner_ref, draw_ref, low_ref, high_ref,
    got_second_ref, got_first_ref, wide_ref, x_link_ref, beside_ref, sketch_ref, cells_ref,
):
    planes, rows = b_ref.shape[:2]
    (image_low, image_high), (b_low, b_high), (c_low, c_high) = (
        by_turn(*(ref[k * rows : (k + 1) * rows] for ref in (got_first_ref, got_second_ref)), "gx")
        for k in range(3)
    )
    below, above = has_beside("gx")
    c_low, c_high = jnp.where(below, c_low, 0.0), jnp.where(above, c_high, 0.0)
    for k, plane in enumerate((b_low, b_high, c_low, c_high)):
        beside_ref[k] = plane
    conds = [c_low] + [cond_ref[i] for i in range(planes)] + [c_high]
    x_links = [link(conds[i], conds[i + 1]) for i in range(planes + 1)]
    for i, conductance in enumerate(x_links):
        x_link_ref[i] = conductance
    low_flow = x_links[0] * (b_low - b_ref[0])
    high_flow = x_links[-1] * (b_ref[planes - 1] - b_high)
    images = [image_low + low_flow] + [inner_ref[i] for i in range(planes)]
    images.append(image_high - high_flow)
    images[1] = images[1] - low_flow
    images[-2] = images[-2] + high_flow
    for i, image in enumerate(images):
        wide_ref[i] = image
    links = [(y_link_ref[i], z_link_ref[i]) for i in range(planes)]
    twice = apply_inside(images, x_links, links, [cap_ref[i] for i in range(planes)])
    chosen = reached(rows)[1]
    cells = [((images[i + 1], twice[i]), draw_ref[i], chosen) for i in range(planes)]
    sketch_ref[...] = sketch_rows(cells, low_ref, high_ref, cells_ref)


def third_kernel(
    b_ref, cap_ref, y_link_ref, z_link_ref, draw_ref, low_ref, high_ref, own_second_ref,
    own_first_ref, wide_ref, x_link_ref, beside_ref, x_second_ref, x_first_ref, y_second_ref,
    y_first_ref, b_sketch_ref, inside_ref, image_ref, twice_ref, sketch_ref, corner_first_ref,
    corner_second_ref, ends_ref, cells_ref, extra_ref,
):
    planes, rows, depth = b_ref.shape
    index = lax.broadcasted_iota(jnp.int32, (rows, depth), 0)
    images = [wide_ref[i] for i in range(planes + 2)]
    x_links = [x_link_ref[i] for i in range(planes + 1)]
    b_beside, c_beside = (beside_ref[0], beside_ref[1]), (beside_ref[2], beside_ref[3])
    x_ends = []
    for end, i in enumerate((0, planes - 1)):
        conductance = x_links[-end]
        x_ends.append((i, conductance, conductance * (b_ref[i] - b_beside[end])))
    x_tails = by_turn(x_first_ref[3 * rows :], x_second_ref[3 * rows :], "gx")
    own_lines = by_turn(own_first_ref[...], own_second_ref[...], "gy")
    y_lines = by_turn(y_first_ref[...], y_second_ref[...], "gy")
    beside = []
    for side, (j, here, own, line) in enumerate(
        zip((0, rows - 1), has_beside("gy"), own_lines, y_lines)
    ):
        row = slice(j, j + 1)
        beyond, b_line, c_line = (line[k * planes : (k + 1) * planes] for k in range(3))
        c_line = jnp.where(here, c_line, 0.0)
        y_link = link(own[2 * planes : 3 * planes], c_line)
        y_flow = y_link * (own[planes : 2 * planes] - b_line)
        beyond = beyond - y_flow
        for i in range(planes):
            at = slice(i, i + 1)
            images[i + 1] = images[i + 1] + jnp.where(index == j, y_flow[at], 0.0)
            beside.append((i, jnp.where(index == j, y_link[at], 0.0), beyond[at]))
        for end, (i, x_link, x_flow) in enumerate(x_ends):
            line_at, at = slice(i, i + 1), 4 * side + 2 * end
            tail = x_tails[end]
            values = -x_link[row] * y_flow[line_at], tail[side:][:1], tail[2 + side :][:1]
            for k, value in enumerate(values):
                extra_ref[k, at : at + 1] = value
            tail = line[3 * planes :]
            values = -y_link[line_at] * x_flow[row], tail[end:][:1], tail[2 + end :][:1]
            for k, value in enumerate(values):
                extra_ref[k, at + 1 : at + 2] = value
            at = 6 * (2 * side + end)
            values = x_link[row], b_beside[end][row], c_beside[end][row]
            values += y_link[line_at], b_line[line_at], c_line[line_at]
            for k, value in enumerate(values):
                ends_ref[at + k : at + k + 1] = value
    links = [(y_link_ref[i], z_link_ref[i]) for i in range(planes)]
    twice = apply_inside(images, x_links, links, [cap_ref[i] for i in range(planes)])
    for i, conductance, value in beside:
        twice[i] = twice[i] + conductance * (images[i + 1] - value)
    for i in range(planes):
        image_ref[i] = images[i + 1]
        twice_ref[i] = twice[i]
    chosen = reached(rows)[0]
    cells = [((images[i + 1], twice[i]), draw_ref[i], chosen) for i in range(planes)]
    total = inside_ref[...] + sketch_rows(cells, low_ref, high_ref, cells_ref)
    start = planes * rows * 8
    put_cells((jnp.zeros((8, depth), jnp.float32), extra_ref[0]), extra_ref[1], start, cells_ref)
    low, high = parts_of(extra_ref[2])
    left, right = [], []
    for j in range(8):
        mask = one_hot(high, j, HIGH, 2 * PAIR)
        left.append(masked_cells(mask, start, j, cells_ref))
        right.append(one_hot(low, j, LOW, 1))
    sketch_ref[1 : 1 + PAIR] = as_sketch(total + product(left, right))
    sketch_ref[:1] = b_sketch_ref[:1]
    sketch_ref[1 + PAIR :] = b_sketch_ref[:1]
    for k, plane in enumerate(b_beside + c_beside):
        at = slice(k, k + 1)
        corner_first_ref[at], corner_second_ref[at] = by_turn(
            plane[:1], plane[rows - 1 :], "gy"
        )


def last_kernel(
    sketch_ref, b_ref, image_ref, twice_ref, ends_ref, corner_first_ref, corner_second_ref,
    solution_ref, residual_ref,
):
    sketches = jnp.sum(sketch_ref[...], axis=0)

    def inner(first, second):
        return jnp.sum(first * second, axis=1, keepdims=True)

    s0, s1, s2 = (sketches[i : i + 1] for i in range(FIELDS))
    beta_inverse = 1.0 / jnp.sqrt(inner(s0, s0) + epsilon)
    h00 = inner(s0, s1) * beta_inverse * beta_inverse
    q0, p0 = s0 * beta_inverse, s1 * beta_inverse
    t0 = p0 - h00 * q0
    p1 = s2 * beta_inverse - h00 * p0
    n0 = jnp.sqrt(inner(t0, t0) + epsilon)
    n0_inverse = 1.0 / n0
    h01 = inner(q0, p1) * n0_inverse
    h11 = inner(t0, p1) * n0_inverse * n0_inverse
    t1 = p1 * n0_inverse - h01 * q0 - h11 * (t0 * n0_inverse)
    n1_square = inner(t1, t1) + epsilon
    first = h00 * h00 + n0 * n0
    cross = h00 * h01 + n0 * h11
    ratio = cross / first
    second = h01 * h01 + h11 * h11 + n1_square - cross * ratio
    y1 = (h01 - ratio * h00) / second
    y0 = h00 / first - ratio * y1
    c1 = y1 * n0_inverse
    c0 = y0 - h00 * c1
    planes, rows, depth = b_ref.shape
    for i in range(planes):
        b, image = b_ref[i], image_ref[i]
        solution_ref[i] = c0 * b + c1 * image
        residual_ref[i] = b - c0 * image - c1 * twice_ref[i]
    corners = by_turn(corner_first_ref[...], corner_second_ref[...], "gy")
    for side, (j, here, corner) in enumerate(zip((0, rows - 1), has_beside("gy"), corners)):
        for end, i in enumerate((0, planes - 1)):
            b, cond = corner[end : end + 1], corner[2 + end : 3 + end]
            cond = jnp.where(here, cond, 0.0)
            at = 6 * (2 * side + end)
            x_link, x_b, x_cond, y_link, y_b, y_cond = (
                ends_ref[at + k : at + k + 1] for k in range(6)
            )
            lacked = x_link * link(x_cond, cond) * (x_b - b)
            lacked = lacked + y_link * link(y_cond, cond) * (y_b - b)
            residual_ref[i, j : j + 1] = residual_ref[i, j : j + 1] + c1 * lacked


def call(kernel, shapes, *operands, scratch=(), inputs=pltpu.VMEM, flops=0):
    return pl.pallas_call(
        kernel,
        out_shape=[
            shape if hasattr(shape, "dtype") else jax.ShapeDtypeStruct(shape, jnp.float32)
            for shape in shapes
        ],
        in_specs=[pl.BlockSpec(memory_space=inputs)] * len(operands),
        out_specs=[pl.BlockSpec(memory_space=pltpu.VMEM)] * len(shapes),
        scratch_shapes=scratch,
        compiler_params=pltpu.CompilerParams(vmem_limit_bytes=48 * 1024 * 1024),
        cost_estimate=pl.CostEstimate(flops=flops, bytes_accessed=0, transcendentals=0),
    )(*operands)


def swap(array, axis, turn):
    nx, ny = lax.axis_size("gx"), lax.axis_size("gy")
    pairs = []
    for x in range(nx):
        for y in range(ny):
            here, count = (x, nx) if axis == "gx" else (y, ny)
            there = here + 1 if here % 2 == turn else here - 1
            if 0 <= there < count:
                partner = (there, y) if axis == "gx" else (x, there)
            else:
                partner = (x, y ^ 1) if axis == "gx" else (x ^ 1, y)
            pairs.append((x * ny + y, partner[0] * ny + partner[1]))
    return lax.ppermute(array, ("gx", "gy"), pairs)


def everyones(sketch):
    nx, ny = lax.axis_size("gx"), lax.axis_size("gy")
    middle = nx // 2 - 1, ny // 2
    places = [(x, y) for x in range(nx) for y in range(ny)]
    places.sort(key=lambda at: (at != middle, -abs(at[1] - middle[1]), at[0] % 2, at))
    group = [x * ny + y for x, y in places]
    copies = jnp.broadcast_to(sketch[None], (nx * ny,) + sketch.shape)
    return lax.all_to_all(copies, ("gx", "gy"), 0, 0, axis_index_groups=[group])


def body(b, warmth, phase, slots, draw):
    planes, rows, depth = b.shape
    block, wide = b.shape, (planes + 2, rows, depth)
    face, line, corner = (3 * rows + 4, depth), (3 * planes + 4, depth), (4, depth)
    cells = pltpu.VMEM((depth // LANES, (planes * rows + 8) * 8, LANES), jnp.float32)
    total = HIGH * 2 * PAIR, LOW
    hots = [
        jax.ShapeDtypeStruct((planes * rows * count, depth), jnp.bfloat16)
        for count in (LOW, HIGH * 2 * PAIR)
    ]
    work = b.size * SKETCH * 6
    b, cond, cap, y_link, z_link, inner, draw, slots, x_first, x_second, y_first, y_second = call(
        first_kernel,
        [block] * 8 + [face, face, line, line],
        *(
            pltpu.with_memory_space_constraint(x, pltpu.HBM)
            for x in (b, warmth, phase, draw, slots)
        ),
        scratch=[
            pltpu.VMEM(block, warmth.dtype),
            pltpu.VMEM(block, phase.dtype),
            pltpu.VMEM(block, slots.dtype),
            pltpu.SemaphoreType.DMA((5,)),
        ],
        inputs=pltpu.HBM,
    )
    got_x = swap(x_second, "gx", 1), swap(x_first, "gx", 0)
    got_y = swap(y_second, "gy", 1), swap(y_first, "gy", 0)
    *hots, b_sketch = call(
        slot_kernel, [*hots, (PAIR, SKETCH)], b, draw, slots, scratch=[cells], flops=work
    )
    image_wide, x_link, beside, inside = call(
        inside_kernel,
        [wide, (planes + 1, rows, depth), (4, rows, depth), total],
        b, cond, cap, y_link, z_link, inner, draw, *hots, *got_x,
        scratch=[cells],
        flops=work,
    )
    image, twice, sketch, first, second, ends = call(
        third_kernel,
        [block, block, (FIELDS + 1, SKETCH), corner, corner, (24, depth)],
        b, cap, y_link, z_link, draw, *hots, y_second, y_first, image_wide, x_link, beside,
        *got_x, *got_y, b_sketch, inside,
        scratch=[cells, pltpu.VMEM((3, 8, depth), jnp.float32)],
        flops=work,
    )
    got_corners = [swap(array, "gy", turn) for turn, array in enumerate((first, second))]
    sketches = everyones(sketch)
    return tuple(
        call(last_kernel, [block, block], sketches, b, image, twice, ends, *got_corners)
    )


def solution(mesh):
    spec = P(("parts", "gx"), "gy", None)
    return jax.shard_map(
        body, mesh=mesh, in_specs=(spec,) * 5, out_specs=(spec,) * 2, check_vma=False
    )
```

```python
import jax
import jax.numpy as jnp
from jax import lax
from jax.experimental import pallas as pl
from jax.experimental.pallas import tpu as pltpu
from jax.sharding import PartitionSpec as P

SKETCH = 128
LOW = 32
HIGH = SKETCH // LOW
FIELDS = 3
PAIR = 2
LANES = 128
epsilon = 1e-06


def traits(warmth, phase):
    powder, solid = phase == 0, phase == 1
    offset = jnp.where(powder, 0.2, jnp.where(solid, 1.0, 0.6))
    return offset * (0.5 + warmth), jnp.where(powder, 1.0, jnp.where(solid, 2.0, 1.5))


def link(first, second):
    total = first + second
    return 2.0 * first * second / jnp.where(total > 0.0, total, 1.0)


def ahead(plane, axis):
    return pltpu.roll(plane, plane.shape[axis] - 1, axis)


def inner_links(cond):
    links = []
    for axis in (0, 1):
        index = lax.broadcasted_iota(jnp.int32, cond.shape, axis)
        links.append(
            jnp.where(index < cond.shape[axis] - 1, link(cond, ahead(cond, axis)), 0.0)
        )
    return links


def inner_flow(field, links):
    total = None
    for axis in (0, 1):
        flow = links[axis] * (field - ahead(field, axis))
        part = flow - pltpu.roll(flow, 1, axis)
        total = part if total is None else total + part
    return total


def apply_inside(images, x_links, links, caps):
    results = []
    flow_low = x_links[0] * (images[0] - images[1])
    for i in range(1, len(images) - 1):
        image = images[i]
        flow = x_links[i] * (image - images[i + 1])
        inside = inner_flow(image, links[i - 1])
        results.append(caps[i - 1] * image + inside + (flow - flow_low))
        flow_low = flow
    return results


def parts_of(slot):
    high = jnp.floor(slot * (1.0 / LOW))
    return slot - LOW * high, high


def one_hot(values, j, count, each):
    shape = (count * each, values.shape[1])
    index = lax.broadcasted_iota(jnp.int32, shape, 0) // each
    index = index.astype(jnp.float32).astype(jnp.bfloat16)
    row = jnp.broadcast_to(values[j : j + 1], shape).astype(jnp.bfloat16)
    one = jnp.ones_like(row)
    return jnp.where(row == index, one, jnp.zeros_like(one))


def put_cells(fields, draw, start, cells_ref):
    coarse, fine = [], []
    for field in fields:
        weighted = draw * field
        head = weighted.astype(jnp.bfloat16).astype(jnp.float32)
        coarse.append(head)
        fine.append(weighted - head)
    for f, part in enumerate((coarse + fine) * 2):
        for t in range(cells_ref.shape[0]):
            cells_ref[t, pl.ds(start + f, draw.shape[0], stride=8), :] = part[
                :, t * LANES : (t + 1) * LANES
            ]


def masked_cells(mask, start, j, cells_ref):
    at = pl.ds(start + j * 8, 8)
    cells = jnp.concatenate([cells_ref[t, at, :] for t in range(cells_ref.shape[0])], axis=1)
    return jnp.concatenate([cells, cells], axis=0).astype(jnp.bfloat16) * mask


def product(left, right):
    return lax.dot_general(
        jnp.concatenate(left, axis=1),
        jnp.concatenate(right, axis=1),
        (((1,), (1,)), ((), ())),
        preferred_element_type=jnp.float32,
    )


def as_sketch(total):
    each = 2 * PAIR
    total = jnp.concatenate([total[h * each : (h + 1) * each] for h in range(HIGH)], axis=1)
    return total[:PAIR] + total[PAIR:]


def sketch_rows(planes, low_ref, high_ref, cells_ref):
    total = 0.0
    each = HIGH * 2 * PAIR
    for i, (fields, draw, chosen) in enumerate(planes):
        rows = draw.shape[0]
        start = i * rows * 8
        put_cells(fields, draw, start, cells_ref)
        left, right = [], []
        for j in chosen:
            at = i * rows + j
            mask = high_ref[at * each : (at + 1) * each]
            left.append(masked_cells(mask, start, j, cells_ref))
            right.append(low_ref[at * LOW : (at + 1) * LOW])
        total = total + product(left, right)
    return total


def slot_kernel(b_ref, draw_ref, slot_ref, low_ref, high_ref, sketch_ref, cells_ref):
    planes, rows = b_ref.shape[:2]
    each = HIGH * 2 * PAIR
    total = 0.0
    for i in range(planes):
        start = i * rows * 8
        put_cells((b_ref[i],) * PAIR, draw_ref[i], start, cells_ref)
        low, high = parts_of(slot_ref[i])
        left, right = [], []
        for j in range(rows):
            at = i * rows + j
            mask, hot = one_hot(high, j, HIGH, 2 * PAIR), one_hot(low, j, LOW, 1)
            high_ref[at * each : (at + 1) * each] = mask
            low_ref[at * LOW : (at + 1) * LOW] = hot
            left.append(masked_cells(mask, start, j, cells_ref))
            right.append(hot)
        total = total + product(left, right)
    sketch_ref[...] = as_sketch(total)


def first_kernel(
    b_hbm, warmth_hbm, phase_hbm, draw_hbm, slot_hbm, b_ref, cond_ref, cap_ref, y_link_ref,
    z_link_ref, inner_ref, draw_ref, slot_ref, x_first_ref, x_second_ref, y_first_ref,
    y_second_ref, warmth_ref, phase_ref, number_ref, arrived,
):
    copies = [
        pltpu.make_async_copy(source, target, arrived.at[k])
        for k, (source, target) in enumerate(
            (
                (b_hbm, b_ref),
                (warmth_hbm, warmth_ref),
                (phase_hbm, phase_ref),
                (draw_hbm, draw_ref),
                (slot_hbm, number_ref),
            )
        )
    ]
    for copy in copies:
        copy.start()
    for copy in copies[:3]:
        copy.wait()
    planes, rows = b_ref.shape[:2]
    images, conds = [], []
    for i in range(planes):
        cond, cap = traits(warmth_ref[i], phase_ref[i])
        cap_ref[i] = cap
        cond_ref[i] = cond
        y_link_ref[i], z_link_ref[i] = links = inner_links(cond)
        field = b_ref[i]
        image = cap * field + inner_flow(field, links)
        if i:
            flow = link(conds[-1], cond) * (b_ref[i - 1] - field)
            images[-1] = images[-1] + flow
            image = image - flow
        conds.append(cond)
        images.append(image)
    for i in range(planes):
        inner_ref[i] = images[i]
    for k, field in enumerate((images, [b_ref[i] for i in range(planes)], conds)):
        at = slice(k * rows, (k + 1) * rows)
        x_first_ref[at], x_second_ref[at] = by_turn(field[0], field[-1], "gx")
        for i, plane in enumerate(field):
            at = slice(k * planes + i, k * planes + i + 1)
            y_first_ref[at], y_second_ref[at] = by_turn(plane[:1], plane[rows - 1 :], "gy")
    for copy in copies[3:]:
        copy.wait()
    for i in range(planes):
        slot_ref[i] = number_ref[i].astype(jnp.float32)
    for k, ref in enumerate((draw_ref, slot_ref)):
        ends = [ref[0], ref[planes - 1]]
        for e, j in enumerate((0, rows - 1)):
            at = slice(3 * rows + 2 * k + e, 3 * rows + 2 * k + e + 1)
            lines = [plane[j : j + 1] for plane in ends]
            x_first_ref[at], x_second_ref[at] = by_turn(*lines, "gx")
        for e, plane in enumerate(ends):
            at = slice(3 * planes + 2 * k + e, 3 * planes + 2 * k + e + 1)
            lines = [plane[:1], plane[rows - 1 :]]
            y_first_ref[at], y_second_ref[at] = by_turn(*lines, "gy")


def by_turn(one, other, axis):
    odd = lax.axis_index(axis) % 2 == 1
    return jnp.where(odd, one, other), jnp.where(odd, other, one)


def has_beside(axis):
    at = lax.axis_index(axis)
    return at > 0, at < lax.axis_size(axis) - 1


def reached(rows):
    others = [j for j in range(rows) if 2 <= j < rows - 2]
    return [j for j in range(rows) if j not in others], others


def inside_kernel(
    b_ref, cond_ref, cap_ref, y_link_ref, z_link_ref, inner_ref, draw_ref, low_ref, high_ref,
    got_second_ref, got_first_ref, wide_ref, x_link_ref, beside_ref, sketch_ref, cells_ref,
):
    planes, rows = b_ref.shape[:2]
    (image_low, image_high), (b_low, b_high), (c_low, c_high) = (
        by_turn(*(ref[k * rows : (k + 1) * rows] for ref in (got_first_ref, got_second_ref)), "gx")
        for k in range(3)
    )
    below, above = has_beside("gx")
    c_low, c_high = jnp.where(below, c_low, 0.0), jnp.where(above, c_high, 0.0)
    for k, plane in enumerate((b_low, b_high, c_low, c_high)):
        beside_ref[k] = plane
    conds = [c_low] + [cond_ref[i] for i in range(planes)] + [c_high]
    x_links = [link(conds[i], conds[i + 1]) for i in range(planes + 1)]
    for i, conductance in enumerate(x_links):
        x_link_ref[i] = conductance
    low_flow = x_links[0] * (b_low - b_ref[0])
    high_flow = x_links[-1] * (b_ref[planes - 1] - b_high)
    images = [image_low + low_flow] + [inner_ref[i] for i in range(planes)]
    images.append(image_high - high_flow)
    images[1] = images[1] - low_flow
    images[-2] = images[-2] + high_flow
    for i, image in enumerate(images):
        wide_ref[i] = image
    links = [(y_link_ref[i], z_link_ref[i]) for i in range(planes)]
    twice = apply_inside(images, x_links, links, [cap_ref[i] for i in range(planes)])
    chosen = reached(rows)[1]
    cells = [((images[i + 1], twice[i]), draw_ref[i], chosen) for i in range(planes)]
    sketch_ref[...] = sketch_rows(cells, low_ref, high_ref, cells_ref)


def third_kernel(
    b_ref, cap_ref, y_link_ref, z_link_ref, draw_ref, low_ref, high_ref, own_second_ref,
    own_first_ref, wide_ref, x_link_ref, beside_ref, x_second_ref, x_first_ref, y_second_ref,
    y_first_ref, b_sketch_ref, inside_ref, image_ref, twice_ref, sketch_ref, corner_first_ref,
    corner_second_ref, ends_ref, cells_ref, extra_ref,
):
    planes, rows, depth = b_ref.shape
    index = lax.broadcasted_iota(jnp.int32, (rows, depth), 0)
    images = [wide_ref[i] for i in range(planes + 2)]
    x_links = [x_link_ref[i] for i in range(planes + 1)]
    b_beside, c_beside = (beside_ref[0], beside_ref[1]), (beside_ref[2], beside_ref[3])
    x_ends = []
    for end, i in enumerate((0, planes - 1)):
        conductance = x_links[-end]
        x_ends.append((i, conductance, conductance * (b_ref[i] - b_beside[end])))
    x_tails = by_turn(x_first_ref[3 * rows :], x_second_ref[3 * rows :], "gx")
    own_lines = by_turn(own_first_ref[...], own_second_ref[...], "gy")
    y_lines = by_turn(y_first_ref[...], y_second_ref[...], "gy")
    beside = []
    for side, (j, here, own, line) in enumerate(
        zip((0, rows - 1), has_beside("gy"), own_lines, y_lines)
    ):
        row = slice(j, j + 1)
        beyond, b_line, c_line = (line[k * planes : (k + 1) * planes] for k in range(3))
        c_line = jnp.where(here, c_line, 0.0)
        y_link = link(own[2 * planes : 3 * planes], c_line)
        y_flow = y_link * (own[planes : 2 * planes] - b_line)
        beyond = beyond - y_flow
        for i in range(planes):
            at = slice(i, i + 1)
            images[i + 1] = images[i + 1] + jnp.where(index == j, y_flow[at], 0.0)
            beside.append((i, jnp.where(index == j, y_link[at], 0.0), beyond[at]))
        for end, (i, x_link, x_flow) in enumerate(x_ends):
            line_at, at = slice(i, i + 1), 4 * side + 2 * end
            tail = x_tails[end]
            values = -x_link[row] * y_flow[line_at], tail[side:][:1], tail[2 + side :][:1]
            for k, value in enumerate(values):
                extra_ref[k, at : at + 1] = value
            tail = line[3 * planes :]
            values = -y_link[line_at] * x_flow[row], tail[end:][:1], tail[2 + end :][:1]
            for k, value in enumerate(values):
                extra_ref[k, at + 1 : at + 2] = value
            at = 6 * (2 * side + end)
            values = x_link[row], b_beside[end][row], c_beside[end][row]
            values += y_link[line_at], b_line[line_at], c_line[line_at]
            for k, value in enumerate(values):
                ends_ref[at + k : at + k + 1] = value
    links = [(y_link_ref[i], z_link_ref[i]) for i in range(planes)]
    twice = apply_inside(images, x_links, links, [cap_ref[i] for i in range(planes)])
    for i, conductance, value in beside:
        twice[i] = twice[i] + conductance * (images[i + 1] - value)
    for i in range(planes):
        image_ref[i] = images[i + 1]
        twice_ref[i] = twice[i]
    chosen = reached(rows)[0]
    cells = [((images[i + 1], twice[i]), draw_ref[i], chosen) for i in range(planes)]
    total = inside_ref[...] + sketch_rows(cells, low_ref, high_ref, cells_ref)
    start = planes * rows * 8
    put_cells((jnp.zeros((8, depth), jnp.float32), extra_ref[0]), extra_ref[1], start, cells_ref)
    low, high = parts_of(extra_ref[2])
    left, right = [], []
    for j in range(8):
        mask = one_hot(high, j, HIGH, 2 * PAIR)
        left.append(masked_cells(mask, start, j, cells_ref))
        right.append(one_hot(low, j, LOW, 1))
    sketch_ref[1 : 1 + PAIR] = as_sketch(total + product(left, right))
    sketch_ref[:1] = b_sketch_ref[:1]
    sketch_ref[1 + PAIR :] = b_sketch_ref[:1]
    for k, plane in enumerate(b_beside + c_beside):
        at = slice(k, k + 1)
        corner_first_ref[at], corner_second_ref[at] = by_turn(
            plane[:1], plane[rows - 1 :], "gy"
        )


def last_kernel(
    sketch_ref, b_ref, image_ref, twice_ref, ends_ref, corner_first_ref, corner_second_ref,
    solution_ref, residual_ref,
):
    sketches = jnp.sum(sketch_ref[...], axis=0)

    def inner(first, second):
        return jnp.sum(first * second, axis=1, keepdims=True)

    s0, s1, s2 = (sketches[i : i + 1] for i in range(FIELDS))
    beta_inverse = 1.0 / jnp.sqrt(inner(s0, s0) + epsilon)
    h00 = inner(s0, s1) * beta_inverse * beta_inverse
    q0, p0 = s0 * beta_inverse, s1 * beta_inverse
    t0 = p0 - h00 * q0
    p1 = s2 * beta_inverse - h00 * p0
    n0 = jnp.sqrt(inner(t0, t0) + epsilon)
    n0_inverse = 1.0 / n0
    h01 = inner(q0, p1) * n0_inverse
    h11 = inner(t0, p1) * n0_inverse * n0_inverse
    t1 = p1 * n0_inverse - h01 * q0 - h11 * (t0 * n0_inverse)
    n1_square = inner(t1, t1) + epsilon
    first = h00 * h00 + n0 * n0
    cross = h00 * h01 + n0 * h11
    ratio = cross / first
    second = h01 * h01 + h11 * h11 + n1_square - cross * ratio
    y1 = (h01 - ratio * h00) / second
    y0 = h00 / first - ratio * y1
    c1 = y1 * n0_inverse
    c0 = y0 - h00 * c1
    planes, rows, depth = b_ref.shape
    for i in range(planes):
        b, image = b_ref[i], image_ref[i]
        solution_ref[i] = c0 * b + c1 * image
        residual_ref[i] = b - c0 * image - c1 * twice_ref[i]
    corners = by_turn(corner_first_ref[...], corner_second_ref[...], "gy")
    for side, (j, here, corner) in enumerate(zip((0, rows - 1), has_beside("gy"), corners)):
        for end, i in enumerate((0, planes - 1)):
            b, cond = corner[end : end + 1], corner[2 + end : 3 + end]
            cond = jnp.where(here, cond, 0.0)
            at = 6 * (2 * side + end)
            x_link, x_b, x_cond, y_link, y_b, y_cond = (
                ends_ref[at + k : at + k + 1] for k in range(6)
            )
            lacked = x_link * link(x_cond, cond) * (x_b - b)
            lacked = lacked + y_link * link(y_cond, cond) * (y_b - b)
            residual_ref[i, j : j + 1] = residual_ref[i, j : j + 1] + c1 * lacked


def call(kernel, shapes, *operands, scratch=(), inputs=pltpu.VMEM, flops=0):
    return pl.pallas_call(
        kernel,
        out_shape=[
            shape if hasattr(shape, "dtype") else jax.ShapeDtypeStruct(shape, jnp.float32)
            for shape in shapes
        ],
        in_specs=[pl.BlockSpec(memory_space=inputs)] * len(operands),
        out_specs=[pl.BlockSpec(memory_space=pltpu.VMEM)] * len(shapes),
        scratch_shapes=scratch,
        compiler_params=pltpu.CompilerParams(vmem_limit_bytes=48 * 1024 * 1024),
        cost_estimate=pl.CostEstimate(flops=flops, bytes_accessed=0, transcendentals=0),
    )(*operands)


def swap(array, axis, turn):
    nx, ny = lax.axis_size("gx"), lax.axis_size("gy")
    pairs = []
    for x in range(nx):
        for y in range(ny):
            here, count = (x, nx) if axis == "gx" else (y, ny)
            there = here + 1 if here % 2 == turn else here - 1
            if 0 <= there < count:
                partner = (there, y) if axis == "gx" else (x, there)
            else:
                partner = (x, y ^ 1) if axis == "gx" else (x ^ 1, y)
            pairs.append((x * ny + y, partner[0] * ny + partner[1]))
    return lax.ppermute(array, ("gx", "gy"), pairs)


def everyones(sketch):
    nx, ny = lax.axis_size("gx"), lax.axis_size("gy")
    middle = nx // 2 - 1, (ny - 1) // 2
    places = [(x, y) for x in range(nx) for y in range(ny)]
    places.sort(key=lambda at: (abs(at[1] - middle[1]), abs(at[0] - middle[0]), at))
    group = [x * ny + y for x, y in places]
    copies = jnp.broadcast_to(sketch[None], (nx * ny,) + sketch.shape)
    return lax.all_to_all(copies, ("gx", "gy"), 0, 0, axis_index_groups=[group])


def body(b, warmth, phase, slots, draw):
    planes, rows, depth = b.shape
    block, wide = b.shape, (planes + 2, rows, depth)
    face, line, corner = (3 * rows + 4, depth), (3 * planes + 4, depth), (4, depth)
    cells = pltpu.VMEM((depth // LANES, (planes * rows + 8) * 8, LANES), jnp.float32)
    total = HIGH * 2 * PAIR, LOW
    hots = [
        jax.ShapeDtypeStruct((planes * rows * count, depth), jnp.bfloat16)
        for count in (LOW, HIGH * 2 * PAIR)
    ]
    work = b.size * SKETCH * 6
    b, cond, cap, y_link, z_link, inner, draw, slots, x_first, x_second, y_first, y_second = call(
        first_kernel,
        [block] * 8 + [face, face, line, line],
        *(
            pltpu.with_memory_space_constraint(x, pltpu.HBM)
            for x in (b, warmth, phase, draw, slots)
        ),
        scratch=[
            pltpu.VMEM(block, warmth.dtype),
            pltpu.VMEM(block, phase.dtype),
            pltpu.VMEM(block, slots.dtype),
            pltpu.SemaphoreType.DMA((5,)),
        ],
        inputs=pltpu.HBM,
    )
    got_x = swap(x_second, "gx", 1), swap(x_first, "gx", 0)
    got_y = swap(y_second, "gy", 1), swap(y_first, "gy", 0)
    *hots, b_sketch = call(
        slot_kernel, [*hots, (PAIR, SKETCH)], b, draw, slots, scratch=[cells], flops=work
    )
    image_wide, x_link, beside, inside = call(
        inside_kernel,
        [wide, (planes + 1, rows, depth), (4, rows, depth), total],
        b, cond, cap, y_link, z_link, inner, draw, *hots, *got_x,
        scratch=[cells],
        flops=work,
    )
    image, twice, sketch, first, second, ends = call(
        third_kernel,
        [block, block, (FIELDS + 1, SKETCH), corner, corner, (24, depth)],
        b, cap, y_link, z_link, draw, *hots, y_second, y_first, image_wide, x_link, beside,
        *got_x, *got_y, b_sketch, inside,
        scratch=[cells, pltpu.VMEM((3, 8, depth), jnp.float32)],
        flops=work,
    )
    got_corners = [swap(array, "gy", turn) for turn, array in enumerate((first, second))]
    sketches = everyones(sketch)
    return tuple(
        call(last_kernel, [block, block], sketches, b, image, twice, ends, *got_corners)
    )


def solution(mesh):
    spec = P(("parts", "gx"), "gy", None)
    return jax.shard_map(
        body, mesh=mesh, in_specs=(spec,) * 5, out_specs=(spec,) * 2, check_vma=False
    )
```

```python
import jax
import jax.numpy as jnp
from jax import lax
from jax.experimental import pallas as pl
from jax.experimental.pallas import tpu as pltpu
from jax.sharding import PartitionSpec as P

SKETCH = 128
LOW = 32
HIGH = SKETCH // LOW
FIELDS = 3
PAIR = 2
LANES = 128
epsilon = 1e-06


def traits(warmth, phase):
    powder, solid = phase == 0, phase == 1
    offset = jnp.where(powder, 0.2, jnp.where(solid, 1.0, 0.6))
    return offset * (0.5 + warmth), jnp.where(powder, 1.0, jnp.where(solid, 2.0, 1.5))


def link(first, second):
    total = first + second
    return 2.0 * first * second / jnp.where(total > 0.0, total, 1.0)


def ahead(plane, axis):
    return pltpu.roll(plane, plane.shape[axis] - 1, axis)


def inner_links(cond):
    links = []
    for axis in (0, 1):
        index = lax.broadcasted_iota(jnp.int32, cond.shape, axis)
        links.append(
            jnp.where(index < cond.shape[axis] - 1, link(cond, ahead(cond, axis)), 0.0)
        )
    return links


def inner_flow(field, links):
    total = None
    for axis in (0, 1):
        flow = links[axis] * (field - ahead(field, axis))
        part = flow - pltpu.roll(flow, 1, axis)
        total = part if total is None else total + part
    return total


def apply_inside(images, x_links, links, caps):
    results = []
    flow_low = x_links[0] * (images[0] - images[1])
    for i in range(1, len(images) - 1):
        image = images[i]
        flow = x_links[i] * (image - images[i + 1])
        inside = inner_flow(image, links[i - 1])
        results.append(caps[i - 1] * image + inside + (flow - flow_low))
        flow_low = flow
    return results


def parts_of(slot):
    high = jnp.floor(slot * (1.0 / LOW))
    return slot - LOW * high, high


def one_hot(values, j, count, each):
    shape = (count * each, values.shape[1])
    index = lax.broadcasted_iota(jnp.int32, shape, 0) // each
    index = index.astype(jnp.float32).astype(jnp.bfloat16)
    row = jnp.broadcast_to(values[j : j + 1], shape).astype(jnp.bfloat16)
    one = jnp.ones_like(row)
    return jnp.where(row == index, one, jnp.zeros_like(one))


def put_cells(fields, draw, start, cells_ref):
    coarse, fine = [], []
    for field in fields:
        weighted = draw * field
        head = weighted.astype(jnp.bfloat16).astype(jnp.float32)
        coarse.append(head)
        fine.append(weighted - head)
    for f, part in enumerate((coarse + fine) * 2):
        for t in range(cells_ref.shape[0]):
            cells_ref[t, pl.ds(start + f, draw.shape[0], stride=8), :] = part[
                :, t * LANES : (t + 1) * LANES
            ]


def masked_cells(mask, start, j, cells_ref):
    at = pl.ds(start + j * 8, 8)
    cells = jnp.concatenate([cells_ref[t, at, :] for t in range(cells_ref.shape[0])], axis=1)
    return jnp.concatenate([cells, cells], axis=0).astype(jnp.bfloat16) * mask


def product(left, right):
    return lax.dot_general(
        jnp.concatenate(left, axis=1),
        jnp.concatenate(right, axis=1),
        (((1,), (1,)), ((), ())),
        preferred_element_type=jnp.float32,
    )


def as_sketch(total):
    each = 2 * PAIR
    total = jnp.concatenate([total[h * each : (h + 1) * each] for h in range(HIGH)], axis=1)
    return total[:PAIR] + total[PAIR:]


def sketch_rows(planes, low_ref, high_ref, cells_ref):
    total = 0.0
    each = HIGH * 2 * PAIR
    for i, (fields, draw, chosen) in enumerate(planes):
        rows = draw.shape[0]
        start = i * rows * 8
        put_cells(fields, draw, start, cells_ref)
        left, right = [], []
        for j in chosen:
            at = i * rows + j
            mask = high_ref[at * each : (at + 1) * each]
            left.append(masked_cells(mask, start, j, cells_ref))
            right.append(low_ref[at * LOW : (at + 1) * LOW])
        total = total + product(left, right)
    return total


def slot_kernel(b_ref, draw_ref, slot_ref, low_ref, high_ref, sketch_ref, cells_ref):
    planes, rows = b_ref.shape[:2]
    each = HIGH * 2 * PAIR
    total = 0.0
    for i in range(planes):
        start = i * rows * 8
        put_cells((b_ref[i],) * PAIR, draw_ref[i], start, cells_ref)
        low, high = parts_of(slot_ref[i])
        left, right = [], []
        for j in range(rows):
            at = i * rows + j
            mask, hot = one_hot(high, j, HIGH, 2 * PAIR), one_hot(low, j, LOW, 1)
            high_ref[at * each : (at + 1) * each] = mask
            low_ref[at * LOW : (at + 1) * LOW] = hot
            left.append(masked_cells(mask, start, j, cells_ref))
            right.append(hot)
        total = total + product(left, right)
    sketch_ref[...] = as_sketch(total)


def first_kernel(
    b_hbm, warmth_hbm, phase_hbm, draw_hbm, slot_hbm, b_ref, cond_ref, cap_ref, y_link_ref,
    z_link_ref, inner_ref, draw_ref, slot_ref, x_first_ref, x_second_ref, y_first_ref,
    y_second_ref, warmth_ref, phase_ref, number_ref, arrived,
):
    copies = [
        pltpu.make_async_copy(source, target, arrived.at[k])
        for k, (source, target) in enumerate(
            (
                (b_hbm, b_ref),
                (warmth_hbm, warmth_ref),
                (phase_hbm, phase_ref),
                (draw_hbm, draw_ref),
                (slot_hbm, number_ref),
            )
        )
    ]
    for copy in copies:
        copy.start()
    for copy in copies[:3]:
        copy.wait()
    planes, rows = b_ref.shape[:2]
    images, conds = [], []
    for i in range(planes):
        cond, cap = traits(warmth_ref[i], phase_ref[i])
        cap_ref[i] = cap
        cond_ref[i] = cond
        y_link_ref[i], z_link_ref[i] = links = inner_links(cond)
        field = b_ref[i]
        image = cap * field + inner_flow(field, links)
        if i:
            flow = link(conds[-1], cond) * (b_ref[i - 1] - field)
            images[-1] = images[-1] + flow
            image = image - flow
        conds.append(cond)
        images.append(image)
    for i in range(planes):
        inner_ref[i] = images[i]
    for k, field in enumerate((images, [b_ref[i] for i in range(planes)], conds)):
        at = slice(k * rows, (k + 1) * rows)
        x_first_ref[at], x_second_ref[at] = by_turn(field[0], field[-1], "gx")
        for i, plane in enumerate(field):
            at = slice(k * planes + i, k * planes + i + 1)
            y_first_ref[at], y_second_ref[at] = by_turn(plane[:1], plane[rows - 1 :], "gy")
    for copy in copies[3:]:
        copy.wait()
    for i in range(planes):
        slot_ref[i] = number_ref[i].astype(jnp.float32)
    for k, ref in enumerate((draw_ref, slot_ref)):
        ends = [ref[0], ref[planes - 1]]
        for e, j in enumerate((0, rows - 1)):
            at = slice(3 * rows + 2 * k + e, 3 * rows + 2 * k + e + 1)
            lines = [plane[j : j + 1] for plane in ends]
            x_first_ref[at], x_second_ref[at] = by_turn(*lines, "gx")
        for e, plane in enumerate(ends):
            at = slice(3 * planes + 2 * k + e, 3 * planes + 2 * k + e + 1)
            lines = [plane[:1], plane[rows - 1 :]]
            y_first_ref[at], y_second_ref[at] = by_turn(*lines, "gy")


def by_turn(one, other, axis):
    odd = lax.axis_index(axis) % 2 == 1
    return jnp.where(odd, one, other), jnp.where(odd, other, one)


def has_beside(axis):
    at = lax.axis_index(axis)
    return at > 0, at < lax.axis_size(axis) - 1


def reached(rows):
    others = [j for j in range(rows) if 2 <= j < rows - 2]
    return [j for j in range(rows) if j not in others], others


def inside_kernel(
    b_ref, cond_ref, cap_ref, y_link_ref, z_link_ref, inner_ref, draw_ref, low_ref, high_ref,
    got_second_ref, got_first_ref, wide_ref, x_link_ref, beside_ref, sketch_ref, cells_ref,
):
    planes, rows = b_ref.shape[:2]
    (image_low, image_high), (b_low, b_high), (c_low, c_high) = (
        by_turn(*(ref[k * rows : (k + 1) * rows] for ref in (got_first_ref, got_second_ref)), "gx")
        for k in range(3)
    )
    below, above = has_beside("gx")
    c_low, c_high = jnp.where(below, c_low, 0.0), jnp.where(above, c_high, 0.0)
    for k, plane in enumerate((b_low, b_high, c_low, c_high)):
        beside_ref[k] = plane
    conds = [c_low] + [cond_ref[i] for i in range(planes)] + [c_high]
    x_links = [link(conds[i], conds[i + 1]) for i in range(planes + 1)]
    for i, conductance in enumerate(x_links):
        x_link_ref[i] = conductance
    low_flow = x_links[0] * (b_low - b_ref[0])
    high_flow = x_links[-1] * (b_ref[planes - 1] - b_high)
    images = [image_low + low_flow] + [inner_ref[i] for i in range(planes)]
    images.append(image_high - high_flow)
    images[1] = images[1] - low_flow
    images[-2] = images[-2] + high_flow
    for i, image in enumerate(images):
        wide_ref[i] = image
    links = [(y_link_ref[i], z_link_ref[i]) for i in range(planes)]
    twice = apply_inside(images, x_links, links, [cap_ref[i] for i in range(planes)])
    chosen = reached(rows)[1]
    cells = [((images[i + 1], twice[i]), draw_ref[i], chosen) for i in range(planes)]
    sketch_ref[...] = sketch_rows(cells, low_ref, high_ref, cells_ref)


def third_kernel(
    b_ref, cap_ref, y_link_ref, z_link_ref, draw_ref, low_ref, high_ref, own_second_ref,
    own_first_ref, wide_ref, x_link_ref, beside_ref, x_second_ref, x_first_ref, y_second_ref,
    y_first_ref, b_sketch_ref, inside_ref, image_ref, twice_ref, sketch_hbm, corner_first_ref,
    corner_second_ref, ends_ref, cells_ref, extra_ref, copies_ref, sent,
):
    planes, rows, depth = b_ref.shape
    index = lax.broadcasted_iota(jnp.int32, (rows, depth), 0)
    images = [wide_ref[i] for i in range(planes + 2)]
    x_links = [x_link_ref[i] for i in range(planes + 1)]
    b_beside, c_beside = (beside_ref[0], beside_ref[1]), (beside_ref[2], beside_ref[3])
    x_ends = []
    for end, i in enumerate((0, planes - 1)):
        conductance = x_links[-end]
        x_ends.append((i, conductance, conductance * (b_ref[i] - b_beside[end])))
    x_tails = by_turn(x_first_ref[3 * rows :], x_second_ref[3 * rows :], "gx")
    own_lines = by_turn(own_first_ref[...], own_second_ref[...], "gy")
    y_lines = by_turn(y_first_ref[...], y_second_ref[...], "gy")
    beside, ends = [], []
    for side, (j, here, own, line) in enumerate(
        zip((0, rows - 1), has_beside("gy"), own_lines, y_lines)
    ):
        row = slice(j, j + 1)
        beyond, b_line, c_line = (line[k * planes : (k + 1) * planes] for k in range(3))
        c_line = jnp.where(here, c_line, 0.0)
        y_link = link(own[2 * planes : 3 * planes], c_line)
        y_flow = y_link * (own[planes : 2 * planes] - b_line)
        beyond = beyond - y_flow
        for i in range(planes):
            at = slice(i, i + 1)
            images[i + 1] = images[i + 1] + jnp.where(index == j, y_flow[at], 0.0)
            beside.append((i, jnp.where(index == j, y_link[at], 0.0), beyond[at]))
        for end, (i, x_link, x_flow) in enumerate(x_ends):
            line_at, at = slice(i, i + 1), 4 * side + 2 * end
            tail = x_tails[end]
            values = -x_link[row] * y_flow[line_at], tail[side:][:1], tail[2 + side :][:1]
            for k, value in enumerate(values):
                extra_ref[k, at : at + 1] = value
            tail = line[3 * planes :]
            values = -y_link[line_at] * x_flow[row], tail[end:][:1], tail[2 + end :][:1]
            for k, value in enumerate(values):
                extra_ref[k, at + 1 : at + 2] = value
            values = x_link[row], b_beside[end][row], c_beside[end][row]
            values += y_link[line_at], b_line[line_at], c_line[line_at]
            ends.append(values)
    links = [(y_link_ref[i], z_link_ref[i]) for i in range(planes)]
    twice = apply_inside(images, x_links, links, [cap_ref[i] for i in range(planes)])
    for i, conductance, value in beside:
        twice[i] = twice[i] + conductance * (images[i + 1] - value)
    for i in range(planes):
        image_ref[i] = images[i + 1]
        twice_ref[i] = twice[i]
    chosen = reached(rows)[0]
    cells = [((images[i + 1], twice[i]), draw_ref[i], chosen) for i in range(planes)]
    total = inside_ref[...] + sketch_rows(cells, low_ref, high_ref, cells_ref)
    start = planes * rows * 8
    put_cells((jnp.zeros((8, depth), jnp.float32), extra_ref[0]), extra_ref[1], start, cells_ref)
    low, high = parts_of(extra_ref[2])
    left, right = [], []
    for j in range(8):
        mask = one_hot(high, j, HIGH, 2 * PAIR)
        left.append(masked_cells(mask, start, j, cells_ref))
        right.append(one_hot(low, j, LOW, 1))
    sketch = as_sketch(total + product(left, right))
    for device in range(copies_ref.shape[0]):
        copies_ref[device, 1 : 1 + PAIR] = sketch
        copies_ref[device, :1] = b_sketch_ref[:1]
        copies_ref[device, 1 + PAIR :] = b_sketch_ref[:1]
    copy = pltpu.make_async_copy(copies_ref, sketch_hbm, sent)
    copy.start()
    for at, value in enumerate(sum(ends, ())):
        ends_ref[at : at + 1] = value
    for k, plane in enumerate(b_beside + c_beside):
        at = slice(k, k + 1)
        corner_first_ref[at], corner_second_ref[at] = by_turn(
            plane[:1], plane[rows - 1 :], "gy"
        )
    copy.wait()


def last_kernel(
    sketch_ref, b_ref, image_ref, twice_ref, ends_ref, corner_first_ref, corner_second_ref,
    solution_ref, residual_ref,
):
    sketches = jnp.sum(sketch_ref[...], axis=0)

    def inner(first, second):
        return jnp.sum(first * second, axis=1, keepdims=True)

    s0, s1, s2 = (sketches[i : i + 1] for i in range(FIELDS))
    beta_inverse = 1.0 / jnp.sqrt(inner(s0, s0) + epsilon)
    h00 = inner(s0, s1) * beta_inverse * beta_inverse
    q0, p0 = s0 * beta_inverse, s1 * beta_inverse
    t0 = p0 - h00 * q0
    p1 = s2 * beta_inverse - h00 * p0
    n0 = jnp.sqrt(inner(t0, t0) + epsilon)
    n0_inverse = 1.0 / n0
    h01 = inner(q0, p1) * n0_inverse
    h11 = inner(t0, p1) * n0_inverse * n0_inverse
    t1 = p1 * n0_inverse - h01 * q0 - h11 * (t0 * n0_inverse)
    n1_square = inner(t1, t1) + epsilon
    first = h00 * h00 + n0 * n0
    cross = h00 * h01 + n0 * h11
    ratio = cross / first
    second = h01 * h01 + h11 * h11 + n1_square - cross * ratio
    y1 = (h01 - ratio * h00) / second
    y0 = h00 / first - ratio * y1
    c1 = y1 * n0_inverse
    c0 = y0 - h00 * c1
    planes, rows, depth = b_ref.shape
    for i in range(planes):
        b, image = b_ref[i], image_ref[i]
        solution_ref[i] = c0 * b + c1 * image
        residual_ref[i] = b - c0 * image - c1 * twice_ref[i]
    corners = by_turn(corner_first_ref[...], corner_second_ref[...], "gy")
    for side, (j, here, corner) in enumerate(zip((0, rows - 1), has_beside("gy"), corners)):
        for end, i in enumerate((0, planes - 1)):
            b, cond = corner[end : end + 1], corner[2 + end : 3 + end]
            cond = jnp.where(here, cond, 0.0)
            at = 6 * (2 * side + end)
            x_link, x_b, x_cond, y_link, y_b, y_cond = (
                ends_ref[at + k : at + k + 1] for k in range(6)
            )
            lacked = x_link * link(x_cond, cond) * (x_b - b)
            lacked = lacked + y_link * link(y_cond, cond) * (y_b - b)
            residual_ref[i, j : j + 1] = residual_ref[i, j : j + 1] + c1 * lacked


def call(kernel, shapes, *operands, scratch=(), inputs=pltpu.VMEM, in_hbm=(), flops=0):
    return pl.pallas_call(
        kernel,
        out_shape=[
            shape if hasattr(shape, "dtype") else jax.ShapeDtypeStruct(shape, jnp.float32)
            for shape in shapes
        ],
        in_specs=[pl.BlockSpec(memory_space=inputs)] * len(operands),
        out_specs=[
            pl.BlockSpec(memory_space=pltpu.HBM if k in in_hbm else pltpu.VMEM)
            for k in range(len(shapes))
        ],
        scratch_shapes=scratch,
        compiler_params=pltpu.CompilerParams(vmem_limit_bytes=48 * 1024 * 1024),
        cost_estimate=pl.CostEstimate(flops=flops, bytes_accessed=0, transcendentals=0),
    )(*operands)


def swap(array, axis, turn):
    nx, ny = lax.axis_size("gx"), lax.axis_size("gy")
    pairs = []
    for x in range(nx):
        for y in range(ny):
            here, count = (x, nx) if axis == "gx" else (y, ny)
            there = here + 1 if here % 2 == turn else here - 1
            if 0 <= there < count:
                partner = (there, y) if axis == "gx" else (x, there)
            else:
                partner = (x, y ^ 1) if axis == "gx" else (x ^ 1, y)
            pairs.append((x * ny + y, partner[0] * ny + partner[1]))
    return lax.ppermute(array, ("gx", "gy"), pairs)


def everyones(copies):
    nx, ny = lax.axis_size("gx"), lax.axis_size("gy")
    middle = nx // 2 - 1, ny // 2
    places = [(x, y) for x in range(nx) for y in range(ny)]
    places.sort(key=lambda at: (abs(at[1] - middle[1]), abs(at[0] - middle[0]), at))
    group = [x * ny + y for x, y in places]
    return lax.all_to_all(copies, ("gx", "gy"), 0, 0, axis_index_groups=[group])


def body(b, warmth, phase, slots, draw):
    planes, rows, depth = b.shape
    block, wide = b.shape, (planes + 2, rows, depth)
    face, line, corner = (3 * rows + 4, depth), (3 * planes + 4, depth), (4, depth)
    cells = pltpu.VMEM((depth // LANES, (planes * rows + 8) * 8, LANES), jnp.float32)
    total = HIGH * 2 * PAIR, LOW
    hots = [
        jax.ShapeDtypeStruct((planes * rows * count, depth), jnp.bfloat16)
        for count in (LOW, HIGH * 2 * PAIR)
    ]
    work = b.size * SKETCH * 6
    b, cond, cap, y_link, z_link, inner, draw, slots, x_first, x_second, y_first, y_second = call(
        first_kernel,
        [block] * 8 + [face, face, line, line],
        *(
            pltpu.with_memory_space_constraint(x, pltpu.HBM)
            for x in (b, warmth, phase, draw, slots)
        ),
        scratch=[
            pltpu.VMEM(block, warmth.dtype),
            pltpu.VMEM(block, phase.dtype),
            pltpu.VMEM(block, slots.dtype),
            pltpu.SemaphoreType.DMA((5,)),
        ],
        inputs=pltpu.HBM,
    )
    got_x = swap(x_second, "gx", 1), swap(x_first, "gx", 0)
    got_y = swap(y_second, "gy", 1), swap(y_first, "gy", 0)
    *hots, b_sketch = call(
        slot_kernel, [*hots, (PAIR, SKETCH)], b, draw, slots, scratch=[cells], flops=work
    )
    image_wide, x_link, beside, inside = call(
        inside_kernel,
        [wide, (planes + 1, rows, depth), (4, rows, depth), total],
        b, cond, cap, y_link, z_link, inner, draw, *hots, *got_x,
        scratch=[cells],
        flops=work,
    )
    copies = lax.axis_size("gx") * lax.axis_size("gy"), FIELDS + 1, SKETCH
    image, twice, copies, first, second, ends = call(
        third_kernel,
        [block, block, copies, corner, corner, (24, depth)],
        b, cap, y_link, z_link, draw, *hots, y_second, y_first, image_wide, x_link, beside,
        *got_x, *got_y, b_sketch, inside,
        scratch=[
            cells,
            pltpu.VMEM((3, 8, depth), jnp.float32),
            pltpu.VMEM(copies, jnp.float32),
            pltpu.SemaphoreType.DMA,
        ],
        in_hbm=(2,),
        flops=work,
    )
    got_corners = [swap(array, "gy", turn) for turn, array in enumerate((first, second))]
    sketches = everyones(copies)
    return tuple(
        call(last_kernel, [block, block], sketches, b, image, twice, ends, *got_corners)
    )


def solution(mesh):
    spec = P(("parts", "gx"), "gy", None)
    return jax.shard_map(
        body, mesh=mesh, in_specs=(spec,) * 5, out_specs=(spec,) * 2, check_vma=False
    )
```

```python
import jax
import jax.numpy as jnp
from jax import lax
from jax.experimental import pallas as pl
from jax.experimental.pallas import tpu as pltpu
from jax.sharding import PartitionSpec as P

SKETCH = 128
LOW = 32
HIGH = SKETCH // LOW
FIELDS = 3
PAIR = 2
LANES = 128
epsilon = 1e-06


def traits(warmth, phase):
    powder, solid = phase == 0, phase == 1
    offset = jnp.where(powder, 0.2, jnp.where(solid, 1.0, 0.6))
    return offset * (0.5 + warmth), jnp.where(powder, 1.0, jnp.where(solid, 2.0, 1.5))


def link(first, second):
    total = first + second
    return 2.0 * first * second / jnp.where(total > 0.0, total, 1.0)


def ahead(plane, axis):
    return pltpu.roll(plane, plane.shape[axis] - 1, axis)


def inner_links(cond):
    links = []
    for axis in (0, 1):
        index = lax.broadcasted_iota(jnp.int32, cond.shape, axis)
        links.append(
            jnp.where(index < cond.shape[axis] - 1, link(cond, ahead(cond, axis)), 0.0)
        )
    return links


def inner_flow(field, links):
    total = None
    for axis in (0, 1):
        flow = links[axis] * (field - ahead(field, axis))
        part = flow - pltpu.roll(flow, 1, axis)
        total = part if total is None else total + part
    return total


def apply_inside(images, x_links, links, caps):
    results = []
    flow_low = x_links[0] * (images[0] - images[1])
    for i in range(1, len(images) - 1):
        image = images[i]
        flow = x_links[i] * (image - images[i + 1])
        inside = inner_flow(image, links[i - 1])
        results.append(caps[i - 1] * image + inside + (flow - flow_low))
        flow_low = flow
    return results


def parts_of(slot):
    high = jnp.floor(slot * (1.0 / LOW))
    return slot - LOW * high, high


def one_hot(values, j, count, each):
    shape = (count * each, values.shape[1])
    index = lax.broadcasted_iota(jnp.int32, shape, 0) // each
    index = index.astype(jnp.float32).astype(jnp.bfloat16)
    row = jnp.broadcast_to(values[j : j + 1], shape).astype(jnp.bfloat16)
    one = jnp.ones_like(row)
    return jnp.where(row == index, one, jnp.zeros_like(one))


def put_cells(fields, draw, start, cells_ref):
    coarse, fine = [], []
    for field in fields:
        weighted = draw * field
        head = weighted.astype(jnp.bfloat16).astype(jnp.float32)
        coarse.append(head)
        fine.append(weighted - head)
    for f, part in enumerate((coarse + fine) * 2):
        for t in range(cells_ref.shape[0]):
            cells_ref[t, pl.ds(start + f, draw.shape[0], stride=8), :] = part[
                :, t * LANES : (t + 1) * LANES
            ]


def masked_cells(mask, start, j, cells_ref):
    at = pl.ds(pl.multiple_of(start + j * 8, 8), 8)
    cells = jnp.concatenate([cells_ref[t, at, :] for t in range(cells_ref.shape[0])], axis=1)
    return jnp.concatenate([cells, cells], axis=0).astype(jnp.bfloat16) * mask


def product(left, right):
    return lax.dot_general(
        jnp.concatenate(left, axis=1),
        jnp.concatenate(right, axis=1),
        (((1,), (1,)), ((), ())),
        preferred_element_type=jnp.float32,
    )


def as_sketch(total):
    each = 2 * PAIR
    total = jnp.concatenate([total[h * each : (h + 1) * each] for h in range(HIGH)], axis=1)
    return total[:PAIR] + total[PAIR:]


def sketch_rows(planes, low_ref, high_ref, cells_ref):
    total = 0.0
    each = HIGH * 2 * PAIR
    for i, (fields, draw, chosen) in enumerate(planes):
        rows = draw.shape[0]
        start = i * rows * 8
        put_cells(fields, draw, start, cells_ref)
        left, right = [], []
        for j in chosen:
            at = i * rows + j
            mask = high_ref[pl.ds(pl.multiple_of(at * each, each), each)]
            left.append(masked_cells(mask, start, j, cells_ref))
            right.append(low_ref[pl.ds(pl.multiple_of(at * LOW, LOW), LOW)])
        total = total + product(left, right)
    return total


def slot_kernel(b_ref, draw_ref, slot_ref, low_ref, high_ref, sketch_ref, cells_ref):
    planes, rows = b_ref.shape[:2]
    each = HIGH * 2 * PAIR
    total = 0.0
    for i in range(planes):
        start = i * rows * 8
        put_cells((b_ref[i],) * PAIR, draw_ref[i], start, cells_ref)
        low, high = parts_of(slot_ref[i])
        left, right = [], []
        for j in range(rows):
            at = i * rows + j
            mask, hot = one_hot(high, j, HIGH, 2 * PAIR), one_hot(low, j, LOW, 1)
            high_ref[at * each : (at + 1) * each] = mask
            low_ref[at * LOW : (at + 1) * LOW] = hot
            left.append(masked_cells(mask, start, j, cells_ref))
            right.append(hot)
        total = total + product(left, right)
    sketch_ref[...] = as_sketch(total)


def first_kernel(
    b_hbm, warmth_hbm, phase_hbm, draw_hbm, slot_hbm, b_ref, cond_ref, cap_ref, y_link_ref,
    z_link_ref, inner_ref, draw_ref, slot_ref, x_first_ref, x_second_ref, y_first_ref,
    y_second_ref, warmth_ref, phase_ref, number_ref, arrived,
):
    copies = [
        pltpu.make_async_copy(source, target, arrived.at[k])
        for k, (source, target) in enumerate(
            (
                (b_hbm, b_ref),
                (warmth_hbm, warmth_ref),
                (phase_hbm, phase_ref),
                (draw_hbm, draw_ref),
                (slot_hbm, number_ref),
            )
        )
    ]
    for copy in copies:
        copy.start()
    for copy in copies[:3]:
        copy.wait()
    planes, rows = b_ref.shape[:2]
    images, conds = [], []
    for i in range(planes):
        cond, cap = traits(warmth_ref[i], phase_ref[i])
        cap_ref[i] = cap
        cond_ref[i] = cond
        y_link_ref[i], z_link_ref[i] = links = inner_links(cond)
        field = b_ref[i]
        image = cap * field + inner_flow(field, links)
        if i:
            flow = link(conds[-1], cond) * (b_ref[i - 1] - field)
            images[-1] = images[-1] + flow
            image = image - flow
        conds.append(cond)
        images.append(image)
    for i in range(planes):
        inner_ref[i] = images[i]
    for k, field in enumerate((images, [b_ref[i] for i in range(planes)], conds)):
        at = slice(k * rows, (k + 1) * rows)
        x_first_ref[at], x_second_ref[at] = by_turn(field[0], field[-1], "gx")
        for i, plane in enumerate(field):
            at = slice(k * planes + i, k * planes + i + 1)
            y_first_ref[at], y_second_ref[at] = by_turn(plane[:1], plane[rows - 1 :], "gy")
    for copy in copies[3:]:
        copy.wait()
    for i in range(planes):
        slot_ref[i] = number_ref[i].astype(jnp.float32)
    for k, ref in enumerate((draw_ref, slot_ref)):
        ends = [ref[0], ref[planes - 1]]
        for e, j in enumerate((0, rows - 1)):
            at = slice(3 * rows + 2 * k + e, 3 * rows + 2 * k + e + 1)
            lines = [plane[j : j + 1] for plane in ends]
            x_first_ref[at], x_second_ref[at] = by_turn(*lines, "gx")
        for e, plane in enumerate(ends):
            at = slice(3 * planes + 2 * k + e, 3 * planes + 2 * k + e + 1)
            lines = [plane[:1], plane[rows - 1 :]]
            y_first_ref[at], y_second_ref[at] = by_turn(*lines, "gy")


def by_turn(one, other, axis):
    odd = lax.axis_index(axis) % 2 == 1
    return jnp.where(odd, one, other), jnp.where(odd, other, one)


def has_beside(axis):
    at = lax.axis_index(axis)
    return at > 0, at < lax.axis_size(axis) - 1


def reached(rows):
    others = [j for j in range(rows) if 2 <= j < rows - 2]
    return [j for j in range(rows) if j not in others], others


def inside_kernel(
    b_ref, cond_ref, cap_ref, y_link_ref, z_link_ref, inner_ref, draw_ref, low_ref, high_ref,
    got_second_ref, got_first_ref, wide_ref, x_link_ref, beside_ref, sketch_ref, cells_ref,
):
    planes, rows = b_ref.shape[:2]
    (image_low, image_high), (b_low, b_high), (c_low, c_high) = (
        by_turn(*(ref[k * rows : (k + 1) * rows] for ref in (got_first_ref, got_second_ref)), "gx")
        for k in range(3)
    )
    below, above = has_beside("gx")
    c_low, c_high = jnp.where(below, c_low, 0.0), jnp.where(above, c_high, 0.0)
    for k, plane in enumerate((b_low, b_high, c_low, c_high)):
        beside_ref[k] = plane
    conds = [c_low] + [cond_ref[i] for i in range(planes)] + [c_high]
    x_links = [link(conds[i], conds[i + 1]) for i in range(planes + 1)]
    for i, conductance in enumerate(x_links):
        x_link_ref[i] = conductance
    low_flow = x_links[0] * (b_low - b_ref[0])
    high_flow = x_links[-1] * (b_ref[planes - 1] - b_high)
    images = [image_low + low_flow] + [inner_ref[i] for i in range(planes)]
    images.append(image_high - high_flow)
    images[1] = images[1] - low_flow
    images[-2] = images[-2] + high_flow
    for i, image in enumerate(images):
        wide_ref[i] = image
    links = [(y_link_ref[i], z_link_ref[i]) for i in range(planes)]
    twice = apply_inside(images, x_links, links, [cap_ref[i] for i in range(planes)])
    chosen = reached(rows)[1]
    cells = [((images[i + 1], twice[i]), draw_ref[i], chosen) for i in range(planes)]
    sketch_ref[...] = sketch_rows(cells, low_ref, high_ref, cells_ref)


def side_of(turn):
    is_low = (lax.axis_index("gy") + turn) % 2 == 1
    below, above = has_beside("gy")
    return is_low, jnp.where(is_low, below, above)


def at_row(plane, is_low):
    return jnp.where(is_low, plane[:1], plane[plane.shape[0] - 1 :])


def add_side(
    turn, images, b_ref, x_links, beside_ref, own_ref, line_ref, x_first_ref, x_second_ref,
    extra_ref, ends_ref,
):
    planes, rows, depth = b_ref.shape
    is_low, here = side_of(turn)
    index = lax.broadcasted_iota(jnp.int32, (rows, depth), 0)
    edge = index == jnp.where(is_low, 0, rows - 1)
    beyond, b_line, c_line = (line_ref[k * planes : (k + 1) * planes] for k in range(3))
    c_line = jnp.where(here, c_line, 0.0)
    y_link = link(own_ref[2 * planes : 3 * planes], c_line)
    y_flow = y_link * (own_ref[planes : 2 * planes] - b_line)
    for i in range(planes):
        images[i + 1] = images[i + 1] + jnp.where(edge, y_flow[i : i + 1], 0.0)
    tails = by_turn(x_first_ref[3 * rows :], x_second_ref[3 * rows :], "gx")
    for end, (i, tail) in enumerate(zip((0, planes - 1), tails)):
        at = slice(i, i + 1)
        x_link = at_row(x_links[-end], is_low)
        x_b, x_cond = at_row(beside_ref[end], is_low), at_row(beside_ref[2 + end], is_low)
        x_flow = x_link * (at_row(b_ref[i], is_low) - x_b)
        values = -x_link * y_flow[at], at_row(tail[:2], is_low), at_row(tail[2:], is_low)
        for k, value in enumerate(values):
            extra_ref[k, 2 * end : 2 * end + 1] = value
        tail = line_ref[3 * planes :]
        values = -y_link[at] * x_flow, tail[end:][:1], tail[2 + end :][:1]
        for k, value in enumerate(values):
            extra_ref[k, 2 * end + 1 : 2 * end + 2] = value
        values = x_link, x_b, x_cond, y_link[at], b_line[at], c_line[at]
        for k, value in enumerate(values):
            ends_ref[6 * end + k : 6 * end + k + 1] = value
    return y_link, beyond - y_flow


def add_beside(turn, twice, images, y_link, beyond):
    rows, depth = twice[0].shape
    is_low, unused = side_of(turn)
    index = lax.broadcasted_iota(jnp.int32, (rows, depth), 0)
    edge = index == jnp.where(is_low, 0, rows - 1)
    for i in range(len(twice)):
        at = slice(i, i + 1)
        conductance = jnp.where(edge, y_link[at], 0.0)
        twice[i] = twice[i] + conductance * (images[i + 1] - beyond[at])


def side_sketch(turn, images, twice, draw_ref, low_ref, high_ref, cells_ref, extra_ref):
    planes, rows, depth = draw_ref.shape
    is_low, unused = side_of(turn)
    first = jnp.where(is_low, 0, rows - 2)
    cells = [((images[i + 1], twice[i]), draw_ref[i], (first, first + 1)) for i in range(planes)]
    total = sketch_rows(cells, low_ref, high_ref, cells_ref)
    start = planes * rows * 8
    nothing = jnp.zeros(extra_ref.shape[1:], jnp.float32)
    put_cells((nothing, extra_ref[0]), extra_ref[1], start, cells_ref)
    low, high = parts_of(extra_ref[2])
    left, right = [], []
    for j in range(extra_ref.shape[1]):
        mask = one_hot(high, j, HIGH, 2 * PAIR)
        left.append(masked_cells(mask, start, j, cells_ref))
        right.append(one_hot(low, j, LOW, 1))
    return total + product(left, right)


def third_kernel(
    b_ref, cap_ref, y_link_ref, z_link_ref, draw_ref, low_ref, high_ref, own_ref, wide_ref,
    x_link_ref, beside_ref, x_second_ref, x_first_ref, line_ref, inside_ref, more_ref, edge_ref,
    ends_ref, sketch_ref, cells_ref, extra_ref,
):
    planes = b_ref.shape[0]
    images = [wide_ref[i] for i in range(planes + 2)]
    x_links = [x_link_ref[i] for i in range(planes + 1)]
    y_link, beyond = add_side(
        1, images, b_ref, x_links, beside_ref, own_ref, line_ref, x_first_ref, x_second_ref,
        extra_ref, ends_ref,
    )
    edge_ref[0], edge_ref[1] = y_link, beyond
    links = [(y_link_ref[i], z_link_ref[i]) for i in range(planes)]
    twice = apply_inside(images, x_links, links, [cap_ref[i] for i in range(planes)])
    add_beside(1, twice, images, y_link, beyond)
    for i, image in enumerate(images):
        more_ref[i] = image
    sketch_ref[...] = inside_ref[...] + side_sketch(
        1, images, twice, draw_ref, low_ref, high_ref, cells_ref, extra_ref
    )


def fourth_kernel(
    b_ref, cap_ref, y_link_ref, z_link_ref, draw_ref, low_ref, high_ref, own_ref, more_ref,
    x_link_ref, beside_ref, x_second_ref, x_first_ref, line_ref, edge_ref, b_sketch_ref,
    others_ref, image_ref, twice_ref, sketch_ref, corner_first_ref, corner_second_ref, ends_ref,
    cells_ref, extra_ref,
):
    planes, rows, depth = b_ref.shape
    images = [more_ref[i] for i in range(planes + 2)]
    x_links = [x_link_ref[i] for i in range(planes + 1)]
    y_link, beyond = add_side(
        0, images, b_ref, x_links, beside_ref, own_ref, line_ref, x_first_ref, x_second_ref,
        extra_ref, ends_ref,
    )
    links = [(y_link_ref[i], z_link_ref[i]) for i in range(planes)]
    twice = apply_inside(images, x_links, links, [cap_ref[i] for i in range(planes)])
    add_beside(1, twice, images, edge_ref[0], edge_ref[1])
    add_beside(0, twice, images, y_link, beyond)
    for i in range(planes):
        image_ref[i] = images[i + 1]
        twice_ref[i] = twice[i]
    total = others_ref[...] + side_sketch(
        0, images, twice, draw_ref, low_ref, high_ref, cells_ref, extra_ref
    )
    sketch_ref[1 : 1 + PAIR] = as_sketch(total)
    sketch_ref[:1] = b_sketch_ref[:1]
    sketch_ref[1 + PAIR :] = b_sketch_ref[:1]
    for k in range(4):
        at = slice(k, k + 1)
        corner_first_ref[at], corner_second_ref[at] = by_turn(
            beside_ref[k, :1], beside_ref[k, rows - 1 :], "gy"
        )


def last_kernel(
    sketch_ref, b_ref, image_ref, twice_ref, ends_first_ref, ends_second_ref, corner_first_ref,
    corner_second_ref, solution_ref, residual_ref,
):
    sketches = jnp.sum(sketch_ref[...], axis=0)

    def inner(first, second):
        return jnp.sum(first * second, axis=1, keepdims=True)

    s0, s1, s2 = (sketches[i : i + 1] for i in range(FIELDS))
    beta_inverse = 1.0 / jnp.sqrt(inner(s0, s0) + epsilon)
    h00 = inner(s0, s1) * beta_inverse * beta_inverse
    q0, p0 = s0 * beta_inverse, s1 * beta_inverse
    t0 = p0 - h00 * q0
    p1 = s2 * beta_inverse - h00 * p0
    n0 = jnp.sqrt(inner(t0, t0) + epsilon)
    n0_inverse = 1.0 / n0
    h01 = inner(q0, p1) * n0_inverse
    h11 = inner(t0, p1) * n0_inverse * n0_inverse
    t1 = p1 * n0_inverse - h01 * q0 - h11 * (t0 * n0_inverse)
    n1_square = inner(t1, t1) + epsilon
    first = h00 * h00 + n0 * n0
    cross = h00 * h01 + n0 * h11
    ratio = cross / first
    second = h01 * h01 + h11 * h11 + n1_square - cross * ratio
    y1 = (h01 - ratio * h00) / second
    y0 = h00 / first - ratio * y1
    c1 = y1 * n0_inverse
    c0 = y0 - h00 * c1
    planes, rows, depth = b_ref.shape
    for i in range(planes):
        b, image = b_ref[i], image_ref[i]
        solution_ref[i] = c0 * b + c1 * image
        residual_ref[i] = b - c0 * image - c1 * twice_ref[i]
    corners = by_turn(corner_first_ref[...], corner_second_ref[...], "gy")
    ends = by_turn(ends_first_ref[...], ends_second_ref[...], "gy")
    for j, here, corner, known in zip((0, rows - 1), has_beside("gy"), corners, ends):
        for end, i in enumerate((0, planes - 1)):
            b, cond = corner[end : end + 1], corner[2 + end : 3 + end]
            cond = jnp.where(here, cond, 0.0)
            x_link, x_b, x_cond, y_link, y_b, y_cond = (
                known[6 * end + k :][:1] for k in range(6)
            )
            lacked = x_link * link(x_cond, cond) * (x_b - b)
            lacked = lacked + y_link * link(y_cond, cond) * (y_b - b)
            residual_ref[i, j : j + 1] = residual_ref[i, j : j + 1] + c1 * lacked


def call(kernel, shapes, *operands, scratch=(), inputs=pltpu.VMEM, flops=0):
    return pl.pallas_call(
        kernel,
        out_shape=[
            shape if hasattr(shape, "dtype") else jax.ShapeDtypeStruct(shape, jnp.float32)
            for shape in shapes
        ],
        in_specs=[pl.BlockSpec(memory_space=inputs)] * len(operands),
        out_specs=[pl.BlockSpec(memory_space=pltpu.VMEM)] * len(shapes),
        scratch_shapes=scratch,
        compiler_params=pltpu.CompilerParams(vmem_limit_bytes=48 * 1024 * 1024),
        cost_estimate=pl.CostEstimate(flops=flops, bytes_accessed=0, transcendentals=0),
    )(*operands)


def swap(array, axis, turn):
    nx, ny = lax.axis_size("gx"), lax.axis_size("gy")
    pairs = []
    for x in range(nx):
        for y in range(ny):
            here, count = (x, nx) if axis == "gx" else (y, ny)
            there = here + 1 if here % 2 == turn else here - 1
            if 0 <= there < count:
                partner = (there, y) if axis == "gx" else (x, there)
            else:
                partner = (x, y ^ 1) if axis == "gx" else (x ^ 1, y)
            pairs.append((x * ny + y, partner[0] * ny + partner[1]))
    return lax.ppermute(array, ("gx", "gy"), pairs)


def everyones(sketch):
    nx, ny = lax.axis_size("gx"), lax.axis_size("gy")
    middle = nx // 2 - 1, ny // 2
    places = [(x, y) for x in range(nx) for y in range(ny)]
    places.sort(key=lambda at: (abs(at[1] - middle[1]), abs(at[0] - middle[0]), at))
    group = [x * ny + y for x, y in places]
    copies = jnp.broadcast_to(sketch[None], (nx * ny,) + sketch.shape)
    return lax.all_to_all(copies, ("gx", "gy"), 0, 0, axis_index_groups=[group])


def body(b, warmth, phase, slots, draw):
    planes, rows, depth = b.shape
    block, wide = b.shape, (planes + 2, rows, depth)
    face, line, corner = (3 * rows + 4, depth), (3 * planes + 4, depth), (4, depth)
    cells = pltpu.VMEM((depth // LANES, (planes * rows + 8) * 8, LANES), jnp.float32)
    total = HIGH * 2 * PAIR, LOW
    hots = [
        jax.ShapeDtypeStruct((planes * rows * count, depth), jnp.bfloat16)
        for count in (LOW, HIGH * 2 * PAIR)
    ]
    work = b.size * SKETCH * 6
    b, cond, cap, y_link, z_link, inner, draw, slots, x_first, x_second, y_first, y_second = call(
        first_kernel,
        [block] * 8 + [face, face, line, line],
        *(
            pltpu.with_memory_space_constraint(x, pltpu.HBM)
            for x in (b, warmth, phase, draw, slots)
        ),
        scratch=[
            pltpu.VMEM(block, warmth.dtype),
            pltpu.VMEM(block, phase.dtype),
            pltpu.VMEM(block, slots.dtype),
            pltpu.SemaphoreType.DMA((5,)),
        ],
        inputs=pltpu.HBM,
    )
    got_x = swap(x_second, "gx", 1), swap(x_first, "gx", 0)
    got_y = swap(y_second, "gy", 1), swap(y_first, "gy", 0)
    *hots, b_sketch = call(
        slot_kernel, [*hots, (PAIR, SKETCH)], b, draw, slots, scratch=[cells], flops=work
    )
    image_wide, x_link, beside, inside = call(
        inside_kernel,
        [wide, (planes + 1, rows, depth), (4, rows, depth), total],
        b, cond, cap, y_link, z_link, inner, draw, *hots, *got_x,
        scratch=[cells],
        flops=work,
    )
    extra = pltpu.VMEM((3, 4, depth), jnp.float32)
    more, edge, ends_second, others = call(
        third_kernel,
        [wide, (2, planes, depth), (12, depth), total],
        b, cap, y_link, z_link, draw, *hots, y_second, image_wide, x_link, beside, *got_x,
        got_y[0], inside,
        scratch=[cells, extra],
        flops=work,
    )
    image, twice, sketch, first, second, ends_first = call(
        fourth_kernel,
        [block, block, (FIELDS + 1, SKETCH), corner, corner, (12, depth)],
        b, cap, y_link, z_link, draw, *hots, y_first, more, x_link, beside, *got_x, got_y[1],
        edge, b_sketch, others,
        scratch=[cells, extra],
        flops=work,
    )
    got_corners = [swap(array, "gy", turn) for turn, array in enumerate((first, second))]
    sketches = everyones(sketch)
    return tuple(
        call(
            last_kernel,
            [block, block],
            sketches, b, image, twice, ends_first, ends_second, *got_corners,
        )
    )


def solution(mesh):
    spec = P(("parts", "gx"), "gy", None)
    return jax.shard_map(
        body, mesh=mesh, in_specs=(spec,) * 5, out_specs=(spec,) * 2, check_vma=False
    )
```

```python
import jax
import jax.numpy as jnp
from jax import lax
from jax.experimental import pallas as pl
from jax.experimental.pallas import tpu as pltpu
from jax.sharding import PartitionSpec as P

SKETCH = 128
LOW = 32
HIGH = SKETCH // LOW
FIELDS = 3
PAIR = 2
LANES = 128
epsilon = 1e-06


def traits(warmth, phase):
    powder, solid = phase == 0, phase == 1
    offset = jnp.where(powder, 0.2, jnp.where(solid, 1.0, 0.6))
    return offset * (0.5 + warmth), jnp.where(powder, 1.0, jnp.where(solid, 2.0, 1.5))


def link(first, second):
    total = first + second
    return 2.0 * first * second / jnp.where(total > 0.0, total, 1.0)


def ahead(plane, axis):
    return pltpu.roll(plane, plane.shape[axis] - 1, axis)


def inner_links(cond):
    links = []
    for axis in (0, 1):
        index = lax.broadcasted_iota(jnp.int32, cond.shape, axis)
        links.append(
            jnp.where(index < cond.shape[axis] - 1, link(cond, ahead(cond, axis)), 0.0)
        )
    return links


def inner_flow(field, links):
    total = None
    for axis in (0, 1):
        flow = links[axis] * (field - ahead(field, axis))
        part = flow - pltpu.roll(flow, 1, axis)
        total = part if total is None else total + part
    return total


def apply_inside(images, x_links, links, caps):
    results = []
    flow_low = x_links[0] * (images[0] - images[1])
    for i in range(1, len(images) - 1):
        image = images[i]
        flow = x_links[i] * (image - images[i + 1])
        inside = inner_flow(image, links[i - 1])
        results.append(caps[i - 1] * image + inside + (flow - flow_low))
        flow_low = flow
    return results


def parts_of(slot):
    high = jnp.floor(slot * (1.0 / LOW))
    return slot - LOW * high, high


def one_hot(values, j, count, each):
    shape = (count * each, values.shape[1])
    index = lax.broadcasted_iota(jnp.int32, shape, 0) // each
    index = index.astype(jnp.float32).astype(jnp.bfloat16)
    row = jnp.broadcast_to(values[j : j + 1], shape).astype(jnp.bfloat16)
    one = jnp.ones_like(row)
    return jnp.where(row == index, one, jnp.zeros_like(one))


def put_cells(fields, draw, start, cells_ref):
    coarse, fine = [], []
    for field in fields:
        weighted = draw * field
        head = weighted.astype(jnp.bfloat16).astype(jnp.float32)
        coarse.append(head)
        fine.append(weighted - head)
    for f, part in enumerate((coarse + fine) * 2):
        for t in range(cells_ref.shape[0]):
            cells_ref[t, pl.ds(start + f, draw.shape[0], stride=8), :] = part[
                :, t * LANES : (t + 1) * LANES
            ]


def masked_cells(mask, start, j, cells_ref):
    at = pl.ds(start + j * 8, 8)
    cells = jnp.concatenate([cells_ref[t, at, :] for t in range(cells_ref.shape[0])], axis=1)
    return jnp.concatenate([cells, cells], axis=0).astype(jnp.bfloat16) * mask


def product(left, right):
    return lax.dot_general(
        jnp.concatenate(left, axis=1),
        jnp.concatenate(right, axis=1),
        (((1,), (1,)), ((), ())),
        preferred_element_type=jnp.float32,
    )


def as_sketch(total):
    each = 2 * PAIR
    total = jnp.concatenate([total[h * each : (h + 1) * each] for h in range(HIGH)], axis=1)
    return total[:PAIR] + total[PAIR:]


def sketch_rows(planes, low_ref, high_ref, cells_ref):
    total = 0.0
    each = HIGH * 2 * PAIR
    for i, (fields, draw, chosen) in enumerate(planes):
        rows = draw.shape[0]
        start = i * rows * 8
        put_cells(fields, draw, start, cells_ref)
        left, right = [], []
        for j in chosen:
            at = i * rows + j
            mask = high_ref[at * each : (at + 1) * each]
            left.append(masked_cells(mask, start, j, cells_ref))
            right.append(low_ref[at * LOW : (at + 1) * LOW])
        total = total + product(left, right)
    return total


def slot_kernel(b_ref, draw_ref, slot_ref, low_ref, high_ref, sketch_ref, cells_ref):
    planes, rows = b_ref.shape[:2]
    each = HIGH * 2 * PAIR
    total = 0.0
    for i in range(planes):
        start = i * rows * 8
        put_cells((b_ref[i],) * PAIR, draw_ref[i], start, cells_ref)
        low, high = parts_of(slot_ref[i])
        left, right = [], []
        for j in range(rows):
            at = i * rows + j
            mask, hot = one_hot(high, j, HIGH, 2 * PAIR), one_hot(low, j, LOW, 1)
            high_ref[at * each : (at + 1) * each] = mask
            low_ref[at * LOW : (at + 1) * LOW] = hot
            left.append(masked_cells(mask, start, j, cells_ref))
            right.append(hot)
        total = total + product(left, right)
    sketch_ref[...] = as_sketch(total)


def first_kernel(
    b_hbm, warmth_hbm, phase_hbm, draw_hbm, slot_hbm, b_ref, cond_ref, cap_ref, y_link_ref,
    z_link_ref, inner_ref, draw_ref, slot_ref, x_first_ref, x_second_ref, y_first_ref,
    y_second_ref, warmth_ref, phase_ref, number_ref, arrived,
):
    copies = [
        pltpu.make_async_copy(source, target, arrived.at[k])
        for k, (source, target) in enumerate(
            (
                (b_hbm, b_ref),
                (warmth_hbm, warmth_ref),
                (phase_hbm, phase_ref),
                (draw_hbm, draw_ref),
                (slot_hbm, number_ref),
            )
        )
    ]
    for copy in copies:
        copy.start()
    for copy in copies[:3]:
        copy.wait()
    planes, rows = b_ref.shape[:2]
    images, conds = [], []
    for i in range(planes):
        cond, cap = traits(warmth_ref[i], phase_ref[i])
        cap_ref[i] = cap
        cond_ref[i] = cond
        y_link_ref[i], z_link_ref[i] = links = inner_links(cond)
        field = b_ref[i]
        image = cap * field + inner_flow(field, links)
        if i:
            flow = link(conds[-1], cond) * (b_ref[i - 1] - field)
            images[-1] = images[-1] + flow
            image = image - flow
        conds.append(cond)
        images.append(image)
    for i in range(planes):
        inner_ref[i] = images[i]
    for k, field in enumerate((images, [b_ref[i] for i in range(planes)], conds)):
        at = slice(k * rows, (k + 1) * rows)
        x_first_ref[at], x_second_ref[at] = by_turn(field[0], field[-1], "gx")
        for i, plane in enumerate(field):
            at = slice(k * planes + i, k * planes + i + 1)
            y_first_ref[at], y_second_ref[at] = by_turn(plane[:1], plane[rows - 1 :], "gy")
    for copy in copies[3:]:
        copy.wait()
    for i in range(planes):
        slot_ref[i] = number_ref[i].astype(jnp.float32)
    for k, ref in enumerate((draw_ref, slot_ref)):
        ends = [ref[0], ref[planes - 1]]
        for e, j in enumerate((0, rows - 1)):
            at = slice(3 * rows + 2 * k + e, 3 * rows + 2 * k + e + 1)
            lines = [plane[j : j + 1] for plane in ends]
            x_first_ref[at], x_second_ref[at] = by_turn(*lines, "gx")
        for e, plane in enumerate(ends):
            at = slice(3 * planes + 2 * k + e, 3 * planes + 2 * k + e + 1)
            lines = [plane[:1], plane[rows - 1 :]]
            y_first_ref[at], y_second_ref[at] = by_turn(*lines, "gy")


def by_turn(one, other, axis):
    odd = lax.axis_index(axis) % 2 == 1
    return jnp.where(odd, one, other), jnp.where(odd, other, one)


def has_beside(axis):
    at = lax.axis_index(axis)
    return at > 0, at < lax.axis_size(axis) - 1


def reached(rows):
    others = [j for j in range(rows) if 2 <= j < rows - 2]
    return [j for j in range(rows) if j not in others], others


def inside_kernel(
    b_ref, cond_ref, cap_ref, y_link_ref, z_link_ref, inner_ref, draw_ref, low_ref, high_ref,
    got_second_ref, got_first_ref, wide_ref, x_link_ref, beside_ref, sketch_ref, cells_ref,
):
    planes, rows = b_ref.shape[:2]
    (image_low, image_high), (b_low, b_high), (c_low, c_high) = (
        by_turn(*(ref[k * rows : (k + 1) * rows] for ref in (got_first_ref, got_second_ref)), "gx")
        for k in range(3)
    )
    below, above = has_beside("gx")
    c_low, c_high = jnp.where(below, c_low, 0.0), jnp.where(above, c_high, 0.0)
    for k, plane in enumerate((b_low, b_high, c_low, c_high)):
        beside_ref[k] = plane
    conds = [c_low] + [cond_ref[i] for i in range(planes)] + [c_high]
    x_links = [link(conds[i], conds[i + 1]) for i in range(planes + 1)]
    for i, conductance in enumerate(x_links):
        x_link_ref[i] = conductance
    low_flow = x_links[0] * (b_low - b_ref[0])
    high_flow = x_links[-1] * (b_ref[planes - 1] - b_high)
    images = [image_low + low_flow] + [inner_ref[i] for i in range(planes)]
    images.append(image_high - high_flow)
    images[1] = images[1] - low_flow
    images[-2] = images[-2] + high_flow
    for i, image in enumerate(images):
        wide_ref[i] = image
    links = [(y_link_ref[i], z_link_ref[i]) for i in range(planes)]
    twice = apply_inside(images, x_links, links, [cap_ref[i] for i in range(planes)])
    chosen = reached(rows)[1]
    cells = [((images[i + 1], twice[i]), draw_ref[i], chosen) for i in range(planes)]
    sketch_ref[...] = sketch_rows(cells, low_ref, high_ref, cells_ref)


def third_kernel(
    b_ref, cap_ref, y_link_ref, z_link_ref, draw_ref, low_ref, high_ref, own_second_ref,
    own_first_ref, wide_ref, x_link_ref, beside_ref, x_second_ref, x_first_ref, y_second_ref,
    y_first_ref, b_sketch_ref, inside_ref, image_ref, twice_ref, sketch_ref, corner_first_ref,
    corner_second_ref, ends_ref, cells_ref, extra_ref,
):
    planes, rows, depth = b_ref.shape
    index = lax.broadcasted_iota(jnp.int32, (rows, depth), 0)
    images = [wide_ref[i] for i in range(planes + 2)]
    x_links = [x_link_ref[i] for i in range(planes + 1)]
    b_beside, c_beside = (beside_ref[0], beside_ref[1]), (beside_ref[2], beside_ref[3])
    x_ends = []
    for end, i in enumerate((0, planes - 1)):
        conductance = x_links[-end]
        x_ends.append((i, conductance, conductance * (b_ref[i] - b_beside[end])))
    x_tails = by_turn(x_first_ref[3 * rows :], x_second_ref[3 * rows :], "gx")
    own_lines = by_turn(own_first_ref[...], own_second_ref[...], "gy")
    y_lines = by_turn(y_first_ref[...], y_second_ref[...], "gy")
    beside = []
    for side, (j, here, own, line) in enumerate(
        zip((0, rows - 1), has_beside("gy"), own_lines, y_lines)
    ):
        row = slice(j, j + 1)
        beyond, b_line, c_line = (line[k * planes : (k + 1) * planes] for k in range(3))
        c_line = jnp.where(here, c_line, 0.0)
        y_link = link(own[2 * planes : 3 * planes], c_line)
        y_flow = y_link * (own[planes : 2 * planes] - b_line)
        beyond = beyond - y_flow
        for i in range(planes):
            at = slice(i, i + 1)
            images[i + 1] = images[i + 1] + jnp.where(index == j, y_flow[at], 0.0)
            beside.append((i, jnp.where(index == j, y_link[at], 0.0), beyond[at]))
        for end, (i, x_link, x_flow) in enumerate(x_ends):
            line_at, at = slice(i, i + 1), 4 * side + 2 * end
            tail = x_tails[end]
            values = -x_link[row] * y_flow[line_at], tail[side:][:1], tail[2 + side :][:1]
            for k, value in enumerate(values):
                extra_ref[k, at : at + 1] = value
            tail = line[3 * planes :]
            values = -y_link[line_at] * x_flow[row], tail[end:][:1], tail[2 + end :][:1]
            for k, value in enumerate(values):
                extra_ref[k, at + 1 : at + 2] = value
            at = 6 * (2 * side + end)
            values = x_link[row], b_beside[end][row], c_beside[end][row]
            values += y_link[line_at], b_line[line_at], c_line[line_at]
            for k, value in enumerate(values):
                ends_ref[at + k : at + k + 1] = value
    links = [(y_link_ref[i], z_link_ref[i]) for i in range(planes)]
    twice = apply_inside(images, x_links, links, [cap_ref[i] for i in range(planes)])
    for i, conductance, value in beside:
        twice[i] = twice[i] + conductance * (images[i + 1] - value)
    for i in range(planes):
        image_ref[i] = images[i + 1]
        twice_ref[i] = twice[i]
    chosen = reached(rows)[0]
    cells = [((images[i + 1], twice[i]), draw_ref[i], chosen) for i in range(planes)]
    total = inside_ref[...] + sketch_rows(cells, low_ref, high_ref, cells_ref)
    start = planes * rows * 8
    put_cells((jnp.zeros((8, depth), jnp.float32), extra_ref[0]), extra_ref[1], start, cells_ref)
    low, high = parts_of(extra_ref[2])
    left, right = [], []
    for j in range(8):
        mask = one_hot(high, j, HIGH, 2 * PAIR)
        left.append(masked_cells(mask, start, j, cells_ref))
        right.append(one_hot(low, j, LOW, 1))
    sketch_ref[1 : 1 + PAIR] = as_sketch(total + product(left, right))
    sketch_ref[:1] = b_sketch_ref[:1]
    sketch_ref[1 + PAIR :] = b_sketch_ref[:1]
    for k, plane in enumerate(b_beside + c_beside):
        at = slice(k, k + 1)
        corner_first_ref[at], corner_second_ref[at] = by_turn(
            plane[:1], plane[rows - 1 :], "gy"
        )


def last_kernel(
    sketch_ref, b_ref, image_ref, twice_ref, ends_ref, corner_first_ref, corner_second_ref,
    solution_ref, residual_ref,
):
    sketches = jnp.sum(sketch_ref[...], axis=0)

    def inner(first, second):
        return jnp.sum(first * second, axis=1, keepdims=True)

    s0, s1, s2 = (sketches[i : i + 1] for i in range(FIELDS))
    beta_inverse = 1.0 / jnp.sqrt(inner(s0, s0) + epsilon)
    h00 = inner(s0, s1) * beta_inverse * beta_inverse
    q0, p0 = s0 * beta_inverse, s1 * beta_inverse
    t0 = p0 - h00 * q0
    p1 = s2 * beta_inverse - h00 * p0
    n0 = jnp.sqrt(inner(t0, t0) + epsilon)
    n0_inverse = 1.0 / n0
    h01 = inner(q0, p1) * n0_inverse
    h11 = inner(t0, p1) * n0_inverse * n0_inverse
    t1 = p1 * n0_inverse - h01 * q0 - h11 * (t0 * n0_inverse)
    n1_square = inner(t1, t1) + epsilon
    first = h00 * h00 + n0 * n0
    cross = h00 * h01 + n0 * h11
    ratio = cross / first
    second = h01 * h01 + h11 * h11 + n1_square - cross * ratio
    y1 = (h01 - ratio * h00) / second
    y0 = h00 / first - ratio * y1
    c1 = y1 * n0_inverse
    c0 = y0 - h00 * c1
    planes, rows, depth = b_ref.shape
    for i in range(planes):
        b, image = b_ref[i], image_ref[i]
        solution_ref[i] = c0 * b + c1 * image
        residual_ref[i] = b - c0 * image - c1 * twice_ref[i]
    corners = by_turn(corner_first_ref[...], corner_second_ref[...], "gy")
    for side, (j, here, corner) in enumerate(zip((0, rows - 1), has_beside("gy"), corners)):
        for end, i in enumerate((0, planes - 1)):
            b, cond = corner[end : end + 1], corner[2 + end : 3 + end]
            cond = jnp.where(here, cond, 0.0)
            at = 6 * (2 * side + end)
            x_link, x_b, x_cond, y_link, y_b, y_cond = (
                ends_ref[at + k : at + k + 1] for k in range(6)
            )
            lacked = x_link * link(x_cond, cond) * (x_b - b)
            lacked = lacked + y_link * link(y_cond, cond) * (y_b - b)
            residual_ref[i, j : j + 1] = residual_ref[i, j : j + 1] + c1 * lacked


def call(kernel, shapes, *operands, scratch=(), inputs=pltpu.VMEM, flops=0):
    return pl.pallas_call(
        kernel,
        out_shape=[
            shape if hasattr(shape, "dtype") else jax.ShapeDtypeStruct(shape, jnp.float32)
            for shape in shapes
        ],
        in_specs=[pl.BlockSpec(memory_space=inputs)] * len(operands),
        out_specs=[pl.BlockSpec(memory_space=pltpu.VMEM)] * len(shapes),
        scratch_shapes=scratch,
        compiler_params=pltpu.CompilerParams(vmem_limit_bytes=48 * 1024 * 1024),
        cost_estimate=pl.CostEstimate(flops=flops, bytes_accessed=0, transcendentals=0),
    )(*operands)


def swap(array, axis, turn):
    nx, ny = lax.axis_size("gx"), lax.axis_size("gy")
    pairs = []
    for x in range(nx):
        for y in range(ny):
            here, count = (x, nx) if axis == "gx" else (y, ny)
            there = here + 1 if here % 2 == turn else here - 1
            if 0 <= there < count:
                partner = (there, y) if axis == "gx" else (x, there)
            else:
                partner = (x, y ^ 1) if axis == "gx" else (x ^ 1, y)
            pairs.append((x * ny + y, partner[0] * ny + partner[1]))
    return lax.ppermute(array, ("gx", "gy"), pairs)


def everyones(sketch):
    nx, ny = lax.axis_size("gx"), lax.axis_size("gy")
    sketch = sketch + swap(sketch, "gx", 0)
    groups = []
    for turn, middle in enumerate(((1, ny // 2), (1, ny // 2 - 1))):
        places = [(x, y) for x in range(nx) for y in range(ny) if (x + y // (ny // 2)) % 2 == turn]
        places.sort(key=lambda at: (at != middle, at))
        groups.append([x * ny + y for x, y in places])
    copies = jnp.broadcast_to(sketch[None], (nx * ny // 2,) + sketch.shape)
    return lax.all_to_all(copies, ("gx", "gy"), 0, 0, axis_index_groups=groups)


def body(b, warmth, phase, slots, draw):
    planes, rows, depth = b.shape
    block, wide = b.shape, (planes + 2, rows, depth)
    face, line, corner = (3 * rows + 4, depth), (3 * planes + 4, depth), (4, depth)
    cells = pltpu.VMEM((depth // LANES, (planes * rows + 8) * 8, LANES), jnp.float32)
    total = HIGH * 2 * PAIR, LOW
    hots = [
        jax.ShapeDtypeStruct((planes * rows * count, depth), jnp.bfloat16)
        for count in (LOW, HIGH * 2 * PAIR)
    ]
    work = b.size * SKETCH * 6
    b, cond, cap, y_link, z_link, inner, draw, slots, x_first, x_second, y_first, y_second = call(
        first_kernel,
        [block] * 8 + [face, face, line, line],
        *(
            pltpu.with_memory_space_constraint(x, pltpu.HBM)
            for x in (b, warmth, phase, draw, slots)
        ),
        scratch=[
            pltpu.VMEM(block, warmth.dtype),
            pltpu.VMEM(block, phase.dtype),
            pltpu.VMEM(block, slots.dtype),
            pltpu.SemaphoreType.DMA((5,)),
        ],
        inputs=pltpu.HBM,
    )
    got_x = swap(x_second, "gx", 1), swap(x_first, "gx", 0)
    got_y = swap(y_second, "gy", 1), swap(y_first, "gy", 0)
    *hots, b_sketch = call(
        slot_kernel, [*hots, (PAIR, SKETCH)], b, draw, slots, scratch=[cells], flops=work
    )
    image_wide, x_link, beside, inside = call(
        inside_kernel,
        [wide, (planes + 1, rows, depth), (4, rows, depth), total],
        b, cond, cap, y_link, z_link, inner, draw, *hots, *got_x,
        scratch=[cells],
        flops=work,
    )
    image, twice, sketch, first, second, ends = call(
        third_kernel,
        [block, block, (FIELDS + 1, SKETCH), corner, corner, (24, depth)],
        b, cap, y_link, z_link, draw, *hots, y_second, y_first, image_wide, x_link, beside,
        *got_x, *got_y, b_sketch, inside,
        scratch=[cells, pltpu.VMEM((3, 8, depth), jnp.float32)],
        flops=work,
    )
    got_corners = [swap(array, "gy", turn) for turn, array in enumerate((first, second))]
    sketches = everyones(sketch)
    return tuple(
        call(last_kernel, [block, block], sketches, b, image, twice, ends, *got_corners)
    )


def solution(mesh):
    spec = P(("parts", "gx"), "gy", None)
    return jax.shard_map(
        body, mesh=mesh, in_specs=(spec,) * 5, out_specs=(spec,) * 2, check_vma=False
    )
```

```python
import jax
import jax.numpy as jnp
from jax import lax
from jax.experimental import pallas as pl
from jax.experimental.pallas import tpu as pltpu
from jax.sharding import PartitionSpec as P

SKETCH = 128
LOW = 32
HIGH = SKETCH // LOW
FIELDS = 3
PAIR = 2
LANES = 128
epsilon = 1e-06


def traits(warmth, phase):
    powder, solid = phase == 0, phase == 1
    offset = jnp.where(powder, 0.2, jnp.where(solid, 1.0, 0.6))
    return offset * (0.5 + warmth), jnp.where(powder, 1.0, jnp.where(solid, 2.0, 1.5))


def link(first, second):
    total = first + second
    return 2.0 * first * second / jnp.where(total > 0.0, total, 1.0)


def ahead(plane, axis):
    return pltpu.roll(plane, plane.shape[axis] - 1, axis)


def inner_links(cond):
    links = []
    for axis in (0, 1):
        index = lax.broadcasted_iota(jnp.int32, cond.shape, axis)
        links.append(
            jnp.where(index < cond.shape[axis] - 1, link(cond, ahead(cond, axis)), 0.0)
        )
    return links


def inner_flow(field, links):
    total = None
    for axis in (0, 1):
        flow = links[axis] * (field - ahead(field, axis))
        part = flow - pltpu.roll(flow, 1, axis)
        total = part if total is None else total + part
    return total


def apply_inside(images, x_links, links, caps):
    results = []
    flow_low = x_links[0] * (images[0] - images[1])
    for i in range(1, len(images) - 1):
        image = images[i]
        flow = x_links[i] * (image - images[i + 1])
        inside = inner_flow(image, links[i - 1])
        results.append(caps[i - 1] * image + inside + (flow - flow_low))
        flow_low = flow
    return results


def parts_of(slot):
    high = jnp.floor(slot * (1.0 / LOW))
    return slot - LOW * high, high


def one_hot(values, j, count, each):
    shape = (count * each, values.shape[1])
    index = lax.broadcasted_iota(jnp.int32, shape, 0) // each
    index = index.astype(jnp.float32).astype(jnp.bfloat16)
    row = jnp.broadcast_to(values[j : j + 1], shape).astype(jnp.bfloat16)
    one = jnp.ones_like(row)
    return jnp.where(row == index, one, jnp.zeros_like(one))


def put_cells(fields, draw, start, cells_ref):
    coarse, fine = [], []
    for field in fields:
        weighted = draw * field
        head = weighted.astype(jnp.bfloat16).astype(jnp.float32)
        coarse.append(head)
        fine.append(weighted - head)
    for f, part in enumerate((coarse + fine) * 2):
        for t in range(cells_ref.shape[0]):
            cells_ref[t, pl.ds(start + f, draw.shape[0], stride=8), :] = part[
                :, t * LANES : (t + 1) * LANES
            ]


def masked_cells(mask, start, j, cells_ref):
    at = pl.ds(start + j * 8, 8)
    cells = jnp.concatenate([cells_ref[t, at, :] for t in range(cells_ref.shape[0])], axis=1)
    return jnp.concatenate([cells, cells], axis=0).astype(jnp.bfloat16) * mask


def product(left, right):
    return lax.dot_general(
        jnp.concatenate(left, axis=1),
        jnp.concatenate(right, axis=1),
        (((1,), (1,)), ((), ())),
        preferred_element_type=jnp.float32,
    )


def as_sketch(total):
    each = 2 * PAIR
    total = jnp.concatenate([total[h * each : (h + 1) * each] for h in range(HIGH)], axis=1)
    return total[:PAIR] + total[PAIR:]


def sketch_rows(planes, low_ref, high_ref, cells_ref):
    total = 0.0
    each = HIGH * 2 * PAIR
    for i, (fields, draw, chosen) in enumerate(planes):
        rows = draw.shape[0]
        start = i * rows * 8
        put_cells(fields, draw, start, cells_ref)
        left, right = [], []
        for j in chosen:
            at = i * rows + j
            mask = high_ref[at * each : (at + 1) * each]
            left.append(masked_cells(mask, start, j, cells_ref))
            right.append(low_ref[at * LOW : (at + 1) * LOW])
        total = total + product(left, right)
    return total


def slot_kernel(b_ref, draw_ref, slot_ref, low_ref, high_ref, sketch_ref, cells_ref):
    planes, rows = b_ref.shape[:2]
    each = HIGH * 2 * PAIR
    total = 0.0
    for i in range(planes):
        start = i * rows * 8
        put_cells((b_ref[i],) * PAIR, draw_ref[i], start, cells_ref)
        low, high = parts_of(slot_ref[i])
        left, right = [], []
        for j in range(rows):
            at = i * rows + j
            mask, hot = one_hot(high, j, HIGH, 2 * PAIR), one_hot(low, j, LOW, 1)
            high_ref[at * each : (at + 1) * each] = mask
            low_ref[at * LOW : (at + 1) * LOW] = hot
            left.append(masked_cells(mask, start, j, cells_ref))
            right.append(hot)
        total = total + product(left, right)
    sketch_ref[...] = as_sketch(total)


def first_kernel(
    b_hbm, warmth_hbm, phase_hbm, draw_hbm, slot_hbm, b_ref, cond_ref, cap_ref, y_link_ref,
    z_link_ref, inner_ref, draw_ref, slot_ref, x_first_ref, x_second_ref, y_first_ref,
    y_second_ref, warmth_ref, phase_ref, number_ref, arrived,
):
    copies = [
        pltpu.make_async_copy(source, target, arrived.at[k])
        for k, (source, target) in enumerate(
            (
                (b_hbm, b_ref),
                (warmth_hbm, warmth_ref),
                (phase_hbm, phase_ref),
                (draw_hbm, draw_ref),
                (slot_hbm, number_ref),
            )
        )
    ]
    for copy in copies:
        copy.start()
    for copy in copies[:3]:
        copy.wait()
    planes, rows = b_ref.shape[:2]
    images, conds = [], []
    for i in range(planes):
        cond, cap = traits(warmth_ref[i], phase_ref[i])
        cap_ref[i] = cap
        cond_ref[i] = cond
        y_link_ref[i], z_link_ref[i] = links = inner_links(cond)
        field = b_ref[i]
        image = cap * field + inner_flow(field, links)
        if i:
            flow = link(conds[-1], cond) * (b_ref[i - 1] - field)
            images[-1] = images[-1] + flow
            image = image - flow
        conds.append(cond)
        images.append(image)
    for i in range(planes):
        inner_ref[i] = images[i]
    for k, field in enumerate((images, [b_ref[i] for i in range(planes)], conds)):
        at = slice(k * rows, (k + 1) * rows)
        x_first_ref[at], x_second_ref[at] = by_turn(field[0], field[-1], "gx")
        for i, plane in enumerate(field):
            at = slice(k * planes + i, k * planes + i + 1)
            y_first_ref[at], y_second_ref[at] = by_turn(plane[:1], plane[rows - 1 :], "gy")
    for copy in copies[3:]:
        copy.wait()
    for i in range(planes):
        slot_ref[i] = number_ref[i].astype(jnp.float32)
    for k, ref in enumerate((draw_ref, slot_ref)):
        ends = [ref[0], ref[planes - 1]]
        for e, j in enumerate((0, rows - 1)):
            at = slice(3 * rows + 2 * k + e, 3 * rows + 2 * k + e + 1)
            lines = [plane[j : j + 1] for plane in ends]
            x_first_ref[at], x_second_ref[at] = by_turn(*lines, "gx")
        for e, plane in enumerate(ends):
            at = slice(3 * planes + 2 * k + e, 3 * planes + 2 * k + e + 1)
            lines = [plane[:1], plane[rows - 1 :]]
            y_first_ref[at], y_second_ref[at] = by_turn(*lines, "gy")


def by_turn(one, other, axis):
    odd = lax.axis_index(axis) % 2 == 1
    return jnp.where(odd, one, other), jnp.where(odd, other, one)


def has_beside(axis):
    at = lax.axis_index(axis)
    return at > 0, at < lax.axis_size(axis) - 1


def reached(rows):
    others = [j for j in range(rows) if 2 <= j < rows - 2]
    return [j for j in range(rows) if j not in others], others


def inside_kernel(
    b_ref, cond_ref, cap_ref, y_link_ref, z_link_ref, inner_ref, draw_ref, low_ref, high_ref,
    got_second_ref, got_first_ref, wide_ref, x_link_ref, beside_ref, sketch_ref, cells_ref,
):
    planes, rows = b_ref.shape[:2]
    (image_low, image_high), (b_low, b_high), (c_low, c_high) = (
        by_turn(*(ref[k * rows : (k + 1) * rows] for ref in (got_first_ref, got_second_ref)), "gx")
        for k in range(3)
    )
    below, above = has_beside("gx")
    c_low, c_high = jnp.where(below, c_low, 0.0), jnp.where(above, c_high, 0.0)
    for k, plane in enumerate((b_low, b_high, c_low, c_high)):
        beside_ref[k] = plane
    conds = [c_low] + [cond_ref[i] for i in range(planes)] + [c_high]
    x_links = [link(conds[i], conds[i + 1]) for i in range(planes + 1)]
    for i, conductance in enumerate(x_links):
        x_link_ref[i] = conductance
    low_flow = x_links[0] * (b_low - b_ref[0])
    high_flow = x_links[-1] * (b_ref[planes - 1] - b_high)
    images = [image_low + low_flow] + [inner_ref[i] for i in range(planes)]
    images.append(image_high - high_flow)
    images[1] = images[1] - low_flow
    images[-2] = images[-2] + high_flow
    for i, image in enumerate(images):
        wide_ref[i] = image
    links = [(y_link_ref[i], z_link_ref[i]) for i in range(planes)]
    twice = apply_inside(images, x_links, links, [cap_ref[i] for i in range(planes)])
    chosen = reached(rows)[1]
    cells = [((images[i + 1], twice[i]), draw_ref[i], chosen) for i in range(planes)]
    sketch_ref[...] = sketch_rows(cells, low_ref, high_ref, cells_ref)


def third_kernel(
    b_ref, cap_ref, y_link_ref, z_link_ref, draw_ref, low_ref, high_ref, own_second_ref,
    own_first_ref, wide_ref, x_link_ref, beside_ref, x_second_ref, x_first_ref, y_second_ref,
    y_first_ref, b_sketch_ref, inside_ref, image_ref, twice_ref, sketch_ref, corner_first_ref,
    corner_second_ref, ends_ref, cells_ref, extra_ref,
):
    planes, rows, depth = b_ref.shape
    index = lax.broadcasted_iota(jnp.int32, (rows, depth), 0)
    images = [wide_ref[i] for i in range(planes + 2)]
    x_links = [x_link_ref[i] for i in range(planes + 1)]
    b_beside, c_beside = (beside_ref[0], beside_ref[1]), (beside_ref[2], beside_ref[3])
    x_ends = []
    for end, i in enumerate((0, planes - 1)):
        conductance = x_links[-end]
        x_ends.append((i, conductance, conductance * (b_ref[i] - b_beside[end])))
    x_tails = by_turn(x_first_ref[3 * rows :], x_second_ref[3 * rows :], "gx")
    own_lines = by_turn(own_first_ref[...], own_second_ref[...], "gy")
    y_lines = by_turn(y_first_ref[...], y_second_ref[...], "gy")
    beside = []
    for side, (j, here, own, line) in enumerate(
        zip((0, rows - 1), has_beside("gy"), own_lines, y_lines)
    ):
        row = slice(j, j + 1)
        beyond, b_line, c_line = (line[k * planes : (k + 1) * planes] for k in range(3))
        c_line = jnp.where(here, c_line, 0.0)
        y_link = link(own[2 * planes : 3 * planes], c_line)
        y_flow = y_link * (own[planes : 2 * planes] - b_line)
        beyond = beyond - y_flow
        for i in range(planes):
            at = slice(i, i + 1)
            images[i + 1] = images[i + 1] + jnp.where(index == j, y_flow[at], 0.0)
            beside.append((i, jnp.where(index == j, y_link[at], 0.0), beyond[at]))
        for end, (i, x_link, x_flow) in enumerate(x_ends):
            line_at, at = slice(i, i + 1), 4 * side + 2 * end
            tail = x_tails[end]
            values = -x_link[row] * y_flow[line_at], tail[side:][:1], tail[2 + side :][:1]
            for k, value in enumerate(values):
                extra_ref[k, at : at + 1] = value
            tail = line[3 * planes :]
            values = -y_link[line_at] * x_flow[row], tail[end:][:1], tail[2 + end :][:1]
            for k, value in enumerate(values):
                extra_ref[k, at + 1 : at + 2] = value
            at = 6 * (2 * side + end)
            values = x_link[row], b_beside[end][row], c_beside[end][row]
            values += y_link[line_at], b_line[line_at], c_line[line_at]
            for k, value in enumerate(values):
                ends_ref[at + k : at + k + 1] = value
    links = [(y_link_ref[i], z_link_ref[i]) for i in range(planes)]
    twice = apply_inside(images, x_links, links, [cap_ref[i] for i in range(planes)])
    for i, conductance, value in beside:
        twice[i] = twice[i] + conductance * (images[i + 1] - value)
    for i in range(planes):
        image_ref[i] = images[i + 1]
        twice_ref[i] = twice[i]
    chosen = reached(rows)[0]
    cells = [((images[i + 1], twice[i]), draw_ref[i], chosen) for i in range(planes)]
    total = inside_ref[...] + sketch_rows(cells, low_ref, high_ref, cells_ref)
    start = planes * rows * 8
    put_cells((jnp.zeros((8, depth), jnp.float32), extra_ref[0]), extra_ref[1], start, cells_ref)
    low, high = parts_of(extra_ref[2])
    left, right = [], []
    for j in range(8):
        mask = one_hot(high, j, HIGH, 2 * PAIR)
        left.append(masked_cells(mask, start, j, cells_ref))
        right.append(one_hot(low, j, LOW, 1))
    sketch_ref[1 : 1 + PAIR] = as_sketch(total + product(left, right))
    sketch_ref[:1] = b_sketch_ref[:1]
    sketch_ref[1 + PAIR :] = b_sketch_ref[:1]
    for k, plane in enumerate(b_beside + c_beside):
        at = slice(k, k + 1)
        corner_first_ref[at], corner_second_ref[at] = by_turn(
            plane[:1], plane[rows - 1 :], "gy"
        )


def last_kernel(
    sketch_ref, b_ref, image_ref, twice_ref, ends_ref, corner_first_ref, corner_second_ref,
    solution_ref, residual_ref,
):
    sketches = jnp.sum(sketch_ref[...], axis=0)

    def inner(first, second):
        return jnp.sum(first * second, axis=1, keepdims=True)

    s0, s1, s2 = (sketches[i : i + 1] for i in range(FIELDS))
    beta_inverse = 1.0 / jnp.sqrt(inner(s0, s0) + epsilon)
    h00 = inner(s0, s1) * beta_inverse * beta_inverse
    q0, p0 = s0 * beta_inverse, s1 * beta_inverse
    t0 = p0 - h00 * q0
    p1 = s2 * beta_inverse - h00 * p0
    n0 = jnp.sqrt(inner(t0, t0) + epsilon)
    n0_inverse = 1.0 / n0
    h01 = inner(q0, p1) * n0_inverse
    h11 = inner(t0, p1) * n0_inverse * n0_inverse
    t1 = p1 * n0_inverse - h01 * q0 - h11 * (t0 * n0_inverse)
    n1_square = inner(t1, t1) + epsilon
    first = h00 * h00 + n0 * n0
    cross = h00 * h11 - n0 * h01
    ratio = cross / first
    c1 = -ratio / (cross * ratio + n1_square)
    c0 = h00 / first - (h00 * h01 + n0 * h11) / first * (n0 * c1) - h00 * c1
    planes, rows, depth = b_ref.shape
    for i in range(planes):
        b, image = b_ref[i], image_ref[i]
        solution_ref[i] = c0 * b + c1 * image
        residual_ref[i] = b - c0 * image - c1 * twice_ref[i]
    corners = by_turn(corner_first_ref[...], corner_second_ref[...], "gy")
    for side, (j, here, corner) in enumerate(zip((0, rows - 1), has_beside("gy"), corners)):
        for end, i in enumerate((0, planes - 1)):
            b, cond = corner[end : end + 1], corner[2 + end : 3 + end]
            cond = jnp.where(here, cond, 0.0)
            at = 6 * (2 * side + end)
            x_link, x_b, x_cond, y_link, y_b, y_cond = (
                ends_ref[at + k : at + k + 1] for k in range(6)
            )
            lacked = x_link * link(x_cond, cond) * (x_b - b)
            lacked = lacked + y_link * link(y_cond, cond) * (y_b - b)
            residual_ref[i, j : j + 1] = residual_ref[i, j : j + 1] + c1 * lacked


def call(kernel, shapes, *operands, scratch=(), inputs=pltpu.VMEM, flops=0):
    return pl.pallas_call(
        kernel,
        out_shape=[
            shape if hasattr(shape, "dtype") else jax.ShapeDtypeStruct(shape, jnp.float32)
            for shape in shapes
        ],
        in_specs=[pl.BlockSpec(memory_space=inputs)] * len(operands),
        out_specs=[pl.BlockSpec(memory_space=pltpu.VMEM)] * len(shapes),
        scratch_shapes=scratch,
        compiler_params=pltpu.CompilerParams(vmem_limit_bytes=48 * 1024 * 1024),
        cost_estimate=pl.CostEstimate(flops=flops, bytes_accessed=0, transcendentals=0),
    )(*operands)


def swap(array, axis, turn):
    nx, ny = lax.axis_size("gx"), lax.axis_size("gy")
    pairs = []
    for x in range(nx):
        for y in range(ny):
            here, count = (x, nx) if axis == "gx" else (y, ny)
            there = here + 1 if here % 2 == turn else here - 1
            if 0 <= there < count:
                partner = (there, y) if axis == "gx" else (x, there)
            else:
                partner = (x, y ^ 1) if axis == "gx" else (x ^ 1, y)
            pairs.append((x * ny + y, partner[0] * ny + partner[1]))
    return lax.ppermute(array, ("gx", "gy"), pairs)


def everyones(sketch):
    nx, ny = lax.axis_size("gx"), lax.axis_size("gy")
    middle = nx // 2 - 1, ny // 2
    places = [(x, y) for x in range(nx) for y in range(ny)]
    places.sort(key=lambda at: (abs(at[1] - middle[1]), abs(at[0] - middle[0]), at))
    group = [x * ny + y for x, y in places]
    copies = jnp.broadcast_to(sketch[None], (nx * ny,) + sketch.shape)
    return lax.all_to_all(copies, ("gx", "gy"), 0, 0, axis_index_groups=[group])


def body(b, warmth, phase, slots, draw):
    planes, rows, depth = b.shape
    block, wide = b.shape, (planes + 2, rows, depth)
    face, line, corner = (3 * rows + 4, depth), (3 * planes + 4, depth), (4, depth)
    cells = pltpu.VMEM((depth // LANES, (planes * rows + 8) * 8, LANES), jnp.float32)
    total = HIGH * 2 * PAIR, LOW
    hots = [
        jax.ShapeDtypeStruct((planes * rows * count, depth), jnp.bfloat16)
        for count in (LOW, HIGH * 2 * PAIR)
    ]
    work = b.size * SKETCH * 6
    b, cond, cap, y_link, z_link, inner, draw, slots, x_first, x_second, y_first, y_second = call(
        first_kernel,
        [block] * 8 + [face, face, line, line],
        *(
            pltpu.with_memory_space_constraint(x, pltpu.HBM)
            for x in (b, warmth, phase, draw, slots)
        ),
        scratch=[
            pltpu.VMEM(block, warmth.dtype),
            pltpu.VMEM(block, phase.dtype),
            pltpu.VMEM(block, slots.dtype),
            pltpu.SemaphoreType.DMA((5,)),
        ],
        inputs=pltpu.HBM,
    )
    got_x = swap(x_second, "gx", 1), swap(x_first, "gx", 0)
    got_y = swap(y_second, "gy", 1), swap(y_first, "gy", 0)
    *hots, b_sketch = call(
        slot_kernel, [*hots, (PAIR, SKETCH)], b, draw, slots, scratch=[cells], flops=work
    )
    image_wide, x_link, beside, inside = call(
        inside_kernel,
        [wide, (planes + 1, rows, depth), (4, rows, depth), total],
        b, cond, cap, y_link, z_link, inner, draw, *hots, *got_x,
        scratch=[cells],
        flops=work,
    )
    image, twice, sketch, first, second, ends = call(
        third_kernel,
        [block, block, (FIELDS + 1, SKETCH), corner, corner, (24, depth)],
        b, cap, y_link, z_link, draw, *hots, y_second, y_first, image_wide, x_link, beside,
        *got_x, *got_y, b_sketch, inside,
        scratch=[cells, pltpu.VMEM((3, 8, depth), jnp.float32)],
        flops=work,
    )
    got_corners = [swap(array, "gy", turn) for turn, array in enumerate((first, second))]
    sketches = everyones(sketch)
    return tuple(
        call(last_kernel, [block, block], sketches, b, image, twice, ends, *got_corners)
    )


def solution(mesh):
    spec = P(("parts", "gx"), "gy", None)
    return jax.shard_map(
        body, mesh=mesh, in_specs=(spec,) * 5, out_specs=(spec,) * 2, check_vma=False
    )
```

```python
import jax
import jax.numpy as jnp
from jax import lax
from jax.experimental import pallas as pl
from jax.experimental.pallas import tpu as pltpu
from jax.sharding import PartitionSpec as P

SKETCH = 128
LOW = 32
HIGH = SKETCH // LOW
FIELDS = 3
PAIR = 2
LANES = 128
epsilon = 1e-06


def traits(warmth, phase):
    powder, solid = phase == 0, phase == 1
    offset = jnp.where(powder, 0.2, jnp.where(solid, 1.0, 0.6))
    return offset * (0.5 + warmth), jnp.where(powder, 1.0, jnp.where(solid, 2.0, 1.5))


def link(first, second):
    total = first + second
    return 2.0 * first * second / jnp.where(total > 0.0, total, 1.0)


def ahead(plane, axis):
    return pltpu.roll(plane, plane.shape[axis] - 1, axis)


def inner_links(cond):
    links = []
    for axis in (0, 1):
        index = lax.broadcasted_iota(jnp.int32, cond.shape, axis)
        links.append(
            jnp.where(index < cond.shape[axis] - 1, link(cond, ahead(cond, axis)), 0.0)
        )
    return links


def inner_flow(field, links):
    total = None
    for axis in (0, 1):
        flow = links[axis] * (field - ahead(field, axis))
        part = flow - pltpu.roll(flow, 1, axis)
        total = part if total is None else total + part
    return total


def apply_inside(images, x_links, links, caps):
    results = []
    flow_low = x_links[0] * (images[0] - images[1])
    for i in range(1, len(images) - 1):
        image = images[i]
        flow = x_links[i] * (image - images[i + 1])
        inside = inner_flow(image, links[i - 1])
        results.append(caps[i - 1] * image + inside + (flow - flow_low))
        flow_low = flow
    return results


def parts_of(slot):
    high = jnp.floor(slot * (1.0 / LOW))
    return slot - LOW * high, high


def one_hot(values, j, count, each):
    shape = (count * each, values.shape[1])
    index = lax.broadcasted_iota(jnp.int32, shape, 0) // each
    index = index.astype(jnp.float32).astype(jnp.bfloat16)
    row = jnp.broadcast_to(values[j : j + 1], shape).astype(jnp.bfloat16)
    one = jnp.ones_like(row)
    return jnp.where(row == index, one, jnp.zeros_like(one))


def put_cells(fields, draw, start, cells_ref):
    coarse, fine = [], []
    for field in fields:
        weighted = draw * field
        head = weighted.astype(jnp.bfloat16).astype(jnp.float32)
        coarse.append(head)
        fine.append(weighted - head)
    for f, part in enumerate(coarse + fine):
        for t in range(cells_ref.shape[0]):
            cells_ref[t, pl.ds(start + f, draw.shape[0], stride=8), :] = part[
                :, t * LANES : (t + 1) * LANES
            ]


def masked_cells(mask, start, j, cells_ref):
    at = pl.ds(start + j * 8, 8)
    cells = jnp.concatenate([cells_ref[t, at, :] for t in range(cells_ref.shape[0])], axis=1)
    filled = lax.broadcasted_iota(jnp.int32, cells.shape, 0) < 2 * PAIR
    cells = jnp.where(filled, cells, pltpu.roll(cells, 2 * PAIR, 0))
    return jnp.concatenate([cells, cells], axis=0).astype(jnp.bfloat16) * mask


def product(left, right):
    return lax.dot_general(
        jnp.concatenate(left, axis=1),
        jnp.concatenate(right, axis=1),
        (((1,), (1,)), ((), ())),
        preferred_element_type=jnp.float32,
    )


def as_sketch(total):
    each = 2 * PAIR
    total = jnp.concatenate([total[h * each : (h + 1) * each] for h in range(HIGH)], axis=1)
    return total[:PAIR] + total[PAIR:]


def sketch_rows(planes, low_ref, high_ref, cells_ref):
    total = 0.0
    each = HIGH * 2 * PAIR
    for i, (fields, draw, chosen) in enumerate(planes):
        rows = draw.shape[0]
        start = i * rows * 8
        put_cells(fields, draw, start, cells_ref)
        left, right = [], []
        for j in chosen:
            at = i * rows + j
            mask = high_ref[at * each : (at + 1) * each]
            left.append(masked_cells(mask, start, j, cells_ref))
            right.append(low_ref[at * LOW : (at + 1) * LOW])
        total = total + product(left, right)
    return total


def slot_kernel(b_ref, draw_ref, slot_ref, low_ref, high_ref, sketch_ref, cells_ref):
    planes, rows = b_ref.shape[:2]
    each = HIGH * 2 * PAIR
    total = 0.0
    for i in range(planes):
        start = i * rows * 8
        put_cells((b_ref[i],) * PAIR, draw_ref[i], start, cells_ref)
        low, high = parts_of(slot_ref[i])
        left, right = [], []
        for j in range(rows):
            at = i * rows + j
            mask, hot = one_hot(high, j, HIGH, 2 * PAIR), one_hot(low, j, LOW, 1)
            high_ref[at * each : (at + 1) * each] = mask
            low_ref[at * LOW : (at + 1) * LOW] = hot
            left.append(masked_cells(mask, start, j, cells_ref))
            right.append(hot)
        total = total + product(left, right)
    sketch_ref[...] = as_sketch(total)


def first_kernel(
    b_hbm, warmth_hbm, phase_hbm, draw_hbm, slot_hbm, b_ref, cond_ref, cap_ref, y_link_ref,
    z_link_ref, inner_ref, draw_ref, slot_ref, x_first_ref, x_second_ref, y_first_ref,
    y_second_ref, warmth_ref, phase_ref, number_ref, arrived,
):
    copies = [
        pltpu.make_async_copy(source, target, arrived.at[k])
        for k, (source, target) in enumerate(
            (
                (b_hbm, b_ref),
                (warmth_hbm, warmth_ref),
                (phase_hbm, phase_ref),
                (draw_hbm, draw_ref),
                (slot_hbm, number_ref),
            )
        )
    ]
    for copy in copies:
        copy.start()
    for copy in copies[:3]:
        copy.wait()
    planes, rows = b_ref.shape[:2]
    images, conds = [], []
    for i in range(planes):
        cond, cap = traits(warmth_ref[i], phase_ref[i])
        cap_ref[i] = cap
        cond_ref[i] = cond
        y_link_ref[i], z_link_ref[i] = links = inner_links(cond)
        field = b_ref[i]
        image = cap * field + inner_flow(field, links)
        if i:
            flow = link(conds[-1], cond) * (b_ref[i - 1] - field)
            images[-1] = images[-1] + flow
            image = image - flow
        conds.append(cond)
        images.append(image)
    for i in range(planes):
        inner_ref[i] = images[i]
    for k, field in enumerate((images, [b_ref[i] for i in range(planes)], conds)):
        at = slice(k * rows, (k + 1) * rows)
        x_first_ref[at], x_second_ref[at] = by_turn(field[0], field[-1], "gx")
        for i, plane in enumerate(field):
            at = slice(k * planes + i, k * planes + i + 1)
            y_first_ref[at], y_second_ref[at] = by_turn(plane[:1], plane[rows - 1 :], "gy")
    for copy in copies[3:]:
        copy.wait()
    for i in range(planes):
        slot_ref[i] = number_ref[i].astype(jnp.float32)
    for k, ref in enumerate((draw_ref, slot_ref)):
        ends = [ref[0], ref[planes - 1]]
        for e, j in enumerate((0, rows - 1)):
            at = slice(3 * rows + 2 * k + e, 3 * rows + 2 * k + e + 1)
            lines = [plane[j : j + 1] for plane in ends]
            x_first_ref[at], x_second_ref[at] = by_turn(*lines, "gx")
        for e, plane in enumerate(ends):
            at = slice(3 * planes + 2 * k + e, 3 * planes + 2 * k + e + 1)
            lines = [plane[:1], plane[rows - 1 :]]
            y_first_ref[at], y_second_ref[at] = by_turn(*lines, "gy")


def by_turn(one, other, axis):
    odd = lax.axis_index(axis) % 2 == 1
    return jnp.where(odd, one, other), jnp.where(odd, other, one)


def has_beside(axis):
    at = lax.axis_index(axis)
    return at > 0, at < lax.axis_size(axis) - 1


def reached(rows):
    others = [j for j in range(rows) if 2 <= j < rows - 2]
    return [j for j in range(rows) if j not in others], others


def inside_kernel(
    b_ref, cond_ref, cap_ref, y_link_ref, z_link_ref, inner_ref, draw_ref, low_ref, high_ref,
    got_second_ref, got_first_ref, wide_ref, x_link_ref, beside_ref, sketch_ref, cells_ref,
):
    planes, rows = b_ref.shape[:2]
    (image_low, image_high), (b_low, b_high), (c_low, c_high) = (
        by_turn(*(ref[k * rows : (k + 1) * rows] for ref in (got_first_ref, got_second_ref)), "gx")
        for k in range(3)
    )
    below, above = has_beside("gx")
    c_low, c_high = jnp.where(below, c_low, 0.0), jnp.where(above, c_high, 0.0)
    for k, plane in enumerate((b_low, b_high, c_low, c_high)):
        beside_ref[k] = plane
    conds = [c_low] + [cond_ref[i] for i in range(planes)] + [c_high]
    x_links = [link(conds[i], conds[i + 1]) for i in range(planes + 1)]
    for i, conductance in enumerate(x_links):
        x_link_ref[i] = conductance
    low_flow = x_links[0] * (b_low - b_ref[0])
    high_flow = x_links[-1] * (b_ref[planes - 1] - b_high)
    images = [image_low + low_flow] + [inner_ref[i] for i in range(planes)]
    images.append(image_high - high_flow)
    images[1] = images[1] - low_flow
    images[-2] = images[-2] + high_flow
    for i, image in enumerate(images):
        wide_ref[i] = image
    links = [(y_link_ref[i], z_link_ref[i]) for i in range(planes)]
    twice = apply_inside(images, x_links, links, [cap_ref[i] for i in range(planes)])
    chosen = reached(rows)[1]
    cells = [((images[i + 1], twice[i]), draw_ref[i], chosen) for i in range(planes)]
    sketch_ref[...] = sketch_rows(cells, low_ref, high_ref, cells_ref)


def third_kernel(
    b_ref, cap_ref, y_link_ref, z_link_ref, draw_ref, low_ref, high_ref, own_second_ref,
    own_first_ref, wide_ref, x_link_ref, beside_ref, x_second_ref, x_first_ref, y_second_ref,
    y_first_ref, b_sketch_ref, inside_ref, image_ref, twice_ref, sketch_ref, corner_first_ref,
    corner_second_ref, ends_ref, cells_ref, extra_ref,
):
    planes, rows, depth = b_ref.shape
    index = lax.broadcasted_iota(jnp.int32, (rows, depth), 0)
    images = [wide_ref[i] for i in range(planes + 2)]
    x_links = [x_link_ref[i] for i in range(planes + 1)]
    b_beside, c_beside = (beside_ref[0], beside_ref[1]), (beside_ref[2], beside_ref[3])
    x_ends = []
    for end, i in enumerate((0, planes - 1)):
        conductance = x_links[-end]
        x_ends.append((i, conductance, conductance * (b_ref[i] - b_beside[end])))
    x_tails = by_turn(x_first_ref[3 * rows :], x_second_ref[3 * rows :], "gx")
    own_lines = by_turn(own_first_ref[...], own_second_ref[...], "gy")
    y_lines = by_turn(y_first_ref[...], y_second_ref[...], "gy")
    beside = []
    for side, (j, here, own, line) in enumerate(
        zip((0, rows - 1), has_beside("gy"), own_lines, y_lines)
    ):
        row = slice(j, j + 1)
        beyond, b_line, c_line = (line[k * planes : (k + 1) * planes] for k in range(3))
        c_line = jnp.where(here, c_line, 0.0)
        y_link = link(own[2 * planes : 3 * planes], c_line)
        y_flow = y_link * (own[planes : 2 * planes] - b_line)
        beyond = beyond - y_flow
        for i in range(planes):
            at = slice(i, i + 1)
            images[i + 1] = images[i + 1] + jnp.where(index == j, y_flow[at], 0.0)
            beside.append((i, jnp.where(index == j, y_link[at], 0.0), beyond[at]))
        for end, (i, x_link, x_flow) in enumerate(x_ends):
            line_at, at = slice(i, i + 1), 4 * side + 2 * end
            tail = x_tails[end]
            values = -x_link[row] * y_flow[line_at], tail[side:][:1], tail[2 + side :][:1]
            for k, value in enumerate(values):
                extra_ref[k, at : at + 1] = value
            tail = line[3 * planes :]
            values = -y_link[line_at] * x_flow[row], tail[end:][:1], tail[2 + end :][:1]
            for k, value in enumerate(values):
                extra_ref[k, at + 1 : at + 2] = value
            at = 6 * (2 * side + end)
            values = x_link[row], b_beside[end][row], c_beside[end][row]
            values += y_link[line_at], b_line[line_at], c_line[line_at]
            for k, value in enumerate(values):
                ends_ref[at + k : at + k + 1] = value
    links = [(y_link_ref[i], z_link_ref[i]) for i in range(planes)]
    twice = apply_inside(images, x_links, links, [cap_ref[i] for i in range(planes)])
    for i, conductance, value in beside:
        twice[i] = twice[i] + conductance * (images[i + 1] - value)
    for i in range(planes):
        image_ref[i] = images[i + 1]
        twice_ref[i] = twice[i]
    chosen = reached(rows)[0]
    cells = [((images[i + 1], twice[i]), draw_ref[i], chosen) for i in range(planes)]
    total = inside_ref[...] + sketch_rows(cells, low_ref, high_ref, cells_ref)
    start = planes * rows * 8
    put_cells((jnp.zeros((8, depth), jnp.float32), extra_ref[0]), extra_ref[1], start, cells_ref)
    low, high = parts_of(extra_ref[2])
    left, right = [], []
    for j in range(8):
        mask = one_hot(high, j, HIGH, 2 * PAIR)
        left.append(masked_cells(mask, start, j, cells_ref))
        right.append(one_hot(low, j, LOW, 1))
    sketch_ref[1 : 1 + PAIR] = as_sketch(total + product(left, right))
    sketch_ref[:1] = b_sketch_ref[:1]
    sketch_ref[1 + PAIR :] = b_sketch_ref[:1]
    for k, plane in enumerate(b_beside + c_beside):
        at = slice(k, k + 1)
        corner_first_ref[at], corner_second_ref[at] = by_turn(
            plane[:1], plane[rows - 1 :], "gy"
        )


def last_kernel(
    sketch_ref, b_ref, image_ref, twice_ref, ends_ref, corner_first_ref, corner_second_ref,
    solution_ref, residual_ref,
):
    sketches = jnp.sum(sketch_ref[...], axis=0)

    def inner(first, second):
        return jnp.sum(first * second, axis=1, keepdims=True)

    s0, s1, s2 = (sketches[i : i + 1] for i in range(FIELDS))
    beta_inverse = 1.0 / jnp.sqrt(inner(s0, s0) + epsilon)
    h00 = inner(s0, s1) * beta_inverse * beta_inverse
    q0, p0 = s0 * beta_inverse, s1 * beta_inverse
    t0 = p0 - h00 * q0
    p1 = s2 * beta_inverse - h00 * p0
    n0 = jnp.sqrt(inner(t0, t0) + epsilon)
    n0_inverse = 1.0 / n0
    h01 = inner(q0, p1) * n0_inverse
    h11 = inner(t0, p1) * n0_inverse * n0_inverse
    t1 = p1 * n0_inverse - h01 * q0 - h11 * (t0 * n0_inverse)
    n1_square = inner(t1, t1) + epsilon
    first = h00 * h00 + n0 * n0
    cross = h00 * h11 - n0 * h01
    ratio = cross / first
    c1 = -ratio / (cross * ratio + n1_square)
    c0 = h00 / first - (h00 * h01 + n0 * h11) / first * (n0 * c1) - h00 * c1
    planes, rows, depth = b_ref.shape
    for i in range(planes):
        b, image = b_ref[i], image_ref[i]
        solution_ref[i] = c0 * b + c1 * image
        residual_ref[i] = b - c0 * image - c1 * twice_ref[i]
    corners = by_turn(corner_first_ref[...], corner_second_ref[...], "gy")
    for side, (j, here, corner) in enumerate(zip((0, rows - 1), has_beside("gy"), corners)):
        for end, i in enumerate((0, planes - 1)):
            b, cond = corner[end : end + 1], corner[2 + end : 3 + end]
            cond = jnp.where(here, cond, 0.0)
            at = 6 * (2 * side + end)
            x_link, x_b, x_cond, y_link, y_b, y_cond = (
                ends_ref[at + k : at + k + 1] for k in range(6)
            )
            lacked = x_link * link(x_cond, cond) * (x_b - b)
            lacked = lacked + y_link * link(y_cond, cond) * (y_b - b)
            residual_ref[i, j : j + 1] = residual_ref[i, j : j + 1] + c1 * lacked


def call(kernel, shapes, *operands, scratch=(), inputs=pltpu.VMEM, flops=0):
    return pl.pallas_call(
        kernel,
        out_shape=[
            shape if hasattr(shape, "dtype") else jax.ShapeDtypeStruct(shape, jnp.float32)
            for shape in shapes
        ],
        in_specs=[pl.BlockSpec(memory_space=inputs)] * len(operands),
        out_specs=[pl.BlockSpec(memory_space=pltpu.VMEM)] * len(shapes),
        scratch_shapes=scratch,
        compiler_params=pltpu.CompilerParams(vmem_limit_bytes=48 * 1024 * 1024),
        cost_estimate=pl.CostEstimate(flops=flops, bytes_accessed=0, transcendentals=0),
    )(*operands)


def swap(array, axis, turn):
    nx, ny = lax.axis_size("gx"), lax.axis_size("gy")
    pairs = []
    for x in range(nx):
        for y in range(ny):
            here, count = (x, nx) if axis == "gx" else (y, ny)
            there = here + 1 if here % 2 == turn else here - 1
            if 0 <= there < count:
                partner = (there, y) if axis == "gx" else (x, there)
            else:
                partner = (x, y ^ 1) if axis == "gx" else (x ^ 1, y)
            pairs.append((x * ny + y, partner[0] * ny + partner[1]))
    return lax.ppermute(array, ("gx", "gy"), pairs)


def everyones(sketch):
    nx, ny = lax.axis_size("gx"), lax.axis_size("gy")
    middle = nx // 2 - 1, ny // 2
    places = [(x, y) for x in range(nx) for y in range(ny)]
    places.sort(key=lambda at: (abs(at[1] - middle[1]), abs(at[0] - middle[0]), at))
    group = [x * ny + y for x, y in places]
    copies = jnp.broadcast_to(sketch[None], (nx * ny,) + sketch.shape)
    return lax.all_to_all(copies, ("gx", "gy"), 0, 0, axis_index_groups=[group])


def body(b, warmth, phase, slots, draw):
    planes, rows, depth = b.shape
    block, wide = b.shape, (planes + 2, rows, depth)
    face, line, corner = (3 * rows + 4, depth), (3 * planes + 4, depth), (4, depth)
    cells = pltpu.VMEM((depth // LANES, (planes * rows + 8) * 8, LANES), jnp.float32)
    total = HIGH * 2 * PAIR, LOW
    hots = [
        jax.ShapeDtypeStruct((planes * rows * count, depth), jnp.bfloat16)
        for count in (LOW, HIGH * 2 * PAIR)
    ]
    work = b.size * SKETCH * 6
    b, cond, cap, y_link, z_link, inner, draw, slots, x_first, x_second, y_first, y_second = call(
        first_kernel,
        [block] * 8 + [face, face, line, line],
        *(
            pltpu.with_memory_space_constraint(x, pltpu.HBM)
            for x in (b, warmth, phase, draw, slots)
        ),
        scratch=[
            pltpu.VMEM(block, warmth.dtype),
            pltpu.VMEM(block, phase.dtype),
            pltpu.VMEM(block, slots.dtype),
            pltpu.SemaphoreType.DMA((5,)),
        ],
        inputs=pltpu.HBM,
    )
    got_x = swap(x_second, "gx", 1), swap(x_first, "gx", 0)
    got_y = swap(y_second, "gy", 1), swap(y_first, "gy", 0)
    *hots, b_sketch = call(
        slot_kernel, [*hots, (PAIR, SKETCH)], b, draw, slots, scratch=[cells], flops=work
    )
    image_wide, x_link, beside, inside = call(
        inside_kernel,
        [wide, (planes + 1, rows, depth), (4, rows, depth), total],
        b, cond, cap, y_link, z_link, inner, draw, *hots, *got_x,
        scratch=[cells],
        flops=work,
    )
    image, twice, sketch, first, second, ends = call(
        third_kernel,
        [block, block, (FIELDS + 1, SKETCH), corner, corner, (24, depth)],
        b, cap, y_link, z_link, draw, *hots, y_second, y_first, image_wide, x_link, beside,
        *got_x, *got_y, b_sketch, inside,
        scratch=[cells, pltpu.VMEM((3, 8, depth), jnp.float32)],
        flops=work,
    )
    got_corners = [swap(array, "gy", turn) for turn, array in enumerate((first, second))]
    sketches = everyones(sketch)
    return tuple(
        call(last_kernel, [block, block], sketches, b, image, twice, ends, *got_corners)
    )


def solution(mesh):
    spec = P(("parts", "gx"), "gy", None)
    return jax.shard_map(
        body, mesh=mesh, in_specs=(spec,) * 5, out_specs=(spec,) * 2, check_vma=False
    )
```

```python
import jax
import jax.numpy as jnp
from jax import lax
from jax.experimental import pallas as pl
from jax.experimental.pallas import tpu as pltpu
from jax.sharding import PartitionSpec as P

SKETCH = 128
LOW = 32
HIGH = SKETCH // LOW
FIELDS = 3
PAIR = 2
LANES = 128
epsilon = 1e-06


def traits(warmth, phase):
    powder, solid = phase == 0, phase == 1
    offset = jnp.where(powder, 0.2, jnp.where(solid, 1.0, 0.6))
    return offset * (0.5 + warmth), jnp.where(powder, 1.0, jnp.where(solid, 2.0, 1.5))


def link(first, second):
    total = first + second
    return 2.0 * first * second / jnp.where(total > 0.0, total, 1.0)


def ahead(plane, axis):
    return pltpu.roll(plane, plane.shape[axis] - 1, axis)


def inner_links(cond):
    links = []
    for axis in (0, 1):
        index = lax.broadcasted_iota(jnp.int32, cond.shape, axis)
        links.append(
            jnp.where(index < cond.shape[axis] - 1, link(cond, ahead(cond, axis)), 0.0)
        )
    return links


def inner_flow(field, links):
    total = None
    for axis in (0, 1):
        flow = links[axis] * (field - ahead(field, axis))
        part = flow - pltpu.roll(flow, 1, axis)
        total = part if total is None else total + part
    return total


def apply_inside(images, x_links, links, caps):
    results = []
    flow_low = x_links[0] * (images[0] - images[1])
    for i in range(1, len(images) - 1):
        image = images[i]
        flow = x_links[i] * (image - images[i + 1])
        inside = inner_flow(image, links[i - 1])
        results.append(caps[i - 1] * image + inside + (flow - flow_low))
        flow_low = flow
    return results


def parts_of(slot):
    high = jnp.floor(slot * (1.0 / LOW))
    return slot - LOW * high, high


def one_hot(values, j, count, each):
    shape = (count * each, values.shape[1])
    index = lax.broadcasted_iota(jnp.int32, shape, 0) // each
    index = index.astype(jnp.float32).astype(jnp.bfloat16)
    row = jnp.broadcast_to(values[j : j + 1], shape).astype(jnp.bfloat16)
    one = jnp.ones_like(row)
    return jnp.where(row == index, one, jnp.zeros_like(one))


def put_cells(fields, draw, start, cells_ref):
    coarse, fine = [], []
    for field in fields:
        weighted = draw * field
        head = weighted.astype(jnp.bfloat16).astype(jnp.float32)
        coarse.append(head)
        fine.append(weighted - head)
    for f, part in enumerate(coarse + fine):
        for t in range(cells_ref.shape[0]):
            cells_ref[t, pl.ds(start + f, draw.shape[0], stride=8), :] = part[
                :, t * LANES : (t + 1) * LANES
            ]


def masked_cells(mask, start, j, cells_ref):
    at = pl.ds(start + j * 8, 8)
    cells = jnp.concatenate([cells_ref[t, at, :] for t in range(cells_ref.shape[0])], axis=1)
    filled = lax.broadcasted_iota(jnp.int32, cells.shape, 0) < 2 * PAIR
    cells = jnp.where(filled, cells, pltpu.roll(cells, 2 * PAIR, 0))
    return jnp.concatenate([cells, cells], axis=0).astype(jnp.bfloat16) * mask


def product(left, right):
    return lax.dot_general(
        jnp.concatenate(left, axis=1),
        jnp.concatenate(right, axis=1),
        (((1,), (1,)), ((), ())),
        preferred_element_type=jnp.float32,
    )


def as_sketch(total):
    each = 2 * PAIR
    total = jnp.concatenate([total[h * each : (h + 1) * each] for h in range(HIGH)], axis=1)
    return total[:PAIR] + total[PAIR:]


def sketch_rows(planes, low_ref, high_ref, cells_ref):
    total = 0.0
    each = HIGH * 2 * PAIR
    for i, (fields, draw, chosen) in enumerate(planes):
        rows = draw.shape[0]
        start = i * rows * 8
        put_cells(fields, draw, start, cells_ref)
        left, right = [], []
        for j in chosen:
            at = i * rows + j
            mask = high_ref[at * each : (at + 1) * each]
            left.append(masked_cells(mask, start, j, cells_ref))
            right.append(low_ref[at * LOW : (at + 1) * LOW])
        total = total + product(left, right)
    return total


def slot_kernel(b_ref, draw_ref, slot_ref, low_ref, high_ref, sketch_ref, cells_ref):
    planes, rows = b_ref.shape[:2]
    each = HIGH * 2 * PAIR
    total = 0.0
    for i in range(planes):
        start = i * rows * 8
        put_cells((b_ref[i],) * PAIR, draw_ref[i], start, cells_ref)
        low, high = parts_of(slot_ref[i])
        left, right = [], []
        for j in range(rows):
            at = i * rows + j
            mask, hot = one_hot(high, j, HIGH, 2 * PAIR), one_hot(low, j, LOW, 1)
            high_ref[at * each : (at + 1) * each] = mask
            low_ref[at * LOW : (at + 1) * LOW] = hot
            left.append(masked_cells(mask, start, j, cells_ref))
            right.append(hot)
        total = total + product(left, right)
    sketch_ref[...] = as_sketch(total)


def first_kernel(
    b_hbm, warmth_hbm, phase_hbm, draw_hbm, slot_hbm, b_ref, cond_ref, cap_ref, y_link_ref,
    z_link_ref, inner_ref, draw_ref, slot_ref, x_first_ref, x_second_ref, y_first_ref,
    y_second_ref, warmth_ref, phase_ref, number_ref, arrived,
):
    copies = [
        pltpu.make_async_copy(source, target, arrived.at[k])
        for k, (source, target) in enumerate(
            (
                (b_hbm, b_ref),
                (warmth_hbm, warmth_ref),
                (phase_hbm, phase_ref),
                (draw_hbm, draw_ref),
                (slot_hbm, number_ref),
            )
        )
    ]
    for copy in copies:
        copy.start()
    for copy in copies[:3]:
        copy.wait()
    planes, rows = b_ref.shape[:2]
    images, conds = [], []
    for i in range(planes):
        cond, cap = traits(warmth_ref[i], phase_ref[i])
        cap_ref[i] = cap
        cond_ref[i] = cond
        y_link_ref[i], z_link_ref[i] = links = inner_links(cond)
        field = b_ref[i]
        image = cap * field + inner_flow(field, links)
        if i:
            flow = link(conds[-1], cond) * (b_ref[i - 1] - field)
            images[-1] = images[-1] + flow
            image = image - flow
        conds.append(cond)
        images.append(image)
    for i in range(planes):
        inner_ref[i] = images[i]
    for k, field in enumerate((images, [b_ref[i] for i in range(planes)], conds)):
        at = slice(k * rows, (k + 1) * rows)
        x_first_ref[at], x_second_ref[at] = by_turn(field[0], field[-1], "gx")
        for i, plane in enumerate(field):
            at = slice(k * planes + i, k * planes + i + 1)
            y_first_ref[at], y_second_ref[at] = by_turn(plane[:1], plane[rows - 1 :], "gy")
    for copy in copies[3:]:
        copy.wait()
    for i in range(planes):
        slot_ref[i] = number_ref[i].astype(jnp.float32)
    for k, ref in enumerate((draw_ref, slot_ref)):
        ends = [ref[0], ref[planes - 1]]
        for e, j in enumerate((0, rows - 1)):
            at = slice(3 * rows + 2 * k + e, 3 * rows + 2 * k + e + 1)
            lines = [plane[j : j + 1] for plane in ends]
            x_first_ref[at], x_second_ref[at] = by_turn(*lines, "gx")
        for e, plane in enumerate(ends):
            at = slice(3 * planes + 2 * k + e, 3 * planes + 2 * k + e + 1)
            lines = [plane[:1], plane[rows - 1 :]]
            y_first_ref[at], y_second_ref[at] = by_turn(*lines, "gy")


def by_turn(one, other, axis):
    odd = lax.axis_index(axis) % 2 == 1
    return jnp.where(odd, one, other), jnp.where(odd, other, one)


def has_beside(axis):
    at = lax.axis_index(axis)
    return at > 0, at < lax.axis_size(axis) - 1


def reached(rows):
    others = [j for j in range(rows) if 2 <= j < rows - 2]
    return [j for j in range(rows) if j not in others], others


def inside_kernel(
    b_ref, cond_ref, cap_ref, y_link_ref, z_link_ref, inner_ref, draw_ref, low_ref, high_ref,
    got_second_ref, got_first_ref, wide_ref, x_link_ref, beside_ref, sketch_ref, corner_first_ref,
    cells_ref,
):
    planes, rows = b_ref.shape[:2]
    (image_low, image_high), (b_low, b_high), (c_low, c_high) = (
        by_turn(*(ref[k * rows : (k + 1) * rows] for ref in (got_first_ref, got_second_ref)), "gx")
        for k in range(3)
    )
    below, above = has_beside("gx")
    c_low, c_high = jnp.where(below, c_low, 0.0), jnp.where(above, c_high, 0.0)
    for k, plane in enumerate((b_low, b_high, c_low, c_high)):
        beside_ref[k] = plane
        corner_first_ref[k : k + 1] = by_turn(plane[:1], plane[rows - 1 :], "gy")[0]
    conds = [c_low] + [cond_ref[i] for i in range(planes)] + [c_high]
    x_links = [link(conds[i], conds[i + 1]) for i in range(planes + 1)]
    for i, conductance in enumerate(x_links):
        x_link_ref[i] = conductance
    low_flow = x_links[0] * (b_low - b_ref[0])
    high_flow = x_links[-1] * (b_ref[planes - 1] - b_high)
    images = [image_low + low_flow] + [inner_ref[i] for i in range(planes)]
    images.append(image_high - high_flow)
    images[1] = images[1] - low_flow
    images[-2] = images[-2] + high_flow
    for i, image in enumerate(images):
        wide_ref[i] = image
    links = [(y_link_ref[i], z_link_ref[i]) for i in range(planes)]
    twice = apply_inside(images, x_links, links, [cap_ref[i] for i in range(planes)])
    chosen = reached(rows)[1]
    cells = [((images[i + 1], twice[i]), draw_ref[i], chosen) for i in range(planes)]
    sketch_ref[...] = sketch_rows(cells, low_ref, high_ref, cells_ref)


def third_kernel(
    b_ref, cap_ref, y_link_ref, z_link_ref, draw_ref, low_ref, high_ref, own_second_ref,
    own_first_ref, wide_ref, x_link_ref, beside_ref, x_second_ref, x_first_ref, y_second_ref,
    y_first_ref, b_sketch_ref, inside_ref, image_ref, twice_ref, sketch_ref, corner_second_ref,
    ends_ref, cells_ref, extra_ref,
):
    planes, rows, depth = b_ref.shape
    index = lax.broadcasted_iota(jnp.int32, (rows, depth), 0)
    images = [wide_ref[i] for i in range(planes + 2)]
    x_links = [x_link_ref[i] for i in range(planes + 1)]
    b_beside, c_beside = (beside_ref[0], beside_ref[1]), (beside_ref[2], beside_ref[3])
    x_ends = []
    for end, i in enumerate((0, planes - 1)):
        conductance = x_links[-end]
        x_ends.append((i, conductance, conductance * (b_ref[i] - b_beside[end])))
    x_tails = by_turn(x_first_ref[3 * rows :], x_second_ref[3 * rows :], "gx")
    own_lines = by_turn(own_first_ref[...], own_second_ref[...], "gy")
    y_lines = by_turn(y_first_ref[...], y_second_ref[...], "gy")
    beside = []
    for side, (j, here, own, line) in enumerate(
        zip((0, rows - 1), has_beside("gy"), own_lines, y_lines)
    ):
        row = slice(j, j + 1)
        beyond, b_line, c_line = (line[k * planes : (k + 1) * planes] for k in range(3))
        c_line = jnp.where(here, c_line, 0.0)
        y_link = link(own[2 * planes : 3 * planes], c_line)
        y_flow = y_link * (own[planes : 2 * planes] - b_line)
        beyond = beyond - y_flow
        for i in range(planes):
            at = slice(i, i + 1)
            images[i + 1] = images[i + 1] + jnp.where(index == j, y_flow[at], 0.0)
            beside.append((i, jnp.where(index == j, y_link[at], 0.0), beyond[at]))
        for end, (i, x_link, x_flow) in enumerate(x_ends):
            line_at, at = slice(i, i + 1), 4 * side + 2 * end
            tail = x_tails[end]
            values = -x_link[row] * y_flow[line_at], tail[side:][:1], tail[2 + side :][:1]
            for k, value in enumerate(values):
                extra_ref[k, at : at + 1] = value
            tail = line[3 * planes :]
            values = -y_link[line_at] * x_flow[row], tail[end:][:1], tail[2 + end :][:1]
            for k, value in enumerate(values):
                extra_ref[k, at + 1 : at + 2] = value
            at = 6 * (2 * side + end)
            values = x_link[row], b_beside[end][row], c_beside[end][row]
            values += y_link[line_at], b_line[line_at], c_line[line_at]
            for k, value in enumerate(values):
                ends_ref[at + k : at + k + 1] = value
    links = [(y_link_ref[i], z_link_ref[i]) for i in range(planes)]
    twice = apply_inside(images, x_links, links, [cap_ref[i] for i in range(planes)])
    for i, conductance, value in beside:
        twice[i] = twice[i] + conductance * (images[i + 1] - value)
    for i in range(planes):
        image_ref[i] = images[i + 1]
        twice_ref[i] = twice[i]
    chosen = reached(rows)[0]
    cells = [((images[i + 1], twice[i]), draw_ref[i], chosen) for i in range(planes)]
    total = inside_ref[...] + sketch_rows(cells, low_ref, high_ref, cells_ref)
    start = planes * rows * 8
    put_cells((jnp.zeros((8, depth), jnp.float32), extra_ref[0]), extra_ref[1], start, cells_ref)
    low, high = parts_of(extra_ref[2])
    left, right = [], []
    for j in range(8):
        mask = one_hot(high, j, HIGH, 2 * PAIR)
        left.append(masked_cells(mask, start, j, cells_ref))
        right.append(one_hot(low, j, LOW, 1))
    sketch_ref[1 : 1 + PAIR] = as_sketch(total + product(left, right))
    sketch_ref[:1] = b_sketch_ref[:1]
    sketch_ref[1 + PAIR :] = b_sketch_ref[:1]
    for k, plane in enumerate(b_beside + c_beside):
        corner_second_ref[k : k + 1] = by_turn(plane[:1], plane[rows - 1 :], "gy")[1]


def last_kernel(
    sketch_ref, b_ref, image_ref, twice_ref, ends_ref, corner_first_ref, corner_second_ref,
    solution_ref, residual_ref,
):
    sketches = jnp.sum(sketch_ref[...], axis=0)

    def inner(first, second):
        return jnp.sum(first * second, axis=1, keepdims=True)

    s0, s1, s2 = (sketches[i : i + 1] for i in range(FIELDS))
    beta_inverse = 1.0 / jnp.sqrt(inner(s0, s0) + epsilon)
    h00 = inner(s0, s1) * beta_inverse * beta_inverse
    q0, p0 = s0 * beta_inverse, s1 * beta_inverse
    t0 = p0 - h00 * q0
    p1 = s2 * beta_inverse - h00 * p0
    n0 = jnp.sqrt(inner(t0, t0) + epsilon)
    n0_inverse = 1.0 / n0
    h01 = inner(q0, p1) * n0_inverse
    h11 = inner(t0, p1) * n0_inverse * n0_inverse
    t1 = p1 * n0_inverse - h01 * q0 - h11 * (t0 * n0_inverse)
    n1_square = inner(t1, t1) + epsilon
    first = h00 * h00 + n0 * n0
    cross = h00 * h11 - n0 * h01
    ratio = cross / first
    c1 = -ratio / (cross * ratio + n1_square)
    c0 = h00 / first - (h00 * h01 + n0 * h11) / first * (n0 * c1) - h00 * c1
    planes, rows, depth = b_ref.shape
    for i in range(planes):
        b, image = b_ref[i], image_ref[i]
        solution_ref[i] = c0 * b + c1 * image
        residual_ref[i] = b - c0 * image - c1 * twice_ref[i]
    corners = by_turn(corner_first_ref[...], corner_second_ref[...], "gy")
    for side, (j, here, corner) in enumerate(zip((0, rows - 1), has_beside("gy"), corners)):
        for end, i in enumerate((0, planes - 1)):
            b, cond = corner[end : end + 1], corner[2 + end : 3 + end]
            cond = jnp.where(here, cond, 0.0)
            at = 6 * (2 * side + end)
            x_link, x_b, x_cond, y_link, y_b, y_cond = (
                ends_ref[at + k : at + k + 1] for k in range(6)
            )
            lacked = x_link * link(x_cond, cond) * (x_b - b)
            lacked = lacked + y_link * link(y_cond, cond) * (y_b - b)
            residual_ref[i, j : j + 1] = residual_ref[i, j : j + 1] + c1 * lacked


def call(kernel, shapes, *operands, scratch=(), inputs=pltpu.VMEM, flops=0):
    return pl.pallas_call(
        kernel,
        out_shape=[
            shape if hasattr(shape, "dtype") else jax.ShapeDtypeStruct(shape, jnp.float32)
            for shape in shapes
        ],
        in_specs=[pl.BlockSpec(memory_space=inputs)] * len(operands),
        out_specs=[pl.BlockSpec(memory_space=pltpu.VMEM)] * len(shapes),
        scratch_shapes=scratch,
        compiler_params=pltpu.CompilerParams(vmem_limit_bytes=48 * 1024 * 1024),
        cost_estimate=pl.CostEstimate(flops=flops, bytes_accessed=0, transcendentals=0),
    )(*operands)


def swap(array, axis, turn):
    nx, ny = lax.axis_size("gx"), lax.axis_size("gy")
    pairs = []
    for x in range(nx):
        for y in range(ny):
            here, count = (x, nx) if axis == "gx" else (y, ny)
            there = here + 1 if here % 2 == turn else here - 1
            if 0 <= there < count:
                partner = (there, y) if axis == "gx" else (x, there)
            else:
                partner = (x, y ^ 1) if axis == "gx" else (x ^ 1, y)
            pairs.append((x * ny + y, partner[0] * ny + partner[1]))
    return lax.ppermute(array, ("gx", "gy"), pairs)


def everyones(sketch):
    nx, ny = lax.axis_size("gx"), lax.axis_size("gy")
    middle = nx // 2 - 1, ny // 2
    places = [(x, y) for x in range(nx) for y in range(ny)]
    places.sort(key=lambda at: (abs(at[1] - middle[1]), abs(at[0] - middle[0]), at))
    group = [x * ny + y for x, y in places]
    copies = jnp.broadcast_to(sketch[None], (nx * ny,) + sketch.shape)
    return lax.all_to_all(copies, ("gx", "gy"), 0, 0, axis_index_groups=[group])


def body(b, warmth, phase, slots, draw):
    planes, rows, depth = b.shape
    block, wide = b.shape, (planes + 2, rows, depth)
    face, line, corner = (3 * rows + 4, depth), (3 * planes + 4, depth), (4, depth)
    cells = pltpu.VMEM((depth // LANES, (planes * rows + 8) * 8, LANES), jnp.float32)
    total = HIGH * 2 * PAIR, LOW
    hots = [
        jax.ShapeDtypeStruct((planes * rows * count, depth), jnp.bfloat16)
        for count in (LOW, HIGH * 2 * PAIR)
    ]
    work = b.size * SKETCH * 6
    b, cond, cap, y_link, z_link, inner, draw, slots, x_first, x_second, y_first, y_second = call(
        first_kernel,
        [block] * 8 + [face, face, line, line],
        *(
            pltpu.with_memory_space_constraint(x, pltpu.HBM)
            for x in (b, warmth, phase, draw, slots)
        ),
        scratch=[
            pltpu.VMEM(block, warmth.dtype),
            pltpu.VMEM(block, phase.dtype),
            pltpu.VMEM(block, slots.dtype),
            pltpu.SemaphoreType.DMA((5,)),
        ],
        inputs=pltpu.HBM,
    )
    got_x = swap(x_second, "gx", 1), swap(x_first, "gx", 0)
    got_y = swap(y_second, "gy", 1), swap(y_first, "gy", 0)
    *hots, b_sketch = call(
        slot_kernel, [*hots, (PAIR, SKETCH)], b, draw, slots, scratch=[cells], flops=work
    )
    image_wide, x_link, beside, inside, first = call(
        inside_kernel,
        [wide, (planes + 1, rows, depth), (4, rows, depth), total, corner],
        b, cond, cap, y_link, z_link, inner, draw, *hots, *got_x,
        scratch=[cells],
        flops=work,
    )
    image, twice, sketch, second, ends = call(
        third_kernel,
        [block, block, (FIELDS + 1, SKETCH), corner, (24, depth)],
        b, cap, y_link, z_link, draw, *hots, y_second, y_first, image_wide, x_link, beside,
        *got_x, *got_y, b_sketch, inside,
        scratch=[cells, pltpu.VMEM((3, 8, depth), jnp.float32)],
        flops=work,
    )
    got_corners = [swap(array, "gy", turn) for turn, array in enumerate((first, second))]
    sketches = everyones(sketch)
    return tuple(
        call(last_kernel, [block, block], sketches, b, image, twice, ends, *got_corners)
    )


def solution(mesh):
    spec = P(("parts", "gx"), "gy", None)
    return jax.shard_map(
        body, mesh=mesh, in_specs=(spec,) * 5, out_specs=(spec,) * 2, check_vma=False
    )
```

```python
import jax
import jax.numpy as jnp
from jax import lax
from jax.experimental import pallas as pl
from jax.experimental.pallas import tpu as pltpu
from jax.sharding import PartitionSpec as P

SKETCH = 128
LOW = 32
HIGH = SKETCH // LOW
FIELDS = 3
PAIR = 2
LANES = 128
epsilon = 1e-06


def traits(warmth, phase):
    powder, solid = phase == 0, phase == 1
    offset = jnp.where(powder, 0.2, jnp.where(solid, 1.0, 0.6))
    return offset * (0.5 + warmth), jnp.where(powder, 1.0, jnp.where(solid, 2.0, 1.5))


def link(first, second):
    total = first + second
    return 2.0 * first * second / jnp.where(total > 0.0, total, 1.0)


def ahead(plane, axis):
    return pltpu.roll(plane, plane.shape[axis] - 1, axis)


def inner_links(cond):
    links = []
    for axis in (0, 1):
        index = lax.broadcasted_iota(jnp.int32, cond.shape, axis)
        links.append(
            jnp.where(index < cond.shape[axis] - 1, link(cond, ahead(cond, axis)), 0.0)
        )
    return links


def inner_flow(field, links):
    total = None
    for axis in (0, 1):
        flow = links[axis] * (field - ahead(field, axis))
        part = flow - pltpu.roll(flow, 1, axis)
        total = part if total is None else total + part
    return total


def apply_inside(images, x_links, links, caps):
    results = []
    flow_low = x_links[0] * (images[0] - images[1])
    for i in range(1, len(images) - 1):
        image = images[i]
        flow = x_links[i] * (image - images[i + 1])
        inside = inner_flow(image, links[i - 1])
        results.append(caps[i - 1] * image + inside + (flow - flow_low))
        flow_low = flow
    return results


def parts_of(slot):
    high = jnp.floor(slot * (1.0 / LOW))
    return slot - LOW * high, high


def one_hot(values, j, count, each):
    shape = (count * each, values.shape[1])
    index = lax.broadcasted_iota(jnp.int32, shape, 0) // each
    index = index.astype(jnp.float32).astype(jnp.bfloat16)
    row = jnp.broadcast_to(values[j : j + 1], shape).astype(jnp.bfloat16)
    one = jnp.ones_like(row)
    return jnp.where(row == index, one, jnp.zeros_like(one))


def put_cells(fields, draw, start, cells_ref):
    coarse, fine = [], []
    for field in fields:
        weighted = draw * field
        head = weighted.astype(jnp.bfloat16).astype(jnp.float32)
        coarse.append(head)
        fine.append(weighted - head)
    for f, part in enumerate(coarse + fine):
        for t in range(cells_ref.shape[0]):
            cells_ref[t, pl.ds(start + f, draw.shape[0], stride=8), :] = part[
                :, t * LANES : (t + 1) * LANES
            ]


def masked_cells(mask, start, j, cells_ref):
    at = pl.ds(start + j * 8, 8)
    cells = jnp.concatenate([cells_ref[t, at, :] for t in range(cells_ref.shape[0])], axis=1)
    filled = lax.broadcasted_iota(jnp.int32, cells.shape, 0) < 2 * PAIR
    cells = jnp.where(filled, cells, pltpu.roll(cells, 2 * PAIR, 0))
    return jnp.concatenate([cells, cells], axis=0).astype(jnp.bfloat16) * mask


def product(left, right):
    return lax.dot_general(
        jnp.concatenate(left, axis=1),
        jnp.concatenate(right, axis=1),
        (((1,), (1,)), ((), ())),
        preferred_element_type=jnp.float32,
    )


def as_sketch(total):
    each = 2 * PAIR
    total = jnp.concatenate([total[h * each : (h + 1) * each] for h in range(HIGH)], axis=1)
    return total[:PAIR] + total[PAIR:]


def sketch_rows(planes, low_ref, high_ref, cells_ref):
    total = 0.0
    each = HIGH * 2 * PAIR
    for i, (fields, draw, chosen) in enumerate(planes):
        rows = draw.shape[0]
        start = i * rows * 8
        put_cells(fields, draw, start, cells_ref)
        left, right = [], []
        for j in chosen:
            at = i * rows + j
            mask = high_ref[at * each : (at + 1) * each]
            left.append(masked_cells(mask, start, j, cells_ref))
            right.append(low_ref[at * LOW : (at + 1) * LOW])
        total = total + product(left, right)
    return total


def slot_kernel(b_ref, draw_ref, slot_ref, low_ref, high_ref, sketch_ref, cells_ref):
    planes, rows = b_ref.shape[:2]
    each = HIGH * 2 * PAIR
    total = 0.0
    for i in range(planes):
        start = i * rows * 8
        put_cells((b_ref[i],) * PAIR, draw_ref[i], start, cells_ref)
        low, high = parts_of(slot_ref[i])
        left, right = [], []
        for j in range(rows):
            at = i * rows + j
            mask, hot = one_hot(high, j, HIGH, 2 * PAIR), one_hot(low, j, LOW, 1)
            high_ref[at * each : (at + 1) * each] = mask
            low_ref[at * LOW : (at + 1) * LOW] = hot
            left.append(masked_cells(mask, start, j, cells_ref))
            right.append(hot)
        total = total + product(left, right)
    sketch_ref[...] = as_sketch(total)


def first_kernel(
    b_hbm, warmth_hbm, phase_hbm, draw_hbm, slot_hbm, b_ref, cond_ref, cap_ref, y_link_ref,
    z_link_ref, inner_ref, draw_ref, slot_ref, x_first_ref, x_second_ref, y_first_ref,
    y_second_ref, warmth_ref, phase_ref, number_ref, arrived,
):
    copies = [
        pltpu.make_async_copy(source, target, arrived.at[k])
        for k, (source, target) in enumerate(
            (
                (b_hbm, b_ref),
                (warmth_hbm, warmth_ref),
                (phase_hbm, phase_ref),
                (draw_hbm, draw_ref),
                (slot_hbm, number_ref),
            )
        )
    ]
    for copy in copies:
        copy.start()
    for copy in copies[:3]:
        copy.wait()
    planes, rows = b_ref.shape[:2]
    images, conds = [], []
    for i in range(planes):
        cond, cap = traits(warmth_ref[i], phase_ref[i])
        cap_ref[i] = cap
        cond_ref[i] = cond
        y_link_ref[i], z_link_ref[i] = links = inner_links(cond)
        field = b_ref[i]
        image = cap * field + inner_flow(field, links)
        if i:
            flow = link(conds[-1], cond) * (b_ref[i - 1] - field)
            images[-1] = images[-1] + flow
            image = image - flow
        conds.append(cond)
        images.append(image)
    for i in range(planes):
        inner_ref[i] = images[i]
    for k, field in enumerate((images, [b_ref[i] for i in range(planes)], conds)):
        at = slice(k * rows, (k + 1) * rows)
        x_first_ref[at], x_second_ref[at] = by_turn(field[0], field[-1], "gx")
        for i, plane in enumerate(field):
            at = slice(k * planes + i, k * planes + i + 1)
            y_first_ref[at], y_second_ref[at] = by_turn(plane[:1], plane[rows - 1 :], "gy")
    for copy in copies[3:]:
        copy.wait()
    for i in range(planes):
        slot_ref[i] = number_ref[i].astype(jnp.float32)
    for k, ref in enumerate((draw_ref, slot_ref)):
        ends = [ref[0], ref[planes - 1]]
        for e, j in enumerate((0, rows - 1)):
            at = slice(3 * rows + 2 * k + e, 3 * rows + 2 * k + e + 1)
            lines = [plane[j : j + 1] for plane in ends]
            x_first_ref[at], x_second_ref[at] = by_turn(*lines, "gx")
        for e, plane in enumerate(ends):
            at = slice(3 * planes + 2 * k + e, 3 * planes + 2 * k + e + 1)
            lines = [plane[:1], plane[rows - 1 :]]
            y_first_ref[at], y_second_ref[at] = by_turn(*lines, "gy")


def by_turn(one, other, axis):
    odd = lax.axis_index(axis) % 2 == 1
    return jnp.where(odd, one, other), jnp.where(odd, other, one)


def has_beside(axis):
    at = lax.axis_index(axis)
    return at > 0, at < lax.axis_size(axis) - 1


def reached(rows):
    others = [j for j in range(rows) if 2 <= j < rows - 2]
    return [j for j in range(rows) if j not in others], others


def inside_kernel(
    b_ref, cond_ref, cap_ref, y_link_ref, z_link_ref, inner_ref, draw_ref, low_ref, high_ref,
    got_second_ref, got_first_ref, wide_ref, x_link_ref, beside_ref, sketch_ref, end_low_ref,
    end_high_ref, cells_ref,
):
    planes, rows = b_ref.shape[:2]
    (image_low, image_high), (b_low, b_high), (c_low, c_high) = (
        by_turn(*(ref[k * rows : (k + 1) * rows] for ref in (got_first_ref, got_second_ref)), "gx")
        for k in range(3)
    )
    below, above = has_beside("gx")
    c_low, c_high = jnp.where(below, c_low, 0.0), jnp.where(above, c_high, 0.0)
    for k, plane in enumerate((b_low, b_high, c_low, c_high)):
        beside_ref[k] = plane
    conds = [c_low] + [cond_ref[i] for i in range(planes)] + [c_high]
    x_links = [link(conds[i], conds[i + 1]) for i in range(planes + 1)]
    for i, conductance in enumerate(x_links):
        x_link_ref[i] = conductance
    low_flow = x_links[0] * (b_low - b_ref[0])
    high_flow = x_links[-1] * (b_ref[planes - 1] - b_high)
    images = [image_low + low_flow] + [inner_ref[i] for i in range(planes)]
    images.append(image_high - high_flow)
    images[1] = images[1] - low_flow
    images[-2] = images[-2] + high_flow
    for i, image in enumerate(images):
        wide_ref[i] = image
    links = [(y_link_ref[i], z_link_ref[i]) for i in range(planes)]
    twice = apply_inside(images, x_links, links, [cap_ref[i] for i in range(planes)])
    chosen = reached(rows)[1]
    cells = [((images[i + 1], twice[i]), draw_ref[i], chosen) for i in range(planes)]
    sketch_ref[...] = sketch_rows(cells, low_ref, high_ref, cells_ref)
    each = HIGH * 2 * PAIR
    tails = by_turn(got_first_ref[3 * rows :], got_second_ref[3 * rows :], "gx")
    for side in range(2):
        for end, tail in enumerate(tails):
            at = 2 * side + end
            low, high = parts_of(tail[2 + side :][:1])
            end_low_ref[at * LOW : (at + 1) * LOW] = one_hot(low, 0, LOW, 1)
            end_high_ref[at * each : (at + 1) * each] = one_hot(high, 0, HIGH, 2 * PAIR)


def third_kernel(
    b_ref, cap_ref, y_link_ref, z_link_ref, draw_ref, low_ref, high_ref, own_second_ref,
    own_first_ref, wide_ref, x_link_ref, beside_ref, x_second_ref, x_first_ref, y_second_ref,
    y_first_ref, b_sketch_ref, inside_ref, end_low_ref, end_high_ref, image_ref, twice_ref, sketch_ref, corner_first_ref,
    corner_second_ref, ends_ref, cells_ref, extra_ref,
):
    planes, rows, depth = b_ref.shape
    index = lax.broadcasted_iota(jnp.int32, (rows, depth), 0)
    images = [wide_ref[i] for i in range(planes + 2)]
    x_links = [x_link_ref[i] for i in range(planes + 1)]
    b_beside, c_beside = (beside_ref[0], beside_ref[1]), (beside_ref[2], beside_ref[3])
    x_ends = []
    for end, i in enumerate((0, planes - 1)):
        conductance = x_links[-end]
        x_ends.append((i, conductance, conductance * (b_ref[i] - b_beside[end])))
    x_tails = by_turn(x_first_ref[3 * rows :], x_second_ref[3 * rows :], "gx")
    own_lines = by_turn(own_first_ref[...], own_second_ref[...], "gy")
    y_lines = by_turn(y_first_ref[...], y_second_ref[...], "gy")
    beside = []
    for side, (j, here, own, line) in enumerate(
        zip((0, rows - 1), has_beside("gy"), own_lines, y_lines)
    ):
        row = slice(j, j + 1)
        beyond, b_line, c_line = (line[k * planes : (k + 1) * planes] for k in range(3))
        c_line = jnp.where(here, c_line, 0.0)
        y_link = link(own[2 * planes : 3 * planes], c_line)
        y_flow = y_link * (own[planes : 2 * planes] - b_line)
        beyond = beyond - y_flow
        for i in range(planes):
            at = slice(i, i + 1)
            images[i + 1] = images[i + 1] + jnp.where(index == j, y_flow[at], 0.0)
            beside.append((i, jnp.where(index == j, y_link[at], 0.0), beyond[at]))
        for end, (i, x_link, x_flow) in enumerate(x_ends):
            line_at, at = slice(i, i + 1), 2 * side + end
            tail = x_tails[end]
            values = -x_link[row] * y_flow[line_at], tail[side:][:1], tail[2 + side :][:1]
            for k, value in enumerate(values):
                extra_ref[k, at : at + 1] = value
            tail = line[3 * planes :]
            values = -y_link[line_at] * x_flow[row], tail[end:][:1], tail[2 + end :][:1]
            for k, value in enumerate(values):
                extra_ref[k, at + 4 : at + 5] = value
            at = 6 * (2 * side + end)
            values = x_link[row], b_beside[end][row], c_beside[end][row]
            values += y_link[line_at], b_line[line_at], c_line[line_at]
            for k, value in enumerate(values):
                ends_ref[at + k : at + k + 1] = value
    links = [(y_link_ref[i], z_link_ref[i]) for i in range(planes)]
    twice = apply_inside(images, x_links, links, [cap_ref[i] for i in range(planes)])
    for i, conductance, value in beside:
        twice[i] = twice[i] + conductance * (images[i + 1] - value)
    for i in range(planes):
        image_ref[i] = images[i + 1]
        twice_ref[i] = twice[i]
    chosen = reached(rows)[0]
    cells = [((images[i + 1], twice[i]), draw_ref[i], chosen) for i in range(planes)]
    total = inside_ref[...] + sketch_rows(cells, low_ref, high_ref, cells_ref)
    start = planes * rows * 8
    put_cells((jnp.zeros((8, depth), jnp.float32), extra_ref[0]), extra_ref[1], start, cells_ref)
    low, high = parts_of(extra_ref[2])
    left, right = [], []
    each = HIGH * 2 * PAIR
    for j in range(8):
        if j < 4:
            mask = end_high_ref[j * each : (j + 1) * each]
            hot = end_low_ref[j * LOW : (j + 1) * LOW]
        else:
            mask, hot = one_hot(high, j, HIGH, 2 * PAIR), one_hot(low, j, LOW, 1)
        left.append(masked_cells(mask, start, j, cells_ref))
        right.append(hot)
    sketch_ref[1 : 1 + PAIR] = as_sketch(total + product(left, right))
    sketch_ref[:1] = b_sketch_ref[:1]
    sketch_ref[1 + PAIR :] = b_sketch_ref[:1]
    for k, plane in enumerate(b_beside + c_beside):
        at = slice(k, k + 1)
        corner_first_ref[at], corner_second_ref[at] = by_turn(
            plane[:1], plane[rows - 1 :], "gy"
        )


def last_kernel(
    sketch_ref, b_ref, image_ref, twice_ref, ends_ref, corner_first_ref, corner_second_ref,
    solution_ref, residual_ref,
):
    sketches = jnp.sum(sketch_ref[...], axis=0)

    def inner(first, second):
        return jnp.sum(first * second, axis=1, keepdims=True)

    s0, s1, s2 = (sketches[i : i + 1] for i in range(FIELDS))
    beta_inverse = 1.0 / jnp.sqrt(inner(s0, s0) + epsilon)
    h00 = inner(s0, s1) * beta_inverse * beta_inverse
    q0, p0 = s0 * beta_inverse, s1 * beta_inverse
    t0 = p0 - h00 * q0
    p1 = s2 * beta_inverse - h00 * p0
    n0 = jnp.sqrt(inner(t0, t0) + epsilon)
    n0_inverse = 1.0 / n0
    h01 = inner(q0, p1) * n0_inverse
    h11 = inner(t0, p1) * n0_inverse * n0_inverse
    t1 = p1 * n0_inverse - h01 * q0 - h11 * (t0 * n0_inverse)
    n1_square = inner(t1, t1) + epsilon
    first = h00 * h00 + n0 * n0
    cross = h00 * h11 - n0 * h01
    ratio = cross / first
    c1 = -ratio / (cross * ratio + n1_square)
    c0 = h00 / first - (h00 * h01 + n0 * h11) / first * (n0 * c1) - h00 * c1
    planes, rows, depth = b_ref.shape
    for i in range(planes):
        b, image = b_ref[i], image_ref[i]
        solution_ref[i] = c0 * b + c1 * image
        residual_ref[i] = b - c0 * image - c1 * twice_ref[i]
    corners = by_turn(corner_first_ref[...], corner_second_ref[...], "gy")
    for side, (j, here, corner) in enumerate(zip((0, rows - 1), has_beside("gy"), corners)):
        for end, i in enumerate((0, planes - 1)):
            b, cond = corner[end : end + 1], corner[2 + end : 3 + end]
            cond = jnp.where(here, cond, 0.0)
            at = 6 * (2 * side + end)
            x_link, x_b, x_cond, y_link, y_b, y_cond = (
                ends_ref[at + k : at + k + 1] for k in range(6)
            )
            lacked = x_link * link(x_cond, cond) * (x_b - b)
            lacked = lacked + y_link * link(y_cond, cond) * (y_b - b)
            residual_ref[i, j : j + 1] = residual_ref[i, j : j + 1] + c1 * lacked


def call(kernel, shapes, *operands, scratch=(), inputs=pltpu.VMEM, flops=0):
    return pl.pallas_call(
        kernel,
        out_shape=[
            shape if hasattr(shape, "dtype") else jax.ShapeDtypeStruct(shape, jnp.float32)
            for shape in shapes
        ],
        in_specs=[pl.BlockSpec(memory_space=inputs)] * len(operands),
        out_specs=[pl.BlockSpec(memory_space=pltpu.VMEM)] * len(shapes),
        scratch_shapes=scratch,
        compiler_params=pltpu.CompilerParams(vmem_limit_bytes=48 * 1024 * 1024),
        cost_estimate=pl.CostEstimate(flops=flops, bytes_accessed=0, transcendentals=0),
    )(*operands)


def swap(array, axis, turn):
    nx, ny = lax.axis_size("gx"), lax.axis_size("gy")
    pairs = []
    for x in range(nx):
        for y in range(ny):
            here, count = (x, nx) if axis == "gx" else (y, ny)
            there = here + 1 if here % 2 == turn else here - 1
            if 0 <= there < count:
                partner = (there, y) if axis == "gx" else (x, there)
            else:
                partner = (x, y ^ 1) if axis == "gx" else (x ^ 1, y)
            pairs.append((x * ny + y, partner[0] * ny + partner[1]))
    return lax.ppermute(array, ("gx", "gy"), pairs)


def everyones(sketch):
    nx, ny = lax.axis_size("gx"), lax.axis_size("gy")
    middle = nx // 2 - 1, ny // 2
    places = [(x, y) for x in range(nx) for y in range(ny)]
    places.sort(key=lambda at: (abs(at[1] - middle[1]), abs(at[0] - middle[0]), at))
    group = [x * ny + y for x, y in places]
    copies = jnp.broadcast_to(sketch[None], (nx * ny,) + sketch.shape)
    return lax.all_to_all(copies, ("gx", "gy"), 0, 0, axis_index_groups=[group])


def body(b, warmth, phase, slots, draw):
    planes, rows, depth = b.shape
    block, wide = b.shape, (planes + 2, rows, depth)
    face, line, corner = (3 * rows + 4, depth), (3 * planes + 4, depth), (4, depth)
    cells = pltpu.VMEM((depth // LANES, (planes * rows + 8) * 8, LANES), jnp.float32)
    total = HIGH * 2 * PAIR, LOW
    hots = [
        jax.ShapeDtypeStruct((planes * rows * count, depth), jnp.bfloat16)
        for count in (LOW, HIGH * 2 * PAIR)
    ]
    end_hots = [
        jax.ShapeDtypeStruct((4 * count, depth), jnp.bfloat16)
        for count in (LOW, HIGH * 2 * PAIR)
    ]
    work = b.size * SKETCH * 6
    b, cond, cap, y_link, z_link, inner, draw, slots, x_first, x_second, y_first, y_second = call(
        first_kernel,
        [block] * 8 + [face, face, line, line],
        *(
            pltpu.with_memory_space_constraint(x, pltpu.HBM)
            for x in (b, warmth, phase, draw, slots)
        ),
        scratch=[
            pltpu.VMEM(block, warmth.dtype),
            pltpu.VMEM(block, phase.dtype),
            pltpu.VMEM(block, slots.dtype),
            pltpu.SemaphoreType.DMA((5,)),
        ],
        inputs=pltpu.HBM,
    )
    got_x = swap(x_second, "gx", 1), swap(x_first, "gx", 0)
    got_y = swap(y_second, "gy", 1), swap(y_first, "gy", 0)
    *hots, b_sketch = call(
        slot_kernel, [*hots, (PAIR, SKETCH)], b, draw, slots, scratch=[cells], flops=work
    )
    image_wide, x_link, beside, inside, *end_hots = call(
        inside_kernel,
        [wide, (planes + 1, rows, depth), (4, rows, depth), total, *end_hots],
        b, cond, cap, y_link, z_link, inner, draw, *hots, *got_x,
        scratch=[cells],
        flops=work,
    )
    image, twice, sketch, first, second, ends = call(
        third_kernel,
        [block, block, (FIELDS + 1, SKETCH), corner, corner, (24, depth)],
        b, cap, y_link, z_link, draw, *hots, y_second, y_first, image_wide, x_link, beside,
        *got_x, *got_y, b_sketch, inside, *end_hots,
        scratch=[cells, pltpu.VMEM((3, 8, depth), jnp.float32)],
        flops=work,
    )
    got_corners = [swap(array, "gy", turn) for turn, array in enumerate((first, second))]
    sketches = everyones(sketch)
    return tuple(
        call(last_kernel, [block, block], sketches, b, image, twice, ends, *got_corners)
    )


def solution(mesh):
    spec = P(("parts", "gx"), "gy", None)
    return jax.shard_map(
        body, mesh=mesh, in_specs=(spec,) * 5, out_specs=(spec,) * 2, check_vma=False
    )
```

```python
import jax
import jax.numpy as jnp
from jax import lax
from jax.experimental import pallas as pl
from jax.experimental.pallas import tpu as pltpu
from jax.sharding import PartitionSpec as P

SKETCH = 128
LOW = 32
HIGH = SKETCH // LOW
FIELDS = 3
PAIR = 2
LANES = 128
epsilon = 1e-06


def traits(warmth, phase):
    powder, solid = phase == 0, phase == 1
    offset = jnp.where(powder, 0.2, jnp.where(solid, 1.0, 0.6))
    return offset * (0.5 + warmth), jnp.where(powder, 1.0, jnp.where(solid, 2.0, 1.5))


def link(first, second):
    total = first + second
    return 2.0 * first * second / jnp.where(total > 0.0, total, 1.0)


def ahead(plane, axis):
    return pltpu.roll(plane, plane.shape[axis] - 1, axis)


def inner_links(cond):
    links = []
    for axis in (0, 1):
        index = lax.broadcasted_iota(jnp.int32, cond.shape, axis)
        links.append(
            jnp.where(index < cond.shape[axis] - 1, link(cond, ahead(cond, axis)), 0.0)
        )
    return links


def inner_flow(field, links):
    total = None
    for axis in (0, 1):
        flow = links[axis] * (field - ahead(field, axis))
        part = flow - pltpu.roll(flow, 1, axis)
        total = part if total is None else total + part
    return total


def apply_inside(images, x_links, links, caps):
    results = []
    flow_low = x_links[0] * (images[0] - images[1])
    for i in range(1, len(images) - 1):
        image = images[i]
        flow = x_links[i] * (image - images[i + 1])
        inside = inner_flow(image, links[i - 1])
        results.append(caps[i - 1] * image + inside + (flow - flow_low))
        flow_low = flow
    return results


def parts_of(slot):
    high = jnp.floor(slot * (1.0 / LOW))
    return slot - LOW * high, high


def one_hot(values, j, count, each):
    shape = (count * each, values.shape[1])
    index = lax.broadcasted_iota(jnp.int32, shape, 0) // each
    index = index.astype(jnp.float32).astype(jnp.bfloat16)
    row = jnp.broadcast_to(values[j : j + 1], shape).astype(jnp.bfloat16)
    one = jnp.ones_like(row)
    return jnp.where(row == index, one, jnp.zeros_like(one))


def put_cells(fields, draw, start, cells_ref):
    coarse, fine = [], []
    for field in fields:
        weighted = draw * field
        head = weighted.astype(jnp.bfloat16).astype(jnp.float32)
        coarse.append(head)
        fine.append(weighted - head)
    for f, part in enumerate(coarse + fine):
        for t in range(cells_ref.shape[0]):
            cells_ref[t, pl.ds(start + f, draw.shape[0], stride=8), :] = part[
                :, t * LANES : (t + 1) * LANES
            ]


def masked_cells(mask, start, j, cells_ref):
    at = pl.ds(start + j * 8, 8)
    cells = jnp.concatenate([cells_ref[t, at, :] for t in range(cells_ref.shape[0])], axis=1)
    filled = lax.broadcasted_iota(jnp.int32, cells.shape, 0) < 2 * PAIR
    cells = jnp.where(filled, cells, pltpu.roll(cells, 2 * PAIR, 0))
    return jnp.concatenate([cells, cells], axis=0).astype(jnp.bfloat16) * mask


def product(left, right):
    return lax.dot_general(
        jnp.concatenate(left, axis=1),
        jnp.concatenate(right, axis=1),
        (((1,), (1,)), ((), ())),
        preferred_element_type=jnp.float32,
    )


def as_sketch(total):
    each = 2 * PAIR
    total = jnp.concatenate([total[h * each : (h + 1) * each] for h in range(HIGH)], axis=1)
    return total[:PAIR] + total[PAIR:]


def sketch_rows(planes, low_ref, high_ref, cells_ref):
    total = 0.0
    each = HIGH * 2 * PAIR
    for i, (fields, draw, chosen) in enumerate(planes):
        rows = draw.shape[0]
        start = i * rows * 8
        put_cells(fields, draw, start, cells_ref)
        left, right = [], []
        for j in chosen:
            at = i * rows + j
            mask = high_ref[at * each : (at + 1) * each]
            left.append(masked_cells(mask, start, j, cells_ref))
            right.append(low_ref[at * LOW : (at + 1) * LOW])
        total = total + product(left, right)
    return total


def slot_kernel(b_ref, draw_ref, slot_ref, low_ref, high_ref, sketch_ref, cells_ref):
    planes, rows = b_ref.shape[:2]
    each = HIGH * 2 * PAIR
    total = 0.0
    for i in range(planes):
        start = i * rows * 8
        put_cells((b_ref[i],) * PAIR, draw_ref[i], start, cells_ref)
        low, high = parts_of(slot_ref[i])
        left, right = [], []
        for j in range(rows):
            at = i * rows + j
            mask, hot = one_hot(high, j, HIGH, 2 * PAIR), one_hot(low, j, LOW, 1)
            high_ref[at * each : (at + 1) * each] = mask
            low_ref[at * LOW : (at + 1) * LOW] = hot
            left.append(masked_cells(mask, start, j, cells_ref))
            right.append(hot)
        total = total + product(left, right)
    sketch_ref[...] = as_sketch(total)


def first_kernel(
    b_hbm, warmth_hbm, phase_hbm, draw_hbm, slot_hbm, b_ref, cond_ref, cap_ref, y_link_ref,
    z_link_ref, inner_ref, draw_ref, slot_ref, x_first_ref, x_second_ref, y_first_ref,
    y_second_ref, warmth_ref, phase_ref, number_ref, arrived,
):
    copies = [
        pltpu.make_async_copy(source, target, arrived.at[k])
        for k, (source, target) in enumerate(
            (
                (b_hbm, b_ref),
                (warmth_hbm, warmth_ref),
                (phase_hbm, phase_ref),
                (draw_hbm, draw_ref),
                (slot_hbm, number_ref),
            )
        )
    ]
    for copy in copies:
        copy.start()
    for copy in copies[:3]:
        copy.wait()
    planes, rows = b_ref.shape[:2]
    images, conds = [], []
    for i in range(planes):
        cond, cap = traits(warmth_ref[i], phase_ref[i])
        cap_ref[i] = cap
        cond_ref[i] = cond
        y_link_ref[i], z_link_ref[i] = links = inner_links(cond)
        field = b_ref[i]
        image = cap * field + inner_flow(field, links)
        if i:
            flow = link(conds[-1], cond) * (b_ref[i - 1] - field)
            images[-1] = images[-1] + flow
            image = image - flow
        conds.append(cond)
        images.append(image)
    for i in range(planes):
        inner_ref[i] = images[i]
    for k, field in enumerate((images, [b_ref[i] for i in range(planes)], conds)):
        at = slice(k * rows, (k + 1) * rows)
        x_first_ref[at], x_second_ref[at] = by_turn(field[0], field[-1], "gx")
        for i, plane in enumerate(field):
            at = slice(k * planes + i, k * planes + i + 1)
            y_first_ref[at], y_second_ref[at] = by_turn(plane[:1], plane[rows - 1 :], "gy")
    for copy in copies[3:]:
        copy.wait()
    for i in range(planes):
        slot_ref[i] = number_ref[i].astype(jnp.float32)
    for k, ref in enumerate((draw_ref, slot_ref)):
        ends = [ref[0], ref[planes - 1]]
        for e, j in enumerate((0, rows - 1)):
            at = slice(3 * rows + 2 * k + e, 3 * rows + 2 * k + e + 1)
            lines = [plane[j : j + 1] for plane in ends]
            x_first_ref[at], x_second_ref[at] = by_turn(*lines, "gx")
        for e, plane in enumerate(ends):
            at = slice(3 * planes + 2 * k + e, 3 * planes + 2 * k + e + 1)
            lines = [plane[:1], plane[rows - 1 :]]
            y_first_ref[at], y_second_ref[at] = by_turn(*lines, "gy")


def by_turn(one, other, axis):
    odd = lax.axis_index(axis) % 2 == 1
    return jnp.where(odd, one, other), jnp.where(odd, other, one)


def has_beside(axis):
    at = lax.axis_index(axis)
    return at > 0, at < lax.axis_size(axis) - 1


def reached(rows):
    others = [j for j in range(rows) if 2 <= j < rows - 2]
    return [j for j in range(rows) if j not in others], others


def inside_kernel(
    b_ref, cond_ref, cap_ref, y_link_ref, z_link_ref, inner_ref, draw_ref, low_ref, high_ref,
    got_second_ref, got_first_ref, wide_ref, x_link_ref, beside_ref, sketch_ref, cells_ref,
):
    planes, rows = b_ref.shape[:2]
    (image_low, image_high), (b_low, b_high), (c_low, c_high) = (
        by_turn(*(ref[k * rows : (k + 1) * rows] for ref in (got_first_ref, got_second_ref)), "gx")
        for k in range(3)
    )
    below, above = has_beside("gx")
    c_low, c_high = jnp.where(below, c_low, 0.0), jnp.where(above, c_high, 0.0)
    for k, plane in enumerate((b_low, b_high, c_low, c_high)):
        beside_ref[k] = plane
    conds = [c_low] + [cond_ref[i] for i in range(planes)] + [c_high]
    x_links = [link(conds[i], conds[i + 1]) for i in range(planes + 1)]
    for i, conductance in enumerate(x_links):
        x_link_ref[i] = conductance
    low_flow = x_links[0] * (b_low - b_ref[0])
    high_flow = x_links[-1] * (b_ref[planes - 1] - b_high)
    images = [image_low + low_flow] + [inner_ref[i] for i in range(planes)]
    images.append(image_high - high_flow)
    images[1] = images[1] - low_flow
    images[-2] = images[-2] + high_flow
    for i, image in enumerate(images):
        wide_ref[i] = image
    links = [(y_link_ref[i], z_link_ref[i]) for i in range(planes)]
    twice = apply_inside(images, x_links, links, [cap_ref[i] for i in range(planes)])
    chosen = reached(rows)[1]
    cells = [((images[i + 1], twice[i]), draw_ref[i], chosen) for i in range(planes)]
    sketch_ref[...] = sketch_rows(cells, low_ref, high_ref, cells_ref)


def third_kernel(
    b_ref, cap_ref, y_link_ref, z_link_ref, draw_ref, low_ref, high_ref, own_second_ref,
    own_first_ref, wide_ref, x_link_ref, beside_ref, x_second_ref, x_first_ref, y_second_ref,
    y_first_ref, b_sketch_ref, inside_ref, image_ref, twice_ref, sketch_ref, corner_first_ref,
    corner_second_ref, ends_ref, cells_ref, extra_ref,
):
    planes, rows, depth = b_ref.shape
    index = lax.broadcasted_iota(jnp.int32, (rows, depth), 0)
    images = [wide_ref[i] for i in range(planes + 2)]
    x_links = [x_link_ref[i] for i in range(planes + 1)]
    b_beside, c_beside = (beside_ref[0], beside_ref[1]), (beside_ref[2], beside_ref[3])
    x_ends = []
    for end, i in enumerate((0, planes - 1)):
        conductance = x_links[-end]
        x_ends.append((i, conductance, conductance * (b_ref[i] - b_beside[end])))
    x_tails = by_turn(x_first_ref[3 * rows :], x_second_ref[3 * rows :], "gx")
    own_lines = by_turn(own_first_ref[...], own_second_ref[...], "gy")
    y_lines = by_turn(y_first_ref[...], y_second_ref[...], "gy")
    beside = []
    for side, (j, here, own, line) in enumerate(
        zip((0, rows - 1), has_beside("gy"), own_lines, y_lines)
    ):
        row = slice(j, j + 1)
        beyond, b_line, c_line = (line[k * planes : (k + 1) * planes] for k in range(3))
        c_line = jnp.where(here, c_line, 0.0)
        y_link = link(own[2 * planes : 3 * planes], c_line)
        y_flow = y_link * (own[planes : 2 * planes] - b_line)
        beyond = beyond - y_flow
        for i in range(planes):
            at = slice(i, i + 1)
            images[i + 1] = images[i + 1] + jnp.where(index == j, y_flow[at], 0.0)
            beside.append((i, jnp.where(index == j, y_link[at], 0.0), beyond[at]))
        for end, (i, x_link, x_flow) in enumerate(x_ends):
            line_at, at = slice(i, i + 1), 4 * side + 2 * end
            tail = x_tails[end]
            values = -x_link[row] * y_flow[line_at], tail[side:][:1], tail[2 + side :][:1]
            for k, value in enumerate(values):
                extra_ref[k, at : at + 1] = value
            tail = line[3 * planes :]
            values = -y_link[line_at] * x_flow[row], tail[end:][:1], tail[2 + end :][:1]
            for k, value in enumerate(values):
                extra_ref[k, at + 1 : at + 2] = value
            at = 6 * (2 * side + end)
            values = x_link[row], b_beside[end][row], c_beside[end][row]
            values += y_link[line_at], b_line[line_at], c_line[line_at]
            for k, value in enumerate(values):
                ends_ref[at + k : at + k + 1] = value
    links = [(y_link_ref[i], z_link_ref[i]) for i in range(planes)]
    twice = apply_inside(images, x_links, links, [cap_ref[i] for i in range(planes)])
    for i, conductance, value in beside:
        twice[i] = twice[i] + conductance * (images[i + 1] - value)
    for i in range(planes):
        image_ref[i] = images[i + 1]
        twice_ref[i] = twice[i]
    chosen = reached(rows)[0]
    cells = [((images[i + 1], twice[i]), draw_ref[i], chosen) for i in range(planes)]
    total = inside_ref[...] + sketch_rows(cells, low_ref, high_ref, cells_ref)
    start = planes * rows * 8
    put_cells((jnp.zeros((8, depth), jnp.float32), extra_ref[0]), extra_ref[1], start, cells_ref)
    low, high = parts_of(extra_ref[2])
    left, right = [], []
    for j in range(8):
        mask = one_hot(high, j, HIGH, 2 * PAIR)
        left.append(masked_cells(mask, start, j, cells_ref))
        right.append(one_hot(low, j, LOW, 1))
    sketch_ref[1 : 1 + PAIR] = as_sketch(total + product(left, right))
    sketch_ref[:1] = b_sketch_ref[:1]
    sketch_ref[1 + PAIR :] = b_sketch_ref[:1]
    for k, plane in enumerate(b_beside + c_beside):
        at = slice(k, k + 1)
        corner_first_ref[at], corner_second_ref[at] = by_turn(
            plane[:1], plane[rows - 1 :], "gy"
        )


def last_kernel(
    sketch_ref, b_ref, image_ref, twice_ref, ends_ref, corner_first_ref, corner_second_ref,
    solution_hbm, residual_hbm, solution_ref, residual_ref, sent,
):
    sketches = jnp.sum(sketch_ref[...], axis=0)

    def inner(first, second):
        return jnp.sum(first * second, axis=1, keepdims=True)

    s0, s1, s2 = (sketches[i : i + 1] for i in range(FIELDS))
    beta_inverse = 1.0 / jnp.sqrt(inner(s0, s0) + epsilon)
    h00 = inner(s0, s1) * beta_inverse * beta_inverse
    q0, p0 = s0 * beta_inverse, s1 * beta_inverse
    t0 = p0 - h00 * q0
    p1 = s2 * beta_inverse - h00 * p0
    n0 = jnp.sqrt(inner(t0, t0) + epsilon)
    n0_inverse = 1.0 / n0
    h01 = inner(q0, p1) * n0_inverse
    h11 = inner(t0, p1) * n0_inverse * n0_inverse
    t1 = p1 * n0_inverse - h01 * q0 - h11 * (t0 * n0_inverse)
    n1_square = inner(t1, t1) + epsilon
    first = h00 * h00 + n0 * n0
    cross = h00 * h11 - n0 * h01
    ratio = cross / first
    c1 = -ratio / (cross * ratio + n1_square)
    c0 = h00 / first - (h00 * h01 + n0 * h11) / first * (n0 * c1) - h00 * c1
    planes, rows, depth = b_ref.shape
    copies = [
        pltpu.make_async_copy(source, target, sent.at[k])
        for k, (source, target) in enumerate(
            ((solution_ref, solution_hbm), (residual_ref, residual_hbm))
        )
    ]
    for i in range(planes):
        solution_ref[i] = c0 * b_ref[i] + c1 * image_ref[i]
    copies[0].start()
    for i in range(planes):
        residual_ref[i] = b_ref[i] - c0 * image_ref[i] - c1 * twice_ref[i]
    corners = by_turn(corner_first_ref[...], corner_second_ref[...], "gy")
    for side, (j, here, corner) in enumerate(zip((0, rows - 1), has_beside("gy"), corners)):
        for end, i in enumerate((0, planes - 1)):
            b, cond = corner[end : end + 1], corner[2 + end : 3 + end]
            cond = jnp.where(here, cond, 0.0)
            at = 6 * (2 * side + end)
            x_link, x_b, x_cond, y_link, y_b, y_cond = (
                ends_ref[at + k : at + k + 1] for k in range(6)
            )
            lacked = x_link * link(x_cond, cond) * (x_b - b)
            lacked = lacked + y_link * link(y_cond, cond) * (y_b - b)
            residual_ref[i, j : j + 1] = residual_ref[i, j : j + 1] + c1 * lacked
    copies[1].start()
    for copy in copies:
        copy.wait()


def call(
    kernel, shapes, *operands, scratch=(), inputs=pltpu.VMEM, outputs=pltpu.VMEM, flops=0
):
    return pl.pallas_call(
        kernel,
        out_shape=[
            shape if hasattr(shape, "dtype") else jax.ShapeDtypeStruct(shape, jnp.float32)
            for shape in shapes
        ],
        in_specs=[pl.BlockSpec(memory_space=inputs)] * len(operands),
        out_specs=[pl.BlockSpec(memory_space=outputs)] * len(shapes),
        scratch_shapes=scratch,
        compiler_params=pltpu.CompilerParams(vmem_limit_bytes=48 * 1024 * 1024),
        cost_estimate=pl.CostEstimate(flops=flops, bytes_accessed=0, transcendentals=0),
    )(*operands)


def swap(array, axis, turn):
    nx, ny = lax.axis_size("gx"), lax.axis_size("gy")
    pairs = []
    for x in range(nx):
        for y in range(ny):
            here, count = (x, nx) if axis == "gx" else (y, ny)
            there = here + 1 if here % 2 == turn else here - 1
            if 0 <= there < count:
                partner = (there, y) if axis == "gx" else (x, there)
            else:
                partner = (x, y ^ 1) if axis == "gx" else (x ^ 1, y)
            pairs.append((x * ny + y, partner[0] * ny + partner[1]))
    return lax.ppermute(array, ("gx", "gy"), pairs)


def everyones(sketch):
    nx, ny = lax.axis_size("gx"), lax.axis_size("gy")
    middle = nx // 2 - 1, ny // 2
    places = [(x, y) for x in range(nx) for y in range(ny)]
    places.sort(key=lambda at: (abs(at[1] - middle[1]), abs(at[0] - middle[0]), at))
    group = [x * ny + y for x, y in places]
    copies = jnp.broadcast_to(sketch[None], (nx * ny,) + sketch.shape)
    return lax.all_to_all(copies, ("gx", "gy"), 0, 0, axis_index_groups=[group])


def body(b, warmth, phase, slots, draw):
    planes, rows, depth = b.shape
    block, wide = b.shape, (planes + 2, rows, depth)
    face, line, corner = (3 * rows + 4, depth), (3 * planes + 4, depth), (4, depth)
    cells = pltpu.VMEM((depth // LANES, (planes * rows + 8) * 8, LANES), jnp.float32)
    total = HIGH * 2 * PAIR, LOW
    hots = [
        jax.ShapeDtypeStruct((planes * rows * count, depth), jnp.bfloat16)
        for count in (LOW, HIGH * 2 * PAIR)
    ]
    work = b.size * SKETCH * 6
    b, cond, cap, y_link, z_link, inner, draw, slots, x_first, x_second, y_first, y_second = call(
        first_kernel,
        [block] * 8 + [face, face, line, line],
        *(
            pltpu.with_memory_space_constraint(x, pltpu.HBM)
            for x in (b, warmth, phase, draw, slots)
        ),
        scratch=[
            pltpu.VMEM(block, warmth.dtype),
            pltpu.VMEM(block, phase.dtype),
            pltpu.VMEM(block, slots.dtype),
            pltpu.SemaphoreType.DMA((5,)),
        ],
        inputs=pltpu.HBM,
    )
    got_x = swap(x_second, "gx", 1), swap(x_first, "gx", 0)
    got_y = swap(y_second, "gy", 1), swap(y_first, "gy", 0)
    *hots, b_sketch = call(
        slot_kernel, [*hots, (PAIR, SKETCH)], b, draw, slots, scratch=[cells], flops=work
    )
    image_wide, x_link, beside, inside = call(
        inside_kernel,
        [wide, (planes + 1, rows, depth), (4, rows, depth), total],
        b, cond, cap, y_link, z_link, inner, draw, *hots, *got_x,
        scratch=[cells],
        flops=work,
    )
    image, twice, sketch, first, second, ends = call(
        third_kernel,
        [block, block, (FIELDS + 1, SKETCH), corner, corner, (24, depth)],
        b, cap, y_link, z_link, draw, *hots, y_second, y_first, image_wide, x_link, beside,
        *got_x, *got_y, b_sketch, inside,
        scratch=[cells, pltpu.VMEM((3, 8, depth), jnp.float32)],
        flops=work,
    )
    got_corners = [swap(array, "gy", turn) for turn, array in enumerate((first, second))]
    sketches = everyones(sketch)
    return tuple(
        call(
            last_kernel,
            [block, block],
            sketches, b, image, twice, ends, *got_corners,
            scratch=[
                pltpu.VMEM(block, jnp.float32),
                pltpu.VMEM(block, jnp.float32),
                pltpu.SemaphoreType.DMA((2,)),
            ],
            outputs=pltpu.HBM,
        )
    )


def solution(mesh):
    spec = P(("parts", "gx"), "gy", None)
    return jax.shard_map(
        body, mesh=mesh, in_specs=(spec,) * 5, out_specs=(spec,) * 2, check_vma=False
    )
```

```python
import jax
import jax.numpy as jnp
from jax import lax
from jax.experimental import pallas as pl
from jax.experimental.pallas import tpu as pltpu
from jax.sharding import PartitionSpec as P

SKETCH = 128
LOW = 32
HIGH = SKETCH // LOW
FIELDS = 3
PAIR = 2
LANES = 128
epsilon = 1e-06


def traits(warmth, phase):
    powder, solid = phase == 0, phase == 1
    offset = jnp.where(powder, 0.2, jnp.where(solid, 1.0, 0.6))
    return offset * (0.5 + warmth), jnp.where(powder, 1.0, jnp.where(solid, 2.0, 1.5))


def link(first, second):
    total = first + second
    return 2.0 * first * second / jnp.where(total > 0.0, total, 1.0)


def ahead(plane, axis):
    return pltpu.roll(plane, plane.shape[axis] - 1, axis)


def inner_links(cond):
    links = []
    for axis in (0, 1):
        index = lax.broadcasted_iota(jnp.int32, cond.shape, axis)
        links.append(
            jnp.where(index < cond.shape[axis] - 1, link(cond, ahead(cond, axis)), 0.0)
        )
    return links


def inner_flow(field, links):
    total = None
    for axis in (0, 1):
        flow = links[axis] * (field - ahead(field, axis))
        part = flow - pltpu.roll(flow, 1, axis)
        total = part if total is None else total + part
    return total


def apply_inside(images, x_links, links, caps):
    results = []
    flow_low = x_links[0] * (images[0] - images[1])
    for i in range(1, len(images) - 1):
        image = images[i]
        flow = x_links[i] * (image - images[i + 1])
        inside = inner_flow(image, links[i - 1])
        results.append(caps[i - 1] * image + inside + (flow - flow_low))
        flow_low = flow
    return results


def parts_of(slot):
    high = jnp.floor(slot * (1.0 / LOW))
    return slot - LOW * high, high


def one_hot(values, j, count, each):
    shape = (count * each, values.shape[1])
    index = lax.broadcasted_iota(jnp.int32, shape, 0) // each
    index = index.astype(jnp.float32).astype(jnp.bfloat16)
    row = jnp.broadcast_to(values[j : j + 1], shape).astype(jnp.bfloat16)
    one = jnp.ones_like(row)
    return jnp.where(row == index, one, jnp.zeros_like(one))


def put_cells(fields, draw, start, cells_ref):
    coarse, fine = [], []
    for field in fields:
        weighted = draw * field
        head = weighted.astype(jnp.bfloat16).astype(jnp.float32)
        coarse.append(head)
        fine.append(weighted - head)
    for f, part in enumerate(coarse + fine):
        for t in range(cells_ref.shape[0]):
            cells_ref[t, pl.ds(start + f, draw.shape[0], stride=8), :] = part[
                :, t * LANES : (t + 1) * LANES
            ]


def masked_cells(mask, start, j, cells_ref):
    at = pl.ds(start + j * 8, 8)
    cells = jnp.concatenate([cells_ref[t, at, :] for t in range(cells_ref.shape[0])], axis=1)
    filled = lax.broadcasted_iota(jnp.int32, cells.shape, 0) < 2 * PAIR
    cells = jnp.where(filled, cells, pltpu.roll(cells, 2 * PAIR, 0))
    return jnp.concatenate([cells, cells], axis=0).astype(jnp.bfloat16) * mask


def product(left, right):
    return lax.dot_general(
        jnp.concatenate(left, axis=1),
        jnp.concatenate(right, axis=1),
        (((1,), (1,)), ((), ())),
        preferred_element_type=jnp.float32,
    )


def as_sketch(total):
    each = 2 * PAIR
    total = jnp.concatenate([total[h * each : (h + 1) * each] for h in range(HIGH)], axis=1)
    return total[:PAIR] + total[PAIR:]


def sketch_rows(planes, low_ref, high_ref, cells_ref, left=(), right=()):
    left, right = list(left), list(right)
    each = HIGH * 2 * PAIR
    for i, (fields, draw, chosen) in enumerate(planes):
        rows = draw.shape[0]
        start = i * rows * 8
        put_cells(fields, draw, start, cells_ref)
        for j in chosen:
            at = i * rows + j
            mask = high_ref[at * each : (at + 1) * each]
            left.append(masked_cells(mask, start, j, cells_ref))
            right.append(low_ref[at * LOW : (at + 1) * LOW])
    return product(left, right)


def slot_kernel(b_ref, draw_ref, slot_ref, low_ref, high_ref, sketch_ref, cells_ref):
    planes, rows = b_ref.shape[:2]
    each = HIGH * 2 * PAIR
    total = 0.0
    for i in range(planes):
        start = i * rows * 8
        put_cells((b_ref[i],) * PAIR, draw_ref[i], start, cells_ref)
        low, high = parts_of(slot_ref[i])
        left, right = [], []
        for j in range(rows):
            at = i * rows + j
            mask, hot = one_hot(high, j, HIGH, 2 * PAIR), one_hot(low, j, LOW, 1)
            high_ref[at * each : (at + 1) * each] = mask
            low_ref[at * LOW : (at + 1) * LOW] = hot
            left.append(masked_cells(mask, start, j, cells_ref))
            right.append(hot)
        total = total + product(left, right)
    sketch_ref[...] = as_sketch(total)


def first_kernel(
    b_hbm, warmth_hbm, phase_hbm, draw_hbm, slot_hbm, b_ref, cond_ref, cap_ref, y_link_ref,
    z_link_ref, inner_ref, draw_ref, slot_ref, x_first_ref, x_second_ref, y_first_ref,
    y_second_ref, warmth_ref, phase_ref, number_ref, arrived,
):
    copies = [
        pltpu.make_async_copy(source, target, arrived.at[k])
        for k, (source, target) in enumerate(
            (
                (b_hbm, b_ref),
                (warmth_hbm, warmth_ref),
                (phase_hbm, phase_ref),
                (draw_hbm, draw_ref),
                (slot_hbm, number_ref),
            )
        )
    ]
    for copy in copies:
        copy.start()
    for copy in copies[:3]:
        copy.wait()
    planes, rows = b_ref.shape[:2]
    images, conds = [], []
    for i in range(planes):
        cond, cap = traits(warmth_ref[i], phase_ref[i])
        cap_ref[i] = cap
        cond_ref[i] = cond
        y_link_ref[i], z_link_ref[i] = links = inner_links(cond)
        field = b_ref[i]
        image = cap * field + inner_flow(field, links)
        if i:
            flow = link(conds[-1], cond) * (b_ref[i - 1] - field)
            images[-1] = images[-1] + flow
            image = image - flow
        conds.append(cond)
        images.append(image)
    for i in range(planes):
        inner_ref[i] = images[i]
    for k, field in enumerate((images, [b_ref[i] for i in range(planes)], conds)):
        at = slice(k * rows, (k + 1) * rows)
        x_first_ref[at], x_second_ref[at] = by_turn(field[0], field[-1], "gx")
        for i, plane in enumerate(field):
            at = slice(k * planes + i, k * planes + i + 1)
            y_first_ref[at], y_second_ref[at] = by_turn(plane[:1], plane[rows - 1 :], "gy")
    for copy in copies[3:]:
        copy.wait()
    for i in range(planes):
        slot_ref[i] = number_ref[i].astype(jnp.float32)
    for k, ref in enumerate((draw_ref, slot_ref)):
        ends = [ref[0], ref[planes - 1]]
        for e, j in enumerate((0, rows - 1)):
            at = slice(3 * rows + 2 * k + e, 3 * rows + 2 * k + e + 1)
            lines = [plane[j : j + 1] for plane in ends]
            x_first_ref[at], x_second_ref[at] = by_turn(*lines, "gx")
        for e, plane in enumerate(ends):
            at = slice(3 * planes + 2 * k + e, 3 * planes + 2 * k + e + 1)
            lines = [plane[:1], plane[rows - 1 :]]
            y_first_ref[at], y_second_ref[at] = by_turn(*lines, "gy")


def by_turn(one, other, axis):
    odd = lax.axis_index(axis) % 2 == 1
    return jnp.where(odd, one, other), jnp.where(odd, other, one)


def has_beside(axis):
    at = lax.axis_index(axis)
    return at > 0, at < lax.axis_size(axis) - 1


def reached(rows):
    others = [j for j in range(rows) if 2 <= j < rows - 2]
    return [j for j in range(rows) if j not in others], others


def inside_kernel(
    b_ref, cond_ref, cap_ref, y_link_ref, z_link_ref, inner_ref, draw_ref, low_ref, high_ref,
    got_second_ref, got_first_ref, wide_ref, x_link_ref, beside_ref, sketch_ref, cells_ref,
):
    planes, rows = b_ref.shape[:2]
    (image_low, image_high), (b_low, b_high), (c_low, c_high) = (
        by_turn(*(ref[k * rows : (k + 1) * rows] for ref in (got_first_ref, got_second_ref)), "gx")
        for k in range(3)
    )
    below, above = has_beside("gx")
    c_low, c_high = jnp.where(below, c_low, 0.0), jnp.where(above, c_high, 0.0)
    for k, plane in enumerate((b_low, b_high, c_low, c_high)):
        beside_ref[k] = plane
    conds = [c_low] + [cond_ref[i] for i in range(planes)] + [c_high]
    x_links = [link(conds[i], conds[i + 1]) for i in range(planes + 1)]
    for i, conductance in enumerate(x_links):
        x_link_ref[i] = conductance
    low_flow = x_links[0] * (b_low - b_ref[0])
    high_flow = x_links[-1] * (b_ref[planes - 1] - b_high)
    images = [image_low + low_flow] + [inner_ref[i] for i in range(planes)]
    images.append(image_high - high_flow)
    images[1] = images[1] - low_flow
    images[-2] = images[-2] + high_flow
    for i, image in enumerate(images):
        wide_ref[i] = image
    links = [(y_link_ref[i], z_link_ref[i]) for i in range(planes)]
    twice = apply_inside(images, x_links, links, [cap_ref[i] for i in range(planes)])
    chosen = reached(rows)[1]
    cells = [((images[i + 1], twice[i]), draw_ref[i], chosen) for i in range(planes)]
    sketch_ref[...] = sketch_rows(cells, low_ref, high_ref, cells_ref)


def third_kernel(
    b_ref, cap_ref, y_link_ref, z_link_ref, draw_ref, low_ref, high_ref, own_second_ref,
    own_first_ref, wide_ref, x_link_ref, beside_ref, x_second_ref, x_first_ref, y_second_ref,
    y_first_ref, b_sketch_ref, inside_ref, image_ref, twice_ref, sketch_ref, corner_first_ref,
    corner_second_ref, ends_ref, cells_ref, extra_ref,
):
    planes, rows, depth = b_ref.shape
    index = lax.broadcasted_iota(jnp.int32, (rows, depth), 0)
    images = [wide_ref[i] for i in range(planes + 2)]
    x_links = [x_link_ref[i] for i in range(planes + 1)]
    b_beside, c_beside = (beside_ref[0], beside_ref[1]), (beside_ref[2], beside_ref[3])
    x_ends = []
    for end, i in enumerate((0, planes - 1)):
        conductance = x_links[-end]
        x_ends.append((i, conductance, conductance * (b_ref[i] - b_beside[end])))
    x_tails = by_turn(x_first_ref[3 * rows :], x_second_ref[3 * rows :], "gx")
    own_lines = by_turn(own_first_ref[...], own_second_ref[...], "gy")
    y_lines = by_turn(y_first_ref[...], y_second_ref[...], "gy")
    beside = []
    for side, (j, here, own, line) in enumerate(
        zip((0, rows - 1), has_beside("gy"), own_lines, y_lines)
    ):
        row = slice(j, j + 1)
        beyond, b_line, c_line = (line[k * planes : (k + 1) * planes] for k in range(3))
        c_line = jnp.where(here, c_line, 0.0)
        y_link = link(own[2 * planes : 3 * planes], c_line)
        y_flow = y_link * (own[planes : 2 * planes] - b_line)
        beyond = beyond - y_flow
        for i in range(planes):
            at = slice(i, i + 1)
            images[i + 1] = images[i + 1] + jnp.where(index == j, y_flow[at], 0.0)
            beside.append((i, jnp.where(index == j, y_link[at], 0.0), beyond[at]))
        for end, (i, x_link, x_flow) in enumerate(x_ends):
            line_at, at = slice(i, i + 1), 4 * side + 2 * end
            tail = x_tails[end]
            values = -x_link[row] * y_flow[line_at], tail[side:][:1], tail[2 + side :][:1]
            for k, value in enumerate(values):
                extra_ref[k, at : at + 1] = value
            tail = line[3 * planes :]
            values = -y_link[line_at] * x_flow[row], tail[end:][:1], tail[2 + end :][:1]
            for k, value in enumerate(values):
                extra_ref[k, at + 1 : at + 2] = value
            at = 6 * (2 * side + end)
            values = x_link[row], b_beside[end][row], c_beside[end][row]
            values += y_link[line_at], b_line[line_at], c_line[line_at]
            for k, value in enumerate(values):
                ends_ref[at + k : at + k + 1] = value
    links = [(y_link_ref[i], z_link_ref[i]) for i in range(planes)]
    twice = apply_inside(images, x_links, links, [cap_ref[i] for i in range(planes)])
    for i, conductance, value in beside:
        twice[i] = twice[i] + conductance * (images[i + 1] - value)
    for i in range(planes):
        image_ref[i] = images[i + 1]
        twice_ref[i] = twice[i]
    chosen = reached(rows)[0]
    cells = [((images[i + 1], twice[i]), draw_ref[i], chosen) for i in range(planes)]
    start = planes * rows * 8
    put_cells((jnp.zeros((8, depth), jnp.float32), extra_ref[0]), extra_ref[1], start, cells_ref)
    low, high = parts_of(extra_ref[2])
    left, right = [], []
    for j in range(8):
        mask = one_hot(high, j, HIGH, 2 * PAIR)
        left.append(masked_cells(mask, start, j, cells_ref))
        right.append(one_hot(low, j, LOW, 1))
    sketch_ref[1 : 1 + PAIR] = as_sketch(
        inside_ref[...] + sketch_rows(cells, low_ref, high_ref, cells_ref, left, right)
    )
    sketch_ref[:1] = b_sketch_ref[:1]
    sketch_ref[1 + PAIR :] = b_sketch_ref[:1]
    for k, plane in enumerate(b_beside + c_beside):
        at = slice(k, k + 1)
        corner_first_ref[at], corner_second_ref[at] = by_turn(
            plane[:1], plane[rows - 1 :], "gy"
        )


def last_kernel(
    sketch_ref, b_ref, image_ref, twice_ref, ends_ref, corner_first_ref, corner_second_ref,
    solution_ref, residual_ref,
):
    sketches = jnp.sum(sketch_ref[...], axis=0)

    def inner(first, second):
        return jnp.sum(first * second, axis=1, keepdims=True)

    s0, s1, s2 = (sketches[i : i + 1] for i in range(FIELDS))
    beta_inverse = 1.0 / jnp.sqrt(inner(s0, s0) + epsilon)
    h00 = inner(s0, s1) * beta_inverse * beta_inverse
    q0, p0 = s0 * beta_inverse, s1 * beta_inverse
    t0 = p0 - h00 * q0
    p1 = s2 * beta_inverse - h00 * p0
    n0 = jnp.sqrt(inner(t0, t0) + epsilon)
    n0_inverse = 1.0 / n0
    h01 = inner(q0, p1) * n0_inverse
    h11 = inner(t0, p1) * n0_inverse * n0_inverse
    t1 = p1 * n0_inverse - h01 * q0 - h11 * (t0 * n0_inverse)
    n1_square = inner(t1, t1) + epsilon
    first = h00 * h00 + n0 * n0
    cross = h00 * h11 - n0 * h01
    ratio = cross / first
    c1 = -ratio / (cross * ratio + n1_square)
    c0 = h00 / first - (h00 * h01 + n0 * h11) / first * (n0 * c1) - h00 * c1
    planes, rows, depth = b_ref.shape
    for i in range(planes):
        b, image = b_ref[i], image_ref[i]
        solution_ref[i] = c0 * b + c1 * image
        residual_ref[i] = b - c0 * image - c1 * twice_ref[i]
    corners = by_turn(corner_first_ref[...], corner_second_ref[...], "gy")
    for side, (j, here, corner) in enumerate(zip((0, rows - 1), has_beside("gy"), corners)):
        for end, i in enumerate((0, planes - 1)):
            b, cond = corner[end : end + 1], corner[2 + end : 3 + end]
            cond = jnp.where(here, cond, 0.0)
            at = 6 * (2 * side + end)
            x_link, x_b, x_cond, y_link, y_b, y_cond = (
                ends_ref[at + k : at + k + 1] for k in range(6)
            )
            lacked = x_link * link(x_cond, cond) * (x_b - b)
            lacked = lacked + y_link * link(y_cond, cond) * (y_b - b)
            residual_ref[i, j : j + 1] = residual_ref[i, j : j + 1] + c1 * lacked


def call(kernel, shapes, *operands, scratch=(), inputs=pltpu.VMEM, flops=0):
    return pl.pallas_call(
        kernel,
        out_shape=[
            shape if hasattr(shape, "dtype") else jax.ShapeDtypeStruct(shape, jnp.float32)
            for shape in shapes
        ],
        in_specs=[pl.BlockSpec(memory_space=inputs)] * len(operands),
        out_specs=[pl.BlockSpec(memory_space=pltpu.VMEM)] * len(shapes),
        scratch_shapes=scratch,
        compiler_params=pltpu.CompilerParams(vmem_limit_bytes=48 * 1024 * 1024),
        cost_estimate=pl.CostEstimate(flops=flops, bytes_accessed=0, transcendentals=0),
    )(*operands)


def swap(array, axis, turn):
    nx, ny = lax.axis_size("gx"), lax.axis_size("gy")
    pairs = []
    for x in range(nx):
        for y in range(ny):
            here, count = (x, nx) if axis == "gx" else (y, ny)
            there = here + 1 if here % 2 == turn else here - 1
            if 0 <= there < count:
                partner = (there, y) if axis == "gx" else (x, there)
            else:
                partner = (x, y ^ 1) if axis == "gx" else (x ^ 1, y)
            pairs.append((x * ny + y, partner[0] * ny + partner[1]))
    return lax.ppermute(array, ("gx", "gy"), pairs)


def everyones(sketch):
    nx, ny = lax.axis_size("gx"), lax.axis_size("gy")
    middle = nx // 2 - 1, ny // 2
    places = [(x, y) for x in range(nx) for y in range(ny)]
    places.sort(key=lambda at: (abs(at[1] - middle[1]), abs(at[0] - middle[0]), at))
    group = [x * ny + y for x, y in places]
    copies = jnp.broadcast_to(sketch[None], (nx * ny,) + sketch.shape)
    return lax.all_to_all(copies, ("gx", "gy"), 0, 0, axis_index_groups=[group])


def body(b, warmth, phase, slots, draw):
    planes, rows, depth = b.shape
    block, wide = b.shape, (planes + 2, rows, depth)
    face, line, corner = (3 * rows + 4, depth), (3 * planes + 4, depth), (4, depth)
    cells = pltpu.VMEM((depth // LANES, (planes * rows + 8) * 8, LANES), jnp.float32)
    total = HIGH * 2 * PAIR, LOW
    hots = [
        jax.ShapeDtypeStruct((planes * rows * count, depth), jnp.bfloat16)
        for count in (LOW, HIGH * 2 * PAIR)
    ]
    work = b.size * SKETCH * 6
    b, cond, cap, y_link, z_link, inner, draw, slots, x_first, x_second, y_first, y_second = call(
        first_kernel,
        [block] * 8 + [face, face, line, line],
        *(
            pltpu.with_memory_space_constraint(x, pltpu.HBM)
            for x in (b, warmth, phase, draw, slots)
        ),
        scratch=[
            pltpu.VMEM(block, warmth.dtype),
            pltpu.VMEM(block, phase.dtype),
            pltpu.VMEM(block, slots.dtype),
            pltpu.SemaphoreType.DMA((5,)),
        ],
        inputs=pltpu.HBM,
    )
    got_x = swap(x_second, "gx", 1), swap(x_first, "gx", 0)
    got_y = swap(y_second, "gy", 1), swap(y_first, "gy", 0)
    *hots, b_sketch = call(
        slot_kernel, [*hots, (PAIR, SKETCH)], b, draw, slots, scratch=[cells], flops=work
    )
    image_wide, x_link, beside, inside = call(
        inside_kernel,
        [wide, (planes + 1, rows, depth), (4, rows, depth), total],
        b, cond, cap, y_link, z_link, inner, draw, *hots, *got_x,
        scratch=[cells],
        flops=work,
    )
    image, twice, sketch, first, second, ends = call(
        third_kernel,
        [block, block, (FIELDS + 1, SKETCH), corner, corner, (24, depth)],
        b, cap, y_link, z_link, draw, *hots, y_second, y_first, image_wide, x_link, beside,
        *got_x, *got_y, b_sketch, inside,
        scratch=[cells, pltpu.VMEM((3, 8, depth), jnp.float32)],
        flops=work,
    )
    got_corners = [swap(array, "gy", turn) for turn, array in enumerate((first, second))]
    sketches = everyones(sketch)
    return tuple(
        call(last_kernel, [block, block], sketches, b, image, twice, ends, *got_corners)
    )


def solution(mesh):
    spec = P(("parts", "gx"), "gy", None)
    return jax.shard_map(
        body, mesh=mesh, in_specs=(spec,) * 5, out_specs=(spec,) * 2, check_vma=False
    )
```

```python
import jax
import jax.numpy as jnp
from jax import lax
from jax.experimental import pallas as pl
from jax.experimental.pallas import tpu as pltpu
from jax.sharding import PartitionSpec as P

SKETCH = 128
LOW = 32
HIGH = SKETCH // LOW
FIELDS = 3
PAIR = 2
LANES = 128
epsilon = 1e-06


def traits(warmth, phase):
    powder, solid = phase == 0, phase == 1
    offset = jnp.where(powder, 0.2, jnp.where(solid, 1.0, 0.6))
    return offset * (0.5 + warmth), jnp.where(powder, 1.0, jnp.where(solid, 2.0, 1.5))


def link(first, second):
    total = first + second
    return 2.0 * first * second / jnp.where(total > 0.0, total, 1.0)


def ahead(plane, axis):
    return pltpu.roll(plane, plane.shape[axis] - 1, axis)


def inner_links(cond):
    links = []
    for axis in (0, 1):
        index = lax.broadcasted_iota(jnp.int32, cond.shape, axis)
        links.append(
            jnp.where(index < cond.shape[axis] - 1, link(cond, ahead(cond, axis)), 0.0)
        )
    return links


def inner_flow(field, links):
    total = None
    for axis in (0, 1):
        flow = links[axis] * (field - ahead(field, axis))
        part = flow - pltpu.roll(flow, 1, axis)
        total = part if total is None else total + part
    return total


def apply_inside(images, x_links, links, caps):
    results = []
    flow_low = x_links[0] * (images[0] - images[1])
    for i in range(1, len(images) - 1):
        image = images[i]
        flow = x_links[i] * (image - images[i + 1])
        inside = inner_flow(image, links[i - 1])
        results.append(caps[i - 1] * image + inside + (flow - flow_low))
        flow_low = flow
    return results


def parts_of(slot):
    high = jnp.floor(slot * (1.0 / LOW))
    return slot - LOW * high, high


def one_hot(values, j, count, each):
    shape = (count * each, values.shape[1])
    index = lax.broadcasted_iota(jnp.int32, shape, 0) // each
    index = index.astype(jnp.float32).astype(jnp.bfloat16)
    row = jnp.broadcast_to(values[j : j + 1], shape).astype(jnp.bfloat16)
    one = jnp.ones_like(row)
    return jnp.where(row == index, one, jnp.zeros_like(one))


def put_cells(fields, draw, start, cells_ref):
    coarse, fine = [], []
    for field in fields:
        weighted = draw * field
        head = weighted.astype(jnp.bfloat16).astype(jnp.float32)
        coarse.append(head)
        fine.append(weighted - head)
    for f, part in enumerate(coarse + fine):
        for t in range(cells_ref.shape[0]):
            cells_ref[t, pl.ds(start + f, draw.shape[0], stride=8), :] = part[
                :, t * LANES : (t + 1) * LANES
            ]


def masked_cells(mask, start, j, cells_ref):
    at = pl.ds(start + j * 8, 8)
    cells = jnp.concatenate([cells_ref[t, at, :] for t in range(cells_ref.shape[0])], axis=1)
    filled = lax.broadcasted_iota(jnp.int32, cells.shape, 0) < 2 * PAIR
    cells = jnp.where(filled, cells, pltpu.roll(cells, 2 * PAIR, 0))
    return jnp.concatenate([cells, cells], axis=0).astype(jnp.bfloat16) * mask


def product(left, right):
    return lax.dot_general(
        jnp.concatenate(left, axis=1),
        jnp.concatenate(right, axis=1),
        (((1,), (1,)), ((), ())),
        preferred_element_type=jnp.float32,
    )


def as_sketch(total):
    each = 2 * PAIR
    total = jnp.concatenate([total[h * each : (h + 1) * each] for h in range(HIGH)], axis=1)
    return total[:PAIR] + total[PAIR:]


def sketch_rows(planes, low_ref, high_ref, cells_ref):
    total = 0.0
    each = HIGH * 2 * PAIR
    for i, (fields, draw, chosen) in enumerate(planes):
        rows = draw.shape[0]
        start = i * rows * 8
        put_cells(fields, draw, start, cells_ref)
        left, right = [], []
        for j in chosen:
            at = i * rows + j
            mask = high_ref[at * each : (at + 1) * each]
            left.append(masked_cells(mask, start, j, cells_ref))
            right.append(low_ref[at * LOW : (at + 1) * LOW])
        total = total + product(left, right)
    return total


def slot_kernel(b_ref, draw_ref, slot_ref, low_ref, high_ref, sketch_ref, cells_ref):
    planes, rows = b_ref.shape[:2]
    each = HIGH * 2 * PAIR
    total = 0.0
    for i in range(planes):
        start = i * rows * 8
        put_cells((b_ref[i],) * PAIR, draw_ref[i], start, cells_ref)
        low, high = parts_of(slot_ref[i])
        left, right = [], []
        for j in range(rows):
            at = i * rows + j
            mask, hot = one_hot(high, j, HIGH, 2 * PAIR), one_hot(low, j, LOW, 1)
            high_ref[at * each : (at + 1) * each] = mask
            low_ref[at * LOW : (at + 1) * LOW] = hot
            left.append(masked_cells(mask, start, j, cells_ref))
            right.append(hot)
        total = total + product(left, right)
    sketch_ref[...] = as_sketch(total)


def first_kernel(
    b_hbm, warmth_hbm, phase_hbm, draw_hbm, slot_hbm, b_ref, cond_ref, cap_ref, y_link_ref,
    z_link_ref, inner_ref, draw_ref, slot_ref, x_first_ref, x_second_ref, y_first_ref,
    y_second_ref, warmth_ref, phase_ref, number_ref, arrived,
):
    copies = [
        pltpu.make_async_copy(source, target, arrived.at[k])
        for k, (source, target) in enumerate(
            (
                (b_hbm, b_ref),
                (warmth_hbm, warmth_ref),
                (phase_hbm, phase_ref),
                (draw_hbm, draw_ref),
                (slot_hbm, number_ref),
            )
        )
    ]
    for copy in copies:
        copy.start()
    for copy in copies[:3]:
        copy.wait()
    planes, rows = b_ref.shape[:2]
    images, conds = [], []
    for i in range(planes):
        cond, cap = traits(warmth_ref[i], phase_ref[i])
        cap_ref[i] = cap
        cond_ref[i] = cond
        y_link_ref[i], z_link_ref[i] = links = inner_links(cond)
        field = b_ref[i]
        image = cap * field + inner_flow(field, links)
        if i:
            flow = link(conds[-1], cond) * (b_ref[i - 1] - field)
            images[-1] = images[-1] + flow
            image = image - flow
        conds.append(cond)
        images.append(image)
    for i in range(planes):
        inner_ref[i] = images[i]
    for k, field in enumerate((images, [b_ref[i] for i in range(planes)], conds)):
        at = slice(k * rows, (k + 1) * rows)
        x_first_ref[at], x_second_ref[at] = by_turn(field[0], field[-1], "gx")
        for i, plane in enumerate(field):
            at = slice(k * planes + i, k * planes + i + 1)
            y_first_ref[at], y_second_ref[at] = by_turn(plane[:1], plane[rows - 1 :], "gy")
    for copy in copies[3:]:
        copy.wait()
    for i in range(planes):
        slot_ref[i] = number_ref[i].astype(jnp.float32)
    for k, ref in enumerate((draw_ref, slot_ref)):
        ends = [ref[0], ref[planes - 1]]
        for e, j in enumerate((0, rows - 1)):
            at = slice(3 * rows + 2 * k + e, 3 * rows + 2 * k + e + 1)
            lines = [plane[j : j + 1] for plane in ends]
            x_first_ref[at], x_second_ref[at] = by_turn(*lines, "gx")
        for e, plane in enumerate(ends):
            at = slice(3 * planes + 2 * k + e, 3 * planes + 2 * k + e + 1)
            lines = [plane[:1], plane[rows - 1 :]]
            y_first_ref[at], y_second_ref[at] = by_turn(*lines, "gy")


def by_turn(one, other, axis):
    odd = lax.axis_index(axis) % 2 == 1
    return jnp.where(odd, one, other), jnp.where(odd, other, one)


def has_beside(axis):
    at = lax.axis_index(axis)
    return at > 0, at < lax.axis_size(axis) - 1


def reached(rows):
    others = [j for j in range(rows) if 2 <= j < rows - 2]
    return [j for j in range(rows) if j not in others], others


def inside_kernel(
    b_ref, cond_ref, cap_ref, y_link_ref, z_link_ref, inner_ref, draw_ref, low_ref, high_ref,
    got_second_ref, got_first_ref, wide_ref, x_link_ref, beside_ref, sketch_ref, cells_ref,
):
    planes, rows = b_ref.shape[:2]
    (image_low, image_high), (b_low, b_high), (c_low, c_high) = (
        by_turn(*(ref[k * rows : (k + 1) * rows] for ref in (got_first_ref, got_second_ref)), "gx")
        for k in range(3)
    )
    below, above = has_beside("gx")
    c_low, c_high = jnp.where(below, c_low, 0.0), jnp.where(above, c_high, 0.0)
    for k, plane in enumerate((b_low, b_high, c_low, c_high)):
        beside_ref[k] = plane
    conds = [c_low] + [cond_ref[i] for i in range(planes)] + [c_high]
    x_links = [link(conds[i], conds[i + 1]) for i in range(planes + 1)]
    for i, conductance in enumerate(x_links):
        x_link_ref[i] = conductance
    low_flow = x_links[0] * (b_low - b_ref[0])
    high_flow = x_links[-1] * (b_ref[planes - 1] - b_high)
    images = [image_low + low_flow] + [inner_ref[i] for i in range(planes)]
    images.append(image_high - high_flow)
    images[1] = images[1] - low_flow
    images[-2] = images[-2] + high_flow
    for i, image in enumerate(images):
        wide_ref[i] = image
    links = [(y_link_ref[i], z_link_ref[i]) for i in range(planes)]
    twice = apply_inside(images, x_links, links, [cap_ref[i] for i in range(planes)])
    chosen = reached(rows)[1]
    cells = [((images[i + 1], twice[i]), draw_ref[i], chosen) for i in range(planes)]
    sketch_ref[...] = sketch_rows(cells, low_ref, high_ref, cells_ref)


def third_kernel(
    b_ref, cap_ref, y_link_ref, z_link_ref, draw_ref, low_ref, high_ref, own_second_ref,
    own_first_ref, wide_ref, x_link_ref, beside_ref, x_second_ref, x_first_ref, y_second_ref,
    y_first_ref, b_sketch_ref, inside_ref, image_ref, twice_ref, sketch_ref, corner_first_ref,
    corner_second_ref, ends_ref, cells_ref, extra_ref,
):
    planes, rows, depth = b_ref.shape
    index = lax.broadcasted_iota(jnp.int32, (rows, depth), 0)
    images = [wide_ref[i] for i in range(planes + 2)]
    x_links = [x_link_ref[i] for i in range(planes + 1)]
    b_beside, c_beside = (beside_ref[0], beside_ref[1]), (beside_ref[2], beside_ref[3])
    x_ends = []
    for end, i in enumerate((0, planes - 1)):
        conductance = x_links[-end]
        x_ends.append((i, conductance, conductance * (b_ref[i] - b_beside[end])))
    x_tails = by_turn(x_first_ref[3 * rows :], x_second_ref[3 * rows :], "gx")
    own_lines = by_turn(own_first_ref[...], own_second_ref[...], "gy")
    y_lines = by_turn(y_first_ref[...], y_second_ref[...], "gy")
    beside = []
    for side, (j, here, own, line) in enumerate(
        zip((0, rows - 1), has_beside("gy"), own_lines, y_lines)
    ):
        row = slice(j, j + 1)
        beyond, b_line, c_line = (line[k * planes : (k + 1) * planes] for k in range(3))
        c_line = jnp.where(here, c_line, 0.0)
        y_link = link(own[2 * planes : 3 * planes], c_line)
        y_flow = y_link * (own[planes : 2 * planes] - b_line)
        beyond = beyond - y_flow
        for i in range(planes):
            at = slice(i, i + 1)
            images[i + 1] = images[i + 1] + jnp.where(index == j, y_flow[at], 0.0)
            beside.append((i, jnp.where(index == j, y_link[at], 0.0), beyond[at]))
        for end, (i, x_link, x_flow) in enumerate(x_ends):
            line_at, at = slice(i, i + 1), 4 * side + 2 * end
            tail = x_tails[end]
            values = -x_link[row] * y_flow[line_at], tail[side:][:1], tail[2 + side :][:1]
            for k, value in enumerate(values):
                extra_ref[k, at : at + 1] = value
            tail = line[3 * planes :]
            values = -y_link[line_at] * x_flow[row], tail[end:][:1], tail[2 + end :][:1]
            for k, value in enumerate(values):
                extra_ref[k, at + 1 : at + 2] = value
            at = 6 * (2 * side + end)
            values = x_link[row], b_beside[end][row], c_beside[end][row]
            values += y_link[line_at], b_line[line_at], c_line[line_at]
            for k, value in enumerate(values):
                ends_ref[at + k : at + k + 1] = value
    links = [(y_link_ref[i], z_link_ref[i]) for i in range(planes)]
    twice = apply_inside(images, x_links, links, [cap_ref[i] for i in range(planes)])
    for i, conductance, value in beside:
        twice[i] = twice[i] + conductance * (images[i + 1] - value)
    for i in range(planes):
        image_ref[i] = images[i + 1]
        twice_ref[i] = twice[i]
    chosen = reached(rows)[0]
    cells = [((images[i + 1], twice[i]), draw_ref[i], chosen) for i in range(planes)]
    total = inside_ref[...] + sketch_rows(cells, low_ref, high_ref, cells_ref)
    start = planes * rows * 8
    put_cells((jnp.zeros((8, depth), jnp.float32), extra_ref[0]), extra_ref[1], start, cells_ref)
    low, high = parts_of(extra_ref[2])
    left, right = [], []
    for j in range(8):
        mask = one_hot(high, j, HIGH, 2 * PAIR)
        left.append(masked_cells(mask, start, j, cells_ref))
        right.append(one_hot(low, j, LOW, 1))
    sketch_ref[1 : 1 + PAIR] = as_sketch(total + product(left, right))
    sketch_ref[:1] = b_sketch_ref[:1]
    sketch_ref[1 + PAIR :] = b_sketch_ref[:1]
    for k, plane in enumerate(b_beside + c_beside):
        at = slice(k, k + 1)
        corner_first_ref[at], corner_second_ref[at] = by_turn(
            plane[:1], plane[rows - 1 :], "gy"
        )


def last_kernel(
    sketch_ref, b_ref, image_ref, twice_ref, ends_ref, corner_first_ref, corner_second_ref,
    solution_ref, residual_ref,
):
    sketches = jnp.sum(sketch_ref[...], axis=0)

    def inner(first, second):
        return jnp.sum(first * second, axis=1, keepdims=True)

    s0, s1, s2 = (sketches[i : i + 1] for i in range(FIELDS))
    beta_inverse = 1.0 / jnp.sqrt(inner(s0, s0) + epsilon)
    h00 = inner(s0, s1) * beta_inverse * beta_inverse
    q0, p0 = s0 * beta_inverse, s1 * beta_inverse
    t0 = p0 - h00 * q0
    p1 = s2 * beta_inverse - h00 * p0
    n0 = jnp.sqrt(inner(t0, t0) + epsilon)
    n0_inverse = 1.0 / n0
    h01 = inner(q0, p1) * n0_inverse
    h11 = inner(t0, p1) * n0_inverse * n0_inverse
    t1 = p1 * n0_inverse - h01 * q0 - h11 * (t0 * n0_inverse)
    n1_square = inner(t1, t1) + epsilon
    first = h00 * h00 + n0 * n0
    cross = h00 * h11 - n0 * h01
    ratio = cross / first
    c1 = -ratio / (cross * ratio + n1_square)
    c0 = h00 / first - (h00 * h01 + n0 * h11) / first * (n0 * c1) - h00 * c1
    planes, rows, depth = b_ref.shape
    for i in range(planes):
        b, image = b_ref[i], image_ref[i]
        solution_ref[i] = c0 * b + c1 * image
        residual_ref[i] = b - c0 * image - c1 * twice_ref[i]
    corners = by_turn(corner_first_ref[...], corner_second_ref[...], "gy")
    for side, (j, here, corner) in enumerate(zip((0, rows - 1), has_beside("gy"), corners)):
        for end, i in enumerate((0, planes - 1)):
            b, cond = corner[end : end + 1], corner[2 + end : 3 + end]
            cond = jnp.where(here, cond, 0.0)
            at = 6 * (2 * side + end)
            x_link, x_b, x_cond, y_link, y_b, y_cond = (
                ends_ref[at + k : at + k + 1] for k in range(6)
            )
            lacked = x_link * link(x_cond, cond) * (x_b - b)
            lacked = lacked + y_link * link(y_cond, cond) * (y_b - b)
            residual_ref[i, j : j + 1] = residual_ref[i, j : j + 1] + c1 * lacked


def call(kernel, shapes, *operands, scratch=(), inputs=pltpu.VMEM, flops=0):
    return pl.pallas_call(
        kernel,
        out_shape=[
            shape if hasattr(shape, "dtype") else jax.ShapeDtypeStruct(shape, jnp.float32)
            for shape in shapes
        ],
        in_specs=[pl.BlockSpec(memory_space=inputs)] * len(operands),
        out_specs=[pl.BlockSpec(memory_space=pltpu.VMEM)] * len(shapes),
        scratch_shapes=scratch,
        compiler_params=pltpu.CompilerParams(vmem_limit_bytes=48 * 1024 * 1024),
        cost_estimate=pl.CostEstimate(flops=flops, bytes_accessed=0, transcendentals=0),
    )(*operands)


def swap(array, axis, turn):
    nx, ny = lax.axis_size("gx"), lax.axis_size("gy")
    pairs = []
    for x in range(nx):
        for y in range(ny):
            here, count = (x, nx) if axis == "gx" else (y, ny)
            there = here + 1 if here % 2 == turn else here - 1
            if 0 <= there < count:
                partner = (there, y) if axis == "gx" else (x, there)
            else:
                partner = (x, y ^ 1) if axis == "gx" else (x ^ 1, y)
            pairs.append((x * ny + y, partner[0] * ny + partner[1]))
    return lax.ppermute(array, ("gx", "gy"), pairs)


def everyones(sketch):
    nx, ny = lax.axis_size("gx"), lax.axis_size("gy")
    middle = nx - 1, ny // 2
    places = [(x, y) for x in range(nx) for y in range(ny)]
    places.sort(key=lambda at: (abs(at[1] - middle[1]), abs(at[0] - middle[0]), at))
    group = [x * ny + y for x, y in places]
    copies = jnp.broadcast_to(sketch[None], (nx * ny,) + sketch.shape)
    return lax.all_to_all(copies, ("gx", "gy"), 0, 0, axis_index_groups=[group])


def body(b, warmth, phase, slots, draw):
    planes, rows, depth = b.shape
    block, wide = b.shape, (planes + 2, rows, depth)
    face, line, corner = (3 * rows + 4, depth), (3 * planes + 4, depth), (4, depth)
    cells = pltpu.VMEM((depth // LANES, (planes * rows + 8) * 8, LANES), jnp.float32)
    total = HIGH * 2 * PAIR, LOW
    hots = [
        jax.ShapeDtypeStruct((planes * rows * count, depth), jnp.bfloat16)
        for count in (LOW, HIGH * 2 * PAIR)
    ]
    work = b.size * SKETCH * 6
    b, cond, cap, y_link, z_link, inner, draw, slots, x_first, x_second, y_first, y_second = call(
        first_kernel,
        [block] * 8 + [face, face, line, line],
        *(
            pltpu.with_memory_space_constraint(x, pltpu.HBM)
            for x in (b, warmth, phase, draw, slots)
        ),
        scratch=[
            pltpu.VMEM(block, warmth.dtype),
            pltpu.VMEM(block, phase.dtype),
            pltpu.VMEM(block, slots.dtype),
            pltpu.SemaphoreType.DMA((5,)),
        ],
        inputs=pltpu.HBM,
    )
    got_x = swap(x_second, "gx", 1), swap(x_first, "gx", 0)
    got_y = swap(y_second, "gy", 1), swap(y_first, "gy", 0)
    *hots, b_sketch = call(
        slot_kernel, [*hots, (PAIR, SKETCH)], b, draw, slots, scratch=[cells], flops=work
    )
    image_wide, x_link, beside, inside = call(
        inside_kernel,
        [wide, (planes + 1, rows, depth), (4, rows, depth), total],
        b, cond, cap, y_link, z_link, inner, draw, *hots, *got_x,
        scratch=[cells],
        flops=work,
    )
    image, twice, sketch, first, second, ends = call(
        third_kernel,
        [block, block, (FIELDS + 1, SKETCH), corner, corner, (24, depth)],
        b, cap, y_link, z_link, draw, *hots, y_second, y_first, image_wide, x_link, beside,
        *got_x, *got_y, b_sketch, inside,
        scratch=[cells, pltpu.VMEM((3, 8, depth), jnp.float32)],
        flops=work,
    )
    got_corners = [swap(array, "gy", turn) for turn, array in enumerate((first, second))]
    sketches = everyones(sketch)
    return tuple(
        call(last_kernel, [block, block], sketches, b, image, twice, ends, *got_corners)
    )


def solution(mesh):
    spec = P(("parts", "gx"), "gy", None)
    return jax.shard_map(
        body, mesh=mesh, in_specs=(spec,) * 5, out_specs=(spec,) * 2, check_vma=False
    )
```
